32 devices in a mesh: ctx: 8 (over z, core), fsdp: 4 (over y, x).
Axes of the slice: x: 2, y: 2, z: 4, core: 2. Of those that a mesh axis runs over, the one named last changes fastest.
Arguments:
- tokens: bfloat16 [2048, 8, 1088], P('ctx', 'fsdp'), may hold values from -6 to 6
- cotangent: bfloat16 [2048, 8, 1088], P('ctx', 'fsdp'), may hold values from -6 to 6
- lengths: int32 [8], P('fsdp'), may hold values from 512 to 2048, as said below
- w_rows: float32 [1088, 8704], P('fsdp')
- rows_first: bfloat16 [1088, 8704], P('fsdp')
- rows_second: float32 [1088, 8704], P('fsdp'), may hold values from 204 to 819
- w_down: float32 [4352, 1088], P(None, 'fsdp'), may hold values from -0.09375 to 0.09375
- down_first: bfloat16 [4352, 1088], P(None, 'fsdp')
- down_second: float32 [4352, 1088], P(None, 'fsdp'), may hold values from 204 to 819
- vectors: float32 [12, 1088], P(None, 'fsdp')
- vec_first: bfloat16 [12, 1088], P(None, 'fsdp')
- vec_second: float32 [12, 1088], P(None, 'fsdp'), may hold values from 204 to 819
Outputs:
- output: bfloat16 [2048, 8, 1088], P('ctx', 'fsdp')
- grad_tokens: bfloat16 [2048, 8, 1088], P('ctx', 'fsdp')
- rows_moment: float32 [1088, 8704], P('fsdp')
- rows_square: float32 [1088, 8704], P('fsdp')
- rows_new: float32 [1088, 8704], P('fsdp')
- down_moment: float32 [4352, 1088], P(None, 'fsdp')
- down_square: float32 [4352, 1088], P(None, 'fsdp')
- down_new: float32 [4352, 1088], P(None, 'fsdp')
- vec_moment: float32 [12, 1088], P(None, 'fsdp')
- vec_square: float32 [12, 1088], P(None, 'fsdp')
- vec_new: float32 [12, 1088], P(None, 'fsdp')
The draws below stay inside these ranges and needn't reach their ends.
Inputs may be any that keep to these rules, and one draw needn't show every extreme that they name: `lengths`: in each group of 2 consecutive slots one slot, chosen by the seed, holds a sequence of 2048 positions; the others hold at least a quarter of 2048.
All inputs are finite; a program needn't handle non-finite values.
Results may differ from the reference program's by a relative error of at most 0.0095.
Values may be sent and summed in bfloat16 or wider, within the bound.
A program may use at most 384 MiB of HBM per device.

```python
import math
import jax
import jax.numpy as jnp
from jax import lax

D = 1088
HEADS = 17
HEAD_DIM = 64
FF = 4352
SLOTS_DEV = 2
STEP = 10
SLOT = 2048
SLOTS = 8


def draw_lengths(key, part):
    key = jax.random.fold_in(key, 11)
    drawn = jax.random.randint(key, (SLOTS,), SLOT // 4, SLOT + 1)
    picked = jax.random.randint(jax.random.fold_in(key, 1), (SLOTS // SLOTS_DEV,), 0, SLOTS_DEV)
    full = jnp.arange(SLOTS) % SLOTS_DEV == jnp.repeat(picked, SLOTS_DEV)
    return jnp.where(full, SLOT, drawn).astype(jnp.int32)


def draw_w_rows(key, part):
    key = jax.random.fold_in(key, 12)
    noise = jnp.clip(jax.random.normal(key, (D, 8 * D), jnp.float32), -6.0, 6.0)
    column = jnp.arange(8 * D)
    factor = jnp.where((column >= 3 * D) & (column < 4 * D), 4.0, 1.0) / math.sqrt(D)
    return noise * factor[None, :]


def draw_vectors(key, part):
    key = jax.random.fold_in(key, 13)
    noise = jnp.clip(jax.random.normal(key, (12, D), jnp.float32), -4.0, 4.0)
    which = jnp.arange(12)[:, None]
    gains = (which == 0) | (which == 5)
    return jnp.where(gains, 1.0 + 0.15 * noise, 0.3 * noise)


def draw_rows_first(key, part):
    key = jax.random.fold_in(key, 21)
    noise = jnp.clip(jax.random.normal(key, (D, 8 * D), jnp.float32), -4.0, 4.0)
    return (noise * (0.05 * math.sqrt(SLOT * SLOTS))).astype(jnp.bfloat16)


def draw_down_first(key, part):
    key = jax.random.fold_in(key, 22)
    noise = jnp.clip(jax.random.normal(key, (FF, D), jnp.float32), -4.0, 4.0)
    return (noise * (0.05 * math.sqrt(SLOT * SLOTS))).astype(jnp.bfloat16)


def draw_vec_first(key, part):
    key = jax.random.fold_in(key, 23)
    noise = jnp.clip(jax.random.normal(key, (12, D), jnp.float32), -4.0, 4.0)
    return (noise * (0.05 * math.sqrt(SLOT * SLOTS))).astype(jnp.bfloat16)


def steps_of(key, extent, shards, low, top_value):
    factor_of = 1.0
    for position, shards_of in shards:
        heights = jax.random.uniform(jax.random.fold_in(jax.random.fold_in(key, 6), position), (shards_of,), jnp.float32, low / len(shards), top_value / len(shards))
        factor_of = factor_of * jnp.repeat(jnp.exp(heights), extent[position] // shards_of).reshape((-1,) + (1,) * (len(extent) - 1 - position))
    return factor_of


def scatter_about(rng, dims, scale, limit, cuts=(), dtype=jnp.bfloat16):
    entries = scale * jax.random.normal(rng, dims, jnp.float32)
    if cuts:
        entries = entries * steps_of(rng, dims, cuts, -0.22, 0.18)
    return jnp.clip(entries, -limit, limit).astype(dtype)


def setup_inputs(seed: int = 0) -> dict:
    key_of = jax.random.split(jax.random.key(seed), 13)
    return {
        "tokens": scatter_about(key_of[0], (SLOT, SLOTS, D), 1.0, 6.0, ((0, 8), (1, 4))),
        "cotangent": scatter_about(key_of[1], (SLOT, SLOTS, D), 1.0, 6.0, ((0, 8), (1, 4))),
        "lengths": draw_lengths(jax.random.fold_in(key_of[12], 71), 0),
        "w_rows": draw_w_rows(jax.random.fold_in(key_of[12], 71), 0),
        "rows_first": draw_rows_first(jax.random.fold_in(key_of[12], 71), 0),
        "rows_second": jnp.clip(204.0 + 615.0 * jax.random.uniform(key_of[5], (D, 8 * D), jnp.float32) ** steps_of(key_of[5], (D, 8 * D), ((0, 4),), -0.2, 0.2), 204.0, 819.0),
        "w_down": scatter_about(key_of[6], (FF, D), FF ** -0.5, 0.09375, ((1, 4),), jnp.float32),
        "down_first": draw_down_first(jax.random.fold_in(key_of[12], 71), 0),
        "down_second": jnp.clip(204.0 + 615.0 * jax.random.uniform(key_of[8], (FF, D), jnp.float32) ** steps_of(key_of[8], (FF, D), ((1, 4),), -0.2, 0.2), 204.0, 819.0),
        "vectors": draw_vectors(jax.random.fold_in(key_of[12], 71), 0),
        "vec_first": draw_vec_first(jax.random.fold_in(key_of[12], 71), 0),
        "vec_second": jnp.clip(204.0 + 615.0 * jax.random.uniform(key_of[11], (12, D), jnp.float32) ** steps_of(key_of[11], (12, D), ((1, 4),), -0.2, 0.2), 204.0, 819.0),
    }


@jax.custom_vjp
def low(v):
    return lax.optimization_barrier(v.astype(jnp.bfloat16)).astype(jnp.float32)

@jax.custom_vjp
def low_back(v):
    return v

def low_keep(v):
    return (low(v), None)

def low_pass(kept, grad):
    return (grad,)

def back_keep(v):
    return (v, None)

def back_low(kept, grad):
    return (low(grad),)
low.defvjp(low_keep, low_pass)
low_back.defvjp(back_keep, back_low)
HIGHEST = lax.Precision.HIGHEST
MASKED = -1e+30
NORM_EPS = 1e-05
BETA_ONE = 0.9
BETA_TWO = 0.95
ADAM_EPS = 1e-08

def product(left, right):
    return jnp.dot(left, right, precision=HIGHEST, preferred_element_type=jnp.float32)

def layer_norm(rows, gain, shift):
    middle = lax.optimization_barrier(jnp.mean(rows, axis=-1, keepdims=True))
    centred = rows - middle
    spread = lax.optimization_barrier(jnp.mean(centred * centred, axis=-1, keepdims=True))
    return centred * lax.rsqrt(spread + NORM_EPS) * gain + shift

def attend(queries, key_rows, value_rows, length):
    block = math.gcd(SLOT, 512)
    count = SLOT // block
    scale = 1.0 / math.sqrt(HEAD_DIM)
    key_pos = jnp.arange(SLOT).astype(jnp.int32)

    def one_block(item):
        query_block, start = item
        scores = low_back(jnp.einsum('qhd,khd->hqk', query_block, key_rows, precision=HIGHEST) * scale)
        query_pos = start + jnp.arange(block).astype(jnp.int32)
        allowed = (key_pos[None, :] <= query_pos[:, None]) & (key_pos[None, :] < length)
        scores = jnp.where(allowed[None], scores, MASKED)
        probs = low(jax.nn.softmax(scores, axis=-1))
        return jnp.einsum('hqk,khd->qhd', probs, value_rows, precision=HIGHEST)
    starts = (jnp.arange(count) * block).astype(jnp.int32)
    blocks = queries.reshape(count, block, HEADS, HEAD_DIM)
    result = lax.map(jax.checkpoint(one_block), (blocks, starts))
    return result.reshape(SLOT, HEADS * HEAD_DIM)

def layer(inputs, w_rows, w_down, vectors, length):
    width = D
    rows_low = low(w_rows)
    down_low = low(w_down)
    vec_low = low(vectors)
    act_one = low(layer_norm(inputs, vec_low[0], vec_low[1]))
    proj = product(act_one, rows_low[:, :3 * width])
    queries = low_back(low(proj[:, :width] + vec_low[2]))
    key_rows = low_back(low(proj[:, width:2 * width]))
    value_rows = low_back(low(proj[:, 2 * width:] + vec_low[3]))
    shape = (SLOT, HEADS, HEAD_DIM)
    attended = attend(queries.reshape(shape), key_rows.reshape(shape), value_rows.reshape(shape), length)
    attended = low_back(low(attended))
    mid = inputs + low_back(product(attended, rows_low[:, 3 * width:4 * width]) + vec_low[4])
    act_two = low(layer_norm(mid, vec_low[5], vec_low[6]))
    pre_up = low_back(product(act_two, rows_low[:, 4 * width:]) + vec_low[8:12].reshape(FF))
    hidden = low(jax.nn.gelu(pre_up, approximate=False))
    return mid + low_back(product(hidden, down_low) + vec_low[7])

def adamw(weight, first, second, grad, rate, decay):
    moment = BETA_ONE * first.astype(jnp.float32) + (1.0 - BETA_ONE) * grad
    square = BETA_TWO * second + (1.0 - BETA_TWO) * grad * grad
    corrected = moment / (1.0 - BETA_ONE ** STEP)
    scaled = square / (1.0 - BETA_TWO ** STEP)
    new_weight = weight - rate * (corrected / (jnp.sqrt(scaled) + ADAM_EPS) + decay * weight)
    return (moment, square, new_weight)

def reference(tokens, cotangent, lengths, w_rows, rows_first, rows_second, w_down, down_first, down_second, vectors, vec_first, vec_second):
    positions = jnp.arange(SLOT).astype(jnp.int32)

    def per_slot(totals, item):
        slot_tokens, slot_cot, length = item

        def forward(inputs, rows_w, down_w, vecs):
            return layer(inputs, rows_w, down_w, vecs, length)
        result, back = jax.vjp(forward, slot_tokens.astype(jnp.float32), w_rows, w_down, vectors)
        valid = (positions < length).astype(jnp.float32)
        grad_in, grad_rows, grad_down, grad_vec = back(slot_cot.astype(jnp.float32) * valid[:, None])
        totals = (totals[0] + grad_rows, totals[1] + grad_down, totals[2] + grad_vec)
        return (totals, (result.astype(jnp.bfloat16), grad_in.astype(jnp.bfloat16)))
    zeros = (jnp.zeros(w_rows.shape, jnp.float32), jnp.zeros(w_down.shape, jnp.float32), jnp.zeros(vectors.shape, jnp.float32))
    items = (jnp.transpose(tokens, (1, 0, 2)), jnp.transpose(cotangent, (1, 0, 2)), lengths)
    totals, (outs, grads) = lax.scan(per_slot, zeros, items)
    output = jnp.transpose(outs, (1, 0, 2))
    grad_tokens = jnp.transpose(grads, (1, 0, 2))
    rows_moment, rows_square, rows_new = adamw(w_rows, rows_first, rows_second, totals[0], 0.03, 0.1)
    down_moment, down_square, down_new = adamw(w_down, down_first, down_second, totals[1], 0.02, 0.1)
    vec_moment, vec_square, vec_new = adamw(vectors, vec_first, vec_second, totals[2], 0.3, 0.0)
    return (output, grad_tokens, rows_moment, rows_square, rows_new, down_moment, down_square, down_new, vec_moment, vec_square, vec_new)
```

```python
import functools
import math

import jax
import jax.numpy as jnp
from jax import lax
from jax.experimental import pallas as pl
from jax.experimental.pallas import tpu as pltpu
from jax.sharding import PartitionSpec as P

HEADS = 17
HEAD_DIM = 64
FF = 4352
STEP = 10

MASKED = -1e30
NORM_EPS = 1e-05
BETA_ONE = 0.9
BETA_TWO = 0.95
ADAM_EPS = 1e-08
BF16 = jnp.bfloat16
F32 = jnp.float32


def dot(left, right, dims=((1,), (0,))):
    return lax.dot_general(left, right, (dims, ((), ())), preferred_element_type=F32)


def padded(top, rows, width):
    row = lax.broadcasted_iota(jnp.int32, (rows, width), 0)
    out = jnp.zeros((rows, width), F32)
    for index, value in enumerate(top):
        out = jnp.where(row == index, value, out)
    return out.astype(BF16)


def key_rows(lens_ref, k_ref, length):
    pos = lax.broadcasted_iota(jnp.int32, (1, length), 1)
    bias = jnp.where(pos < lens_ref[pl.program_id(0)], 0.0, MASKED)
    one = jnp.ones((1, length), F32)
    extra = padded([bias, one, one, one], HEAD_DIM, length)
    return jnp.concatenate([k_ref[0], extra], axis=0).T


def causal(block):
    key = lax.broadcasted_iota(jnp.int32, (block, block), 0)
    query = lax.broadcasted_iota(jnp.int32, (block, block), 1)
    return key <= query


def attend_kernel(block, lens_ref, q_ref, k_ref, v_ref, o_ref, low_ref, lse_ref, keys):
    length = k_ref.shape[2]
    step = pl.program_id(1)

    @pl.when(step == 0)
    def _():
        keys[...] = key_rows(lens_ref, k_ref, length)

    query = (q_ref[0].astype(F32) * (1.0 / math.sqrt(HEAD_DIM))).astype(BF16)
    query = jnp.concatenate(
        [query, padded([jnp.ones((1, block), F32)], HEAD_DIM, block)], axis=0
    )

    def one(index, state, mask):
        top, total, accum = state
        start = pl.multiple_of(index * block, block)
        scores = dot(keys[pl.ds(start, block), :], query)
        if mask is not None:
            scores = jnp.where(mask, scores, MASKED)
        new_top = jnp.maximum(top, jnp.max(scores, axis=0, keepdims=True))
        weights = jnp.exp(scores - new_top)
        factor = jnp.exp(top - new_top)
        total = total * factor + jnp.sum(weights, axis=0, keepdims=True)
        value = v_ref[0, :, pl.ds(start, block)]
        accum = accum * factor + dot(value, weights.astype(BF16))
        return new_top, total, accum

    state = (
        jnp.full((1, block), MASKED, F32),
        jnp.zeros((1, block), F32),
        jnp.zeros((HEAD_DIM, block), F32),
    )
    state = lax.fori_loop(0, step, lambda i, s: one(i, s, None), state)
    top, total, accum = one(step, state, causal(block))
    result = accum / total
    o_ref[0] = result
    low_ref[0] = result.astype(BF16)
    lse_ref[0] = top + jnp.log(total)


def attend(lens, query, key, value):
    pairs, dim, length = query.shape
    block = math.gcd(length, 512)
    whole = pl.BlockSpec((1, dim, length), lambda p, i, lens: (p, 0, 0))
    part = pl.BlockSpec((1, dim, block), lambda p, i, lens: (p, 0, i))
    return pl.pallas_call(
        functools.partial(attend_kernel, block),
        grid_spec=pltpu.PrefetchScalarGridSpec(
            num_scalar_prefetch=1,
            grid=(pairs, length // block),
            in_specs=[part, whole, whole],
            out_specs=[part, part, pl.BlockSpec((1, 1, block), lambda p, i, lens: (p, 0, i))],
            scratch_shapes=[pltpu.VMEM((length, 2 * dim), BF16)],
        ),
        out_shape=[
            jax.ShapeDtypeStruct((pairs, dim, length), F32),
            jax.ShapeDtypeStruct((pairs, dim, length), BF16),
            jax.ShapeDtypeStruct((pairs, 1, length), F32),
        ],
        compiler_params=pltpu.CompilerParams(
            dimension_semantics=("arbitrary", "arbitrary"), vmem_limit_bytes=48 * 2**20
        ),
        cost_estimate=pl.CostEstimate(
            flops=pairs * length * length * dim * 8,
            bytes_accessed=pairs * dim * length * 12,
            transcendentals=pairs * length * length // 2,
        ),
    )(lens, query, key, value)


def split_three(value):
    first = value.astype(BF16).astype(F32)
    second = (value - first).astype(BF16).astype(F32)
    third = (value - first - second).astype(BF16).astype(F32)
    return [-first, -second, -third]


def attend_back_kernel(
    block,
    lens_ref,
    q_ref,
    k_ref,
    v_ref,
    o_ref,
    lse_ref,
    grad_ref,
    dq_ref,
    dk_ref,
    dv_ref,
    keys,
    values,
    queries,
    grads,
    total,
):
    length = k_ref.shape[2]
    count = length // block
    step = pl.program_id(1)
    scale = 1.0 / math.sqrt(HEAD_DIM)

    @pl.when(step == 0)
    def _():
        keys[...] = key_rows(lens_ref, k_ref, length)
        one = jnp.ones((1, length), F32)
        extra = padded([one, one, one], HEAD_DIM, length)
        values[...] = jnp.concatenate([v_ref[0], extra], axis=0).T
        queries[0:HEAD_DIM, :] = (q_ref[0].astype(F32) * scale).astype(BF16)
        queries[HEAD_DIM:, :] = padded([one] + split_three(lse_ref[0]), HEAD_DIM, length)
        grads[0:HEAD_DIM, :] = grad_ref[0]
        delta = jnp.sum(grad_ref[0].astype(F32) * o_ref[0], axis=0, keepdims=True)
        grads[HEAD_DIM:, :] = padded(split_three(delta), HEAD_DIM, length)
        total[...] = jnp.zeros_like(total)

    mine = pl.ds(pl.multiple_of(step * block, block), block)
    key = keys[mine, :]
    value = values[mine, :]
    key_t = k_ref[0, :, mine]

    def one(index, state, mask):
        dk, dv = state
        cols = pl.ds(pl.multiple_of(index * block, block), block)
        scores = dot(key, queries[:, cols])
        if mask is not None:
            scores = jnp.where(mask, scores, MASKED)
        probs = jnp.exp(scores)
        grad_scores = (probs * dot(value, grads[:, cols])).astype(BF16)
        probs = probs.astype(BF16)
        dv = dv + dot(grads[0:HEAD_DIM, cols], probs, ((1,), (1,)))
        dk = dk + dot(queries[0:HEAD_DIM, cols], grad_scores, ((1,), (1,)))
        total[:, cols] += dot(key_t, grad_scores)
        return dk, dv

    zero = jnp.zeros((HEAD_DIM, block), F32)
    state = one(step, (zero, zero), causal(block))
    dk, dv = lax.fori_loop(step + 1, count, lambda i, s: one(i, s, None), state)
    dk_ref[0] = dk.astype(BF16)
    dv_ref[0] = dv.astype(BF16)
    dq_ref[0] = (total[:, mine] * scale).astype(BF16)


def attend_back(lens, query, key, value, out, lse, grad):
    pairs, dim, length = query.shape
    block = math.gcd(length, 512)
    whole = pl.BlockSpec((1, dim, length), lambda p, i, lens: (p, 0, 0))
    part = pl.BlockSpec((1, dim, block), lambda p, i, lens: (p, 0, i))
    line = pl.BlockSpec((1, 1, length), lambda p, i, lens: (p, 0, 0))
    shape = jax.ShapeDtypeStruct((pairs, dim, length), BF16)
    return pl.pallas_call(
        functools.partial(attend_back_kernel, block),
        grid_spec=pltpu.PrefetchScalarGridSpec(
            num_scalar_prefetch=1,
            grid=(pairs, length // block),
            in_specs=[whole, whole, whole, whole, line, whole],
            out_specs=[part, part, part],
            scratch_shapes=[
                pltpu.VMEM((length, 2 * dim), BF16),
                pltpu.VMEM((length, 2 * dim), BF16),
                pltpu.VMEM((2 * dim, length), BF16),
                pltpu.VMEM((2 * dim, length), BF16),
                pltpu.VMEM((dim, length), F32),
            ],
        ),
        out_shape=[shape, shape, shape],
        compiler_params=pltpu.CompilerParams(
            dimension_semantics=("arbitrary", "arbitrary"), vmem_limit_bytes=48 * 2**20
        ),
        cost_estimate=pl.CostEstimate(
            flops=pairs * length * length * dim * 20,
            bytes_accessed=pairs * dim * length * 18,
            transcendentals=pairs * length * length // 2,
        ),
    )(lens, query, key, value, out, lse, grad)


def bits_of(count):
    return max(count.bit_length() - 1, 0)


def flip(axis, count, value):
    return [(i, i ^ value) for i in range(count)]


def pick(array, index, axis):
    return lax.dynamic_index_in_dim(array, index, axis, keepdims=False)


def ordered(bit, mine, other, axis):
    first = jnp.where(bit == 0, mine, other)
    second = jnp.where(bit == 0, other, mine)
    return jnp.concatenate([first, second], axis=axis)


def reduce_grad(grad, ctx, fsdp):
    width, columns = grad.shape
    c, f = lax.axis_index("ctx"), lax.axis_index("fsdp")
    half = columns // 2
    core = c % 2
    mine = lax.dynamic_slice_in_dim(grad, core * half, half, 1)
    other = lax.dynamic_slice_in_dim(grad, (1 - core) * half, half, 1).astype(BF16)
    mine = mine + lax.ppermute(other, "ctx", flip("ctx", ctx, 1)).astype(F32)
    levels = bits_of(fsdp)
    rows = width // fsdp
    streams = []
    for stream in range(levels):
        low = half * stream // levels
        high = half * (stream + 1) // levels
        part = mine[:, low:high].reshape((2,) * levels + (rows, high - low))
        done = []
        for step in range(levels):
            bit = (stream + step) % levels
            axis = levels - 1 - bit - sum(1 for b in done if b > bit)
            here = (f // 2**bit) % 2
            sent = pick(part, 1 - here, axis).astype(BF16)
            got = lax.ppermute(sent, "fsdp", flip("fsdp", fsdp, 2**bit))
            part = pick(part, here, axis) + got.astype(F32)
            done.append(bit)
        streams.append(part)
    z = c // 2
    depth = bits_of(ctx) - 1
    total = jnp.concatenate(streams, axis=1)
    for bit in range(depth):
        here = (z // 2**bit) % 2
        part = total.reshape(2, total.shape[0] // 2, half)
        sent = pick(part, 1 - here, 0).astype(BF16)
        got = lax.ppermute(sent, "ctx", flip("ctx", ctx, 2 ** (bit + 1)))
        total = pick(part, here, 0) + got.astype(F32)
    total = total.astype(BF16)
    for bit in reversed(range(depth)):
        here = (z // 2**bit) % 2
        got = lax.ppermute(total, "ctx", flip("ctx", ctx, 2 ** (bit + 1)))
        total = ordered(here, total, got, 0)
    got = lax.ppermute(total, "ctx", flip("ctx", ctx, 1))
    return ordered(core, total, got, 1)


def gather_weight(piece, ctx, extra=None):
    half = piece.shape[1] // 2
    core = lax.axis_index("ctx") % 2
    mine = lax.dynamic_slice_in_dim(piece, core * half, half, 1)
    if extra is not None:
        mine = jnp.concatenate([mine, extra], axis=1)
    mine = lax.all_gather(mine, "fsdp", axis=0, tiled=True)
    rest = mine[:, half:]
    mine = mine[:, :half]
    other = lax.ppermute(mine, "ctx", flip("ctx", ctx, 1))
    return ordered(core, mine, other, 1), rest


def norm_parts(rows, axis):
    middle = jnp.mean(rows, axis=axis, keepdims=True)
    centred = rows - middle
    spread = jnp.mean(centred * centred, axis=axis, keepdims=True)
    inverse = lax.rsqrt(spread + NORM_EPS)
    return centred * inverse, inverse


def norm_back(grad, unit, inverse, gain):
    inner = grad * gain
    mean_inner = jnp.mean(inner, axis=1, keepdims=True)
    mean_cross = jnp.mean(inner * unit, axis=1, keepdims=True)
    rows = inverse * (inner - mean_inner - unit * mean_cross)
    return rows, jnp.sum(grad * unit, axis=(0, 2)), jnp.sum(grad, axis=(0, 2))


def adamw(weight, first, second, grad, rate, decay):
    moment = BETA_ONE * first.astype(F32) + (1.0 - BETA_ONE) * grad
    square = BETA_TWO * second + (1.0 - BETA_TWO) * grad * grad
    corrected = moment / (1.0 - BETA_ONE**STEP)
    scaled = square / (1.0 - BETA_TWO**STEP)
    new_weight = weight - rate * (corrected / (jnp.sqrt(scaled) + ADAM_EPS) + decay * weight)
    return (moment, square, new_weight)


def body(
    ctx,
    fsdp,
    tokens,
    cotangent,
    lengths,
    w_rows,
    rows_first,
    rows_second,
    w_down,
    down_first,
    down_second,
    vectors,
    vec_first,
    vec_second,
):
    tok, slots, width = tokens.shape
    length = tok * ctx
    dim = HEAD_DIM
    regular = HEADS // ctx
    owned = regular + 1
    pairs = slots * regular + 1
    c = lax.axis_index("ctx")
    late = (c >= ctx // 2).astype(jnp.int32)
    owner_of = [0, ctx // 2]

    x_low = tokens.transpose(1, 2, 0)
    x_all = lax.all_gather(x_low, "ctx", axis=0)

    low_rows = w_rows.astype(BF16)
    vec_part = jnp.pad(vectors.astype(BF16).T, ((0, 0), (0, 128 - vectors.shape[0])))
    head_w, vec_low = gather_weight(low_rows[:, : 4 * width], ctx, vec_part)
    up_w, _ = gather_weight(low_rows[:, 4 * width :], ctx)
    down_w, _ = gather_weight(w_down.T.astype(BF16), ctx)
    vec = [vec_low[:, i : i + 1].astype(F32) for i in range(12)]
    up_bias = jnp.concatenate(vec[8:12], axis=0)

    unit_all, _ = norm_parts(x_all.astype(F32), 2)
    act_all = (unit_all * vec[0] + vec[1]).astype(BF16)
    starts = [(i * ctx + c) * dim for i in range(regular)] + [(HEADS - 1) * dim]
    own_w = jnp.concatenate(
        [
            lax.dynamic_slice_in_dim(head_w, part * width + start, dim, 1)
            for part in range(3)
            for start in starts
        ],
        axis=1,
    )
    q_bias = jnp.concatenate([lax.dynamic_slice_in_dim(vec[2], s, dim, 0) for s in starts], axis=0)
    v_bias = jnp.concatenate([lax.dynamic_slice_in_dim(vec[3], s, dim, 0) for s in starts], axis=0)
    own_bias = jnp.concatenate([q_bias, jnp.zeros_like(q_bias), v_bias], axis=0)
    proj = jnp.einsum("dm,csdt->smct", own_w, act_all, preferred_element_type=F32)
    proj = (proj + own_bias[None, :, :, None]).astype(BF16)
    proj = proj.reshape(slots, 3, owned, dim, length)

    def pair_up(array):
        head = array[:, :regular].reshape(slots * regular, dim, length)
        last = pick(array[:, regular], late, 0)
        return jnp.concatenate([head, last[None]], axis=0)

    query, key, value = (pair_up(proj[:, part]) for part in range(3))
    lens = jnp.concatenate(
        [jnp.repeat(lengths, regular), lax.dynamic_slice_in_dim(lengths, late, 1, 0)]
    )
    out, out_low, lse = attend(lens, query, key, value)

    def to_rows(array):
        feat = array.shape[1]
        sent = array.reshape(pairs, feat, ctx, tok).transpose(2, 0, 1, 3)
        got = lax.all_to_all(sent, "ctx", 0, 0)
        head = got[:, :-1].reshape(ctx, slots, regular, feat, tok).transpose(1, 2, 0, 3, 4)
        head = head.reshape(slots, regular * ctx, feat, tok)
        last = jnp.stack([got[owner_of[s], -1] for s in range(slots)])[:, None]
        return jnp.concatenate([head, last], axis=1)

    def to_pairs(array):
        array = array.reshape(slots, HEADS, dim, tok)
        head = array[:, :-1].reshape(slots, regular, ctx, dim, tok).transpose(2, 0, 1, 3, 4)
        head = head.reshape(ctx, slots * regular, dim, tok)
        last = jnp.repeat(array[:, -1], ctx // slots, axis=0)[:, None]
        got = lax.all_to_all(jnp.concatenate([head, last], axis=1), "ctx", 0, 0)
        return got.transpose(1, 2, 0, 3).reshape(pairs, dim, length)

    att = to_rows(out_low).reshape(slots, width, tok)

    x = x_low.astype(F32)
    out_w = head_w[:, 3 * width :]
    mid = x + jnp.einsum("de,sdt->set", out_w, att, preferred_element_type=F32) + vec[4]
    unit_two, inverse_two = norm_parts(mid, 1)
    act_two = (unit_two * vec[5] + vec[6]).astype(BF16)
    pre_up = jnp.einsum("df,sdt->sft", up_w, act_two, preferred_element_type=F32) + up_bias
    cdf = 0.5 * (1.0 + lax.erf(pre_up * math.sqrt(0.5)))
    hidden = (pre_up * cdf).astype(BF16)
    slope = cdf + pre_up * jnp.exp(-0.5 * pre_up * pre_up) * (1.0 / math.sqrt(2.0 * math.pi))
    result = mid + jnp.einsum("df,sft->sdt", down_w, hidden, preferred_element_type=F32) + vec[7]
    output = result.astype(BF16).transpose(2, 0, 1)

    pos = c * tok + jnp.arange(tok, dtype=jnp.int32)
    valid = pos[None, None, :] < lengths[:, None, None]
    g_low = jnp.where(valid, cotangent.transpose(1, 2, 0), jnp.zeros((), BF16))
    g = g_low.astype(F32)
    grad_hidden = jnp.einsum("df,sdt->sft", down_w, g_low, preferred_element_type=F32)
    grad_pre = (grad_hidden * slope).astype(BF16)
    grad_two = jnp.einsum("df,sft->sdt", up_w, grad_pre, preferred_element_type=F32)
    grad_mid, gain_two, shift_two = norm_back(grad_two, unit_two, inverse_two, vec[5])
    grad_mid = g + grad_mid
    grad_attn = grad_mid.astype(BF16)
    grad_att = jnp.einsum("de,set->sdt", out_w, grad_attn, preferred_element_type=F32).astype(BF16)

    grad_pairs = to_pairs(grad_att)
    down_grad = jnp.einsum("sdt,sft->df", g_low, hidden, preferred_element_type=F32)
    up_grad = jnp.einsum("sdt,sft->df", act_two, grad_pre, preferred_element_type=F32)
    out_grad = jnp.einsum("sdt,set->de", att, grad_attn, preferred_element_type=F32)
    down_sum = reduce_grad(down_grad, ctx, fsdp)
    up_sum = reduce_grad(up_grad, ctx, fsdp)
    out_sum = reduce_grad(out_grad, ctx, fsdp)

    dq, dk, dv = attend_back(lens, query, key, value, out, lse, grad_pairs)
    joined = jnp.concatenate([dq, dk, dv], axis=1)
    grad_qkv = to_rows(joined).reshape(slots, HEADS, 3, dim, tok).transpose(0, 2, 1, 3, 4)
    grad_qkv = grad_qkv.reshape(slots, 3 * width, tok)

    last_mask = jnp.stack([c == owner_of[s] for s in range(slots)])[:, None, None]
    head = joined[:-1].reshape(slots, regular * 3 * dim, length)
    last = jnp.where(last_mask, joined[-1][None], jnp.zeros((), BF16))
    own_grad = jnp.concatenate([head, last], axis=1).reshape(slots, owned * 3 * dim, ctx, tok)
    own_sum = jnp.einsum("csdt,smct->dm", act_all, own_grad, preferred_element_type=F32)
    own_sum = lax.psum_scatter(own_sum, "fsdp", scatter_dimension=0, tiled=True).astype(BF16)
    own_all = lax.all_gather(own_sum, "ctx", axis=0)
    rows = own_all.shape[1]
    own_all = own_all.reshape(ctx, rows, owned, 3, dim).astype(F32)
    head = own_all[:, :, :regular].transpose(1, 3, 2, 0, 4).reshape(rows, 3, regular * ctx, dim)
    last = (own_all[owner_of[0], :, regular] + own_all[owner_of[1], :, regular])[:, :, None]
    qkv_sum = jnp.concatenate([head, last], axis=2).reshape(rows, 3 * width)

    grad_one = jnp.einsum(
        "de,set->sdt", head_w[:, : 3 * width], grad_qkv, preferred_element_type=F32
    )
    unit_one, inverse_one = norm_parts(x, 1)
    grad_in, gain_one, shift_one = norm_back(grad_one, unit_one, inverse_one, vec[0])
    grad_tokens = (grad_mid + grad_in).astype(BF16).transpose(2, 0, 1)

    bias_qkv = jnp.sum(grad_qkv.astype(F32), axis=(0, 2))
    vec_grad = jnp.stack(
        [
            gain_one,
            shift_one,
            bias_qkv[:width],
            bias_qkv[2 * width :],
            jnp.sum(grad_attn.astype(F32), axis=(0, 2)),
            gain_two,
            shift_two,
            jnp.sum(g, axis=(0, 2)),
        ]
    )
    bias_up = jnp.sum(grad_pre.astype(F32), axis=(0, 2)).reshape(4, width)
    vec_grad = jnp.concatenate([vec_grad, bias_up], axis=0)
    vec_sum = lax.psum(vec_grad, ("ctx", "fsdp"))
    vec_sum = lax.dynamic_slice_in_dim(
        vec_sum, lax.axis_index("fsdp") * (width // fsdp), width // fsdp, 1
    )

    rows_sum = jnp.concatenate([qkv_sum, out_sum.astype(F32), up_sum.astype(F32)], axis=1)
    rows_out = adamw(w_rows, rows_first, rows_second, rows_sum, 0.03, 0.1)
    down_out = adamw(
        w_down.T, down_first.T, down_second.T, down_sum.astype(F32), 0.02, 0.1
    )
    down_out = tuple(part.T for part in down_out)
    vec_out = adamw(vectors, vec_first, vec_second, vec_sum, 0.3, 0.0)
    return (output, grad_tokens, *rows_out, *down_out, *vec_out)


def solution(mesh):
    placed = (
        P("ctx", "fsdp", None),
        P("ctx", "fsdp", None),
        P("fsdp"),
        P("fsdp", None),
        P("fsdp", None),
        P("fsdp", None),
        P(None, "fsdp"),
        P(None, "fsdp"),
        P(None, "fsdp"),
        P(None, "fsdp"),
        P(None, "fsdp"),
        P(None, "fsdp"),
    )
    return jax.shard_map(
        functools.partial(body, mesh.shape["ctx"], mesh.shape["fsdp"]),
        mesh=mesh,
        in_specs=placed,
        out_specs=placed[:2] + placed[3:6] + placed[6:9] + placed[9:12],
        check_vma=False,
    )
```

```python
import functools
import math

import jax
import jax.numpy as jnp
from jax import lax
from jax.experimental import pallas as pl
from jax.experimental.pallas import tpu as pltpu
from jax.sharding import PartitionSpec as P

HEADS = 17
HEAD_DIM = 64
FF = 4352
STEP = 10

MASKED = -1e30
NORM_EPS = 1e-05
BETA_ONE = 0.9
BETA_TWO = 0.95
ADAM_EPS = 1e-08
BF16 = jnp.bfloat16
F32 = jnp.float32


def dot(left, right, dims=((1,), (0,))):
    return lax.dot_general(left, right, (dims, ((), ())), preferred_element_type=F32)


def padded(top, rows, width):
    row = lax.broadcasted_iota(jnp.int32, (rows, width), 0)
    out = jnp.zeros((rows, width), F32)
    for index, value in enumerate(top):
        out = jnp.where(row == index, value, out)
    return out.astype(BF16)


def key_rows(lens_ref, key, length):
    pos = lax.broadcasted_iota(jnp.int32, (1, length), 1)
    bias = jnp.where(pos < lens_ref[pl.program_id(0)], 0.0, MASKED)
    one = jnp.ones((1, length), F32)
    extra = padded([bias, one, one, one], HEAD_DIM, length)
    return jnp.concatenate([key, extra], axis=0).T


def causal(block):
    key = lax.broadcasted_iota(jnp.int32, (block, block), 0)
    query = lax.broadcasted_iota(jnp.int32, (block, block), 1)
    return key <= query


def attend_kernel(block, lens_ref, slot_ref, q_ref, k_ref, v_ref, o_ref, low_ref, lse_ref, keys):
    length = k_ref.shape[-1]
    tok = low_ref.shape[-1]
    step = pl.program_id(1)

    @pl.when(step == 0)
    def _():
        keys[...] = key_rows(lens_ref, k_ref[0, 0, 0], length)

    query = (q_ref[0, 0, 0].astype(F32) * (1.0 / math.sqrt(HEAD_DIM))).astype(BF16)
    query = jnp.concatenate(
        [query, padded([jnp.ones((1, block), F32)], HEAD_DIM, block)], axis=0
    )

    def one(index, state, mask):
        top, total, accum = state
        start = pl.multiple_of(index * block, block)
        scores = dot(keys[pl.ds(start, block), :], query)
        if mask is not None:
            scores = jnp.where(mask, scores, MASKED)
        new_top = jnp.maximum(top, jnp.max(scores, axis=0, keepdims=True))
        weights = jnp.exp(scores - new_top)
        factor = jnp.exp(top - new_top)
        total = total * factor + jnp.sum(weights, axis=0, keepdims=True)
        value = v_ref[0, 0, 0, :, pl.ds(start, block)]
        accum = accum * factor + dot(value, weights.astype(BF16))
        return new_top, total, accum

    state = (
        jnp.full((1, block), MASKED, F32),
        jnp.zeros((1, block), F32),
        jnp.zeros((HEAD_DIM, block), F32),
    )
    state = lax.fori_loop(0, step, lambda i, s: one(i, s, None), state)
    top, total, accum = one(step, state, causal(block))
    result = accum / total
    o_ref[0] = result
    for i in range(block // tok):
        low_ref[i, 0] = result[:, i * tok : (i + 1) * tok].astype(BF16)
    lse_ref[0] = top + jnp.log(total)


def pair_specs(pairs, owned, dim, length, block):
    def of(part, p, slot):
        last = p == pairs - 1
        return slot[p], part, jnp.where(last, owned - 1, lax.rem(p, owned - 1)), 0

    def whole(part):
        return pl.BlockSpec(
            (1, 1, 1, dim, length), lambda p, i, lens, slot: (*of(part, p, slot), 0)
        )

    def piece(part):
        return pl.BlockSpec(
            (1, 1, 1, dim, block), lambda p, i, lens, slot: (*of(part, p, slot), i)
        )

    return whole, piece


def attend(lens, slot, qkv, tok):
    owned, dim, length = qkv.shape[2:]
    pairs = lens.shape[0]
    block = math.gcd(length, 512)
    whole, piece = pair_specs(pairs, owned, dim, length, block)
    return pl.pallas_call(
        functools.partial(attend_kernel, block),
        grid_spec=pltpu.PrefetchScalarGridSpec(
            num_scalar_prefetch=2,
            grid=(pairs, length // block),
            in_specs=[piece(0), whole(1), whole(2)],
            out_specs=[
                pl.BlockSpec((1, dim, block), lambda p, i, lens, slot: (p, 0, i)),
                pl.BlockSpec((block // tok, 1, dim, tok), lambda p, i, lens, slot: (i, p, 0, 0)),
                pl.BlockSpec((1, 1, block), lambda p, i, lens, slot: (p, 0, i)),
            ],
            scratch_shapes=[pltpu.VMEM((length, 2 * dim), BF16)],
        ),
        out_shape=[
            jax.ShapeDtypeStruct((pairs, dim, length), F32),
            jax.ShapeDtypeStruct((length // tok, pairs, dim, tok), BF16),
            jax.ShapeDtypeStruct((pairs, 1, length), F32),
        ],
        compiler_params=pltpu.CompilerParams(
            dimension_semantics=("arbitrary", "arbitrary"), vmem_limit_bytes=48 * 2**20
        ),
        cost_estimate=pl.CostEstimate(
            flops=pairs * length * length * dim * 8,
            bytes_accessed=pairs * dim * length * 12,
            transcendentals=pairs * length * length // 2,
        ),
    )(lens, slot, qkv, qkv, qkv)


def split_three(value):
    first = value.astype(BF16).astype(F32)
    second = (value - first).astype(BF16).astype(F32)
    third = (value - first - second).astype(BF16).astype(F32)
    return [-first, -second, -third]


def attend_back_kernel(
    block,
    lens_ref,
    slot_ref,
    q_ref,
    k_ref,
    v_ref,
    o_ref,
    lse_ref,
    grad_ref,
    out_ref,
    keys,
    values,
    queries,
    grads,
    total,
):
    length = k_ref.shape[-1]
    tok = grad_ref.shape[-1]
    count = length // block
    step = pl.program_id(1)
    scale = 1.0 / math.sqrt(HEAD_DIM)

    @pl.when(step == 0)
    def _():
        keys[...] = key_rows(lens_ref, k_ref[0, 0, 0], length)
        one = jnp.ones((1, length), F32)
        extra = padded([one, one, one], HEAD_DIM, length)
        values[...] = jnp.concatenate([v_ref[0, 0, 0], extra], axis=0).T
        queries[0:HEAD_DIM, :] = (q_ref[0, 0, 0].astype(F32) * scale).astype(BF16)
        queries[HEAD_DIM:, :] = padded([one] + split_three(lse_ref[0]), HEAD_DIM, length)
        for i in range(length // tok):
            grads[0:HEAD_DIM, i * tok : (i + 1) * tok] = grad_ref[i, 0]
        delta = jnp.sum(grads[0:HEAD_DIM, :].astype(F32) * o_ref[0], axis=0, keepdims=True)
        grads[HEAD_DIM:, :] = padded(split_three(delta), HEAD_DIM, length)
        total[...] = jnp.zeros_like(total)

    mine = pl.ds(pl.multiple_of(step * block, block), block)
    key = keys[mine, :]
    value = values[mine, :]
    key_t = k_ref[0, 0, 0, :, mine]

    def one(index, state, mask):
        dk, dv = state
        cols = pl.ds(pl.multiple_of(index * block, block), block)
        scores = dot(key, queries[:, cols])
        if mask is not None:
            scores = jnp.where(mask, scores, MASKED)
        probs = jnp.exp(scores)
        grad_scores = (probs * dot(value, grads[:, cols])).astype(BF16)
        probs = probs.astype(BF16)
        dv = dv + dot(grads[0:HEAD_DIM, cols], probs, ((1,), (1,)))
        dk = dk + dot(queries[0:HEAD_DIM, cols], grad_scores, ((1,), (1,)))
        total[:, cols] += dot(key_t, grad_scores)
        return dk, dv

    zero = jnp.zeros((HEAD_DIM, block), F32)
    state = one(step, (zero, zero), causal(block))
    dk, dv = lax.fori_loop(step + 1, count, lambda i, s: one(i, s, None), state)
    dq = total[:, mine] * scale
    for i in range(block // tok):
        cols = slice(i * tok, (i + 1) * tok)
        out_ref[i, 0, 0:HEAD_DIM] = dq[:, cols].astype(BF16)
        out_ref[i, 0, HEAD_DIM : 2 * HEAD_DIM] = dk[:, cols].astype(BF16)
        out_ref[i, 0, 2 * HEAD_DIM :] = dv[:, cols].astype(BF16)


def attend_back(lens, slot, qkv, out, lse, grad):
    owned, dim, length = qkv.shape[2:]
    pairs, tok = lens.shape[0], grad.shape[-1]
    ctx = length // tok
    block = math.gcd(length, 512)
    whole, _ = pair_specs(pairs, owned, dim, length, block)
    return pl.pallas_call(
        functools.partial(attend_back_kernel, block),
        grid_spec=pltpu.PrefetchScalarGridSpec(
            num_scalar_prefetch=2,
            grid=(pairs, length // block),
            in_specs=[
                whole(0),
                whole(1),
                whole(2),
                pl.BlockSpec((1, dim, length), lambda p, i, lens, slot: (p, 0, 0)),
                pl.BlockSpec((1, 1, length), lambda p, i, lens, slot: (p, 0, 0)),
                pl.BlockSpec((ctx, 1, dim, tok), lambda p, i, lens, slot: (0, p, 0, 0)),
            ],
            out_specs=pl.BlockSpec(
                (block // tok, 1, 3 * dim, tok), lambda p, i, lens, slot: (i, p, 0, 0)
            ),
            scratch_shapes=[
                pltpu.VMEM((length, 2 * dim), BF16),
                pltpu.VMEM((length, 2 * dim), BF16),
                pltpu.VMEM((2 * dim, length), BF16),
                pltpu.VMEM((2 * dim, length), BF16),
                pltpu.VMEM((dim, length), F32),
            ],
        ),
        out_shape=jax.ShapeDtypeStruct((ctx, pairs, 3 * dim, tok), BF16),
        compiler_params=pltpu.CompilerParams(
            dimension_semantics=("arbitrary", "arbitrary"), vmem_limit_bytes=48 * 2**20
        ),
        cost_estimate=pl.CostEstimate(
            flops=pairs * length * length * dim * 20,
            bytes_accessed=pairs * dim * length * 18,
            transcendentals=pairs * length * length // 2,
        ),
    )(lens, slot, qkv, qkv, qkv, out, lse, grad)


def project_kernel(x_ref, w_ref, bias_ref, gain_ref, shift_ref, act_ref, out_ref):
    unit, _ = norm_parts(x_ref[0, 0].astype(F32), 0)
    act = (unit * gain_ref[...] + shift_ref[...]).astype(BF16)
    act_ref[0, 0] = act
    out_ref[0] = (dot(w_ref[...], act) + bias_ref[...]).astype(BF16)


def project(x_all, weight, bias, gain, shift):
    ctx, slots, width, tok = x_all.shape
    feat = weight.shape[0]
    block = pl.BlockSpec((1, 1, width, tok), lambda i, s: (i, s, 0, 0))

    def fixed(shape):
        return pl.BlockSpec(shape, lambda i, s: (0, 0))

    return pl.pallas_call(
        project_kernel,
        grid=(ctx, slots),
        in_specs=[
            block,
            fixed((feat, width)),
            fixed((feat, 1)),
            fixed((width, 1)),
            fixed((width, 1)),
        ],
        out_specs=[block, pl.BlockSpec((1, feat, tok), lambda i, s: (s, 0, i))],
        out_shape=[
            jax.ShapeDtypeStruct(x_all.shape, BF16),
            jax.ShapeDtypeStruct((slots, feat, ctx * tok), BF16),
        ],
        compiler_params=pltpu.CompilerParams(vmem_limit_bytes=48 * 2**20),
        cost_estimate=pl.CostEstimate(
            flops=2 * feat * width * ctx * slots * tok,
            bytes_accessed=4 * x_all.size,
            transcendentals=0,
        ),
    )(x_all, weight, bias, gain, shift)


def mlp_kernel(
    width,
    a_ref,
    g_ref,
    up_ref,
    down_ref,
    bias_ref,
    y_ref,
    ga_ref,
    dup_ref,
    ddown_ref,
    db_ref,
    a_rows,
    g_rows,
):
    step = pl.program_id(0)
    slots, _, tok = a_ref.shape
    block = up_ref.shape[1]

    @pl.when(step == 0)
    def _():
        for s in range(slots):
            a_rows[s * tok : (s + 1) * tok, :] = a_ref[s].T
            g_rows[s * tok : (s + 1) * tok, :] = g_ref[s].T
        y_ref[...] = jnp.zeros_like(y_ref)
        ga_ref[...] = jnp.zeros_like(ga_ref)

    def run(size):
        up = up_ref[:, :size]
        down = down_ref[:, :size]
        pre = dot(a_rows[...], up) + bias_ref[:, :size]
        cdf = 0.5 * (1.0 + lax.erf(pre * math.sqrt(0.5)))
        hidden = (pre * cdf).astype(BF16)
        slope = cdf + pre * jnp.exp(-0.5 * pre * pre) * (1.0 / math.sqrt(2.0 * math.pi))
        grad = (dot(g_rows[...], down) * slope).astype(BF16)
        db_ref[:, :size] = jnp.sum(grad.astype(F32), axis=0, keepdims=True)
        nt = ((1,), (1,))
        for s in range(slots):
            rows = slice(s * tok, (s + 1) * tok)
            y_ref[s] += dot(down, hidden[rows], nt)
            ga_ref[s] += dot(up, grad[rows], nt)
        dup = sum(dot(a_ref[s], grad[s * tok : (s + 1) * tok]) for s in range(slots))
        dup_ref[:, :size] = dup.astype(dup_ref.dtype)
        ddown = sum(dot(g_ref[s], hidden[s * tok : (s + 1) * tok]) for s in range(slots))
        ddown_ref[:, :size] = ddown.astype(ddown_ref.dtype)

    full = width // block

    @pl.when(step < full)
    def _():
        run(block)

    if width % block:

        @pl.when(step == full)
        def _():
            run(width % block)


def mlp(act, grad, up, down, bias, low):
    slots, width, tok = act.shape
    units = up.shape[1]
    block = 256
    kind = BF16 if low else F32

    def fixed(shape):
        return pl.BlockSpec(shape, lambda i: (0,) * len(shape))

    cols = pl.BlockSpec((width, block), lambda i: (0, i))
    line = pl.BlockSpec((1, block), lambda i: (0, i))
    total = jax.ShapeDtypeStruct((slots, width, tok), F32)
    grads = jax.ShapeDtypeStruct((width, units), kind)
    return pl.pallas_call(
        functools.partial(mlp_kernel, units),
        grid=(pl.cdiv(units, block),),
        in_specs=[fixed(act.shape), fixed(act.shape), cols, cols, line],
        out_specs=[fixed(act.shape), fixed(act.shape), cols, cols, line],
        out_shape=[total, total, grads, grads, jax.ShapeDtypeStruct((1, units), F32)],
        scratch_shapes=[pltpu.VMEM((slots * tok, width), BF16)] * 2,
        compiler_params=pltpu.CompilerParams(vmem_limit_bytes=56 * 2**20),
        cost_estimate=pl.CostEstimate(
            flops=12 * slots * tok * width * units,
            bytes_accessed=12 * width * units + 12 * act.size,
            transcendentals=2 * slots * tok * units,
        ),
    )(act, grad, up, down, bias)


def other_index(index, bit):
    return index + bit * (1 - 2 * lax.rem(index // bit, 2))


def split_columns(start, size, count):
    tiles = size // 128
    cuts = [start + 128 * (-(-tiles * i // count)) for i in range(count)] + [start + size]
    return [(cuts[i], cuts[i + 1] - cuts[i]) for i in range(count)]


def gather_kernel(
    ctx,
    fsdp,
    x_ref,
    w_ref,
    v_ref,
    xo_ref,
    wo_ref,
    vo_ref,
    x_send,
    x_recv,
    xc_send,
    xc_recv,
    w_send,
    w_recv,
    wc_send,
    wc_recv,
    v_send,
    v_recv,
    local,
):
    c, f = lax.axis_index("ctx"), lax.axis_index("fsdp")
    chips = ctx // 2
    z, core = c // 2, lax.rem(c, 2)
    partner = 2 * z + 1 - core
    slots = x_ref.shape[0]
    levels = bits_of(fsdp)
    half = w_ref.shape[1] // 2

    def combine(number):
        place = f
        for bit in range(levels):
            if number & (1 << bit):
                place = other_index(place, 1 << bit)
        return place

    barrier = pltpu.get_barrier_semaphore()

    def greet(where):
        pl.semaphore_signal(barrier, inc=1, device_id=where, device_id_type=pl.DeviceIdType.MESH)

    greet((partner, f))
    for number in range(1, fsdp):
        greet((c, combine(number)))

    @pl.when(z > 0)
    def _():
        greet((c - 2, f))

    @pl.when(z < chips - 1)
    def _():
        greet((c + 2, f))

    beside = (z > 0).astype(jnp.int32) + (z < chips - 1).astype(jnp.int32)
    pl.semaphore_wait(barrier, fsdp + beside)

    def remote(source, target, send, recv, where):
        return pltpu.make_async_remote_copy(
            src_ref=source,
            dst_ref=target,
            send_sem=send,
            recv_sem=recv,
            device_id=where,
            device_id_type=pl.DeviceIdType.MESH,
        )

    def x_copy(side, s, h):
        sign = 1 - 2 * side
        block = c - 2 * sign * s
        source = x_ref.at[h] if s == 0 else xo_ref.at[block, h]
        return remote(
            source, xo_ref.at[block, h], x_send.at[side, s, h], x_recv.at[side, s, h], (c + 2 * sign, f)
        )

    def x_sends(side, s):
        return (z - s >= 0) & (z < chips - 1) if side == 0 else (z + s < chips) & (z > 0)

    def x_gets(side, s):
        return z - 1 - s >= 0 if side == 0 else z + 1 + s < chips

    def x_arrival(side, s, h):
        sign = 1 - 2 * side
        block = c - 2 * sign * (s + 1)
        return remote(
            xo_ref.at[block, h],
            xo_ref.at[block, h],
            x_send.at[side, s, h],
            x_recv.at[side, s, h],
            (c + 2 * sign, f),
        )

    def x_share(side, s, h):
        sign = 1 - 2 * side
        block = c - 2 * sign * (s + 1)
        return remote(
            xo_ref.at[block, h],
            xo_ref.at[block, h],
            xc_send.at[side, s, h],
            xc_recv.at[side, s, h],
            (partner, f),
        )

    def x_share_arrival(side, s, h):
        sign = 1 - 2 * side
        block = partner - 2 * sign * (s + 1)
        return remote(
            xo_ref.at[block, h],
            xo_ref.at[block, h],
            xc_send.at[side, s, h],
            xc_recv.at[side, s, h],
            (partner, f),
        )

    def x_own(h):
        return remote(
            x_ref.at[h],
            xo_ref.at[c, h],
            xc_send.at[0, chips - 1, h],
            xc_recv.at[0, chips - 1, h],
            (partner, f),
        )

    def x_own_arrival(h):
        return remote(
            x_ref.at[h],
            xo_ref.at[partner, h],
            xc_send.at[0, chips - 1, h],
            xc_recv.at[0, chips - 1, h],
            (partner, f),
        )

    runs = split_columns(0, half, levels)

    def columns(stream, which):
        start, size = runs[stream]
        return pl.ds(pl.multiple_of(which * half + start, 128), size)

    def w_copy(stream, step, number):
        cols = columns(stream, core)
        bit = 1 << ((stream + step) % levels)
        place = combine(number)
        source = w_ref.at[:, cols] if number == 0 else wo_ref.at[place, :, cols]
        return remote(
            source,
            wo_ref.at[place, :, cols],
            w_send.at[stream, number | bit],
            w_recv.at[stream, number | bit],
            (c, other_index(f, bit)),
        )

    def w_arrival(stream, number):
        block = wo_ref.at[combine(number), :, columns(stream, core)]
        return remote(
            block, block, w_send.at[stream, number], w_recv.at[stream, number], (partner, f)
        )

    def w_share(stream, number):
        block = wo_ref.at[combine(number), :, columns(stream, core)]
        return remote(
            block, block, wc_send.at[stream, number], wc_recv.at[stream, number], (partner, f)
        )

    def w_share_arrival(stream, number):
        block = wo_ref.at[combine(number), :, columns(stream, 1 - core)]
        return remote(
            block, block, wc_send.at[stream, number], wc_recv.at[stream, number], (partner, f)
        )

    def held(stream, step):
        numbers = [0]
        for i in range(step):
            bit = 1 << ((stream + i) % levels)
            numbers += [n | bit for n in numbers]
        return numbers

    def v_copy(number):
        return remote(
            v_ref, vo_ref.at[f], v_send.at[number], v_recv.at[number], (c, combine(number))
        )

    def v_arrival(number):
        return remote(
            v_ref,
            vo_ref.at[combine(number)],
            v_send.at[number],
            v_recv.at[number],
            (c, combine(number)),
        )

    sides = [(side, h) for h in range(slots) for side in range(2)]
    for side, h in sides:

        @pl.when(x_sends(side, 0))
        def _(side=side, h=h):
            x_copy(side, 0, h).start()

    for stream in range(levels):
        w_copy(stream, 0, 0).start()
    for number in range(1, fsdp):
        v_copy(number).start()
    for h in range(slots):
        x_own(h).start()
    own = [
        pltpu.make_async_copy(x_ref, xo_ref.at[c], local.at[0]),
        pltpu.make_async_copy(w_ref, wo_ref.at[f], local.at[1]),
        pltpu.make_async_copy(v_ref, vo_ref.at[f], local.at[2]),
    ]
    for copy in own:
        copy.start()

    for s in range(max(chips - 1, levels)):
        if s < chips - 1:
            for side, h in sides:

                @pl.when(x_gets(side, s))
                def _(side=side, h=h, s=s):
                    x_arrival(side, s, h).wait_recv()
                    x_share(side, s, h).start()

                if s + 1 < chips - 1:

                    @pl.when(x_sends(side, s + 1))
                    def _(side=side, h=h, s=s):
                        x_copy(side, s + 1, h).start()

        if s < levels:
            for stream in range(levels):
                bit = 1 << ((stream + s) % levels)
                arrived = [number | bit for number in held(stream, s)]
                for number in arrived:
                    w_arrival(stream, number).wait_recv()
                if s + 1 < levels:
                    for number in held(stream, s + 1):
                        w_copy(stream, s + 1, number).start()
                for number in arrived:
                    w_share(stream, number).start()

    for copy in own:
        copy.wait()
    for number in range(1, fsdp):
        v_copy(number).wait_send()
        v_arrival(number).wait_recv()
        for stream in range(levels):
            w_arrival(stream, number).wait_send()
            w_share(stream, number).wait_send()
            w_share_arrival(stream, number).wait_recv()
    for h in range(slots):
        x_own(h).wait_send()
        x_own_arrival(h).wait_recv()
    for s in range(chips - 1):
        for side, h in sides:

            @pl.when(x_sends(side, s))
            def _(side=side, h=h, s=s):
                x_copy(side, s, h).wait_send()

            @pl.when(x_gets(side, s))
            def _(side=side, h=h, s=s):
                x_share(side, s, h).wait_send()
                x_share_arrival(side, s, h).wait_recv()


def gather_first(ctx, fsdp, x, w, v):
    slots = x.shape[0]
    levels, chips = bits_of(fsdp), ctx // 2
    anywhere = pl.BlockSpec(memory_space=pl.ANY)
    dma = pltpu.SemaphoreType.DMA
    return pl.pallas_call(
        functools.partial(gather_kernel, ctx, fsdp),
        in_specs=[anywhere] * 3,
        out_specs=[anywhere] * 3,
        out_shape=[
            jax.ShapeDtypeStruct((ctx,) + x.shape, x.dtype),
            jax.ShapeDtypeStruct((fsdp,) + w.shape, w.dtype),
            jax.ShapeDtypeStruct((fsdp,) + v.shape, v.dtype),
        ],
        scratch_shapes=[
            dma((2, chips - 1, slots)),
            dma((2, chips - 1, slots)),
            dma((2, chips, slots)),
            dma((2, chips, slots)),
            dma((levels, fsdp)),
            dma((levels, fsdp)),
            dma((levels, fsdp)),
            dma((levels, fsdp)),
            dma((fsdp,)),
            dma((fsdp,)),
            dma((3,)),
        ],
        compiler_params=pltpu.CompilerParams(collective_id=0, has_side_effects=True),
        cost_estimate=pl.CostEstimate(flops=0, bytes_accessed=200_000_000, transcendentals=0),
    )(x, w, v)


def bits_of(count):
    return max(count.bit_length() - 1, 0)


def flip(count, value):
    return [(i, i ^ value) for i in range(count)]


def pick(array, index, axis):
    return lax.dynamic_index_in_dim(array, index, axis, keepdims=False)


def ordered(bit, mine, other, axis):
    first = jnp.where(bit == 0, mine, other)
    second = jnp.where(bit == 0, other, mine)
    return jnp.concatenate([first, second], axis=axis)


def add_cores(mine, other, ctx):
    return mine + lax.ppermute(other, "ctx", flip(ctx, 1)).astype(F32)


def scatter_fsdp(grad, fsdp):
    f = lax.axis_index("fsdp")
    levels = bits_of(fsdp)
    rows = grad.shape[0] // fsdp
    result = []
    for stream, (start, size) in enumerate(split_columns(0, grad.shape[1], levels)):
        part = grad[:, start : start + size].reshape((2,) * levels + (rows, size))
        done = []
        for step in range(levels):
            bit = (stream + step) % levels
            axis = levels - 1 - bit - sum(1 for b in done if b > bit)
            here = (f // 2**bit) % 2
            sent = pick(part, 1 - here, axis).astype(BF16)
            got = lax.ppermute(sent, "fsdp", flip(fsdp, 2**bit))
            part = pick(part, here, axis) + got.astype(F32)
            done.append(bit)
        result.append(part)
    return jnp.concatenate(result, axis=1)


def sum_chips(part, ctx):
    chips = ctx // 2
    z = lax.axis_index("ctx") // 2
    if part.shape[0] % chips:
        blocks = part.reshape(chips, 1, part.size // chips)
    else:
        blocks = part.reshape(chips, part.shape[0] // chips, part.shape[1])
    total = pick(blocks, z, 0)
    for value in range(1, chips):
        sent = pick(blocks, z ^ value, 0).astype(BF16)
        total = total + lax.ppermute(sent, "ctx", flip(ctx, 2 * value)).astype(F32)
    return gather_chips(total.astype(BF16), ctx).reshape(part.shape)


def gather_chips(mine, ctx):
    z = lax.axis_index("ctx") // 2
    every = [mine]
    for value in range(1, ctx // 2):
        every.append(lax.ppermute(mine, "ctx", flip(ctx, 2 * value)))
    every = jnp.stack(every)
    return jnp.stack([pick(every, z ^ i, 0) for i in range(ctx // 2)])


def swap_cores(mine, ctx):
    return lax.ppermute(mine, "ctx", flip(ctx, 1))


def norm_parts(rows, axis):
    middle = jnp.mean(rows, axis=axis, keepdims=True)
    centred = rows - middle
    spread = jnp.mean(centred * centred, axis=axis, keepdims=True)
    inverse = lax.rsqrt(spread + NORM_EPS)
    return centred * inverse, inverse


def norm_back(grad, unit, inverse, gain):
    inner = grad * gain
    mean_inner = jnp.mean(inner, axis=1, keepdims=True)
    mean_cross = jnp.mean(inner * unit, axis=1, keepdims=True)
    rows = inverse * (inner - mean_inner - unit * mean_cross)
    return rows, jnp.sum(grad * unit, axis=(0, 2)), jnp.sum(grad, axis=(0, 2))


def adamw(weight, first, second, grad, rate, decay):
    moment = BETA_ONE * first.astype(F32) + (1.0 - BETA_ONE) * grad
    square = BETA_TWO * second + (1.0 - BETA_TWO) * grad * grad
    corrected = moment / (1.0 - BETA_ONE**STEP)
    scaled = square / (1.0 - BETA_TWO**STEP)
    new_weight = weight - rate * (corrected / (jnp.sqrt(scaled) + ADAM_EPS) + decay * weight)
    return (moment, square, new_weight)


def body(
    ctx,
    fsdp,
    tokens,
    cotangent,
    lengths,
    w_rows,
    rows_first,
    rows_second,
    w_down,
    down_first,
    down_second,
    vectors,
    vec_first,
    vec_second,
):
    tok, slots, width = tokens.shape
    dim = HEAD_DIM
    regular = HEADS // ctx
    owned = regular + 1
    pairs = slots * regular + 1
    share = width // fsdp
    c = lax.axis_index("ctx")
    core = c % 2
    late = (c >= ctx // 2).astype(jnp.int32)
    half = FF // 2

    def my_half(array):
        return lax.dynamic_slice_in_dim(array, core * half, half, 1)

    x_low = tokens.transpose(1, 2, 0)
    vec_part = jnp.pad(vectors.astype(BF16).T, ((0, 0), (0, 128 - vectors.shape[0])))
    head_part = w_rows[:, : 4 * width].astype(BF16)
    up_mine = lax.all_gather(
        my_half(w_rows[:, 4 * width :]).astype(BF16), "fsdp", axis=0, tiled=True
    )
    down_mine = lax.all_gather(my_half(w_down.T).astype(BF16), "fsdp", axis=0, tiled=True)
    x_all, head_w, vec_low = gather_first(ctx, fsdp, x_low, head_part, vec_part)
    head_w = head_w.reshape(width, 4 * width)
    vec_low = vec_low.reshape(width, 128)
    vec = [vec_low[:, i : i + 1].astype(F32) for i in range(12)]
    up_bias = vec_low[:, 8:12].T.astype(F32).reshape(1, FF)
    up_other, down_other = swap_cores(up_mine, ctx), swap_cores(down_mine, ctx)

    starts = [(i * ctx + c) * dim for i in range(regular)] + [(HEADS - 1) * dim]
    own_w = jnp.concatenate(
        [
            lax.dynamic_slice_in_dim(head_w, part * width + start, dim, 1)
            for part in range(3)
            for start in starts
        ],
        axis=1,
    )
    q_bias = jnp.concatenate([lax.dynamic_slice_in_dim(vec[2], s, dim, 0) for s in starts], axis=0)
    v_bias = jnp.concatenate([lax.dynamic_slice_in_dim(vec[3], s, dim, 0) for s in starts], axis=0)
    own_bias = jnp.concatenate([q_bias, jnp.zeros_like(q_bias), v_bias], axis=0)
    act_all, qkv = project(x_all, own_w.T, own_bias, vec[0], vec[1])
    qkv = qkv.reshape(slots, 3, owned, dim, ctx * tok)

    slot = jnp.concatenate([jnp.repeat(jnp.arange(slots, dtype=jnp.int32), regular), late[None]])
    lens = lengths[slot]
    out, out_low, lse = attend(lens, slot, qkv, tok)

    def to_rows(array):
        feat = array.shape[2]
        got = lax.all_to_all(array[:, :-1], "ctx", 0, 0)
        head = got.reshape(ctx, slots, regular, feat, tok).transpose(1, 2, 0, 3, 4)
        head = head.reshape(slots, regular * ctx, feat, tok)
        far = (c + ctx // 2) % ctx
        mine = pick(array, c, 0)[-1]
        got = lax.ppermute(pick(array, far, 0)[-1], "ctx", flip(ctx, ctx // 2))
        first = jnp.where(late == 0, mine, got)
        second = jnp.where(late == 0, got, mine)
        return jnp.concatenate([head, jnp.stack([first, second])[:, None]], axis=1)

    def to_pairs(array):
        array = array.reshape(slots, HEADS, dim, tok)
        head = array[:, :-1].reshape(slots, regular, ctx, dim, tok).transpose(2, 0, 1, 3, 4)
        head = head.reshape(ctx, slots * regular, dim, tok)
        last = jnp.repeat(array[:, -1], ctx // slots, axis=0)[:, None]
        return lax.all_to_all(jnp.concatenate([head, last], axis=1), "ctx", 0, 0)

    att = to_rows(out_low).reshape(slots, width, tok)

    x = x_low.astype(F32)
    out_w = head_w[:, 3 * width :]
    mid = x + jnp.einsum("de,sdt->set", out_w, att, preferred_element_type=F32) + vec[4]
    unit_two, inverse_two = norm_parts(mid, 1)
    act_two = (unit_two * vec[5] + vec[6]).astype(BF16)

    pos = c * tok + jnp.arange(tok, dtype=jnp.int32)
    valid = pos[None, None, :] < lengths[:, None, None]
    g_low = jnp.where(valid, cotangent.transpose(1, 2, 0), jnp.zeros((), BF16))
    g = g_low.astype(F32)

    bias_mine = lax.dynamic_slice_in_dim(up_bias, core * half, half, 1)
    bias_other = lax.dynamic_slice_in_dim(up_bias, (1 - core) * half, half, 1)
    y_other, ga_other, dup_other, ddown_other, db_other = mlp(
        act_two, g_low, up_other, down_other, bias_other, True
    )
    y_mine, ga_mine, dup_mine, ddown_mine, db_mine = mlp(
        act_two, g_low, up_mine, down_mine, bias_mine, False
    )
    output = (mid + (y_mine + y_other + vec[7])).astype(BF16).transpose(2, 0, 1)

    grad_mid, gain_two, shift_two = norm_back(ga_mine + ga_other, unit_two, inverse_two, vec[5])
    grad_mid = g + grad_mid
    grad_attn = grad_mid.astype(BF16)
    grad_att = jnp.einsum("de,set->sdt", out_w, grad_attn, preferred_element_type=F32).astype(BF16)
    grad_pairs = to_pairs(grad_att)

    up_part = scatter_fsdp(add_cores(dup_mine, dup_other, ctx), fsdp)
    down_part = scatter_fsdp(add_cores(ddown_mine, ddown_other, ctx), fsdp)
    mlp_sum = sum_chips(jnp.concatenate([up_part, down_part], axis=0), ctx)
    mlp_sum = ordered(core, mlp_sum, swap_cores(mlp_sum, ctx), 1)

    out_grad = jnp.einsum("sdt,set->de", att, grad_attn, preferred_element_type=F32)
    out_grad = out_grad.reshape(fsdp, 2, share // 2, width)
    out_part = add_cores(pick(out_grad, core, 1), pick(out_grad, 1 - core, 1).astype(BF16), ctx)
    out_part = scatter_fsdp(out_part.reshape(width // 2, width), fsdp)
    out_sum = sum_chips(out_part, ctx)
    out_sum = ordered(core, out_sum, swap_cores(out_sum, ctx), 0)

    grad_heads = attend_back(lens, slot, qkv, out, lse, grad_pairs)
    grad_qkv = to_rows(grad_heads).reshape(slots, HEADS, 3, dim, tok).transpose(0, 2, 1, 3, 4)
    grad_qkv = grad_qkv.reshape(slots, 3 * width, tok)

    owner_of = [0, ctx // 2]
    last_mask = jnp.stack([c == owner_of[s] for s in range(slots)])[None, :, None, None, None]
    head = grad_heads[:, :-1].reshape(ctx, slots, regular, 3 * dim, tok)
    last = jnp.where(last_mask, grad_heads[:, -1][:, None, None], jnp.zeros((), BF16))
    own_grad = jnp.concatenate([head, last], axis=2).reshape(ctx, slots, owned * 3 * dim, tok)
    own_sum = jnp.einsum("csdt,csmt->dm", act_all, own_grad, preferred_element_type=F32)
    own_sum = scatter_fsdp(own_sum, fsdp).astype(BF16)
    own_all = gather_chips(own_sum, ctx)
    own_other = swap_cores(own_all, ctx)
    own_all = ordered(core, own_all[:, None], own_other[:, None], 1)
    own_all = own_all.reshape(ctx, share, owned, 3, dim)
    head = own_all[:, :, :regular].transpose(1, 3, 2, 0, 4).reshape(share, 3, regular * ctx, dim)
    last = own_all[owner_of[0], :, regular].astype(F32) + own_all[owner_of[1], :, regular]
    qkv_sum = jnp.concatenate([head, last.astype(BF16)[:, :, None]], axis=2)
    qkv_sum = qkv_sum.reshape(share, 3 * width)

    grad_one = jnp.einsum(
        "de,set->sdt", head_w[:, : 3 * width], grad_qkv, preferred_element_type=F32
    )
    unit_one, inverse_one = norm_parts(x, 1)
    grad_in, gain_one, shift_one = norm_back(grad_one, unit_one, inverse_one, vec[0])
    grad_tokens = (grad_mid + grad_in).astype(BF16).transpose(2, 0, 1)

    bias_qkv = jnp.sum(grad_qkv.astype(F32), axis=(0, 2))
    vec_grad = jnp.stack(
        [
            gain_one,
            shift_one,
            bias_qkv[:width],
            bias_qkv[2 * width :],
            jnp.sum(grad_attn.astype(F32), axis=(0, 2)),
            gain_two,
            shift_two,
            jnp.sum(g, axis=(0, 2)),
        ]
    )
    bias_up = ordered(core, db_mine, db_other, 1).reshape(4, width)
    vec_grad = jnp.concatenate([vec_grad, bias_up], axis=0).reshape(12, fsdp, share)
    f = lax.axis_index("fsdp")
    vec_sum = pick(vec_grad, f, 1)
    for value in range(1, fsdp):
        vec_sum = vec_sum + lax.ppermute(pick(vec_grad, f ^ value, 1), "fsdp", flip(fsdp, value))
    for level in range(bits_of(ctx)):
        vec_sum = vec_sum + lax.ppermute(vec_sum, "ctx", flip(ctx, 2**level))

    rows_sum = jnp.concatenate([qkv_sum, out_sum, mlp_sum[:share]], axis=1).astype(F32)
    rows_out = adamw(w_rows, rows_first, rows_second, rows_sum, 0.03, 0.1)
    down_out = adamw(
        w_down.T, down_first.T, down_second.T, mlp_sum[share:].astype(F32), 0.02, 0.1
    )
    down_out = tuple(part.T for part in down_out)
    vec_out = adamw(vectors, vec_first, vec_second, vec_sum, 0.3, 0.0)
    return (output, grad_tokens, *rows_out, *down_out, *vec_out)


def solution(mesh):
    placed = (
        P("ctx", "fsdp", None),
        P("ctx", "fsdp", None),
        P("fsdp"),
        P("fsdp", None),
        P("fsdp", None),
        P("fsdp", None),
        P(None, "fsdp"),
        P(None, "fsdp"),
        P(None, "fsdp"),
        P(None, "fsdp"),
        P(None, "fsdp"),
        P(None, "fsdp"),
    )
    return jax.shard_map(
        functools.partial(body, mesh.shape["ctx"], mesh.shape["fsdp"]),
        mesh=mesh,
        in_specs=placed,
        out_specs=placed[:2] + placed[3:6] + placed[6:9] + placed[9:12],
        check_vma=False,
    )
```

```python
import functools
import math

import jax
import jax.numpy as jnp
from jax import lax
from jax.experimental import pallas as pl
from jax.experimental.pallas import tpu as pltpu
from jax.sharding import PartitionSpec as P

HEADS = 17
HEAD_DIM = 64
FF = 4352
STEP = 10

MASKED = -1e30
NORM_EPS = 1e-05
BETA_ONE = 0.9
BETA_TWO = 0.95
ADAM_EPS = 1e-08
BF16 = jnp.bfloat16
F32 = jnp.float32


def dot(left, right, dims=((1,), (0,))):
    return lax.dot_general(left, right, (dims, ((), ())), preferred_element_type=F32)


def padded(top, rows, width):
    row = lax.broadcasted_iota(jnp.int32, (rows, width), 0)
    out = jnp.zeros((rows, width), F32)
    for index, value in enumerate(top):
        out = jnp.where(row == index, value, out)
    return out.astype(BF16)


def key_rows(lens_ref, key, length):
    pos = lax.broadcasted_iota(jnp.int32, (1, length), 1)
    bias = jnp.where(pos < lens_ref[pl.program_id(0)], 0.0, MASKED)
    one = jnp.ones((1, length), F32)
    extra = padded([bias, one, one, one], HEAD_DIM, length)
    return jnp.concatenate([key, extra], axis=0).T


def causal(block):
    key = lax.broadcasted_iota(jnp.int32, (block, block), 0)
    query = lax.broadcasted_iota(jnp.int32, (block, block), 1)
    return key <= query


def attend_kernel(block, lens_ref, q_ref, k_ref, v_ref, o_ref, low_ref, lse_ref, keys):
    length = k_ref.shape[-1]
    tok = low_ref.shape[-1]
    step = pl.program_id(1)

    @pl.when(step == 0)
    def _():
        keys[...] = key_rows(lens_ref, k_ref[0, 0], length)

    query = (q_ref[0, 0].astype(F32) * (1.0 / math.sqrt(HEAD_DIM))).astype(BF16)
    query = jnp.concatenate(
        [query, padded([jnp.ones((1, block), F32)], HEAD_DIM, block)], axis=0
    )

    def one(index, state, mask):
        top, total, accum = state
        start = pl.multiple_of(index * block, block)
        scores = dot(keys[pl.ds(start, block), :], query)
        if mask is not None:
            scores = jnp.where(mask, scores, MASKED)
        new_top = jnp.maximum(top, jnp.max(scores, axis=0, keepdims=True))
        weights = jnp.exp(scores - new_top)
        factor = jnp.exp(top - new_top)
        total = total * factor + jnp.sum(weights, axis=0, keepdims=True)
        value = v_ref[0, 0, :, pl.ds(start, block)]
        accum = accum * factor + dot(value, weights.astype(BF16))
        return new_top, total, accum

    state = (
        jnp.full((1, block), MASKED, F32),
        jnp.zeros((1, block), F32),
        jnp.zeros((HEAD_DIM, block), F32),
    )
    state = lax.fori_loop(0, step, lambda i, s: one(i, s, None), state)
    top, total, accum = one(step, state, causal(block))
    result = accum / total
    o_ref[0] = result
    for i in range(block // tok):
        low_ref[i, 0] = result[:, i * tok : (i + 1) * tok].astype(BF16)
    lse_ref[0] = top + jnp.log(total)


def pair_specs(dim, length, block):
    def whole(part):
        return pl.BlockSpec((1, 1, dim, length), lambda p, i, lens: (part, p, 0, 0))

    def piece(part):
        return pl.BlockSpec((1, 1, dim, block), lambda p, i, lens: (part, p, 0, i))

    return whole, piece


def attend(lens, qkv, tok):
    dim, length = qkv.shape[2:]
    pairs = lens.shape[0]
    block = math.gcd(length, 512)
    whole, piece = pair_specs(dim, length, block)
    return pl.pallas_call(
        functools.partial(attend_kernel, block),
        grid_spec=pltpu.PrefetchScalarGridSpec(
            num_scalar_prefetch=1,
            grid=(pairs, length // block),
            in_specs=[piece(0), whole(1), whole(2)],
            out_specs=[
                pl.BlockSpec((1, dim, block), lambda p, i, lens: (p, 0, i)),
                pl.BlockSpec((block // tok, 1, dim, tok), lambda p, i, lens: (i, p, 0, 0)),
                pl.BlockSpec((1, 1, block), lambda p, i, lens: (p, 0, i)),
            ],
            scratch_shapes=[pltpu.VMEM((length, 2 * dim), BF16)],
        ),
        out_shape=[
            jax.ShapeDtypeStruct((pairs, dim, length), F32),
            jax.ShapeDtypeStruct((length // tok, pairs, dim, tok), BF16),
            jax.ShapeDtypeStruct((pairs, 1, length), F32),
        ],
        compiler_params=pltpu.CompilerParams(
            dimension_semantics=("arbitrary", "arbitrary"), vmem_limit_bytes=48 * 2**20
        ),
        cost_estimate=pl.CostEstimate(flops=1000, bytes_accessed=1000, transcendentals=0),
    )(lens, qkv, qkv, qkv)


def split_three(value):
    first = value.astype(BF16).astype(F32)
    second = (value - first).astype(BF16).astype(F32)
    third = (value - first - second).astype(BF16).astype(F32)
    return [-first, -second, -third]


def attend_back_kernel(
    block,
    lens_ref,
    q_ref,
    k_ref,
    v_ref,
    o_ref,
    lse_ref,
    grad_ref,
    out_ref,
    keys,
    values,
    queries,
    grads,
    total,
):
    length = k_ref.shape[-1]
    tok = grad_ref.shape[-1]
    count = length // block
    step = pl.program_id(1)
    scale = 1.0 / math.sqrt(HEAD_DIM)

    @pl.when(step == 0)
    def _():
        keys[...] = key_rows(lens_ref, k_ref[0, 0], length)
        one = jnp.ones((1, length), F32)
        extra = padded([one, one, one], HEAD_DIM, length)
        values[...] = jnp.concatenate([v_ref[0, 0], extra], axis=0).T
        queries[0:HEAD_DIM, :] = (q_ref[0, 0].astype(F32) * scale).astype(BF16)
        queries[HEAD_DIM:, :] = padded([one] + split_three(lse_ref[0]), HEAD_DIM, length)
        for i in range(length // tok):
            grads[0:HEAD_DIM, i * tok : (i + 1) * tok] = grad_ref[i, 0]
        delta = jnp.sum(grads[0:HEAD_DIM, :].astype(F32) * o_ref[0], axis=0, keepdims=True)
        grads[HEAD_DIM:, :] = padded(split_three(delta), HEAD_DIM, length)
        total[...] = jnp.zeros_like(total)

    mine = pl.ds(pl.multiple_of(step * block, block), block)
    key = keys[mine, :]
    value = values[mine, :]
    key_t = k_ref[0, 0, :, mine]

    def one(index, state, mask):
        dk, dv = state
        cols = pl.ds(pl.multiple_of(index * block, block), block)
        scores = dot(key, queries[:, cols])
        if mask is not None:
            scores = jnp.where(mask, scores, MASKED)
        probs = jnp.exp(scores)
        grad_scores = (probs * dot(value, grads[:, cols])).astype(BF16)
        probs = probs.astype(BF16)
        dv = dv + dot(grads[0:HEAD_DIM, cols], probs, ((1,), (1,)))
        dk = dk + dot(queries[0:HEAD_DIM, cols], grad_scores, ((1,), (1,)))
        total[:, cols] += dot(key_t, grad_scores)
        return dk, dv

    zero = jnp.zeros((HEAD_DIM, block), F32)
    state = one(step, (zero, zero), causal(block))
    dk, dv = lax.fori_loop(step + 1, count, lambda i, s: one(i, s, None), state)
    dq = total[:, mine] * scale
    for i in range(block // tok):
        cols = slice(i * tok, (i + 1) * tok)
        out_ref[i, 0, 0:HEAD_DIM] = dq[:, cols].astype(BF16)
        out_ref[i, 0, HEAD_DIM : 2 * HEAD_DIM] = dk[:, cols].astype(BF16)
        out_ref[i, 0, 2 * HEAD_DIM :] = dv[:, cols].astype(BF16)


def attend_back(lens, qkv, out, lse, grad):
    dim, length = qkv.shape[2:]
    pairs, tok = lens.shape[0], grad.shape[-1]
    ctx = length // tok
    block = math.gcd(length, 512)
    whole, _ = pair_specs(dim, length, block)
    return pl.pallas_call(
        functools.partial(attend_back_kernel, block),
        grid_spec=pltpu.PrefetchScalarGridSpec(
            num_scalar_prefetch=1,
            grid=(pairs, length // block),
            in_specs=[
                whole(0),
                whole(1),
                whole(2),
                pl.BlockSpec((1, dim, length), lambda p, i, lens: (p, 0, 0)),
                pl.BlockSpec((1, 1, length), lambda p, i, lens: (p, 0, 0)),
                pl.BlockSpec((ctx, 1, dim, tok), lambda p, i, lens: (0, p, 0, 0)),
            ],
            out_specs=pl.BlockSpec(
                (block // tok, 1, 3 * dim, tok), lambda p, i, lens: (i, p, 0, 0)
            ),
            scratch_shapes=[
                pltpu.VMEM((length, 2 * dim), BF16),
                pltpu.VMEM((length, 2 * dim), BF16),
                pltpu.VMEM((2 * dim, length), BF16),
                pltpu.VMEM((2 * dim, length), BF16),
                pltpu.VMEM((dim, length), F32),
            ],
        ),
        out_shape=jax.ShapeDtypeStruct((ctx, pairs, 3 * dim, tok), BF16),
        compiler_params=pltpu.CompilerParams(
            dimension_semantics=("arbitrary", "arbitrary"), vmem_limit_bytes=48 * 2**20
        ),
        cost_estimate=pl.CostEstimate(flops=1000, bytes_accessed=1000, transcendentals=0),
    )(lens, qkv, qkv, qkv, out, lse, grad)


def project_kernel(x_ref, w_ref, bias_ref, gain_ref, shift_ref, act_ref, out_ref):
    unit, _ = norm_parts(x_ref[0, 0].astype(F32), 0)
    act = (unit * gain_ref[...] + shift_ref[...]).astype(BF16)
    act_ref[0] = act
    out_ref[...] = (dot(w_ref[...], act) + bias_ref[...]).astype(BF16)


def project(x_all, slot, weight, bias, gain, shift):
    ctx, _, width, tok = x_all.shape
    feat = weight.shape[0]

    def fixed(shape):
        return pl.BlockSpec(shape, lambda i: (0, 0))

    return pl.pallas_call(
        project_kernel,
        grid=(ctx,),
        in_specs=[
            pl.BlockSpec((1, 1, width, tok), lambda i: (i, slot, 0, 0)),
            fixed((feat, width)),
            fixed((feat, 1)),
            fixed((width, 1)),
            fixed((width, 1)),
        ],
        out_specs=[
            pl.BlockSpec((1, width, tok), lambda i: (i, 0, 0)),
            pl.BlockSpec((feat, tok), lambda i: (0, i)),
        ],
        out_shape=[
            jax.ShapeDtypeStruct((ctx, width, tok), BF16),
            jax.ShapeDtypeStruct((feat, ctx * tok), BF16),
        ],
        compiler_params=pltpu.CompilerParams(vmem_limit_bytes=48 * 2**20),
        cost_estimate=pl.CostEstimate(flops=1000, bytes_accessed=1000, transcendentals=0),
    )(x_all, weight, bias, gain, shift)


def own_grad_kernel(late_ref, first_ref, second_ref, first_grad_ref, second_grad_ref, last_grad_ref, out_ref, total):
    step = pl.program_id(0)
    nt = ((1,), (1,))
    first, second = first_ref[0], second_ref[0]
    head = dot(first, first_grad_ref[0], nt) + dot(second, second_grad_ref[0], nt)
    last = dot(jnp.where(late_ref[0] == 0, first, second), last_grad_ref[0], nt)
    part = jnp.concatenate([head, last], axis=1)

    @pl.when(step == 0)
    def _():
        total[...] = part

    @pl.when(step > 0)
    def _():
        total[...] += part

    @pl.when(step == pl.num_programs(0) - 1)
    def _():
        out_ref[...] = total[...]


def own_grad(late, first, second, first_grad, second_grad, last_grad):
    ctx, width, tok = first.shape
    feat, last = first_grad.shape[1], last_grad.shape[1]

    def block(rows):
        return pl.BlockSpec((1, rows, tok), lambda i, late: (i, 0, 0))

    return pl.pallas_call(
        own_grad_kernel,
        grid_spec=pltpu.PrefetchScalarGridSpec(
            num_scalar_prefetch=1,
            grid=(ctx,),
            in_specs=[block(width), block(width), block(feat), block(feat), block(last)],
            out_specs=pl.BlockSpec((width, feat + last), lambda i, late: (0, 0)),
            scratch_shapes=[pltpu.VMEM((width, feat + last), F32)],
        ),
        out_shape=jax.ShapeDtypeStruct((width, feat + last), F32),
        compiler_params=pltpu.CompilerParams(vmem_limit_bytes=48 * 2**20),
        cost_estimate=pl.CostEstimate(flops=1000, bytes_accessed=1000, transcendentals=0),
    )(late[None], first, second, first_grad, second_grad, last_grad)


def mlp_kernel(
    width,
    a_ref,
    g_ref,
    up_ref,
    down_ref,
    bias_ref,
    y_ref,
    ga_ref,
    dup_ref,
    ddown_ref,
    db_ref,
    a_rows,
    g_rows,
):
    step = pl.program_id(0)
    slots, _, tok = a_ref.shape
    block = up_ref.shape[1]

    @pl.when(step == 0)
    def _():
        for s in range(slots):
            a_rows[s * tok : (s + 1) * tok, :] = a_ref[s].T
            g_rows[s * tok : (s + 1) * tok, :] = g_ref[s].T
        y_ref[...] = jnp.zeros_like(y_ref)
        ga_ref[...] = jnp.zeros_like(ga_ref)

    def run(size):
        up = up_ref[:, :size]
        down = down_ref[:, :size]
        pre = dot(a_rows[...], up) + bias_ref[:, :size]
        cdf = 0.5 * (1.0 + lax.erf(pre * math.sqrt(0.5)))
        hidden = (pre * cdf).astype(BF16)
        slope = cdf + pre * jnp.exp(-0.5 * pre * pre) * (1.0 / math.sqrt(2.0 * math.pi))
        grad = (dot(g_rows[...], down) * slope).astype(BF16)
        db_ref[:, :size] = jnp.sum(grad.astype(F32), axis=0, keepdims=True)
        nt = ((1,), (1,))
        for s in range(slots):
            rows = slice(s * tok, (s + 1) * tok)
            y_ref[s] += dot(down, hidden[rows], nt)
            ga_ref[s] += dot(up, grad[rows], nt)
        dup = sum(dot(a_ref[s], grad[s * tok : (s + 1) * tok]) for s in range(slots))
        dup_ref[:, :size] = dup.astype(dup_ref.dtype)
        ddown = sum(dot(g_ref[s], hidden[s * tok : (s + 1) * tok]) for s in range(slots))
        ddown_ref[:, :size] = ddown.astype(ddown_ref.dtype)

    full = width // block

    @pl.when(step < full)
    def _():
        run(block)

    if width % block:

        @pl.when(step == full)
        def _():
            run(width % block)


def mlp(act, grad, up, down, bias):
    slots, width, tok = act.shape
    units = up.shape[1]
    block = 256

    def fixed(shape):
        return pl.BlockSpec(shape, lambda i: (0,) * len(shape))

    cols = pl.BlockSpec((width, block), lambda i: (0, i))
    line = pl.BlockSpec((1, block), lambda i: (0, i))
    total = jax.ShapeDtypeStruct((slots, width, tok), F32)
    grads = jax.ShapeDtypeStruct((width, units), BF16)
    return pl.pallas_call(
        functools.partial(mlp_kernel, units),
        grid=(pl.cdiv(units, block),),
        in_specs=[fixed(act.shape), fixed(act.shape), cols, cols, line],
        out_specs=[fixed(act.shape), fixed(act.shape), cols, cols, line],
        out_shape=[total, total, grads, grads, jax.ShapeDtypeStruct((1, units), F32)],
        scratch_shapes=[pltpu.VMEM((slots * tok, width), BF16)] * 2,
        compiler_params=pltpu.CompilerParams(vmem_limit_bytes=56 * 2**20),
        cost_estimate=pl.CostEstimate(flops=1000, bytes_accessed=1000, transcendentals=0),
    )(act, grad, up, down, bias)


def other_index(index, bit):
    return index + bit * (1 - 2 * lax.rem(index // bit, 2))


def split_columns(start, size, count):
    tiles = size // 128
    cuts = [start + 128 * (-(-tiles * i // count)) for i in range(count)] + [start + size]
    return [(cuts[i], cuts[i + 1] - cuts[i]) for i in range(count)]


def gather_kernel(
    ctx,
    fsdp,
    x_ref,
    w_ref,
    v_ref,
    xo_ref,
    wo_ref,
    um_ref,
    uo_ref,
    vo_ref,
    x_send,
    x_recv,
    xc_send,
    xc_recv,
    w_send,
    w_recv,
    wc_send,
    wc_recv,
    v_send,
    v_recv,
    local,
):
    c, f = lax.axis_index("ctx"), lax.axis_index("fsdp")
    chips = ctx // 2
    z, core = c // 2, lax.rem(c, 2)
    partner = 2 * z + 1 - core
    slots = x_ref.shape[0]
    levels = bits_of(fsdp)
    half = um_ref.shape[2]

    def combine(number):
        place = f
        for bit in range(levels):
            if number & (1 << bit):
                place = other_index(place, 1 << bit)
        return place

    barrier = pltpu.get_barrier_semaphore()

    def greet(where):
        pl.semaphore_signal(barrier, inc=1, device_id=where, device_id_type=pl.DeviceIdType.MESH)

    greet((partner, f))
    for number in range(1, fsdp):
        greet((c, combine(number)))

    @pl.when(z > 0)
    def _():
        greet((c - 2, f))

    @pl.when(z < chips - 1)
    def _():
        greet((c + 2, f))

    beside = (z > 0).astype(jnp.int32) + (z < chips - 1).astype(jnp.int32)
    pl.semaphore_wait(barrier, fsdp + beside)

    def remote(source, target, send, recv, where):
        return pltpu.make_async_remote_copy(
            src_ref=source,
            dst_ref=target,
            send_sem=send,
            recv_sem=recv,
            device_id=where,
            device_id_type=pl.DeviceIdType.MESH,
        )

    def x_copy(side, s, h):
        sign = 1 - 2 * side
        block = c - 2 * sign * s
        source = x_ref.at[h] if s == 0 else xo_ref.at[block, h]
        return remote(
            source, xo_ref.at[block, h], x_send.at[side, s, h], x_recv.at[side, s, h], (c + 2 * sign, f)
        )

    def x_sends(side, s):
        return (z - s >= 0) & (z < chips - 1) if side == 0 else (z + s < chips) & (z > 0)

    def x_gets(side, s):
        return z - 1 - s >= 0 if side == 0 else z + 1 + s < chips

    def x_arrival(side, s, h):
        sign = 1 - 2 * side
        block = c - 2 * sign * (s + 1)
        return remote(
            xo_ref.at[block, h],
            xo_ref.at[block, h],
            x_send.at[side, s, h],
            x_recv.at[side, s, h],
            (c + 2 * sign, f),
        )

    def x_share(side, s, h):
        sign = 1 - 2 * side
        block = c - 2 * sign * (s + 1)
        return remote(
            xo_ref.at[block, h],
            xo_ref.at[block, h],
            xc_send.at[side, s, h],
            xc_recv.at[side, s, h],
            (partner, f),
        )

    def x_share_arrival(side, s, h):
        sign = 1 - 2 * side
        block = partner - 2 * sign * (s + 1)
        return remote(
            xo_ref.at[block, h],
            xo_ref.at[block, h],
            xc_send.at[side, s, h],
            xc_recv.at[side, s, h],
            (partner, f),
        )

    def x_own(h):
        return remote(
            x_ref.at[h],
            xo_ref.at[c, h],
            xc_send.at[0, chips - 1, h],
            xc_recv.at[0, chips - 1, h],
            (partner, f),
        )

    def x_own_arrival(h):
        return remote(
            x_ref.at[h],
            xo_ref.at[partner, h],
            xc_send.at[0, chips - 1, h],
            xc_recv.at[0, chips - 1, h],
            (partner, f),
        )

    runs = split_columns(0, half, levels)

    def source(unit, stream):
        start, size = runs[stream]
        return w_ref.at[:, pl.ds(pl.multiple_of((2 * unit + core) * half + start, 128), size)]

    def kept(unit, stream, place, which):
        start, size = runs[stream]
        if unit == 0:
            return wo_ref.at[place, :, pl.ds(pl.multiple_of(which * half + start, 128), size)]
        return um_ref.at[place, :, pl.ds(start, size)]

    def shared(unit, stream, place, which):
        start, size = runs[stream]
        if unit == 0:
            return kept(unit, stream, place, which)
        return uo_ref.at[place, :, pl.ds(start, size)]

    def w_copy(unit, stream, step, number):
        bit = 1 << ((stream + step) % levels)
        place = combine(number)
        there = kept(unit, stream, place, core)
        return remote(
            source(unit, stream) if number == 0 else there,
            there,
            w_send.at[unit, stream, number | bit],
            w_recv.at[unit, stream, number | bit],
            (c, other_index(f, bit)),
        )

    def w_arrival(unit, stream, number):
        block = kept(unit, stream, combine(number), core)
        sems = w_send.at[unit, stream, number], w_recv.at[unit, stream, number]
        return remote(block, block, *sems, (partner, f))

    def w_share(unit, stream, number):
        place = combine(number)
        sems = wc_send.at[unit, stream, number], wc_recv.at[unit, stream, number]
        block = kept(unit, stream, place, core)
        return remote(block, shared(unit, stream, place, core), *sems, (partner, f))

    def w_share_arrival(unit, stream, number):
        block = shared(unit, stream, combine(number), 1 - core)
        sems = wc_send.at[unit, stream, number], wc_recv.at[unit, stream, number]
        return remote(block, block, *sems, (partner, f))

    def held(stream, step):
        numbers = [0]
        for i in range(step):
            bit = 1 << ((stream + i) % levels)
            numbers += [n | bit for n in numbers]
        return numbers

    def v_copy(number):
        return remote(
            v_ref, vo_ref.at[f], v_send.at[number], v_recv.at[number], (c, combine(number))
        )

    def v_arrival(number):
        return remote(
            v_ref,
            vo_ref.at[combine(number)],
            v_send.at[number],
            v_recv.at[number],
            (c, combine(number)),
        )

    sides = [(side, h) for h in range(slots) for side in range(2)]
    for side, h in sides:

        @pl.when(x_sends(side, 0))
        def _(side=side, h=h):
            x_copy(side, 0, h).start()

    for stream in range(levels):
        w_copy(0, stream, 0, 0).start()
    for number in range(1, fsdp):
        v_copy(number).start()
    for h in range(slots):
        x_own(h).start()
    up_mine = w_ref.at[:, pl.ds(pl.multiple_of((2 + core) * half, 128), half)]
    up_other = w_ref.at[:, pl.ds(pl.multiple_of((3 - core) * half, 128), half)]
    own = [
        pltpu.make_async_copy(x_ref, xo_ref.at[c], local.at[0]),
        pltpu.make_async_copy(w_ref.at[:, pl.ds(0, 2 * half)], wo_ref.at[f], local.at[1]),
        pltpu.make_async_copy(v_ref, vo_ref.at[f], local.at[2]),
        pltpu.make_async_copy(up_mine, um_ref.at[f], local.at[3]),
        pltpu.make_async_copy(up_other, uo_ref.at[f], local.at[4]),
    ]
    for copy in own:
        copy.start()

    def x_step(s):
        for side, h in sides:

            @pl.when(x_gets(side, s))
            def _(side=side, h=h):
                x_arrival(side, s, h).wait_recv()
                x_share(side, s, h).start()

            if s + 1 < chips - 1:

                @pl.when(x_sends(side, s + 1))
                def _(side=side, h=h):
                    x_copy(side, s + 1, h).start()

    def w_step(unit, step):
        for stream in range(levels):
            bit = 1 << ((stream + step) % levels)
            arrived = [number | bit for number in held(stream, step)]
            for number in arrived:
                w_arrival(unit, stream, number).wait_recv()
            if step + 1 < levels:
                for number in held(stream, step + 1):
                    w_copy(unit, stream, step + 1, number).start()
            for number in arrived:
                w_share(unit, stream, number).start()

    def w_begin(unit):
        for stream in range(levels):
            w_copy(unit, stream, 0, 0).start()

    plan = [(1.9 * (s + 1), functools.partial(x_step, s)) for s in range(chips - 1)]
    time = 0.0
    for unit in range(2):
        for step in range(levels):
            if unit == 0 and step == levels - 1:
                plan.append((time + 0.95, functools.partial(w_begin, 1)))
            time += 2.0 ** (step + 1) / levels
            plan.append((time, functools.partial(w_step, unit, step)))
    plan = [step for _, step in sorted(plan, key=lambda entry: entry[0])]
    for step in plan:
        step()

    for copy in own:
        copy.wait()
    for number in range(1, fsdp):
        v_copy(number).wait_send()
        v_arrival(number).wait_recv()
        for unit in range(2):
            for stream in range(levels):
                w_arrival(unit, stream, number).wait_send()
                w_share(unit, stream, number).wait_send()
                w_share_arrival(unit, stream, number).wait_recv()
    for h in range(slots):
        x_own(h).wait_send()
        x_own_arrival(h).wait_recv()
    for s in range(chips - 1):
        for side, h in sides:

            @pl.when(x_sends(side, s))
            def _(side=side, h=h, s=s):
                x_copy(side, s, h).wait_send()

            @pl.when(x_gets(side, s))
            def _(side=side, h=h, s=s):
                x_share(side, s, h).wait_send()
                x_share_arrival(side, s, h).wait_recv()


def gather_first(ctx, fsdp, x, w, v):
    slots = x.shape[0]
    rows, columns = w.shape
    levels, chips = bits_of(fsdp), ctx // 2
    anywhere = pl.BlockSpec(memory_space=pl.ANY)
    dma = pltpu.SemaphoreType.DMA
    return pl.pallas_call(
        functools.partial(gather_kernel, ctx, fsdp),
        in_specs=[pl.BlockSpec(memory_space=pltpu.VMEM)] * 3,
        out_specs=[anywhere] * 5,
        out_shape=[
            jax.ShapeDtypeStruct((ctx,) + x.shape, x.dtype),
            jax.ShapeDtypeStruct((fsdp, rows, columns // 2), w.dtype),
            jax.ShapeDtypeStruct((fsdp, rows, columns // 4), w.dtype),
            jax.ShapeDtypeStruct((fsdp, rows, columns // 4), w.dtype),
            jax.ShapeDtypeStruct((fsdp,) + v.shape, v.dtype),
        ],
        scratch_shapes=[
            dma((2, chips - 1, slots)),
            dma((2, chips - 1, slots)),
            dma((2, chips, slots)),
            dma((2, chips, slots)),
            dma((2, levels, fsdp)),
            dma((2, levels, fsdp)),
            dma((2, levels, fsdp)),
            dma((2, levels, fsdp)),
            dma((fsdp,)),
            dma((fsdp,)),
            dma((5,)),
        ],
        compiler_params=pltpu.CompilerParams(
            collective_id=0, has_side_effects=True, vmem_limit_bytes=32 * 2**20
        ),
        cost_estimate=pl.CostEstimate(flops=1000, bytes_accessed=1000, transcendentals=0),
    )(x, w, v)


def bits_of(count):
    return max(count.bit_length() - 1, 0)


def flip(count, value):
    return [(i, i ^ value) for i in range(count)]


def pick(array, index, axis):
    return lax.dynamic_index_in_dim(array, index, axis, keepdims=False)


def ordered(bit, mine, other, axis):
    first = jnp.where(bit == 0, mine, other)
    second = jnp.where(bit == 0, other, mine)
    return jnp.concatenate([first, second], axis=axis)


def after(value, *others):
    return lax.optimization_barrier((value, others))[0]


class Scatter:
    def __init__(self, groups, fsdp, first):
        self.fsdp, self.first, self.levels = fsdp, first, bits_of(fsdp)
        rows = groups[0][0].shape[0] // fsdp
        self.groups = [
            [term.reshape((2,) * self.levels + (rows, term.shape[1])) for term in terms]
            for terms in groups
        ]
        self.done = []

    def send(self):
        bit = (self.first + len(self.done)) % self.levels
        axis = self.levels - 1 - bit - sum(1 for b in self.done if b > bit)
        here = (lax.axis_index("fsdp") // 2**bit) % 2
        sent = jnp.concatenate(
            [
                sum(pick(term, 1 - here, axis).astype(F32) for term in terms).astype(BF16)
                for terms in self.groups
            ],
            axis=-1,
        )
        self.got = lax.ppermute(sent, "fsdp", flip(self.fsdp, 2**bit))
        self.groups = [[pick(term, here, axis) for term in terms] for terms in self.groups]
        self.done.append(bit)
        return sent

    def receive(self, *gate):
        got = after(self.got, *gate) if gate else self.got
        start = 0
        for terms in self.groups:
            size = terms[0].shape[-1]
            terms.append(lax.slice_in_dim(got, start, start + size, axis=got.ndim - 1))
            start += size

    def result(self):
        return jnp.concatenate(
            [sum(term.astype(F32) for term in terms) for terms in self.groups], axis=-1
        )


def bar_signal(where):
    pl.semaphore_signal(
        pltpu.get_barrier_semaphore(), inc=1, device_id=where, device_id_type=pl.DeviceIdType.MESH
    )


def remote_copy(source, target, send, recv, where):
    return pltpu.make_async_remote_copy(
        src_ref=source,
        dst_ref=target,
        send_sem=send,
        recv_sem=recv,
        device_id=where,
        device_id_type=pl.DeviceIdType.MESH,
    )


def line_gather(chips, c, f, mine, slot, share, sems, core_sems):
    z, core = c // 2, lax.rem(c, 2)
    partner = 2 * z + 1 - core
    send, recv = sems
    core_send, core_recv = core_sems

    def passing(side, s):
        sign = 1 - 2 * side
        chip = z - sign * s
        source = mine if s == 0 else slot(chip)
        return remote_copy(
            source, slot(chip), send.at[side, s], recv.at[side, s], (c + 2 * sign, f)
        )

    def arrival(side, s):
        block = slot(z - (1 - 2 * side) * (s + 1))
        return remote_copy(block, block, send.at[side, s], recv.at[side, s], (partner, f))

    def sends(side, s):
        return (z - s >= 0) & (z < chips - 1) if side == 0 else (z + s < chips) & (z > 0)

    def gets(side, s):
        return z - 1 - s >= 0 if side == 0 else z + 1 + s < chips

    def shared(side, s):
        chip = z - (1 - 2 * side) * (s + 1)
        return remote_copy(
            slot(chip), share(chip), core_send.at[side, s], core_recv.at[side, s], (partner, f)
        )

    def share_arrival(side, s):
        block = share(z - (1 - 2 * side) * (s + 1))
        sems = core_send.at[side, s], core_recv.at[side, s]
        return remote_copy(block, block, *sems, (partner, f))

    own_sems = core_send.at[0, chips - 1], core_recv.at[0, chips - 1]
    own_share = remote_copy(mine, share(z), *own_sems, (partner, f))

    def start():
        for side in range(2):

            @pl.when(sends(side, 0))
            def _(side=side):
                passing(side, 0).start()

        own_share.start()

    def step(s):
        for side in range(2):

            @pl.when(gets(side, s))
            def _(side=side):
                arrival(side, s).wait_recv()
                shared(side, s).start()

            if s + 1 < chips - 1:

                @pl.when(sends(side, s + 1))
                def _(side=side):
                    passing(side, s + 1).start()

    def end():
        own_share.wait_send()
        remote_copy(share(z), share(z), *own_sems, (partner, f)).wait_recv()
        for s in range(chips - 1):
            for side in range(2):

                @pl.when(sends(side, s))
                def _(side=side, s=s):
                    passing(side, s).wait_send()

                @pl.when(gets(side, s))
                def _(side=side, s=s):
                    shared(side, s).wait_send()
                    share_arrival(side, s).wait_recv()

    return start, [functools.partial(step, s) for s in range(chips - 1)], end


def sum_kernel(ctx, fsdp, batches, *refs):
    levels, chips = bits_of(fsdp), ctx // 2
    pieces = refs[0:2]
    own_ref, mine_out, other_out, own_out, last_out = refs[2:7]
    rest = list(refs[7:])
    own_kept, own_low = rest.pop(0), rest.pop(0)
    own_sent = [rest.pop(0) for _ in range(levels)]
    own_got = [rest.pop(0) for _ in range(levels)]
    z_sent, z_got = rest.pop(0), rest.pop(0)
    op_send, op_recv, zs_send, zs_recv, zg_send, zg_recv = (rest.pop(0) for _ in range(6))
    zc_send, zc_recv, og_send, og_recv, oc_send, oc_recv, far_send, far_recv, local = (
        rest.pop(0) for _ in range(9)
    )
    c, f = lax.axis_index("ctx"), lax.axis_index("fsdp")
    z, core = c // 2, lax.rem(c, 2)
    partner = 2 * z + 1 - core
    far = lax.rem(c + ctx // 2, ctx)
    rows = own_low.shape[0]
    chunk = z_sent.shape[-1]
    width = chunk * chips // 2
    parts = chips // 2
    strip = 16 if rows % 16 == 0 else 8

    def own_bit(bit):
        return lax.rem(f // (1 << bit), 2)

    def strips(work):
        def body(i, carry):
            work(pl.ds(pl.multiple_of(i * strip, strip), strip))
            return carry

        lax.fori_loop(0, rows // strip, body, 0)

    bar_signal((partner, f))
    bar_signal((far, f))
    for bit in range(levels):
        bar_signal((c, other_index(f, 1 << bit)))

    @pl.when(z > 0)
    def _():
        bar_signal((c - 2, f))

    @pl.when(z < chips - 1)
    def _():
        bar_signal((c + 2, f))

    beside = (z > 0).astype(jnp.int32) + (z < chips - 1).astype(jnp.int32)
    pl.semaphore_wait(pltpu.get_barrier_semaphore(), levels + 2 + beside)

    def order(q):
        return [(q + i) % levels for i in range(levels)]

    def place_of(q, flipped, free):
        bits = order(q)
        first = own_bit(bits[0])
        total = (1 - first if flipped else first) * (1 << bits[0])
        for i, bit in enumerate(bits[1:]):
            total += ((free >> i) & 1) * (1 << bit)
        return total

    def kept_index(q, step, flipped, free):
        bits = order(q)
        total = 0
        for i, bit in enumerate(bits[1:]):
            mine = own_bit(bit)
            if i + 1 < step:
                value = mine
            elif i + 1 == step:
                value = 1 - mine if flipped else mine
            else:
                value = (free >> (i - step)) & 1
            total += value * (1 << i)
        return total

    def across(step, q):
        return (c, other_index(f, 1 << order(q)[step]))

    def own_copy(step):
        return remote_copy(
            own_sent[step], own_got[step], op_send.at[step], op_recv.at[step], across(step, 0)
        )

    def own_begin():
        for free in range(fsdp // 2):
            there, here = place_of(0, True, free), place_of(0, False, free)

            def work(at, free=free, there=there, here=here):
                own_sent[0][free, at, :] = own_ref[there, at, :]
                own_kept[free, at, :] = own_ref[here, at, :].astype(F32)

            strips(work)
        own_copy(0).start()

    def later(step, kept_ref, got_ref, sent_ref, q):
        for free in range(fsdp >> (step + 2)):
            there, here = (kept_index(q, step + 1, flipped, free) for flipped in (True, False))
            mine = own_bit(order(q)[step + 1])
            there_got, here_got = free * 2 + 1 - mine, free * 2 + mine

            def work(at, free=free):
                value = kept_ref[there, at, :] + got_ref[there_got, at, :].astype(F32)
                sent_ref[free, at, :] = value.astype(BF16)
                kept_ref[here, at, :] += got_ref[here_got, at, :].astype(F32)

            strips(work)

    def last(kept_ref, got_ref, q, place):
        def work(at):
            place(at, kept_ref[kept_index(q, levels, False, 0), at, :] + got_ref[0, at, :].astype(F32))

        strips(work)

    def own_step(step):
        own_copy(step).wait_recv()
        if step + 1 < levels:
            later(step, own_kept, own_got[step], own_sent[step + 1], 0)
            own_copy(step + 1).start()
            return

        def place(at, value):
            own_low[at, :] = value.astype(BF16)

        last(own_kept, own_got[step], 0, place)
        for copy in far_copies:
            copy.start()
        own_start()

    head = own_out.shape[2]
    tail = last_out.shape[2]
    far_copies = [
        remote_copy(
            own_low.at[:, pl.ds(head, tail)], last_out.at[1], far_send.at[0], far_recv.at[0], (far, f)
        ),
        pltpu.make_async_copy(own_low.at[:, pl.ds(head, tail)], last_out.at[0], local.at[0]),
        pltpu.make_async_copy(own_low.at[:, pl.ds(0, head)], own_out.at[c], local.at[1]),
    ]
    own_start, own_steps, own_end = line_gather(
        chips,
        c,
        f,
        own_low.at[:, pl.ds(0, head)],
        lambda chip: own_out.at[2 * chip + core],
        lambda chip: own_out.at[2 * chip + core],
        (og_send, og_recv),
        (oc_send, oc_recv),
    )

    def total_of(j, b, at):
        return pieces[j // parts][at, pl.ds(b * width + (j % parts) * chunk, chunk)]

    def z_copy(side, i, b):
        return remote_copy(
            z_sent.at[side, b, i],
            z_got.at[side, b, i],
            zs_send.at[side, b, i],
            zs_recv.at[side, b, i],
            (c + 2 * (1 - 2 * side), f),
        )

    def z_last(side, chip):
        return chips - 1 - chip if side == 0 else chip

    def z_step(turn, b):
        for chip in range(chips):

            @pl.when(z == chip)
            def _(chip=chip):
                for side in range(2):
                    j_of = (lambda i: chips - 1 - i) if side == 0 else (lambda i: i)
                    begun = chip if side == 0 else chips - 1 - chip
                    i = turn - begun
                    sends = z_last(side, chip)
                    if begun > 0 and 0 <= i <= sends and i < chips - 1:
                        z_copy(side, i, b).wait_recv()
                    if 0 <= i < sends:
                        if i > 0:
                            z_copy(side, i - 1, b).wait_send()

                        def work(at, side=side, i=i, j=j_of(i), begun=begun):
                            value = total_of(j, b, at)
                            if begun > 0:
                                value += z_got[side, b, i, at, :].astype(F32)
                            z_sent[side, b, i, at, :] = value.astype(BF16)

                        strips(work)
                        z_copy(side, i, b).start()

    def chunk_of(ref, chip, b):
        start = pl.multiple_of(b * width + lax.rem(chip, parts) * chunk, 128)
        return ref.at[chip // parts, :, pl.ds(start, chunk)]

    gathers = []
    for b in range(batches):
        gathers.append(
            line_gather(
                chips,
                c,
                f,
                chunk_of(mine_out, z, b),
                lambda chip, b=b: chunk_of(mine_out, chip, b),
                lambda chip, b=b: chunk_of(other_out, chip, b),
                (zg_send.at[:, b], zg_recv.at[:, b]),
                (zc_send.at[:, b], zc_recv.at[:, b]),
            )
        )

    def finish(b):
        for j in range(chips):

            @pl.when(z == j)
            def _(j=j):
                def work(at):
                    value = total_of(j, b, at)
                    if j > 0:
                        value += z_got[0, b, chips - 1 - j, at, :].astype(F32)
                    if j < chips - 1:
                        value += z_got[1, b, j, at, :].astype(F32)
                    start = b * width + (j % parts) * chunk
                    mine_out[j // parts, at, pl.ds(start, chunk)] = value.astype(BF16)

                strips(work)

        gathers[b][0]()

    own_begin()
    waiting = list(own_steps)
    for turn in range(batches + 1):
        for i in range(chips):
            if turn < batches:
                z_step(i, turn)
            if i < chips - 1 and turn > 0:
                gathers[turn - 1][1][i]()
        if turn < batches:
            finish(turn)
        if turn < levels:
            own_step(turn)
        else:
            for step in waiting[:2]:
                step()
            waiting = waiting[2:]
    for turn in range(batches + 1, levels):
        own_step(turn)
    for step in waiting:
        step()

    far_copies[0].wait()
    far_copies[1].wait()
    far_copies[2].wait()
    own_end()
    for step in range(levels):
        own_copy(step).wait_send()
    for b in range(batches):
        gathers[b][2]()
        for chip in range(chips):

            @pl.when(z == chip)
            def _(chip=chip, b=b):
                for side in range(2):
                    if z_last(side, chip):
                        z_copy(side, z_last(side, chip) - 1, b).wait_send()


def sum_grads(ctx, fsdp, pieces, own, head):
    levels, chips = bits_of(fsdp), ctx // 2
    rows, whole = pieces[0].shape
    batches = max(n for n in range(1, 3) if whole % n == 0 and 2 * whole // n % (chips * 128) == 0)
    width = whole // batches
    chunk = 2 * width // chips
    own_width = own.shape[-1]
    vmem = pl.BlockSpec(memory_space=pltpu.VMEM)
    dma = pltpu.SemaphoreType.DMA
    steps = [fsdp >> (i + 1) for i in range(levels)]
    result = jax.ShapeDtypeStruct((2, rows, whole), BF16)
    mine, other, own_all, last = pl.pallas_call(
        functools.partial(sum_kernel, ctx, fsdp, batches),
        in_specs=[vmem] * 3,
        out_specs=[vmem] * 4,
        out_shape=[
            result,
            result,
            jax.ShapeDtypeStruct((ctx, rows, head), BF16),
            jax.ShapeDtypeStruct((2, rows, own_width - head), BF16),
        ],
        scratch_shapes=[
            pltpu.VMEM((fsdp // 2, rows, own_width), F32),
            pltpu.VMEM((rows, own_width), BF16),
        ]
        + [pltpu.VMEM((n, rows, own_width), BF16) for n in steps * 2]
        + [pltpu.VMEM((2, batches, chips - 1, rows, chunk), BF16)] * 2
        + [dma((levels,))] * 2
        + [dma((2, batches, chips - 1))] * 4
        + [dma((2, batches, chips))] * 2
        + [dma((2, chips - 1))] * 2
        + [dma((2, chips))] * 2
        + [dma((1,))] * 2
        + [dma((6,))],
        compiler_params=pltpu.CompilerParams(
            collective_id=1, has_side_effects=True, vmem_limit_bytes=60 * 2**20
        ),
        cost_estimate=pl.CostEstimate(flops=1000, bytes_accessed=1000, transcendentals=0),
    )(*pieces, own)

    return mine, other, own_all, last


def swap_cores(mine, ctx):
    return lax.ppermute(mine, "ctx", flip(ctx, 1))


def norm_parts(rows, axis):
    middle = jnp.mean(rows, axis=axis, keepdims=True)
    centred = rows - middle
    spread = jnp.mean(centred * centred, axis=axis, keepdims=True)
    inverse = lax.rsqrt(spread + NORM_EPS)
    return centred * inverse, inverse


def norm_back(grad, unit, inverse, gain):
    inner = grad * gain
    mean_inner = jnp.mean(inner, axis=1, keepdims=True)
    mean_cross = jnp.mean(inner * unit, axis=1, keepdims=True)
    rows = inverse * (inner - mean_inner - unit * mean_cross)
    return rows, jnp.sum(grad * unit, axis=(0, 2)), jnp.sum(grad, axis=(0, 2))


def adamw(weight, first, second, grad, rate, decay):
    moment = BETA_ONE * first.astype(F32) + (1.0 - BETA_ONE) * grad
    square = BETA_TWO * second + (1.0 - BETA_TWO) * grad * grad
    corrected = moment / (1.0 - BETA_ONE**STEP)
    scaled = square / (1.0 - BETA_TWO**STEP)
    new_weight = weight - rate * (corrected / (jnp.sqrt(scaled) + ADAM_EPS) + decay * weight)
    return (moment, square, new_weight)


def body(
    ctx,
    fsdp,
    tokens,
    cotangent,
    lengths,
    w_rows,
    rows_first,
    rows_second,
    w_down,
    down_first,
    down_second,
    vectors,
    vec_first,
    vec_second,
):
    tok, slots, width = tokens.shape
    dim = HEAD_DIM
    regular = HEADS // ctx
    owned = regular + 1
    share = width // fsdp
    c = lax.axis_index("ctx")
    core = c % 2
    late = (c >= ctx // 2).astype(jnp.int32)
    half = FF // 2

    def my_half(array):
        return lax.dynamic_slice_in_dim(array, core * half, half, 1)

    x_low = tokens.transpose(1, 2, 0)
    vec_part = jnp.pad(vectors.astype(BF16).T, ((0, 0), (0, 128 - vectors.shape[0])))
    x_all, head_w, up_mine, up_other, vec_low = gather_first(
        ctx, fsdp, x_low, w_rows.astype(BF16), vec_part
    )
    head_w = head_w.reshape(width, 4 * width)
    up_mine, up_other = up_mine.reshape(width, half), up_other.reshape(width, half)
    vec_low = vec_low.reshape(width, 128)
    down_mine, vec_low = lax.optimization_barrier((my_half(w_down.T).astype(BF16), vec_low))
    down_mine = lax.all_gather(down_mine, "fsdp", axis=0, tiled=True)
    vec = [vec_low[:, i : i + 1].astype(F32) for i in range(12)]
    up_bias = vec_low[:, 8:12].T.astype(F32).reshape(1, FF)

    starts = [(i * ctx + c) * dim for i in range(regular)] + [(HEADS - 1) * dim]
    own_w = jnp.concatenate(
        [
            lax.dynamic_slice_in_dim(head_w, part * width + start, dim, 1)
            for part in range(3)
            for start in starts
        ],
        axis=1,
    )
    q_bias = jnp.concatenate([lax.dynamic_slice_in_dim(vec[2], s, dim, 0) for s in starts], axis=0)
    v_bias = jnp.concatenate([lax.dynamic_slice_in_dim(vec[3], s, dim, 0) for s in starts], axis=0)
    own_bias = jnp.concatenate([q_bias, jnp.zeros_like(q_bias), v_bias], axis=0)
    own_w = own_w.T
    far = (c + ctx // 2) % ctx
    acts, results = [], []
    lens = [jnp.repeat(lengths[s : s + 1], regular) for s in range(slots)]
    last = []
    for s in range(slots):
        act, qkv = project(x_all, s, own_w, own_bias, vec[0], vec[1])
        qkv = qkv.reshape(3, owned, dim, ctx * tok)
        acts.append(act)
        last.append(qkv[:, regular:])
        results.append((lens[s], qkv, *attend(lens[s], qkv, tok)))
    last_qkv = after(jnp.where(late == 0, last[0], last[1]), results[1][2])
    last_len = lax.dynamic_slice_in_dim(lengths, late, 1, 0)
    results.append((last_len, last_qkv, *attend(last_len, last_qkv, tok)))

    def to_rows(array, *gate):
        feat = array.shape[2]
        got = after(lax.all_to_all(array, "ctx", 0, 0), *gate)
        return got.transpose(1, 0, 2, 3).reshape(regular * ctx, feat, tok)

    def last_to_rows(array, *gate):
        mine = pick(array, c, 0)
        got = after(lax.ppermute(pick(array, far, 0), "ctx", flip(ctx, ctx // 2)), *gate)
        return jnp.where(late == 0, mine, got), jnp.where(late == 0, got, mine)

    def to_send(array):
        return array.reshape(regular, ctx, dim, tok).transpose(1, 0, 2, 3)

    down_mine = after(down_mine, results[2][2])
    down_other = swap_cores(down_mine, ctx)
    last_rows = last_to_rows(results[2][3])
    att = [
        jnp.concatenate([to_rows(results[s][3]), last_rows[s]]).reshape(width, tok)
        for s in range(slots)
    ]
    att = jnp.stack(att)

    x = x_low.astype(F32)
    out_w = head_w[:, 3 * width :]
    mid = x + jnp.einsum("de,sdt->set", out_w, att, preferred_element_type=F32) + vec[4]
    unit_two, inverse_two = norm_parts(mid, 1)
    act_two = (unit_two * vec[5] + vec[6]).astype(BF16)

    pos = c * tok + jnp.arange(tok, dtype=jnp.int32)
    valid = pos[None, None, :] < lengths[:, None, None]
    g_low = jnp.where(valid, cotangent.transpose(1, 2, 0), jnp.zeros((), BF16))
    g = g_low.astype(F32)

    bias_mine = lax.dynamic_slice_in_dim(up_bias, core * half, half, 1)
    bias_other = lax.dynamic_slice_in_dim(up_bias, (1 - core) * half, half, 1)
    y_other, ga_other, dup_other, ddown_other, db_other = mlp(
        act_two, g_low, up_other, down_other, bias_other
    )
    y_mine, ga_mine, dup_mine, ddown_mine, db_mine = mlp(
        act_two, g_low, up_mine, down_mine, bias_mine
    )
    output = (mid + (y_mine + y_other + vec[7])).astype(BF16).transpose(2, 0, 1)

    grad_mid, gain_two, shift_two = norm_back(ga_mine + ga_other, unit_two, inverse_two, vec[5])
    grad_mid = g + grad_mid
    grad_attn = grad_mid.astype(BF16)
    grad_att = jnp.einsum("de,set->sdt", out_w, grad_attn, preferred_element_type=F32).astype(BF16)
    grad_att = grad_att.reshape(slots, HEADS, dim, tok)
    last = jnp.repeat(grad_att[:, -1], ctx // slots, axis=0)[:, None]
    first_pairs = lax.all_to_all(to_send(grad_att[0, :-1]), "ctx", 0, 0)
    other_pairs = lax.all_to_all(
        jnp.concatenate([to_send(grad_att[1, :-1]), last], axis=1), "ctx", 0, 0
    )

    up_swapped, down_swapped = swap_cores(dup_other, ctx), swap_cores(ddown_other, ctx)
    quarter = width // 4
    spread = jnp.pad(
        grad_attn.reshape(slots, 4, quarter, tok), ((0, 0), (0, 0), (0, -quarter % 128), (0, 0))
    )
    out_grad = jnp.einsum("sdt,sket->kde", att, spread, preferred_element_type=F32).astype(BF16)
    out_grad = out_grad.reshape(2, 2, fsdp, share, spread.shape[2])

    def out_half(which):
        return pick(out_grad, which, 0).reshape(2, width, spread.shape[2])

    out_mine, out_swapped = out_half(core), swap_cores(out_half(1 - core), ctx)
    scatters = [
        Scatter([[dup_mine, up_swapped], [out_mine[0], out_swapped[0]]], fsdp, 0),
        Scatter([[ddown_mine, down_swapped], [out_mine[1], out_swapped[1]]], fsdp, 1),
    ]
    sent = [scatter.send() for scatter in scatters]
    grad_heads = [
        attend_back(*results[0][:3], results[0][4], after(first_pairs, *sent)),
    ]
    grad_heads.append(
        attend_back(*results[1][:3], results[1][4], after(other_pairs[:, :-1], grad_heads[0]))
    )
    for _ in range(scatters[0].levels - 1):
        for scatter in scatters:
            scatter.receive(grad_heads[1])
        sent = [scatter.send() for scatter in scatters]
    for scatter in scatters:
        scatter.receive()
    grad_heads.append(
        attend_back(*results[2][:3], results[2][4], after(other_pairs[:, -1:], *sent))
    )

    feat = 3 * dim
    own_sum = own_grad(
        late,
        acts[0],
        acts[1],
        grad_heads[0].reshape(ctx, regular * feat, tok),
        grad_heads[1].reshape(ctx, regular * feat, tok),
        grad_heads[2].reshape(ctx, feat, tok),
    )
    own_sum = own_sum.astype(BF16)
    own_sum = jnp.concatenate(
        [
            jnp.pad(part, ((0, 0), (0, -part.shape[1] % 128)))
            for part in (own_sum[:, : regular * feat], own_sum[:, regular * feat :])
        ],
        axis=1,
    )
    head_columns = regular * feat + -regular * feat % 128
    blocks = (fsdp, share)
    sum_mine, sum_other, own_all, last = sum_grads(
        ctx,
        fsdp,
        [scatter.result() for scatter in scatters],
        own_sum.reshape(*blocks, own_sum.shape[1]),
        head_columns,
    )
    last_rows = last_to_rows(grad_heads[2], sum_mine)
    grad_qkv = []
    for s in range(slots):
        rows = jnp.concatenate([to_rows(grad_heads[s], sum_mine), last_rows[s]])
        rows = rows.reshape(HEADS, 3, dim, tok).transpose(1, 0, 2, 3)
        grad_qkv.append(rows.reshape(3 * width, tok))
    grad_qkv = jnp.stack(grad_qkv)

    up_sum = ordered(core, sum_mine[0, :, :half], sum_other[0, :, :half], 1)
    down_sum = ordered(core, sum_mine[1, :, :half], sum_other[1, :, :half], 1)

    def out_columns(array):
        return jnp.concatenate([array[q, :, half : half + quarter] for q in range(2)], axis=1)

    out_sum = ordered(core, out_columns(sum_mine), out_columns(sum_other), 1)
    own_all = own_all[:, :, : regular * feat].reshape(ctx, share, regular, 3, dim)
    head = own_all.transpose(1, 3, 2, 0, 4).reshape(share, 3, regular * ctx, dim)
    both = (last[0].astype(F32) + last[1].astype(F32))[:, :feat]
    both = both.astype(BF16).reshape(share, 3, 1, dim)
    qkv_sum = jnp.concatenate([head, both], axis=2).reshape(share, 3 * width)

    grad_one = jnp.einsum(
        "de,set->sdt", head_w[:, : 3 * width], grad_qkv, preferred_element_type=F32
    )
    unit_one, inverse_one = norm_parts(x, 1)
    grad_in, gain_one, shift_one = norm_back(grad_one, unit_one, inverse_one, vec[0])
    grad_tokens = (grad_mid + grad_in).astype(BF16).transpose(2, 0, 1)

    bias_qkv = jnp.sum(grad_qkv.astype(F32), axis=(0, 2))
    vec_grad = jnp.stack(
        [
            gain_one,
            shift_one,
            bias_qkv[:width],
            bias_qkv[2 * width :],
            jnp.sum(grad_attn.astype(F32), axis=(0, 2)),
            gain_two,
            shift_two,
            jnp.sum(g, axis=(0, 2)),
        ]
    )
    bias_up = ordered(core, db_mine, db_other, 1).reshape(4, width)
    vec_grad = jnp.concatenate([vec_grad, bias_up], axis=0).reshape(12, fsdp, share)
    f = lax.axis_index("fsdp")
    vec_sum = pick(vec_grad, f, 1)
    for value in range(1, fsdp):
        vec_sum = vec_sum + lax.ppermute(pick(vec_grad, f ^ value, 1), "fsdp", flip(fsdp, value))
    for level in range(bits_of(ctx)):
        vec_sum = vec_sum + lax.ppermute(vec_sum, "ctx", flip(ctx, 2**level))

    rows_sum = jnp.concatenate([qkv_sum, out_sum, up_sum], axis=1).astype(F32)
    rows_out = adamw(w_rows, rows_first, rows_second, rows_sum, 0.03, 0.1)
    down_out = adamw(
        w_down.T, down_first.T, down_second.T, down_sum.astype(F32), 0.02, 0.1
    )
    down_out = tuple(part.T for part in down_out)
    vec_out = adamw(vectors, vec_first, vec_second, vec_sum, 0.3, 0.0)
    return (output, grad_tokens, *rows_out, *down_out, *vec_out)


def solution(mesh):
    placed = (
        P("ctx", "fsdp", None),
        P("ctx", "fsdp", None),
        P("fsdp"),
        P("fsdp", None),
        P("fsdp", None),
        P("fsdp", None),
        P(None, "fsdp"),
        P(None, "fsdp"),
        P(None, "fsdp"),
        P(None, "fsdp"),
        P(None, "fsdp"),
        P(None, "fsdp"),
    )
    return jax.shard_map(
        functools.partial(body, mesh.shape["ctx"], mesh.shape["fsdp"]),
        mesh=mesh,
        in_specs=placed,
        out_specs=placed[:2] + placed[3:6] + placed[6:9] + placed[9:12],
        check_vma=False,
    )
```

```python
import functools
import math

import jax
import jax.numpy as jnp
from jax import lax
from jax.experimental import pallas as pl
from jax.experimental.pallas import tpu as pltpu
from jax.sharding import PartitionSpec as P

HEADS = 17
HEAD_DIM = 64
FF = 4352
STEP = 10

MASKED = -1e30
NORM_EPS = 1e-05
BETA_ONE = 0.9
BETA_TWO = 0.95
ADAM_EPS = 1e-08
BF16 = jnp.bfloat16
F32 = jnp.float32


def dot(left, right, dims=((1,), (0,))):
    return lax.dot_general(left, right, (dims, ((), ())), preferred_element_type=F32)


def padded(top, rows, width):
    row = lax.broadcasted_iota(jnp.int32, (rows, width), 0)
    out = jnp.zeros((rows, width), F32)
    for index, value in enumerate(top):
        out = jnp.where(row == index, value, out)
    return out.astype(BF16)


def key_rows(lens_ref, key, length):
    pos = lax.broadcasted_iota(jnp.int32, (1, length), 1)
    bias = jnp.where(pos < lens_ref[pl.program_id(0)], 0.0, MASKED)
    one = jnp.ones((1, length), F32)
    extra = padded([bias, one, one, one], HEAD_DIM, length)
    return jnp.concatenate([key, extra], axis=0).T


def causal(block):
    key = lax.broadcasted_iota(jnp.int32, (block, block), 0)
    query = lax.broadcasted_iota(jnp.int32, (block, block), 1)
    return key <= query


def attend_kernel(block, lens_ref, q_ref, k_ref, v_ref, o_ref, low_ref, lse_ref, keys):
    length = k_ref.shape[-1]
    tok = low_ref.shape[-1]
    step = pl.program_id(1)

    @pl.when(step == 0)
    def _():
        keys[...] = key_rows(lens_ref, k_ref[0, 0], length)

    query = (q_ref[0, 0].astype(F32) * (1.0 / math.sqrt(HEAD_DIM))).astype(BF16)
    query = jnp.concatenate(
        [query, padded([jnp.ones((1, block), F32)], HEAD_DIM, block)], axis=0
    )

    def one(index, state, mask):
        top, total, accum = state
        start = pl.multiple_of(index * block, block)
        scores = dot(keys[pl.ds(start, block), :], query)
        if mask is not None:
            scores = jnp.where(mask, scores, MASKED)
        new_top = jnp.maximum(top, jnp.max(scores, axis=0, keepdims=True))
        weights = jnp.exp(scores - new_top)
        factor = jnp.exp(top - new_top)
        total = total * factor + jnp.sum(weights, axis=0, keepdims=True)
        value = v_ref[0, 0, :, pl.ds(start, block)]
        accum = accum * factor + dot(value, weights.astype(BF16))
        return new_top, total, accum

    state = (
        jnp.full((1, block), MASKED, F32),
        jnp.zeros((1, block), F32),
        jnp.zeros((HEAD_DIM, block), F32),
    )
    state = lax.fori_loop(0, step, lambda i, s: one(i, s, None), state)
    top, total, accum = one(step, state, causal(block))
    result = accum / total
    o_ref[0] = result
    for i in range(block // tok):
        low_ref[i, 0] = result[:, i * tok : (i + 1) * tok].astype(BF16)
    lse_ref[0] = top + jnp.log(total)


def pair_specs(dim, length, block):
    def whole(part):
        return pl.BlockSpec((1, 1, dim, length), lambda p, i, lens: (part, p, 0, 0))

    def piece(part):
        return pl.BlockSpec((1, 1, dim, block), lambda p, i, lens: (part, p, 0, i))

    return whole, piece


def attend(lens, qkv, tok):
    dim, length = qkv.shape[2:]
    pairs = lens.shape[0]
    block = math.gcd(length, 512)
    whole, piece = pair_specs(dim, length, block)
    return pl.pallas_call(
        functools.partial(attend_kernel, block),
        grid_spec=pltpu.PrefetchScalarGridSpec(
            num_scalar_prefetch=1,
            grid=(pairs, length // block),
            in_specs=[piece(0), whole(1), whole(2)],
            out_specs=[
                pl.BlockSpec((1, dim, block), lambda p, i, lens: (p, 0, i)),
                pl.BlockSpec((block // tok, 1, dim, tok), lambda p, i, lens: (i, p, 0, 0)),
                pl.BlockSpec((1, 1, block), lambda p, i, lens: (p, 0, i)),
            ],
            scratch_shapes=[pltpu.VMEM((length, 2 * dim), BF16)],
        ),
        out_shape=[
            jax.ShapeDtypeStruct((pairs, dim, length), F32),
            jax.ShapeDtypeStruct((length // tok, pairs, dim, tok), BF16),
            jax.ShapeDtypeStruct((pairs, 1, length), F32),
        ],
        compiler_params=pltpu.CompilerParams(
            dimension_semantics=("arbitrary", "arbitrary"), vmem_limit_bytes=48 * 2**20
        ),
        cost_estimate=pl.CostEstimate(flops=1000, bytes_accessed=1000, transcendentals=0),
    )(lens, qkv, qkv, qkv)


def split_three(value):
    first = value.astype(BF16).astype(F32)
    second = (value - first).astype(BF16).astype(F32)
    third = (value - first - second).astype(BF16).astype(F32)
    return [-first, -second, -third]


def attend_back_kernel(
    block,
    lens_ref,
    q_ref,
    k_ref,
    v_ref,
    o_ref,
    lse_ref,
    grad_ref,
    out_ref,
    keys,
    values,
    queries,
    grads,
    total,
):
    length = k_ref.shape[-1]
    tok = grad_ref.shape[-1]
    count = length // block
    step = pl.program_id(1)
    scale = 1.0 / math.sqrt(HEAD_DIM)

    @pl.when(step == 0)
    def _():
        keys[...] = key_rows(lens_ref, k_ref[0, 0], length)
        one = jnp.ones((1, length), F32)
        extra = padded([one, one, one], HEAD_DIM, length)
        values[...] = jnp.concatenate([v_ref[0, 0], extra], axis=0).T
        queries[0:HEAD_DIM, :] = (q_ref[0, 0].astype(F32) * scale).astype(BF16)
        queries[HEAD_DIM:, :] = padded([one] + split_three(lse_ref[0]), HEAD_DIM, length)
        for i in range(length // tok):
            grads[0:HEAD_DIM, i * tok : (i + 1) * tok] = grad_ref[i, 0]
        delta = jnp.sum(grads[0:HEAD_DIM, :].astype(F32) * o_ref[0], axis=0, keepdims=True)
        grads[HEAD_DIM:, :] = padded(split_three(delta), HEAD_DIM, length)
        total[...] = jnp.zeros_like(total)

    mine = pl.ds(pl.multiple_of(step * block, block), block)
    key = keys[mine, :]
    value = values[mine, :]
    key_t = k_ref[0, 0, :, mine]

    def one(index, state, mask):
        dk, dv = state
        cols = pl.ds(pl.multiple_of(index * block, block), block)
        scores = dot(key, queries[:, cols])
        if mask is not None:
            scores = jnp.where(mask, scores, MASKED)
        probs = jnp.exp(scores)
        grad_scores = (probs * dot(value, grads[:, cols])).astype(BF16)
        probs = probs.astype(BF16)
        dv = dv + dot(grads[0:HEAD_DIM, cols], probs, ((1,), (1,)))
        dk = dk + dot(queries[0:HEAD_DIM, cols], grad_scores, ((1,), (1,)))
        total[:, cols] += dot(key_t, grad_scores)
        return dk, dv

    zero = jnp.zeros((HEAD_DIM, block), F32)
    state = one(step, (zero, zero), causal(block))
    dk, dv = lax.fori_loop(step + 1, count, lambda i, s: one(i, s, None), state)
    dq = total[:, mine] * scale
    for i in range(block // tok):
        cols = slice(i * tok, (i + 1) * tok)
        out_ref[i, 0, 0:HEAD_DIM] = dq[:, cols].astype(BF16)
        out_ref[i, 0, HEAD_DIM : 2 * HEAD_DIM] = dk[:, cols].astype(BF16)
        out_ref[i, 0, 2 * HEAD_DIM :] = dv[:, cols].astype(BF16)


def attend_back(lens, qkv, out, lse, grad):
    dim, length = qkv.shape[2:]
    pairs, tok = lens.shape[0], grad.shape[-1]
    ctx = length // tok
    block = math.gcd(length, 512)
    whole, _ = pair_specs(dim, length, block)
    return pl.pallas_call(
        functools.partial(attend_back_kernel, block),
        grid_spec=pltpu.PrefetchScalarGridSpec(
            num_scalar_prefetch=1,
            grid=(pairs, length // block),
            in_specs=[
                whole(0),
                whole(1),
                whole(2),
                pl.BlockSpec((1, dim, length), lambda p, i, lens: (p, 0, 0)),
                pl.BlockSpec((1, 1, length), lambda p, i, lens: (p, 0, 0)),
                pl.BlockSpec((ctx, 1, dim, tok), lambda p, i, lens: (0, p, 0, 0)),
            ],
            out_specs=pl.BlockSpec(
                (block // tok, 1, 3 * dim, tok), lambda p, i, lens: (i, p, 0, 0)
            ),
            scratch_shapes=[
                pltpu.VMEM((length, 2 * dim), BF16),
                pltpu.VMEM((length, 2 * dim), BF16),
                pltpu.VMEM((2 * dim, length), BF16),
                pltpu.VMEM((2 * dim, length), BF16),
                pltpu.VMEM((dim, length), F32),
            ],
        ),
        out_shape=jax.ShapeDtypeStruct((ctx, pairs, 3 * dim, tok), BF16),
        compiler_params=pltpu.CompilerParams(
            dimension_semantics=("arbitrary", "arbitrary"), vmem_limit_bytes=48 * 2**20
        ),
        cost_estimate=pl.CostEstimate(flops=1000, bytes_accessed=1000, transcendentals=0),
    )(lens, qkv, qkv, qkv, out, lse, grad)


def project_kernel(x_ref, w_ref, bias_ref, gain_ref, shift_ref, act_ref, out_ref):
    unit, _ = norm_parts(x_ref[0, 0].astype(F32), 0)
    act = (unit * gain_ref[...] + shift_ref[...]).astype(BF16)
    act_ref[0] = act
    out_ref[...] = (dot(w_ref[...], act) + bias_ref[...]).astype(BF16)


def project(x_all, slot, weight, bias, gain, shift):
    ctx, _, width, tok = x_all.shape
    feat = weight.shape[0]

    def fixed(shape):
        return pl.BlockSpec(shape, lambda i: (0, 0))

    return pl.pallas_call(
        project_kernel,
        grid=(ctx,),
        in_specs=[
            pl.BlockSpec((1, 1, width, tok), lambda i: (i, slot, 0, 0)),
            fixed((feat, width)),
            fixed((feat, 1)),
            fixed((width, 1)),
            fixed((width, 1)),
        ],
        out_specs=[
            pl.BlockSpec((1, width, tok), lambda i: (i, 0, 0)),
            pl.BlockSpec((feat, tok), lambda i: (0, i)),
        ],
        out_shape=[
            jax.ShapeDtypeStruct((ctx, width, tok), BF16),
            jax.ShapeDtypeStruct((feat, ctx * tok), BF16),
        ],
        compiler_params=pltpu.CompilerParams(vmem_limit_bytes=48 * 2**20),
        cost_estimate=pl.CostEstimate(flops=1000, bytes_accessed=1000, transcendentals=0),
    )(x_all, weight, bias, gain, shift)


def own_grad_kernel(late_ref, first_ref, second_ref, first_grad_ref, second_grad_ref, last_grad_ref, out_ref, total):
    step = pl.program_id(0)
    nt = ((1,), (1,))
    first, second = first_ref[0], second_ref[0]
    head = dot(first, first_grad_ref[0], nt) + dot(second, second_grad_ref[0], nt)
    last = dot(jnp.where(late_ref[0] == 0, first, second), last_grad_ref[0], nt)
    part = jnp.concatenate([head, last], axis=1)

    @pl.when(step == 0)
    def _():
        total[...] = part

    @pl.when(step > 0)
    def _():
        total[...] += part

    @pl.when(step == pl.num_programs(0) - 1)
    def _():
        out_ref[...] = total[...]


def own_grad(late, first, second, first_grad, second_grad, last_grad):
    ctx, width, tok = first.shape
    feat, last = first_grad.shape[1], last_grad.shape[1]

    def block(rows):
        return pl.BlockSpec((1, rows, tok), lambda i, late: (i, 0, 0))

    return pl.pallas_call(
        own_grad_kernel,
        grid_spec=pltpu.PrefetchScalarGridSpec(
            num_scalar_prefetch=1,
            grid=(ctx,),
            in_specs=[block(width), block(width), block(feat), block(feat), block(last)],
            out_specs=pl.BlockSpec((width, feat + last), lambda i, late: (0, 0)),
            scratch_shapes=[pltpu.VMEM((width, feat + last), F32)],
        ),
        out_shape=jax.ShapeDtypeStruct((width, feat + last), F32),
        compiler_params=pltpu.CompilerParams(vmem_limit_bytes=48 * 2**20),
        cost_estimate=pl.CostEstimate(flops=1000, bytes_accessed=1000, transcendentals=0),
    )(late[None], first, second, first_grad, second_grad, last_grad)


def mlp_kernel(
    width,
    a_ref,
    g_ref,
    up_ref,
    down_ref,
    bias_ref,
    y_ref,
    ga_ref,
    dup_ref,
    ddown_ref,
    db_ref,
    a_rows,
    g_rows,
):
    step = pl.program_id(0)
    slots, _, tok = a_ref.shape
    block = up_ref.shape[1]

    @pl.when(step == 0)
    def _():
        for s in range(slots):
            a_rows[s * tok : (s + 1) * tok, :] = a_ref[s].T
            g_rows[s * tok : (s + 1) * tok, :] = g_ref[s].T
        y_ref[...] = jnp.zeros_like(y_ref)
        ga_ref[...] = jnp.zeros_like(ga_ref)

    def run(size):
        up = up_ref[:, :size]
        down = down_ref[:, :size]
        pre = dot(a_rows[...], up) + bias_ref[:, :size]
        cdf = 0.5 * (1.0 + lax.erf(pre * math.sqrt(0.5)))
        hidden = (pre * cdf).astype(BF16)
        slope = cdf + pre * jnp.exp(-0.5 * pre * pre) * (1.0 / math.sqrt(2.0 * math.pi))
        grad = (dot(g_rows[...], down) * slope).astype(BF16)
        db_ref[:, :size] = jnp.sum(grad.astype(F32), axis=0, keepdims=True)
        nt = ((1,), (1,))
        for s in range(slots):
            rows = slice(s * tok, (s + 1) * tok)
            y_ref[s] += dot(down, hidden[rows], nt)
            ga_ref[s] += dot(up, grad[rows], nt)
        dup = sum(dot(a_ref[s], grad[s * tok : (s + 1) * tok]) for s in range(slots))
        dup_ref[:, :size] = dup.astype(dup_ref.dtype)
        ddown = sum(dot(g_ref[s], hidden[s * tok : (s + 1) * tok]) for s in range(slots))
        ddown_ref[:, :size] = ddown.astype(ddown_ref.dtype)

    full = width // block

    @pl.when(step < full)
    def _():
        run(block)

    if width % block:

        @pl.when(step == full)
        def _():
            run(width % block)


def mlp(act, grad, up, down, bias):
    slots, width, tok = act.shape
    units = up.shape[1]
    block = 256

    def fixed(shape):
        return pl.BlockSpec(shape, lambda i: (0,) * len(shape))

    cols = pl.BlockSpec((width, block), lambda i: (0, i))
    line = pl.BlockSpec((1, block), lambda i: (0, i))
    total = jax.ShapeDtypeStruct((slots, width, tok), F32)
    grads = jax.ShapeDtypeStruct((width, units), BF16)
    return pl.pallas_call(
        functools.partial(mlp_kernel, units),
        grid=(pl.cdiv(units, block),),
        in_specs=[fixed(act.shape), fixed(act.shape), cols, cols, line],
        out_specs=[fixed(act.shape), fixed(act.shape), cols, cols, line],
        out_shape=[total, total, grads, grads, jax.ShapeDtypeStruct((1, units), F32)],
        scratch_shapes=[pltpu.VMEM((slots * tok, width), BF16)] * 2,
        compiler_params=pltpu.CompilerParams(vmem_limit_bytes=56 * 2**20),
        cost_estimate=pl.CostEstimate(flops=1000, bytes_accessed=1000, transcendentals=0),
    )(act, grad, up, down, bias)


def other_index(index, bit):
    return index + bit * (1 - 2 * lax.rem(index // bit, 2))


def split_columns(start, size, count):
    tiles = size // 128
    cuts = [start + 128 * (-(-tiles * i // count)) for i in range(count)] + [start + size]
    return [(cuts[i], cuts[i + 1] - cuts[i]) for i in range(count)]


def gather_kernel(
    ctx,
    fsdp,
    x_ref,
    w_ref,
    v_ref,
    xo_ref,
    wo_ref,
    um_ref,
    uo_ref,
    vo_ref,
    x_send,
    x_recv,
    xc_send,
    xc_recv,
    w_send,
    w_recv,
    wc_send,
    wc_recv,
    v_send,
    v_recv,
    local,
):
    c, f = lax.axis_index("ctx"), lax.axis_index("fsdp")
    chips = ctx // 2
    z, core = c // 2, lax.rem(c, 2)
    partner = 2 * z + 1 - core
    slots = x_ref.shape[0]
    levels = bits_of(fsdp)
    half = um_ref.shape[2]

    def combine(number):
        place = f
        for bit in range(levels):
            if number & (1 << bit):
                place = other_index(place, 1 << bit)
        return place

    barrier = pltpu.get_barrier_semaphore()

    def greet(where):
        pl.semaphore_signal(barrier, inc=1, device_id=where, device_id_type=pl.DeviceIdType.MESH)

    greet((partner, f))
    for number in range(1, fsdp):
        greet((c, combine(number)))

    @pl.when(z > 0)
    def _():
        greet((c - 2, f))

    @pl.when(z < chips - 1)
    def _():
        greet((c + 2, f))

    beside = (z > 0).astype(jnp.int32) + (z < chips - 1).astype(jnp.int32)
    pl.semaphore_wait(barrier, fsdp + beside)

    def remote(source, target, send, recv, where):
        return pltpu.make_async_remote_copy(
            src_ref=source,
            dst_ref=target,
            send_sem=send,
            recv_sem=recv,
            device_id=where,
            device_id_type=pl.DeviceIdType.MESH,
        )

    def x_copy(side, s, h):
        sign = 1 - 2 * side
        block = c - 2 * sign * s
        source = x_ref.at[h] if s == 0 else xo_ref.at[block, h]
        return remote(
            source, xo_ref.at[block, h], x_send.at[side, s, h], x_recv.at[side, s, h], (c + 2 * sign, f)
        )

    def x_sends(side, s):
        return (z - s >= 0) & (z < chips - 1) if side == 0 else (z + s < chips) & (z > 0)

    def x_gets(side, s):
        return z - 1 - s >= 0 if side == 0 else z + 1 + s < chips

    def x_arrival(side, s, h):
        sign = 1 - 2 * side
        block = c - 2 * sign * (s + 1)
        return remote(
            xo_ref.at[block, h],
            xo_ref.at[block, h],
            x_send.at[side, s, h],
            x_recv.at[side, s, h],
            (c + 2 * sign, f),
        )

    def x_share(side, s, h):
        sign = 1 - 2 * side
        block = c - 2 * sign * (s + 1)
        return remote(
            xo_ref.at[block, h],
            xo_ref.at[block, h],
            xc_send.at[side, s, h],
            xc_recv.at[side, s, h],
            (partner, f),
        )

    def x_share_arrival(side, s, h):
        sign = 1 - 2 * side
        block = partner - 2 * sign * (s + 1)
        return remote(
            xo_ref.at[block, h],
            xo_ref.at[block, h],
            xc_send.at[side, s, h],
            xc_recv.at[side, s, h],
            (partner, f),
        )

    def x_own(h):
        return remote(
            x_ref.at[h],
            xo_ref.at[c, h],
            xc_send.at[0, chips - 1, h],
            xc_recv.at[0, chips - 1, h],
            (partner, f),
        )

    def x_own_arrival(h):
        return remote(
            x_ref.at[h],
            xo_ref.at[partner, h],
            xc_send.at[0, chips - 1, h],
            xc_recv.at[0, chips - 1, h],
            (partner, f),
        )

    runs = split_columns(0, half, levels)

    def source(unit, stream):
        start, size = runs[stream]
        return w_ref.at[:, pl.ds(pl.multiple_of((2 * unit + core) * half + start, 128), size)]

    def kept(unit, stream, place, which):
        start, size = runs[stream]
        if unit == 0:
            return wo_ref.at[place, :, pl.ds(pl.multiple_of(which * half + start, 128), size)]
        return um_ref.at[place, :, pl.ds(start, size)]

    def shared(unit, stream, place, which):
        start, size = runs[stream]
        if unit == 0:
            return kept(unit, stream, place, which)
        return uo_ref.at[place, :, pl.ds(start, size)]

    def w_copy(unit, stream, step, number):
        bit = 1 << ((stream + step) % levels)
        place = combine(number)
        there = kept(unit, stream, place, core)
        return remote(
            source(unit, stream) if number == 0 else there,
            there,
            w_send.at[unit, stream, number | bit],
            w_recv.at[unit, stream, number | bit],
            (c, other_index(f, bit)),
        )

    def w_arrival(unit, stream, number):
        block = kept(unit, stream, combine(number), core)
        sems = w_send.at[unit, stream, number], w_recv.at[unit, stream, number]
        return remote(block, block, *sems, (partner, f))

    def w_share(unit, stream, number):
        place = combine(number)
        sems = wc_send.at[unit, stream, number], wc_recv.at[unit, stream, number]
        block = kept(unit, stream, place, core)
        return remote(block, shared(unit, stream, place, core), *sems, (partner, f))

    def w_share_arrival(unit, stream, number):
        block = shared(unit, stream, combine(number), 1 - core)
        sems = wc_send.at[unit, stream, number], wc_recv.at[unit, stream, number]
        return remote(block, block, *sems, (partner, f))

    def held(stream, step):
        numbers = [0]
        for i in range(step):
            bit = 1 << ((stream + i) % levels)
            numbers += [n | bit for n in numbers]
        return numbers

    def v_copy(number):
        return remote(
            v_ref, vo_ref.at[f], v_send.at[number], v_recv.at[number], (c, combine(number))
        )

    def v_arrival(number):
        return remote(
            v_ref,
            vo_ref.at[combine(number)],
            v_send.at[number],
            v_recv.at[number],
            (c, combine(number)),
        )

    sides = [(side, h) for h in range(slots) for side in range(2)]
    for side, h in sides:

        @pl.when(x_sends(side, 0))
        def _(side=side, h=h):
            x_copy(side, 0, h).start()

    for stream in range(levels):
        w_copy(0, stream, 0, 0).start()
    for number in range(1, fsdp):
        v_copy(number).start()
    for h in range(slots):
        x_own(h).start()
    up_mine = w_ref.at[:, pl.ds(pl.multiple_of((2 + core) * half, 128), half)]
    up_other = w_ref.at[:, pl.ds(pl.multiple_of((3 - core) * half, 128), half)]
    own = [
        pltpu.make_async_copy(x_ref, xo_ref.at[c], local.at[0]),
        pltpu.make_async_copy(w_ref.at[:, pl.ds(0, 2 * half)], wo_ref.at[f], local.at[1]),
        pltpu.make_async_copy(v_ref, vo_ref.at[f], local.at[2]),
        pltpu.make_async_copy(up_mine, um_ref.at[f], local.at[3]),
        pltpu.make_async_copy(up_other, uo_ref.at[f], local.at[4]),
    ]
    for copy in own:
        copy.start()

    def x_step(s):
        for side, h in sides:

            @pl.when(x_gets(side, s))
            def _(side=side, h=h):
                x_arrival(side, s, h).wait_recv()
                x_share(side, s, h).start()

            if s + 1 < chips - 1:

                @pl.when(x_sends(side, s + 1))
                def _(side=side, h=h):
                    x_copy(side, s + 1, h).start()

    def w_step(unit, step):
        for stream in range(levels):
            bit = 1 << ((stream + step) % levels)
            arrived = [number | bit for number in held(stream, step)]
            for number in arrived:
                w_arrival(unit, stream, number).wait_recv()
            if step + 1 < levels:
                for number in held(stream, step + 1):
                    w_copy(unit, stream, step + 1, number).start()
            for number in arrived:
                w_share(unit, stream, number).start()

    def w_begin(unit):
        for stream in range(levels):
            w_copy(unit, stream, 0, 0).start()

    plan = [(1.9 * (s + 1), functools.partial(x_step, s)) for s in range(chips - 1)]
    time = 0.0
    for unit in range(2):
        for step in range(levels):
            if unit == 0 and step == levels - 1:
                plan.append((time + 0.95, functools.partial(w_begin, 1)))
            time += 2.0 ** (step + 1) / levels
            plan.append((time, functools.partial(w_step, unit, step)))
    plan = [step for _, step in sorted(plan, key=lambda entry: entry[0])]
    for step in plan:
        step()

    for copy in own:
        copy.wait()
    for number in range(1, fsdp):
        v_copy(number).wait_send()
        v_arrival(number).wait_recv()
        for unit in range(2):
            for stream in range(levels):
                w_arrival(unit, stream, number).wait_send()
                w_share(unit, stream, number).wait_send()
                w_share_arrival(unit, stream, number).wait_recv()
    for h in range(slots):
        x_own(h).wait_send()
        x_own_arrival(h).wait_recv()
    for s in range(chips - 1):
        for side, h in sides:

            @pl.when(x_sends(side, s))
            def _(side=side, h=h, s=s):
                x_copy(side, s, h).wait_send()

            @pl.when(x_gets(side, s))
            def _(side=side, h=h, s=s):
                x_share(side, s, h).wait_send()
                x_share_arrival(side, s, h).wait_recv()


def gather_first(ctx, fsdp, x, w, v):
    slots = x.shape[0]
    rows, columns = w.shape
    levels, chips = bits_of(fsdp), ctx // 2
    anywhere = pl.BlockSpec(memory_space=pl.ANY)
    dma = pltpu.SemaphoreType.DMA
    return pl.pallas_call(
        functools.partial(gather_kernel, ctx, fsdp),
        in_specs=[pl.BlockSpec(memory_space=pltpu.VMEM)] * 3,
        out_specs=[anywhere] * 5,
        out_shape=[
            jax.ShapeDtypeStruct((ctx,) + x.shape, x.dtype),
            jax.ShapeDtypeStruct((fsdp, rows, columns // 2), w.dtype),
            jax.ShapeDtypeStruct((fsdp, rows, columns // 4), w.dtype),
            jax.ShapeDtypeStruct((fsdp, rows, columns // 4), w.dtype),
            jax.ShapeDtypeStruct((fsdp,) + v.shape, v.dtype),
        ],
        scratch_shapes=[
            dma((2, chips - 1, slots)),
            dma((2, chips - 1, slots)),
            dma((2, chips, slots)),
            dma((2, chips, slots)),
            dma((2, levels, fsdp)),
            dma((2, levels, fsdp)),
            dma((2, levels, fsdp)),
            dma((2, levels, fsdp)),
            dma((fsdp,)),
            dma((fsdp,)),
            dma((5,)),
        ],
        compiler_params=pltpu.CompilerParams(
            collective_id=0, has_side_effects=True, vmem_limit_bytes=32 * 2**20
        ),
        cost_estimate=pl.CostEstimate(flops=1000, bytes_accessed=1000, transcendentals=0),
    )(x, w, v)


def bits_of(count):
    return max(count.bit_length() - 1, 0)


def flip(count, value):
    return [(i, i ^ value) for i in range(count)]


def pick(array, index, axis):
    return lax.dynamic_index_in_dim(array, index, axis, keepdims=False)


def ordered(bit, mine, other, axis):
    first = jnp.where(bit == 0, mine, other)
    second = jnp.where(bit == 0, other, mine)
    return jnp.concatenate([first, second], axis=axis)


def after(value, *others):
    return lax.optimization_barrier((value, others))[0]


def add_low(mine, swapped):
    return (mine.astype(F32) + swapped.astype(F32)).astype(BF16)


def scatter_fsdp(total):
    return lax.psum_scatter(total, "fsdp", scatter_dimension=0, tiled=True)


def bar_signal(where):
    pl.semaphore_signal(
        pltpu.get_barrier_semaphore(), inc=1, device_id=where, device_id_type=pl.DeviceIdType.MESH
    )


def remote_copy(source, target, send, recv, where):
    return pltpu.make_async_remote_copy(
        src_ref=source,
        dst_ref=target,
        send_sem=send,
        recv_sem=recv,
        device_id=where,
        device_id_type=pl.DeviceIdType.MESH,
    )


def line_gather(chips, c, f, mine, slot, share, sems, core_sems):
    z, core = c // 2, lax.rem(c, 2)
    partner = 2 * z + 1 - core
    send, recv = sems
    core_send, core_recv = core_sems

    def passing(side, s):
        sign = 1 - 2 * side
        chip = z - sign * s
        source = mine if s == 0 else slot(chip)
        return remote_copy(
            source, slot(chip), send.at[side, s], recv.at[side, s], (c + 2 * sign, f)
        )

    def arrival(side, s):
        block = slot(z - (1 - 2 * side) * (s + 1))
        return remote_copy(block, block, send.at[side, s], recv.at[side, s], (partner, f))

    def sends(side, s):
        return (z - s >= 0) & (z < chips - 1) if side == 0 else (z + s < chips) & (z > 0)

    def gets(side, s):
        return z - 1 - s >= 0 if side == 0 else z + 1 + s < chips

    def shared(side, s):
        chip = z - (1 - 2 * side) * (s + 1)
        return remote_copy(
            slot(chip), share(chip), core_send.at[side, s], core_recv.at[side, s], (partner, f)
        )

    def share_arrival(side, s):
        block = share(z - (1 - 2 * side) * (s + 1))
        sems = core_send.at[side, s], core_recv.at[side, s]
        return remote_copy(block, block, *sems, (partner, f))

    own_sems = core_send.at[0, chips - 1], core_recv.at[0, chips - 1]
    own_share = remote_copy(mine, share(z), *own_sems, (partner, f))

    def start():
        for side in range(2):

            @pl.when(sends(side, 0))
            def _(side=side):
                passing(side, 0).start()

        own_share.start()

    def step(s):
        for side in range(2):

            @pl.when(gets(side, s))
            def _(side=side):
                arrival(side, s).wait_recv()
                shared(side, s).start()

            if s + 1 < chips - 1:

                @pl.when(sends(side, s + 1))
                def _(side=side):
                    passing(side, s + 1).start()

    def end():
        own_share.wait_send()
        remote_copy(share(z), share(z), *own_sems, (partner, f)).wait_recv()
        for s in range(chips - 1):
            for side in range(2):

                @pl.when(sends(side, s))
                def _(side=side, s=s):
                    passing(side, s).wait_send()

                @pl.when(gets(side, s))
                def _(side=side, s=s):
                    shared(side, s).wait_send()
                    share_arrival(side, s).wait_recv()

    return start, [functools.partial(step, s) for s in range(chips - 1)], end


def sum_kernel(ctx, fsdp, batches, *refs):
    levels, chips = bits_of(fsdp), ctx // 2
    pieces = refs[0:2]
    own_ref, _, mine_out, other_out, own_out, last_out = refs[2:8]
    rest = list(refs[8:])
    own_kept, own_low = rest.pop(0), rest.pop(0)
    own_sent = [rest.pop(0) for _ in range(levels)]
    own_got = [rest.pop(0) for _ in range(levels)]
    z_sent, z_got = rest.pop(0), rest.pop(0)
    op_send, op_recv, zs_send, zs_recv, zg_send, zg_recv = (rest.pop(0) for _ in range(6))
    zc_send, zc_recv, og_send, og_recv, oc_send, oc_recv, far_send, far_recv, local = (
        rest.pop(0) for _ in range(9)
    )
    c, f = lax.axis_index("ctx"), lax.axis_index("fsdp")
    z, core = c // 2, lax.rem(c, 2)
    partner = 2 * z + 1 - core
    far = lax.rem(c + ctx // 2, ctx)
    rows = own_low.shape[0]
    chunk = z_sent.shape[-1]
    width = chunk * chips // 2
    parts = chips // 2
    strip = 16 if rows % 16 == 0 else 8

    def own_bit(bit):
        return lax.rem(f // (1 << bit), 2)

    def strips(work):
        def body(i, carry):
            work(pl.ds(pl.multiple_of(i * strip, strip), strip))
            return carry

        lax.fori_loop(0, rows // strip, body, 0)

    bar_signal((partner, f))
    bar_signal((far, f))
    for bit in range(levels):
        bar_signal((c, other_index(f, 1 << bit)))

    @pl.when(z > 0)
    def _():
        bar_signal((c - 2, f))

    @pl.when(z < chips - 1)
    def _():
        bar_signal((c + 2, f))

    beside = (z > 0).astype(jnp.int32) + (z < chips - 1).astype(jnp.int32)
    pl.semaphore_wait(pltpu.get_barrier_semaphore(), levels + 2 + beside)

    def order(q):
        return [(q + i) % levels for i in range(levels)]

    def place_of(q, flipped, free):
        bits = order(q)
        first = own_bit(bits[0])
        total = (1 - first if flipped else first) * (1 << bits[0])
        for i, bit in enumerate(bits[1:]):
            total += ((free >> i) & 1) * (1 << bit)
        return total

    def kept_index(q, step, flipped, free):
        bits = order(q)
        total = 0
        for i, bit in enumerate(bits[1:]):
            mine = own_bit(bit)
            if i + 1 < step:
                value = mine
            elif i + 1 == step:
                value = 1 - mine if flipped else mine
            else:
                value = (free >> (i - step)) & 1
            total += value * (1 << i)
        return total

    def across(step, q):
        return (c, other_index(f, 1 << order(q)[step]))

    def own_copy(step):
        return remote_copy(
            own_sent[step], own_got[step], op_send.at[step], op_recv.at[step], across(step, 0)
        )

    def own_begin():
        for free in range(fsdp // 2):
            there, here = place_of(0, True, free), place_of(0, False, free)

            def work(at, free=free, there=there, here=here):
                own_sent[0][free, at, :] = own_ref[there, at, :]
                own_kept[free, at, :] = own_ref[here, at, :].astype(F32)

            strips(work)
        own_copy(0).start()

    def later(step, kept_ref, got_ref, sent_ref, q):
        for free in range(fsdp >> (step + 2)):
            there, here = (kept_index(q, step + 1, flipped, free) for flipped in (True, False))
            mine = own_bit(order(q)[step + 1])
            there_got, here_got = free * 2 + 1 - mine, free * 2 + mine

            def work(at, free=free):
                value = kept_ref[there, at, :] + got_ref[there_got, at, :].astype(F32)
                sent_ref[free, at, :] = value.astype(BF16)
                kept_ref[here, at, :] += got_ref[here_got, at, :].astype(F32)

            strips(work)

    def last(kept_ref, got_ref, q, place):
        def work(at):
            place(at, kept_ref[kept_index(q, levels, False, 0), at, :] + got_ref[0, at, :].astype(F32))

        strips(work)

    def own_step(step):
        own_copy(step).wait_recv()
        if step + 1 < levels:
            later(step, own_kept, own_got[step], own_sent[step + 1], 0)
            own_copy(step + 1).start()
            return

        def place(at, value):
            own_low[at, :] = value.astype(BF16)

        last(own_kept, own_got[step], 0, place)
        for copy in far_copies:
            copy.start()
        own_start()

    head = own_out.shape[2]
    tail = last_out.shape[2]
    far_copies = [
        remote_copy(
            own_low.at[:, pl.ds(head, tail)], last_out.at[1], far_send.at[0], far_recv.at[0], (far, f)
        ),
        pltpu.make_async_copy(own_low.at[:, pl.ds(head, tail)], last_out.at[0], local.at[0]),
        pltpu.make_async_copy(own_low.at[:, pl.ds(0, head)], own_out.at[c], local.at[1]),
    ]
    own_start, own_steps, own_end = line_gather(
        chips,
        c,
        f,
        own_low.at[:, pl.ds(0, head)],
        lambda chip: own_out.at[2 * chip + core],
        lambda chip: own_out.at[2 * chip + core],
        (og_send, og_recv),
        (oc_send, oc_recv),
    )

    def total_of(j, b, at):
        part = pieces[j // parts][at, pl.ds(b * width + (j % parts) * chunk, chunk)]
        return part.astype(F32)

    def z_copy(side, i, b):
        return remote_copy(
            z_sent.at[side, b, i],
            z_got.at[side, b, i],
            zs_send.at[side, b, i],
            zs_recv.at[side, b, i],
            (c + 2 * (1 - 2 * side), f),
        )

    def z_last(side, chip):
        return chips - 1 - chip if side == 0 else chip

    def z_step(turn, b):
        for chip in range(chips):

            @pl.when(z == chip)
            def _(chip=chip):
                for side in range(2):
                    j_of = (lambda i: chips - 1 - i) if side == 0 else (lambda i: i)
                    begun = chip if side == 0 else chips - 1 - chip
                    i = turn - begun
                    sends = z_last(side, chip)
                    if begun > 0 and 0 <= i <= sends and i < chips - 1:
                        z_copy(side, i, b).wait_recv()
                    if 0 <= i < sends:
                        if i > 0:
                            z_copy(side, i - 1, b).wait_send()

                        def work(at, side=side, i=i, j=j_of(i), begun=begun):
                            value = total_of(j, b, at)
                            if begun > 0:
                                value += z_got[side, b, i, at, :].astype(F32)
                            z_sent[side, b, i, at, :] = value.astype(BF16)

                        strips(work)
                        z_copy(side, i, b).start()

    def chunk_of(ref, chip, b):
        start = pl.multiple_of(b * width + lax.rem(chip, parts) * chunk, 128)
        return ref.at[chip // parts, :, pl.ds(start, chunk)]

    gathers = []
    for b in range(batches):
        gathers.append(
            line_gather(
                chips,
                c,
                f,
                chunk_of(mine_out, z, b),
                lambda chip, b=b: chunk_of(mine_out, chip, b),
                lambda chip, b=b: chunk_of(other_out, chip, b),
                (zg_send.at[:, b], zg_recv.at[:, b]),
                (zc_send.at[:, b], zc_recv.at[:, b]),
            )
        )

    def finish(b):
        for j in range(chips):

            @pl.when(z == j)
            def _(j=j):
                def work(at):
                    value = total_of(j, b, at)
                    if j > 0:
                        value += z_got[0, b, chips - 1 - j, at, :].astype(F32)
                    if j < chips - 1:
                        value += z_got[1, b, j, at, :].astype(F32)
                    start = b * width + (j % parts) * chunk
                    mine_out[j // parts, at, pl.ds(start, chunk)] = value.astype(BF16)

                strips(work)

        gathers[b][0]()

    own_begin()
    waiting = list(own_steps)
    for turn in range(batches + 1):
        for i in range(chips):
            if turn < batches:
                z_step(i, turn)
            if i < chips - 1 and turn > 0:
                gathers[turn - 1][1][i]()
        if turn < batches:
            finish(turn)
        if turn < levels:
            own_step(turn)
        else:
            for step in waiting[:2]:
                step()
            waiting = waiting[2:]
    for turn in range(batches + 1, levels):
        own_step(turn)
    for step in waiting:
        step()

    far_copies[0].wait()
    far_copies[1].wait()
    far_copies[2].wait()
    own_end()
    for step in range(levels):
        own_copy(step).wait_send()
    for b in range(batches):
        gathers[b][2]()
        for chip in range(chips):

            @pl.when(z == chip)
            def _(chip=chip, b=b):
                for side in range(2):
                    if z_last(side, chip):
                        z_copy(side, z_last(side, chip) - 1, b).wait_send()


def sum_grads(ctx, fsdp, pieces, own, head, gate):
    levels, chips = bits_of(fsdp), ctx // 2
    rows, whole = pieces[0].shape
    batches = max(n for n in range(1, 3) if whole % n == 0 and 2 * whole // n % (chips * 128) == 0)
    width = whole // batches
    chunk = 2 * width // chips
    own_width = own.shape[-1]
    vmem = pl.BlockSpec(memory_space=pltpu.VMEM)
    dma = pltpu.SemaphoreType.DMA
    steps = [fsdp >> (i + 1) for i in range(levels)]
    result = jax.ShapeDtypeStruct((2, rows, whole), BF16)
    mine, other, own_all, last = pl.pallas_call(
        functools.partial(sum_kernel, ctx, fsdp, batches),
        in_specs=[vmem] * 3 + [pl.BlockSpec(memory_space=pl.ANY)],
        out_specs=[vmem] * 4,
        out_shape=[
            result,
            result,
            jax.ShapeDtypeStruct((ctx, rows, head), BF16),
            jax.ShapeDtypeStruct((2, rows, own_width - head), BF16),
        ],
        scratch_shapes=[
            pltpu.VMEM((fsdp // 2, rows, own_width), F32),
            pltpu.VMEM((rows, own_width), BF16),
        ]
        + [pltpu.VMEM((n, rows, own_width), BF16) for n in steps * 2]
        + [pltpu.VMEM((2, batches, chips - 1, rows, chunk), BF16)] * 2
        + [dma((levels,))] * 2
        + [dma((2, batches, chips - 1))] * 4
        + [dma((2, batches, chips))] * 2
        + [dma((2, chips - 1))] * 2
        + [dma((2, chips))] * 2
        + [dma((1,))] * 2
        + [dma((6,))],
        compiler_params=pltpu.CompilerParams(
            collective_id=1, has_side_effects=True, vmem_limit_bytes=60 * 2**20
        ),
        cost_estimate=pl.CostEstimate(flops=1000, bytes_accessed=1000, transcendentals=0),
    )(*pieces, own, gate)

    return mine, other, own_all, last


def swap_cores(mine, ctx):
    return lax.ppermute(mine, "ctx", flip(ctx, 1))


def norm_parts(rows, axis):
    middle = jnp.mean(rows, axis=axis, keepdims=True)
    centred = rows - middle
    spread = jnp.mean(centred * centred, axis=axis, keepdims=True)
    inverse = lax.rsqrt(spread + NORM_EPS)
    return centred * inverse, inverse


def norm_back(grad, unit, inverse, gain):
    inner = grad * gain
    mean_inner = jnp.mean(inner, axis=1, keepdims=True)
    mean_cross = jnp.mean(inner * unit, axis=1, keepdims=True)
    rows = inverse * (inner - mean_inner - unit * mean_cross)
    return rows, jnp.sum(grad * unit, axis=(0, 2)), jnp.sum(grad, axis=(0, 2))


def adamw(weight, first, second, grad, rate, decay):
    moment = BETA_ONE * first.astype(F32) + (1.0 - BETA_ONE) * grad
    square = BETA_TWO * second + (1.0 - BETA_TWO) * grad * grad
    corrected = moment / (1.0 - BETA_ONE**STEP)
    scaled = square / (1.0 - BETA_TWO**STEP)
    new_weight = weight - rate * (corrected / (jnp.sqrt(scaled) + ADAM_EPS) + decay * weight)
    return (moment, square, new_weight)


def update_kernel(units, regular, *refs):
    (w, first, second, dw, dfirst, dsecond, own, last, mine, other) = refs[:10]
    outs = refs[10:]
    core = lax.rem(lax.axis_index("ctx"), 2)
    width = (w.shape[1] - 2 * units) // 4
    quarter = width // 4
    ctx = own.shape[0]
    dim = HEAD_DIM

    def halves(q, start, size):
        here = mine[q, :, start : start + size].astype(F32)
        there = other[q, :, start : start + size].astype(F32)
        return jnp.where(core == 0, here, there), jnp.where(core == 0, there, here)

    def both(q, start, size):
        return jnp.concatenate(halves(q, start, size), axis=1)

    heads = []
    for part in range(3):
        for i in range(regular):
            for c in range(ctx):
                column = (i * 3 + part) * dim
                heads.append(own[c, :, column : column + dim].astype(F32))
        column = part * dim
        heads.append(
            last[0, :, column : column + dim].astype(F32)
            + last[1, :, column : column + dim].astype(F32)
        )
    out = [halves(q, units, quarter) for q in range(2)]
    heads += [out[0][0], out[1][0], out[0][1], out[1][1]]
    grad = jnp.concatenate(heads, axis=1)

    def put(targets, cols, values):
        for target, value in zip(targets, values):
            target[:, cols] = value

    cols = slice(0, 4 * width)
    put(outs[:3], cols, adamw(w[:, cols], first[:, cols], second[:, cols], grad, 0.03, 0.1))
    cols = slice(4 * width, w.shape[1])
    grad = both(0, 0, units)
    put(outs[:3], cols, adamw(w[:, cols], first[:, cols], second[:, cols], grad, 0.03, 0.1))
    grad = both(1, 0, units)
    put(outs[3:], slice(None), adamw(dw[...], dfirst[...], dsecond[...], grad, 0.02, 0.1))


def update(rows_state, down_state, own, last, mine, other, units, regular):
    rows = rows_state[0].shape[0]
    strip = 16 if rows % 16 == 0 else 8

    def flat(array):
        return pl.BlockSpec((strip, array.shape[1]), lambda i: (i, 0))

    def deep(array):
        return pl.BlockSpec((array.shape[0], strip, array.shape[2]), lambda i: (0, i, 0))

    states, sums = [*rows_state, *down_state], [own, last, mine, other]
    results = [rows_state[0]] * 3 + [down_state[0]] * 3
    return pl.pallas_call(
        functools.partial(update_kernel, units, regular),
        grid=(rows // strip,),
        in_specs=[flat(a) for a in states] + [deep(a) for a in sums],
        out_specs=[flat(a) for a in results],
        out_shape=[jax.ShapeDtypeStruct(a.shape, F32) for a in results],
        compiler_params=pltpu.CompilerParams(vmem_limit_bytes=56 * 2**20),
        cost_estimate=pl.CostEstimate(flops=1000, bytes_accessed=1000, transcendentals=0),
    )(*states, *sums)


def body(
    ctx,
    fsdp,
    tokens,
    cotangent,
    lengths,
    w_rows,
    rows_first,
    rows_second,
    w_down,
    down_first,
    down_second,
    vectors,
    vec_first,
    vec_second,
):
    tok, slots, width = tokens.shape
    dim = HEAD_DIM
    regular = HEADS // ctx
    owned = regular + 1
    share = width // fsdp
    c = lax.axis_index("ctx")
    core = c % 2
    late = (c >= ctx // 2).astype(jnp.int32)
    half = FF // 2

    def my_half(array):
        return lax.dynamic_slice_in_dim(array, core * half, half, 1)

    x_low = tokens.transpose(1, 2, 0)
    vec_part = jnp.pad(vectors.astype(BF16).T, ((0, 0), (0, 128 - vectors.shape[0])))
    x_all, head_w, up_mine, up_other, vec_low = gather_first(
        ctx, fsdp, x_low, w_rows.astype(BF16), vec_part
    )
    head_w = head_w.reshape(width, 4 * width)
    up_mine, up_other = up_mine.reshape(width, half), up_other.reshape(width, half)
    vec_low = vec_low.reshape(width, 128)
    down_mine, vec_low = lax.optimization_barrier((my_half(w_down.T).astype(BF16), vec_low))
    down_mine = lax.all_gather(down_mine, "fsdp", axis=0, tiled=True)
    vec = [vec_low[:, i : i + 1].astype(F32) for i in range(12)]
    up_bias = vec_low[:, 8:12].T.astype(F32).reshape(1, FF)

    starts = [(i * ctx + c) * dim for i in range(regular)] + [(HEADS - 1) * dim]
    own_w = jnp.concatenate(
        [
            lax.dynamic_slice_in_dim(head_w, part * width + start, dim, 1)
            for part in range(3)
            for start in starts
        ],
        axis=1,
    )
    q_bias = jnp.concatenate([lax.dynamic_slice_in_dim(vec[2], s, dim, 0) for s in starts], axis=0)
    v_bias = jnp.concatenate([lax.dynamic_slice_in_dim(vec[3], s, dim, 0) for s in starts], axis=0)
    own_bias = jnp.concatenate([q_bias, jnp.zeros_like(q_bias), v_bias], axis=0)
    own_w = own_w.T
    far = (c + ctx // 2) % ctx
    def to_rows(array):
        feat = array.shape[2]
        got = lax.all_to_all(array, "ctx", 0, 0)
        return got.transpose(1, 0, 2, 3).reshape(regular * ctx, feat, tok)

    def last_to_rows(array):
        mine = pick(array, c, 0)
        got = lax.ppermute(pick(array, far, 0), "ctx", flip(ctx, ctx // 2))
        return jnp.where(late == 0, mine, got), jnp.where(late == 0, got, mine)

    def to_send(array):
        return array.reshape(regular, ctx, dim, tok).transpose(1, 0, 2, 3)

    acts, projected = [], []

    def project_slot(s, x_all):
        act, qkv = project(x_all, s, own_w, own_bias, vec[0], vec[1])
        acts.append(act)
        projected.append(qkv.reshape(3, owned, dim, ctx * tok))

    def attend_slot(s, *gate):
        lens = after(jnp.repeat(lengths[s : s + 1], regular), *gate)
        return (lens, projected[s], *attend(lens, projected[s], tok))

    project_slot(0, x_all)
    results = [attend_slot(0)]
    rows = [to_rows(results[0][3])]
    project_slot(1, after(x_all, results[0][2]))
    last_qkv = jnp.where(late == 0, *(qkv[:, regular:] for qkv in projected))
    last_len = lax.dynamic_slice_in_dim(lengths, late, 1, 0)
    last_result = (last_len, last_qkv, *attend(last_len, last_qkv, tok))
    results += [attend_slot(1, last_result[2], rows[0]), last_result]
    rows.append(to_rows(results[1][3]))
    down_mine = after(down_mine, results[1][2])
    down_other = swap_cores(down_mine, ctx)
    last_rows = last_to_rows(results[2][3])
    att = [jnp.concatenate([rows[s], last_rows[s]]).reshape(width, tok) for s in range(slots)]
    att = jnp.stack(att)

    x = x_low.astype(F32)
    out_w = head_w[:, 3 * width :]
    mid = x + jnp.einsum("de,sdt->set", out_w, att, preferred_element_type=F32) + vec[4]
    unit_two, inverse_two = norm_parts(mid, 1)
    act_two = (unit_two * vec[5] + vec[6]).astype(BF16)

    pos = c * tok + jnp.arange(tok, dtype=jnp.int32)
    valid = pos[None, None, :] < lengths[:, None, None]
    g_low = jnp.where(valid, cotangent.transpose(1, 2, 0), jnp.zeros((), BF16))
    g = g_low.astype(F32)

    bias_mine = lax.dynamic_slice_in_dim(up_bias, core * half, half, 1)
    bias_other = lax.dynamic_slice_in_dim(up_bias, (1 - core) * half, half, 1)
    y_other, ga_other, dup_other, ddown_other, db_other = mlp(
        act_two, g_low, up_other, down_other, bias_other
    )
    y_mine, ga_mine, dup_mine, ddown_mine, db_mine = mlp(
        act_two, g_low, up_mine, down_mine, bias_mine
    )
    output = (mid + (y_mine + y_other + vec[7])).astype(BF16).transpose(2, 0, 1)

    up_swapped, down_swapped = swap_cores(dup_other, ctx), swap_cores(ddown_other, ctx)
    up_total, down_total = add_low(dup_mine, up_swapped), add_low(ddown_mine, down_swapped)
    up_part, down_part = scatter_fsdp(up_total), scatter_fsdp(down_total)
    ga_mine = after(ga_mine, up_total, down_total)

    grad_mid, gain_two, shift_two = norm_back(ga_mine + ga_other, unit_two, inverse_two, vec[5])
    grad_mid = g + grad_mid
    grad_attn = grad_mid.astype(BF16)
    grad_att = jnp.einsum("de,set->sdt", out_w, grad_attn, preferred_element_type=F32).astype(BF16)
    grad_att = grad_att.reshape(slots, HEADS, dim, tok)
    last = jnp.repeat(grad_att[:, -1], ctx // slots, axis=0)[:, None]
    first_pairs = lax.all_to_all(to_send(grad_att[0, :-1]), "ctx", 0, 0)
    other_pairs = lax.all_to_all(
        after(jnp.concatenate([to_send(grad_att[1, :-1]), last], axis=1), first_pairs), "ctx", 0, 0
    )

    quarter = width // 4
    spread = jnp.pad(
        grad_attn.reshape(slots, 4, quarter, tok), ((0, 0), (0, 0), (0, -quarter % 128), (0, 0))
    )
    out_grad = jnp.einsum("sdt,sket->kde", att, spread, preferred_element_type=F32).astype(BF16)
    out_grad = out_grad.reshape(2, 2, fsdp, share, spread.shape[2])

    def out_half(which):
        return pick(out_grad, which, 0).reshape(2, width, spread.shape[2])

    out_mine, out_swapped = out_half(core), swap_cores(out_half(1 - core), ctx)
    out_total = add_low(out_mine, out_swapped)
    out_part = scatter_fsdp(jnp.concatenate([out_total[0], out_total[1]], axis=1))
    out_part = jnp.split(out_part, 2, axis=1)
    grad_heads = [attend_back(*results[0][:3], results[0][4], first_pairs)]
    grad_heads.append(
        attend_back(*results[1][:3], results[1][4], after(other_pairs[:, :-1], grad_heads[0], up_part))
    )
    first_rows = to_rows(grad_heads[0])
    grad_heads.append(
        attend_back(*results[2][:3], results[2][4], after(other_pairs[:, -1:], first_rows, grad_heads[1]))
    )
    other_rows = to_rows(grad_heads[1])
    last_rows = last_to_rows(grad_heads[2])

    feat = 3 * dim
    own_sum = own_grad(
        late,
        acts[0],
        acts[1],
        grad_heads[0].reshape(ctx, regular * feat, tok),
        grad_heads[1].reshape(ctx, regular * feat, tok),
        grad_heads[2].reshape(ctx, feat, tok),
    )
    own_sum = own_sum.astype(BF16)
    own_sum = jnp.concatenate(
        [
            jnp.pad(part, ((0, 0), (0, -part.shape[1] % 128)))
            for part in (own_sum[:, : regular * feat], own_sum[:, regular * feat :])
        ],
        axis=1,
    )
    head_columns = regular * feat + -regular * feat % 128
    blocks = (fsdp, share)
    sum_mine, sum_other, own_all, last = sum_grads(
        ctx,
        fsdp,
        [
            jnp.concatenate([part, out_part[q]], axis=1)
            for q, part in enumerate((up_part, down_part))
        ],
        own_sum.reshape(*blocks, own_sum.shape[1]),
        head_columns,
        other_rows,
    )
    grad_qkv = []
    for s, rows in enumerate((first_rows, other_rows)):
        rows = after(jnp.concatenate([rows, last_rows[s]]), sum_mine)
        rows = rows.reshape(HEADS, 3, dim, tok).transpose(1, 0, 2, 3)
        grad_qkv.append(rows.reshape(3 * width, tok))
    grad_qkv = jnp.stack(grad_qkv)
    grad_one = jnp.einsum(
        "de,set->sdt", head_w[:, : 3 * width], grad_qkv, preferred_element_type=F32
    )

    unit_one, inverse_one = norm_parts(x, 1)
    grad_in, gain_one, shift_one = norm_back(grad_one, unit_one, inverse_one, vec[0])
    grad_tokens = (grad_mid + grad_in).astype(BF16)

    bias_qkv = jnp.sum(grad_qkv.astype(F32), axis=(0, 2))
    vec_grad = jnp.stack(
        [
            gain_one,
            shift_one,
            bias_qkv[:width],
            bias_qkv[2 * width :],
            jnp.sum(grad_attn.astype(F32), axis=(0, 2)),
            gain_two,
            shift_two,
            jnp.sum(g, axis=(0, 2)),
        ]
    )
    bias_up = ordered(core, db_mine, db_other, 1).reshape(4, width)
    vec_grad = jnp.concatenate([vec_grad, bias_up], axis=0).reshape(12, fsdp, share)
    f = lax.axis_index("fsdp")
    vec_sum = pick(vec_grad, f, 1)
    for value in range(1, fsdp):
        vec_sum = vec_sum + lax.ppermute(pick(vec_grad, f ^ value, 1), "fsdp", flip(fsdp, value))
    for level in range(bits_of(ctx)):
        vec_sum = vec_sum + lax.ppermute(vec_sum, "ctx", flip(ctx, 2**level))

    rows_state = (w_rows, rows_first, rows_second)
    down_state = (w_down.T, down_first.T, down_second.T)
    updated = update(
        rows_state, down_state, own_all, last, sum_mine, sum_other, half, regular
    )
    rows_out, down_out = updated[:3], tuple(part.T for part in updated[3:])
    vec_out = adamw(vectors, vec_first, vec_second, vec_sum, 0.3, 0.0)
    return (output, grad_tokens.transpose(2, 0, 1), *rows_out, *down_out, *vec_out)


def solution(mesh):
    placed = (
        P("ctx", "fsdp", None),
        P("ctx", "fsdp", None),
        P("fsdp"),
        P("fsdp", None),
        P("fsdp", None),
        P("fsdp", None),
        P(None, "fsdp"),
        P(None, "fsdp"),
        P(None, "fsdp"),
        P(None, "fsdp"),
        P(None, "fsdp"),
        P(None, "fsdp"),
    )
    return jax.shard_map(
        functools.partial(body, mesh.shape["ctx"], mesh.shape["fsdp"]),
        mesh=mesh,
        in_specs=placed,
        out_specs=placed[:2] + placed[3:6] + placed[6:9] + placed[9:12],
        check_vma=False,
    )
```

```python
import functools
import math

import jax
import jax.numpy as jnp
from jax import lax
from jax.experimental import pallas as pl
from jax.experimental.pallas import tpu as pltpu
from jax.sharding import PartitionSpec as P

HEADS = 17
HEAD_DIM = 64
FF = 4352
STEP = 10

MASKED = -1e30
NORM_EPS = 1e-05
BETA_ONE = 0.9
BETA_TWO = 0.95
ADAM_EPS = 1e-08
BF16 = jnp.bfloat16
F32 = jnp.float32


def dot(left, right, dims=((1,), (0,))):
    return lax.dot_general(left, right, (dims, ((), ())), preferred_element_type=F32)


def padded(top, rows, width):
    row = lax.broadcasted_iota(jnp.int32, (rows, width), 0)
    out = jnp.zeros((rows, width), F32)
    for index, value in enumerate(top):
        out = jnp.where(row == index, value, out)
    return out.astype(BF16)


def key_rows(lens_ref, key, length):
    pos = lax.broadcasted_iota(jnp.int32, (1, length), 1)
    bias = jnp.where(pos < lens_ref[pl.program_id(0)], 0.0, MASKED)
    one = jnp.ones((1, length), F32)
    extra = padded([bias, one, one, one], HEAD_DIM, length)
    return jnp.concatenate([key, extra], axis=0).T


def causal(block):
    key = lax.broadcasted_iota(jnp.int32, (block, block), 0)
    query = lax.broadcasted_iota(jnp.int32, (block, block), 1)
    return key <= query


def attend_kernel(block, lens_ref, q_ref, k_ref, v_ref, o_ref, low_ref, lse_ref, keys):
    length = k_ref.shape[-1]
    tok = low_ref.shape[-1]
    step = pl.program_id(1)

    @pl.when(step == 0)
    def _():
        keys[...] = key_rows(lens_ref, k_ref[0, 0], length)

    query = (q_ref[0, 0].astype(F32) * (1.0 / math.sqrt(HEAD_DIM))).astype(BF16)
    query = jnp.concatenate(
        [query, padded([jnp.ones((1, block), F32)], HEAD_DIM, block)], axis=0
    )

    def one(index, state, mask):
        top, total, accum = state
        start = pl.multiple_of(index * block, block)
        scores = dot(keys[pl.ds(start, block), :], query)
        if mask is not None:
            scores = jnp.where(mask, scores, MASKED)
        new_top = jnp.maximum(top, jnp.max(scores, axis=0, keepdims=True))
        weights = jnp.exp(scores - new_top)
        factor = jnp.exp(top - new_top)
        total = total * factor + jnp.sum(weights, axis=0, keepdims=True)
        value = v_ref[0, 0, :, pl.ds(start, block)]
        accum = accum * factor + dot(value, weights.astype(BF16))
        return new_top, total, accum

    state = (
        jnp.full((1, block), MASKED, F32),
        jnp.zeros((1, block), F32),
        jnp.zeros((HEAD_DIM, block), F32),
    )
    state = lax.fori_loop(0, step, lambda i, s: one(i, s, None), state)
    top, total, accum = one(step, state, causal(block))
    result = accum / total
    o_ref[0] = result
    for i in range(block // tok):
        low_ref[i, 0] = result[:, i * tok : (i + 1) * tok].astype(BF16)
    lse_ref[0] = top + jnp.log(total)


def pair_specs(dim, length, block):
    def whole(part):
        return pl.BlockSpec((1, 1, dim, length), lambda p, i, lens: (part, p, 0, 0))

    def piece(part):
        return pl.BlockSpec((1, 1, dim, block), lambda p, i, lens: (part, p, 0, i))

    return whole, piece


def attend(lens, qkv, tok):
    dim, length = qkv.shape[2:]
    pairs = lens.shape[0]
    block = math.gcd(length, 512)
    whole, piece = pair_specs(dim, length, block)
    return pl.pallas_call(
        functools.partial(attend_kernel, block),
        grid_spec=pltpu.PrefetchScalarGridSpec(
            num_scalar_prefetch=1,
            grid=(pairs, length // block),
            in_specs=[piece(0), whole(1), whole(2)],
            out_specs=[
                pl.BlockSpec((1, dim, block), lambda p, i, lens: (p, 0, i)),
                pl.BlockSpec((block // tok, 1, dim, tok), lambda p, i, lens: (i, p, 0, 0)),
                pl.BlockSpec((1, 1, block), lambda p, i, lens: (p, 0, i)),
            ],
            scratch_shapes=[pltpu.VMEM((length, 2 * dim), BF16)],
        ),
        out_shape=[
            jax.ShapeDtypeStruct((pairs, dim, length), F32),
            jax.ShapeDtypeStruct((length // tok, pairs, dim, tok), BF16),
            jax.ShapeDtypeStruct((pairs, 1, length), F32),
        ],
        compiler_params=pltpu.CompilerParams(
            dimension_semantics=("arbitrary", "arbitrary"), vmem_limit_bytes=48 * 2**20
        ),
        cost_estimate=pl.CostEstimate(flops=1000, bytes_accessed=1000, transcendentals=0),
    )(lens, qkv, qkv, qkv)


def split_three(value):
    first = value.astype(BF16).astype(F32)
    second = (value - first).astype(BF16).astype(F32)
    third = (value - first - second).astype(BF16).astype(F32)
    return [-first, -second, -third]


def attend_back_kernel(
    block,
    lens_ref,
    q_ref,
    k_ref,
    v_ref,
    o_ref,
    lse_ref,
    grad_ref,
    out_ref,
    keys,
    values,
    queries,
    grads,
    total,
):
    length = k_ref.shape[-1]
    tok = grad_ref.shape[-1]
    count = length // block
    step = pl.program_id(1)
    scale = 1.0 / math.sqrt(HEAD_DIM)

    @pl.when(step == 0)
    def _():
        keys[...] = key_rows(lens_ref, k_ref[0, 0], length)
        one = jnp.ones((1, length), F32)
        extra = padded([one, one, one], HEAD_DIM, length)
        values[...] = jnp.concatenate([v_ref[0, 0], extra], axis=0).T
        queries[0:HEAD_DIM, :] = (q_ref[0, 0].astype(F32) * scale).astype(BF16)
        queries[HEAD_DIM:, :] = padded([one] + split_three(lse_ref[0]), HEAD_DIM, length)
        for i in range(length // tok):
            grads[0:HEAD_DIM, i * tok : (i + 1) * tok] = grad_ref[i, 0]
        delta = jnp.sum(grads[0:HEAD_DIM, :].astype(F32) * o_ref[0], axis=0, keepdims=True)
        grads[HEAD_DIM:, :] = padded(split_three(delta), HEAD_DIM, length)
        total[...] = jnp.zeros_like(total)

    mine = pl.ds(pl.multiple_of(step * block, block), block)
    key = keys[mine, :]
    value = values[mine, :]
    key_t = k_ref[0, 0, :, mine]

    def one(index, state, mask):
        dk, dv = state
        cols = pl.ds(pl.multiple_of(index * block, block), block)
        scores = dot(key, queries[:, cols])
        if mask is not None:
            scores = jnp.where(mask, scores, MASKED)
        probs = jnp.exp(scores)
        grad_scores = (probs * dot(value, grads[:, cols])).astype(BF16)
        probs = probs.astype(BF16)
        dv = dv + dot(grads[0:HEAD_DIM, cols], probs, ((1,), (1,)))
        dk = dk + dot(queries[0:HEAD_DIM, cols], grad_scores, ((1,), (1,)))
        total[:, cols] += dot(key_t, grad_scores)
        return dk, dv

    zero = jnp.zeros((HEAD_DIM, block), F32)
    state = one(step, (zero, zero), causal(block))
    dk, dv = lax.fori_loop(step + 1, count, lambda i, s: one(i, s, None), state)
    dq = total[:, mine] * scale
    for i in range(block // tok):
        cols = slice(i * tok, (i + 1) * tok)
        out_ref[i, 0, 0:HEAD_DIM] = dq[:, cols].astype(BF16)
        out_ref[i, 0, HEAD_DIM : 2 * HEAD_DIM] = dk[:, cols].astype(BF16)
        out_ref[i, 0, 2 * HEAD_DIM :] = dv[:, cols].astype(BF16)


def attend_back(lens, qkv, out, lse, grad):
    dim, length = qkv.shape[2:]
    pairs, tok = lens.shape[0], grad.shape[-1]
    ctx = length // tok
    block = math.gcd(length, 512)
    whole, _ = pair_specs(dim, length, block)
    return pl.pallas_call(
        functools.partial(attend_back_kernel, block),
        grid_spec=pltpu.PrefetchScalarGridSpec(
            num_scalar_prefetch=1,
            grid=(pairs, length // block),
            in_specs=[
                whole(0),
                whole(1),
                whole(2),
                pl.BlockSpec((1, dim, length), lambda p, i, lens: (p, 0, 0)),
                pl.BlockSpec((1, 1, length), lambda p, i, lens: (p, 0, 0)),
                pl.BlockSpec((ctx, 1, dim, tok), lambda p, i, lens: (0, p, 0, 0)),
            ],
            out_specs=pl.BlockSpec(
                (block // tok, 1, 3 * dim, tok), lambda p, i, lens: (i, p, 0, 0)
            ),
            scratch_shapes=[
                pltpu.VMEM((length, 2 * dim), BF16),
                pltpu.VMEM((length, 2 * dim), BF16),
                pltpu.VMEM((2 * dim, length), BF16),
                pltpu.VMEM((2 * dim, length), BF16),
                pltpu.VMEM((dim, length), F32),
            ],
        ),
        out_shape=jax.ShapeDtypeStruct((ctx, pairs, 3 * dim, tok), BF16),
        compiler_params=pltpu.CompilerParams(
            dimension_semantics=("arbitrary", "arbitrary"), vmem_limit_bytes=48 * 2**20
        ),
        cost_estimate=pl.CostEstimate(flops=1000, bytes_accessed=1000, transcendentals=0),
    )(lens, qkv, qkv, qkv, out, lse, grad)


def project_kernel(x_ref, w_ref, bias_ref, gain_ref, shift_ref, act_ref, out_ref):
    unit, _ = norm_parts(x_ref[0, 0].astype(F32), 0)
    act = (unit * gain_ref[...] + shift_ref[...]).astype(BF16)
    act_ref[0] = act
    out_ref[...] = (dot(w_ref[...], act) + bias_ref[...]).astype(BF16)


def project(x_all, slot, weight, bias, gain, shift):
    ctx, _, width, tok = x_all.shape
    feat = weight.shape[0]

    def fixed(shape):
        return pl.BlockSpec(shape, lambda i: (0, 0))

    return pl.pallas_call(
        project_kernel,
        grid=(ctx,),
        in_specs=[
            pl.BlockSpec((1, 1, width, tok), lambda i: (i, slot, 0, 0)),
            fixed((feat, width)),
            fixed((feat, 1)),
            fixed((width, 1)),
            fixed((width, 1)),
        ],
        out_specs=[
            pl.BlockSpec((1, width, tok), lambda i: (i, 0, 0)),
            pl.BlockSpec((feat, tok), lambda i: (0, i)),
        ],
        out_shape=[
            jax.ShapeDtypeStruct((ctx, width, tok), BF16),
            jax.ShapeDtypeStruct((feat, ctx * tok), BF16),
        ],
        compiler_params=pltpu.CompilerParams(vmem_limit_bytes=48 * 2**20),
        cost_estimate=pl.CostEstimate(flops=1000, bytes_accessed=1000, transcendentals=0),
    )(x_all, weight, bias, gain, shift)


def own_grad_kernel(late_ref, first_ref, second_ref, first_grad_ref, second_grad_ref, last_grad_ref, out_ref, total):
    step = pl.program_id(0)
    nt = ((1,), (1,))
    first, second = first_ref[0], second_ref[0]
    head = dot(first, first_grad_ref[0], nt) + dot(second, second_grad_ref[0], nt)
    last = dot(jnp.where(late_ref[0] == 0, first, second), last_grad_ref[0], nt)
    part = jnp.concatenate([head, last], axis=1)

    @pl.when(step == 0)
    def _():
        total[...] = part

    @pl.when(step > 0)
    def _():
        total[...] += part

    @pl.when(step == pl.num_programs(0) - 1)
    def _():
        out_ref[...] = total[...]


def own_grad(late, first, second, first_grad, second_grad, last_grad):
    ctx, width, tok = first.shape
    feat, last = first_grad.shape[1], last_grad.shape[1]

    def block(rows):
        return pl.BlockSpec((1, rows, tok), lambda i, late: (i, 0, 0))

    return pl.pallas_call(
        own_grad_kernel,
        grid_spec=pltpu.PrefetchScalarGridSpec(
            num_scalar_prefetch=1,
            grid=(ctx,),
            in_specs=[block(width), block(width), block(feat), block(feat), block(last)],
            out_specs=pl.BlockSpec((width, feat + last), lambda i, late: (0, 0)),
            scratch_shapes=[pltpu.VMEM((width, feat + last), F32)],
        ),
        out_shape=jax.ShapeDtypeStruct((width, feat + last), F32),
        compiler_params=pltpu.CompilerParams(vmem_limit_bytes=48 * 2**20),
        cost_estimate=pl.CostEstimate(flops=1000, bytes_accessed=1000, transcendentals=0),
    )(late[None], first, second, first_grad, second_grad, last_grad)


def mlp_kernel(
    width,
    a_ref,
    g_ref,
    up_ref,
    down_ref,
    bias_ref,
    y_ref,
    ga_ref,
    dup_ref,
    ddown_ref,
    db_ref,
    a_rows,
    g_rows,
):
    step = pl.program_id(0)
    slots, _, tok = a_ref.shape
    block = up_ref.shape[1]

    @pl.when(step == 0)
    def _():
        for s in range(slots):
            a_rows[s * tok : (s + 1) * tok, :] = a_ref[s].T
            g_rows[s * tok : (s + 1) * tok, :] = g_ref[s].T
        y_ref[...] = jnp.zeros_like(y_ref)
        ga_ref[...] = jnp.zeros_like(ga_ref)

    def run(size):
        up = up_ref[:, :size]
        down = down_ref[:, :size]
        pre = dot(a_rows[...], up) + bias_ref[:, :size]
        cdf = 0.5 * (1.0 + lax.erf(pre * math.sqrt(0.5)))
        hidden = (pre * cdf).astype(BF16)
        slope = cdf + pre * jnp.exp(-0.5 * pre * pre) * (1.0 / math.sqrt(2.0 * math.pi))
        grad = (dot(g_rows[...], down) * slope).astype(BF16)
        db_ref[:, :size] = jnp.sum(grad.astype(F32), axis=0, keepdims=True)
        nt = ((1,), (1,))
        for s in range(slots):
            rows = slice(s * tok, (s + 1) * tok)
            y_ref[s] += dot(down, hidden[rows], nt)
            ga_ref[s] += dot(up, grad[rows], nt)
        dup = sum(dot(a_ref[s], grad[s * tok : (s + 1) * tok]) for s in range(slots))
        dup_ref[:, :size] = dup.astype(dup_ref.dtype)
        ddown = sum(dot(g_ref[s], hidden[s * tok : (s + 1) * tok]) for s in range(slots))
        ddown_ref[:, :size] = ddown.astype(ddown_ref.dtype)

    full = width // block

    @pl.when(step < full)
    def _():
        run(block)

    if width % block:

        @pl.when(step == full)
        def _():
            run(width % block)


def mlp(act, grad, up, down, bias):
    slots, width, tok = act.shape
    units = up.shape[1]
    block = 256

    def fixed(shape):
        return pl.BlockSpec(shape, lambda i: (0,) * len(shape))

    cols = pl.BlockSpec((width, block), lambda i: (0, i))
    line = pl.BlockSpec((1, block), lambda i: (0, i))
    total = jax.ShapeDtypeStruct((slots, width, tok), F32)
    grads = jax.ShapeDtypeStruct((width, units), BF16)
    return pl.pallas_call(
        functools.partial(mlp_kernel, units),
        grid=(pl.cdiv(units, block),),
        in_specs=[fixed(act.shape), fixed(act.shape), cols, cols, line],
        out_specs=[fixed(act.shape), fixed(act.shape), cols, cols, line],
        out_shape=[total, total, grads, grads, jax.ShapeDtypeStruct((1, units), F32)],
        scratch_shapes=[pltpu.VMEM((slots * tok, width), BF16)] * 2,
        compiler_params=pltpu.CompilerParams(vmem_limit_bytes=56 * 2**20),
        cost_estimate=pl.CostEstimate(flops=1000, bytes_accessed=1000, transcendentals=0),
    )(act, grad, up, down, bias)


def other_index(index, bit):
    return index + bit * (1 - 2 * lax.rem(index // bit, 2))


def split_columns(start, size, count):
    tiles = size // 128
    cuts = [start + 128 * (-(-tiles * i // count)) for i in range(count)] + [start + size]
    return [(cuts[i], cuts[i + 1] - cuts[i]) for i in range(count)]


def gather_kernel(
    ctx,
    fsdp,
    x_ref,
    w_ref,
    v_ref,
    xo_ref,
    wo_ref,
    um_ref,
    uo_ref,
    vo_ref,
    x_send,
    x_recv,
    xc_send,
    xc_recv,
    w_send,
    w_recv,
    wc_send,
    wc_recv,
    v_send,
    v_recv,
    local,
):
    c, f = lax.axis_index("ctx"), lax.axis_index("fsdp")
    chips = ctx // 2
    z, core = c // 2, lax.rem(c, 2)
    partner = 2 * z + 1 - core
    slots = x_ref.shape[0]
    levels = bits_of(fsdp)
    half = um_ref.shape[2]

    def combine(number):
        place = f
        for bit in range(levels):
            if number & (1 << bit):
                place = other_index(place, 1 << bit)
        return place

    barrier = pltpu.get_barrier_semaphore()

    def greet(where):
        pl.semaphore_signal(barrier, inc=1, device_id=where, device_id_type=pl.DeviceIdType.MESH)

    greet((partner, f))
    for number in range(1, fsdp):
        greet((c, combine(number)))

    @pl.when(z > 0)
    def _():
        greet((c - 2, f))

    @pl.when(z < chips - 1)
    def _():
        greet((c + 2, f))

    beside = (z > 0).astype(jnp.int32) + (z < chips - 1).astype(jnp.int32)
    pl.semaphore_wait(barrier, fsdp + beside)

    def remote(source, target, send, recv, where):
        return pltpu.make_async_remote_copy(
            src_ref=source,
            dst_ref=target,
            send_sem=send,
            recv_sem=recv,
            device_id=where,
            device_id_type=pl.DeviceIdType.MESH,
        )

    def x_copy(side, s, h):
        sign = 1 - 2 * side
        block = c - 2 * sign * s
        source = x_ref.at[h] if s == 0 else xo_ref.at[block, h]
        return remote(
            source, xo_ref.at[block, h], x_send.at[side, s, h], x_recv.at[side, s, h], (c + 2 * sign, f)
        )

    def x_sends(side, s):
        return (z - s >= 0) & (z < chips - 1) if side == 0 else (z + s < chips) & (z > 0)

    def x_gets(side, s):
        return z - 1 - s >= 0 if side == 0 else z + 1 + s < chips

    def x_arrival(side, s, h):
        sign = 1 - 2 * side
        block = c - 2 * sign * (s + 1)
        return remote(
            xo_ref.at[block, h],
            xo_ref.at[block, h],
            x_send.at[side, s, h],
            x_recv.at[side, s, h],
            (c + 2 * sign, f),
        )

    def x_share(side, s, h):
        sign = 1 - 2 * side
        block = c - 2 * sign * (s + 1)
        return remote(
            xo_ref.at[block, h],
            xo_ref.at[block, h],
            xc_send.at[side, s, h],
            xc_recv.at[side, s, h],
            (partner, f),
        )

    def x_share_arrival(side, s, h):
        sign = 1 - 2 * side
        block = partner - 2 * sign * (s + 1)
        return remote(
            xo_ref.at[block, h],
            xo_ref.at[block, h],
            xc_send.at[side, s, h],
            xc_recv.at[side, s, h],
            (partner, f),
        )

    def x_own(h):
        return remote(
            x_ref.at[h],
            xo_ref.at[c, h],
            xc_send.at[0, chips - 1, h],
            xc_recv.at[0, chips - 1, h],
            (partner, f),
        )

    def x_own_arrival(h):
        return remote(
            x_ref.at[h],
            xo_ref.at[partner, h],
            xc_send.at[0, chips - 1, h],
            xc_recv.at[0, chips - 1, h],
            (partner, f),
        )

    runs = split_columns(0, half, levels)

    def source(unit, stream):
        start, size = runs[stream]
        return w_ref.at[:, pl.ds(pl.multiple_of((2 * unit + core) * half + start, 128), size)]

    def kept(unit, stream, place, which):
        start, size = runs[stream]
        if unit == 0:
            return wo_ref.at[place, :, pl.ds(pl.multiple_of(which * half + start, 128), size)]
        return um_ref.at[place, :, pl.ds(start, size)]

    def shared(unit, stream, place, which):
        start, size = runs[stream]
        if unit == 0:
            return kept(unit, stream, place, which)
        return uo_ref.at[place, :, pl.ds(start, size)]

    def w_copy(unit, stream, step, number):
        bit = 1 << ((stream + step) % levels)
        place = combine(number)
        there = kept(unit, stream, place, core)
        return remote(
            source(unit, stream) if number == 0 else there,
            there,
            w_send.at[unit, stream, number | bit],
            w_recv.at[unit, stream, number | bit],
            (c, other_index(f, bit)),
        )

    def w_arrival(unit, stream, number):
        block = kept(unit, stream, combine(number), core)
        sems = w_send.at[unit, stream, number], w_recv.at[unit, stream, number]
        return remote(block, block, *sems, (partner, f))

    def w_share(unit, stream, number):
        place = combine(number)
        sems = wc_send.at[unit, stream, number], wc_recv.at[unit, stream, number]
        block = kept(unit, stream, place, core)
        return remote(block, shared(unit, stream, place, core), *sems, (partner, f))

    def w_share_arrival(unit, stream, number):
        block = shared(unit, stream, combine(number), 1 - core)
        sems = wc_send.at[unit, stream, number], wc_recv.at[unit, stream, number]
        return remote(block, block, *sems, (partner, f))

    def held(stream, step):
        numbers = [0]
        for i in range(step):
            bit = 1 << ((stream + i) % levels)
            numbers += [n | bit for n in numbers]
        return numbers

    def v_copy(number):
        return remote(
            v_ref, vo_ref.at[f], v_send.at[number], v_recv.at[number], (c, combine(number))
        )

    def v_arrival(number):
        return remote(
            v_ref,
            vo_ref.at[combine(number)],
            v_send.at[number],
            v_recv.at[number],
            (c, combine(number)),
        )

    sides = [(side, h) for h in range(slots) for side in range(2)]
    for side, h in sides:

        @pl.when(x_sends(side, 0))
        def _(side=side, h=h):
            x_copy(side, 0, h).start()

    for stream in range(levels):
        w_copy(0, stream, 0, 0).start()
    for number in range(1, fsdp):
        v_copy(number).start()
    for h in range(slots):
        x_own(h).start()
    up_mine = w_ref.at[:, pl.ds(pl.multiple_of((2 + core) * half, 128), half)]
    up_other = w_ref.at[:, pl.ds(pl.multiple_of((3 - core) * half, 128), half)]
    own = [
        pltpu.make_async_copy(x_ref, xo_ref.at[c], local.at[0]),
        pltpu.make_async_copy(w_ref.at[:, pl.ds(0, 2 * half)], wo_ref.at[f], local.at[1]),
        pltpu.make_async_copy(v_ref, vo_ref.at[f], local.at[2]),
        pltpu.make_async_copy(up_mine, um_ref.at[f], local.at[3]),
        pltpu.make_async_copy(up_other, uo_ref.at[f], local.at[4]),
    ]
    for copy in own:
        copy.start()

    def x_step(s):
        for side, h in sides:

            @pl.when(x_gets(side, s))
            def _(side=side, h=h):
                x_arrival(side, s, h).wait_recv()
                x_share(side, s, h).start()

            if s + 1 < chips - 1:

                @pl.when(x_sends(side, s + 1))
                def _(side=side, h=h):
                    x_copy(side, s + 1, h).start()

    def w_step(unit, step):
        for stream in range(levels):
            bit = 1 << ((stream + step) % levels)
            arrived = [number | bit for number in held(stream, step)]
            for number in arrived:
                w_arrival(unit, stream, number).wait_recv()
            if step + 1 < levels:
                for number in held(stream, step + 1):
                    w_copy(unit, stream, step + 1, number).start()
            for number in arrived:
                w_share(unit, stream, number).start()

    def w_begin(unit):
        for stream in range(levels):
            w_copy(unit, stream, 0, 0).start()

    plan = [(1.9 * (s + 1), functools.partial(x_step, s)) for s in range(chips - 1)]
    time = 0.0
    for unit in range(2):
        for step in range(levels):
            if unit == 0 and step == levels - 1:
                plan.append((time + 0.95, functools.partial(w_begin, 1)))
            time += 2.0 ** (step + 1) / levels
            plan.append((time, functools.partial(w_step, unit, step)))
    plan = [step for _, step in sorted(plan, key=lambda entry: entry[0])]
    for step in plan:
        step()

    for copy in own:
        copy.wait()
    for number in range(1, fsdp):
        v_copy(number).wait_send()
        v_arrival(number).wait_recv()
        for unit in range(2):
            for stream in range(levels):
                w_arrival(unit, stream, number).wait_send()
                w_share(unit, stream, number).wait_send()
                w_share_arrival(unit, stream, number).wait_recv()
    for h in range(slots):
        x_own(h).wait_send()
        x_own_arrival(h).wait_recv()
    for s in range(chips - 1):
        for side, h in sides:

            @pl.when(x_sends(side, s))
            def _(side=side, h=h, s=s):
                x_copy(side, s, h).wait_send()

            @pl.when(x_gets(side, s))
            def _(side=side, h=h, s=s):
                x_share(side, s, h).wait_send()
                x_share_arrival(side, s, h).wait_recv()


def gather_first(ctx, fsdp, x, w, v):
    slots = x.shape[0]
    rows, columns = w.shape
    levels, chips = bits_of(fsdp), ctx // 2
    anywhere = pl.BlockSpec(memory_space=pl.ANY)
    dma = pltpu.SemaphoreType.DMA
    return pl.pallas_call(
        functools.partial(gather_kernel, ctx, fsdp),
        in_specs=[pl.BlockSpec(memory_space=pltpu.VMEM)] * 3,
        out_specs=[anywhere] * 5,
        out_shape=[
            jax.ShapeDtypeStruct((ctx,) + x.shape, x.dtype),
            jax.ShapeDtypeStruct((fsdp, rows, columns // 2), w.dtype),
            jax.ShapeDtypeStruct((fsdp, rows, columns // 4), w.dtype),
            jax.ShapeDtypeStruct((fsdp, rows, columns // 4), w.dtype),
            jax.ShapeDtypeStruct((fsdp,) + v.shape, v.dtype),
        ],
        scratch_shapes=[
            dma((2, chips - 1, slots)),
            dma((2, chips - 1, slots)),
            dma((2, chips, slots)),
            dma((2, chips, slots)),
            dma((2, levels, fsdp)),
            dma((2, levels, fsdp)),
            dma((2, levels, fsdp)),
            dma((2, levels, fsdp)),
            dma((fsdp,)),
            dma((fsdp,)),
            dma((5,)),
        ],
        compiler_params=pltpu.CompilerParams(
            collective_id=0, has_side_effects=True, vmem_limit_bytes=32 * 2**20
        ),
        cost_estimate=pl.CostEstimate(flops=1000, bytes_accessed=1000, transcendentals=0),
    )(x, w, v)


def bits_of(count):
    return max(count.bit_length() - 1, 0)


def flip(count, value):
    return [(i, i ^ value) for i in range(count)]


def pick(array, index, axis):
    return lax.dynamic_index_in_dim(array, index, axis, keepdims=False)


def ordered(bit, mine, other, axis):
    first = jnp.where(bit == 0, mine, other)
    second = jnp.where(bit == 0, other, mine)
    return jnp.concatenate([first, second], axis=axis)


def after(value, *others):
    return lax.optimization_barrier((value, others))[0]


def add_low(mine, swapped):
    return (mine.astype(F32) + swapped.astype(F32)).astype(BF16)


def scatter_fsdp(total):
    return lax.psum_scatter(total, "fsdp", scatter_dimension=0, tiled=True)


def bar_signal(where):
    pl.semaphore_signal(
        pltpu.get_barrier_semaphore(), inc=1, device_id=where, device_id_type=pl.DeviceIdType.MESH
    )


def remote_copy(source, target, send, recv, where):
    return pltpu.make_async_remote_copy(
        src_ref=source,
        dst_ref=target,
        send_sem=send,
        recv_sem=recv,
        device_id=where,
        device_id_type=pl.DeviceIdType.MESH,
    )


def line_gather(chips, c, f, mine, slot, share, sems, core_sems):
    z, core = c // 2, lax.rem(c, 2)
    partner = 2 * z + 1 - core
    send, recv = sems
    core_send, core_recv = core_sems

    def passing(side, s):
        sign = 1 - 2 * side
        chip = z - sign * s
        source = mine if s == 0 else slot(chip)
        return remote_copy(
            source, slot(chip), send.at[side, s], recv.at[side, s], (c + 2 * sign, f)
        )

    def arrival(side, s):
        block = slot(z - (1 - 2 * side) * (s + 1))
        return remote_copy(block, block, send.at[side, s], recv.at[side, s], (partner, f))

    def sends(side, s):
        return (z - s >= 0) & (z < chips - 1) if side == 0 else (z + s < chips) & (z > 0)

    def gets(side, s):
        return z - 1 - s >= 0 if side == 0 else z + 1 + s < chips

    def shared(side, s):
        chip = z - (1 - 2 * side) * (s + 1)
        return remote_copy(
            slot(chip), share(chip), core_send.at[side, s], core_recv.at[side, s], (partner, f)
        )

    def share_arrival(side, s):
        block = share(z - (1 - 2 * side) * (s + 1))
        sems = core_send.at[side, s], core_recv.at[side, s]
        return remote_copy(block, block, *sems, (partner, f))

    own_sems = core_send.at[0, chips - 1], core_recv.at[0, chips - 1]
    own_share = remote_copy(mine, share(z), *own_sems, (partner, f))

    def start():
        for side in range(2):

            @pl.when(sends(side, 0))
            def _(side=side):
                passing(side, 0).start()

        own_share.start()

    def step(s):
        for side in range(2):

            @pl.when(gets(side, s))
            def _(side=side):
                arrival(side, s).wait_recv()
                shared(side, s).start()

            if s + 1 < chips - 1:

                @pl.when(sends(side, s + 1))
                def _(side=side):
                    passing(side, s + 1).start()

    def end():
        own_share.wait_send()
        remote_copy(share(z), share(z), *own_sems, (partner, f)).wait_recv()
        for s in range(chips - 1):
            for side in range(2):

                @pl.when(sends(side, s))
                def _(side=side, s=s):
                    passing(side, s).wait_send()

                @pl.when(gets(side, s))
                def _(side=side, s=s):
                    shared(side, s).wait_send()
                    share_arrival(side, s).wait_recv()

    return start, [functools.partial(step, s) for s in range(chips - 1)], end


def sum_kernel(ctx, fsdp, batches, *refs):
    levels, chips = bits_of(fsdp), ctx // 2
    pieces = refs[0:2]
    own_ref, mine_out, other_out, own_out, last_out = refs[2:7]
    rest = list(refs[7:])
    own_kept, own_low, beside = rest.pop(0), rest.pop(0), rest.pop(0)
    own_sent = [rest.pop(0) for _ in range(levels)]
    own_got = [rest.pop(0) for _ in range(levels)]
    z_sent, z_got = rest.pop(0), rest.pop(0)
    op_send, op_recv, zs_send, zs_recv, zg_send, zg_recv = (rest.pop(0) for _ in range(6))
    zc_send, zc_recv, og_send, og_recv, oc_send, oc_recv, far_send, far_recv, local = (
        rest.pop(0) for _ in range(9)
    )
    c, f = lax.axis_index("ctx"), lax.axis_index("fsdp")
    z, core = c // 2, lax.rem(c, 2)
    partner = 2 * z + 1 - core
    far = lax.rem(c + ctx // 2, ctx)
    rows = own_low.shape[0]
    chunk = z_sent.shape[-1]
    width = chunk * chips // 2
    parts = chips // 2
    strip = 16 if rows % 16 == 0 else 8

    def own_bit(bit):
        return lax.rem(f // (1 << bit), 2)

    def strips(work):
        def body(i, carry):
            work(pl.ds(pl.multiple_of(i * strip, strip), strip))
            return carry

        lax.fori_loop(0, rows // strip, body, 0)

    bar_signal((partner, f))
    bar_signal((far, f))
    for bit in range(levels):
        bar_signal((c, other_index(f, 1 << bit)))

    @pl.when(z > 0)
    def _():
        bar_signal((c - 2, f))

    @pl.when(z < chips - 1)
    def _():
        bar_signal((c + 2, f))

    neighbours = (z > 0).astype(jnp.int32) + (z < chips - 1).astype(jnp.int32)
    pl.semaphore_wait(pltpu.get_barrier_semaphore(), levels + 2 + neighbours)

    def order(q):
        return [(q + i) % levels for i in range(levels)]

    def place_of(q, flipped, free):
        bits = order(q)
        first = own_bit(bits[0])
        total = (1 - first if flipped else first) * (1 << bits[0])
        for i, bit in enumerate(bits[1:]):
            total += ((free >> i) & 1) * (1 << bit)
        return total

    def kept_index(q, step, flipped, free):
        bits = order(q)
        total = 0
        for i, bit in enumerate(bits[1:]):
            mine = own_bit(bit)
            if i + 1 < step:
                value = mine
            elif i + 1 == step:
                value = 1 - mine if flipped else mine
            else:
                value = (free >> (i - step)) & 1
            total += value * (1 << i)
        return total

    def across(step, q):
        return (c, other_index(f, 1 << order(q)[step]))

    def own_copy(step):
        return remote_copy(
            own_sent[step], own_got[step], op_send.at[step], op_recv.at[step], across(step, 0)
        )

    def own_begin():
        for free in range(fsdp // 2):
            there, here = place_of(0, True, free), place_of(0, False, free)

            def work(at, free=free, there=there, here=here):
                own_sent[0][free, at, :] = own_ref[there, at, :]
                own_kept[free, at, :] = own_ref[here, at, :].astype(F32)

            strips(work)
        own_copy(0).start()

    def later(step, kept_ref, got_ref, sent_ref, q):
        for free in range(fsdp >> (step + 2)):
            there, here = (kept_index(q, step + 1, flipped, free) for flipped in (True, False))
            mine = own_bit(order(q)[step + 1])
            there_got, here_got = free * 2 + 1 - mine, free * 2 + mine

            def work(at, free=free):
                value = kept_ref[there, at, :] + got_ref[there_got, at, :].astype(F32)
                sent_ref[free, at, :] = value.astype(BF16)
                kept_ref[here, at, :] += got_ref[here_got, at, :].astype(F32)

            strips(work)

    def last(kept_ref, got_ref, q, place):
        def work(at):
            place(at, kept_ref[kept_index(q, levels, False, 0), at, :] + got_ref[0, at, :].astype(F32))

        strips(work)

    def own_step(step):
        own_copy(step).wait_recv()
        if step + 1 < levels:
            later(step, own_kept, own_got[step], own_sent[step + 1], 0)
            own_copy(step + 1).start()
            return

        def place(at, value):
            own_low[at, :] = value[:, : head + tail].astype(BF16)
            beside[at, :] = value[:, head + tail :]

        last(own_kept, own_got[step], 0, place)
        for copy in far_copies:
            copy.start()
        own_start()

    head = own_out.shape[2]
    tail = last_out.shape[2]
    far_copies = [
        remote_copy(
            own_low.at[:, pl.ds(head, tail)], last_out.at[1], far_send.at[0], far_recv.at[0], (far, f)
        ),
        pltpu.make_async_copy(own_low.at[:, pl.ds(head, tail)], last_out.at[0], local.at[0]),
        pltpu.make_async_copy(own_low.at[:, pl.ds(0, head)], own_out.at[c], local.at[1]),
    ]
    own_start, own_steps, own_end = line_gather(
        chips,
        c,
        f,
        own_low.at[:, pl.ds(0, head)],
        lambda chip: own_out.at[2 * chip + core],
        lambda chip: own_out.at[2 * chip + core],
        (og_send, og_recv),
        (oc_send, oc_recv),
    )

    def total_of(j, b, at):
        q = j // parts
        start = b * width + (j % parts) * chunk
        stop = start + chunk
        units, room = pieces[q].shape[1], beside.shape[1] // 2
        found = []
        if start < units:
            found.append(pieces[q][at, start : min(stop, units)].astype(F32))
        if stop > units:
            first = max(start, units) - units + q * room
            found.append(beside[at, first : stop - units + q * room])
        return found[0] if len(found) == 1 else jnp.concatenate(found, axis=1)

    def z_copy(side, i, b):
        return remote_copy(
            z_sent.at[side, b, i],
            z_got.at[side, b, i],
            zs_send.at[side, b, i],
            zs_recv.at[side, b, i],
            (c + 2 * (1 - 2 * side), f),
        )

    def z_last(side, chip):
        return chips - 1 - chip if side == 0 else chip

    def z_step(turn, b):
        for chip in range(chips):

            @pl.when(z == chip)
            def _(chip=chip):
                for side in range(2):
                    j_of = (lambda i: chips - 1 - i) if side == 0 else (lambda i: i)
                    begun = chip if side == 0 else chips - 1 - chip
                    i = turn - begun
                    sends = z_last(side, chip)
                    if begun > 0 and 0 <= i <= sends and i < chips - 1:
                        z_copy(side, i, b).wait_recv()
                    if 0 <= i < sends:
                        if i > 0:
                            z_copy(side, i - 1, b).wait_send()

                        def work(at, side=side, i=i, j=j_of(i), begun=begun):
                            value = total_of(j, b, at)
                            if begun > 0:
                                value += z_got[side, b, i, at, :].astype(F32)
                            z_sent[side, b, i, at, :] = value.astype(BF16)

                        strips(work)
                        z_copy(side, i, b).start()

    def chunk_of(ref, chip, b):
        start = pl.multiple_of(b * width + lax.rem(chip, parts) * chunk, 128)
        return ref.at[chip // parts, :, pl.ds(start, chunk)]

    gathers = []
    for b in range(batches):
        gathers.append(
            line_gather(
                chips,
                c,
                f,
                chunk_of(mine_out, z, b),
                lambda chip, b=b: chunk_of(mine_out, chip, b),
                lambda chip, b=b: chunk_of(other_out, chip, b),
                (zg_send.at[:, b], zg_recv.at[:, b]),
                (zc_send.at[:, b], zc_recv.at[:, b]),
            )
        )

    def finish(b):
        for j in range(chips):

            @pl.when(z == j)
            def _(j=j):
                def work(at):
                    value = total_of(j, b, at)
                    if j > 0:
                        value += z_got[0, b, chips - 1 - j, at, :].astype(F32)
                    if j < chips - 1:
                        value += z_got[1, b, j, at, :].astype(F32)
                    start = b * width + (j % parts) * chunk
                    mine_out[j // parts, at, pl.ds(start, chunk)] = value.astype(BF16)

                strips(work)

        gathers[b][0]()

    own_begin()
    waiting = []

    def one_more():
        if waiting:
            waiting.pop(0)()

    def batch(b):
        for i in range(chips):
            z_step(i, b)
            one_more()
        finish(b)
        waiting.extend(gathers[b][1])

    for b in range(batches - 1):
        batch(b)
    for step in range(levels):
        own_step(step)
        one_more()
    waiting.extend(own_steps)
    batch(batches - 1)
    while waiting:
        one_more()

    far_copies[0].wait()
    far_copies[1].wait()
    far_copies[2].wait()
    own_end()
    for step in range(levels):
        own_copy(step).wait_send()
    for b in range(batches):
        gathers[b][2]()
        for chip in range(chips):

            @pl.when(z == chip)
            def _(chip=chip, b=b):
                for side in range(2):
                    if z_last(side, chip):
                        z_copy(side, z_last(side, chip) - 1, b).wait_send()


def sum_grads(ctx, fsdp, pieces, own, head, tail):
    levels, chips = bits_of(fsdp), ctx // 2
    rows, units = pieces[0].shape
    rest = own.shape[-1] - head - tail
    whole = units + rest // 2
    batches = max(n for n in range(1, 3) if whole % n == 0 and 2 * whole // n % (chips * 128) == 0)
    width = whole // batches
    chunk = 2 * width // chips
    own_width = own.shape[-1]
    vmem = pl.BlockSpec(memory_space=pltpu.VMEM)
    dma = pltpu.SemaphoreType.DMA
    steps = [fsdp >> (i + 1) for i in range(levels)]
    result = jax.ShapeDtypeStruct((2, rows, whole), BF16)
    mine, other, own_all, last = pl.pallas_call(
        functools.partial(sum_kernel, ctx, fsdp, batches),
        in_specs=[vmem] * 3,
        out_specs=[vmem] * 4,
        out_shape=[
            result,
            result,
            jax.ShapeDtypeStruct((ctx, rows, head), BF16),
            jax.ShapeDtypeStruct((2, rows, tail), BF16),
        ],
        scratch_shapes=[
            pltpu.VMEM((fsdp // 2, rows, own_width), F32),
            pltpu.VMEM((rows, head + tail), BF16),
            pltpu.VMEM((rows, rest), F32),
        ]
        + [pltpu.VMEM((n, rows, own_width), BF16) for n in steps * 2]
        + [pltpu.VMEM((2, batches, chips - 1, rows, chunk), BF16)] * 2
        + [dma((levels,))] * 2
        + [dma((2, batches, chips - 1))] * 4
        + [dma((2, batches, chips))] * 2
        + [dma((2, chips - 1))] * 2
        + [dma((2, chips))] * 2
        + [dma((1,))] * 2
        + [dma((6,))],
        compiler_params=pltpu.CompilerParams(
            collective_id=1, has_side_effects=True, vmem_limit_bytes=60 * 2**20
        ),
        cost_estimate=pl.CostEstimate(flops=1000, bytes_accessed=1000, transcendentals=0),
    )(*pieces, own)

    return mine, other, own_all, last


def swap_cores(mine, ctx):
    return lax.ppermute(mine, "ctx", flip(ctx, 1))


def norm_parts(rows, axis):
    middle = jnp.mean(rows, axis=axis, keepdims=True)
    centred = rows - middle
    spread = jnp.mean(centred * centred, axis=axis, keepdims=True)
    inverse = lax.rsqrt(spread + NORM_EPS)
    return centred * inverse, inverse


def norm_back(grad, unit, inverse, gain):
    inner = grad * gain
    mean_inner = jnp.mean(inner, axis=1, keepdims=True)
    mean_cross = jnp.mean(inner * unit, axis=1, keepdims=True)
    rows = inverse * (inner - mean_inner - unit * mean_cross)
    return rows, jnp.sum(grad * unit, axis=(0, 2)), jnp.sum(grad, axis=(0, 2))


def adamw(weight, first, second, grad, rate, decay):
    moment = BETA_ONE * first.astype(F32) + (1.0 - BETA_ONE) * grad
    square = BETA_TWO * second + (1.0 - BETA_TWO) * grad * grad
    corrected = moment / (1.0 - BETA_ONE**STEP)
    scaled = square / (1.0 - BETA_TWO**STEP)
    new_weight = weight - rate * (corrected / (jnp.sqrt(scaled) + ADAM_EPS) + decay * weight)
    return (moment, square, new_weight)


def update_kernel(units, regular, *refs):
    (w, first, second, dw, dfirst, dsecond, own, last, mine, other) = refs[:10]
    outs = refs[10:]
    core = lax.rem(lax.axis_index("ctx"), 2)
    width = (w.shape[1] - 2 * units) // 4
    quarter = width // 4
    ctx = own.shape[0]
    dim = HEAD_DIM

    def halves(q, start, size):
        here = mine[q, :, start : start + size].astype(F32)
        there = other[q, :, start : start + size].astype(F32)
        return jnp.where(core == 0, here, there), jnp.where(core == 0, there, here)

    def both(q, start, size):
        return jnp.concatenate(halves(q, start, size), axis=1)

    heads = []
    for part in range(3):
        for i in range(regular):
            for c in range(ctx):
                column = (i * 3 + part) * dim
                heads.append(own[c, :, column : column + dim].astype(F32))
        column = part * dim
        heads.append(
            last[0, :, column : column + dim].astype(F32)
            + last[1, :, column : column + dim].astype(F32)
        )
    out = [halves(q, units, quarter) for q in range(2)]
    heads += [out[0][0], out[1][0], out[0][1], out[1][1]]
    grad = jnp.concatenate(heads, axis=1)

    def put(targets, cols, values):
        for target, value in zip(targets, values):
            target[:, cols] = value

    cols = slice(0, 4 * width)
    put(outs[:3], cols, adamw(w[:, cols], first[:, cols], second[:, cols], grad, 0.03, 0.1))
    cols = slice(4 * width, w.shape[1])
    grad = both(0, 0, units)
    put(outs[:3], cols, adamw(w[:, cols], first[:, cols], second[:, cols], grad, 0.03, 0.1))
    grad = both(1, 0, units)
    put(outs[3:], slice(None), adamw(dw[...], dfirst[...], dsecond[...], grad, 0.02, 0.1))


def update(rows_state, down_state, own, last, mine, other, units, regular):
    rows = rows_state[0].shape[0]
    strip = 16 if rows % 16 == 0 else 8

    def flat(array):
        return pl.BlockSpec((strip, array.shape[1]), lambda i: (i, 0))

    def deep(array):
        return pl.BlockSpec((array.shape[0], strip, array.shape[2]), lambda i: (0, i, 0))

    states, sums = [*rows_state, *down_state], [own, last, mine, other]
    results = [rows_state[0]] * 3 + [down_state[0]] * 3
    return pl.pallas_call(
        functools.partial(update_kernel, units, regular),
        grid=(rows // strip,),
        in_specs=[flat(a) for a in states] + [deep(a) for a in sums],
        out_specs=[flat(a) for a in results],
        out_shape=[jax.ShapeDtypeStruct(a.shape, F32) for a in results],
        compiler_params=pltpu.CompilerParams(vmem_limit_bytes=56 * 2**20),
        cost_estimate=pl.CostEstimate(flops=1000, bytes_accessed=1000, transcendentals=0),
    )(*states, *sums)


def body(
    ctx,
    fsdp,
    tokens,
    cotangent,
    lengths,
    w_rows,
    rows_first,
    rows_second,
    w_down,
    down_first,
    down_second,
    vectors,
    vec_first,
    vec_second,
):
    tok, slots, width = tokens.shape
    dim = HEAD_DIM
    regular = HEADS // ctx
    owned = regular + 1
    share = width // fsdp
    c = lax.axis_index("ctx")
    core = c % 2
    late = (c >= ctx // 2).astype(jnp.int32)
    half = FF // 2

    def my_half(array):
        return lax.dynamic_slice_in_dim(array, core * half, half, 1)

    x_low = tokens.transpose(1, 2, 0)
    vec_part = jnp.pad(vectors.astype(BF16).T, ((0, 0), (0, 128 - vectors.shape[0])))
    x_all, head_w, up_mine, up_other, vec_low = gather_first(
        ctx, fsdp, x_low, w_rows.astype(BF16), vec_part
    )
    head_w = head_w.reshape(width, 4 * width)
    up_mine, up_other = up_mine.reshape(width, half), up_other.reshape(width, half)
    vec_low = vec_low.reshape(width, 128)
    down_mine, vec_low = lax.optimization_barrier((my_half(w_down.T).astype(BF16), vec_low))
    down_mine = lax.all_gather(down_mine, "fsdp", axis=0, tiled=True)
    vec = [vec_low[:, i : i + 1].astype(F32) for i in range(12)]
    up_bias = vec_low[:, 8:12].T.astype(F32).reshape(1, FF)

    starts = [(i * ctx + c) * dim for i in range(regular)] + [(HEADS - 1) * dim]
    own_w = jnp.concatenate(
        [
            lax.dynamic_slice_in_dim(head_w, part * width + start, dim, 1)
            for part in range(3)
            for start in starts
        ],
        axis=1,
    )
    q_bias = jnp.concatenate([lax.dynamic_slice_in_dim(vec[2], s, dim, 0) for s in starts], axis=0)
    v_bias = jnp.concatenate([lax.dynamic_slice_in_dim(vec[3], s, dim, 0) for s in starts], axis=0)
    own_bias = jnp.concatenate([q_bias, jnp.zeros_like(q_bias), v_bias], axis=0)
    own_w = own_w.T
    far = (c + ctx // 2) % ctx
    def to_rows(array, *gate):
        feat = array.shape[2]
        got = lax.all_to_all(array, "ctx", 0, 0)
        got = after(got, *gate) if gate else got
        return got.transpose(1, 0, 2, 3).reshape(regular * ctx, feat, tok)

    def last_to_rows(array, *gate):
        mine = pick(array, c, 0)
        got = lax.ppermute(pick(array, far, 0), "ctx", flip(ctx, ctx // 2))
        got = after(got, *gate) if gate else got
        return jnp.where(late == 0, mine, got), jnp.where(late == 0, got, mine)

    def to_send(array):
        return array.reshape(regular, ctx, dim, tok).transpose(1, 0, 2, 3)

    acts, projected = [], []

    def project_slot(s, x_all):
        act, qkv = project(x_all, s, own_w, own_bias, vec[0], vec[1])
        acts.append(act)
        projected.append(qkv.reshape(3, owned, dim, ctx * tok))

    def attend_slot(s, *gate):
        lens = after(jnp.repeat(lengths[s : s + 1], regular), *gate)
        return (lens, projected[s], *attend(lens, projected[s], tok))

    project_slot(0, x_all)
    results = [attend_slot(0)]
    rows = [to_rows(results[0][3])]
    project_slot(1, after(x_all, results[0][2]))
    last_qkv = jnp.where(late == 0, *(qkv[:, regular:] for qkv in projected))
    last_len = lax.dynamic_slice_in_dim(lengths, late, 1, 0)
    results.append(attend_slot(1, rows[0]))
    last_len = after(last_len, results[1][2])
    results.append((last_len, last_qkv, *attend(last_len, last_qkv, tok)))
    rows.append(to_rows(results[1][3]))
    down_mine = after(down_mine, results[1][2])
    down_other = swap_cores(down_mine, ctx)
    last_rows = last_to_rows(results[2][3])
    att = [jnp.concatenate([rows[s], last_rows[s]]).reshape(width, tok) for s in range(slots)]
    att = jnp.stack(att)

    x = x_low.astype(F32)
    out_w = head_w[:, 3 * width :]
    mid = x + jnp.einsum("de,sdt->set", out_w, att, preferred_element_type=F32) + vec[4]
    unit_two, inverse_two = norm_parts(mid, 1)
    act_two = (unit_two * vec[5] + vec[6]).astype(BF16)

    pos = c * tok + jnp.arange(tok, dtype=jnp.int32)
    valid = pos[None, None, :] < lengths[:, None, None]
    g_low = jnp.where(valid, cotangent.transpose(1, 2, 0), jnp.zeros((), BF16))
    g = g_low.astype(F32)

    bias_mine = lax.dynamic_slice_in_dim(up_bias, core * half, half, 1)
    bias_other = lax.dynamic_slice_in_dim(up_bias, (1 - core) * half, half, 1)
    y_other, ga_other, dup_other, ddown_other, db_other = mlp(
        act_two, g_low, up_other, down_other, bias_other
    )
    y_mine, ga_mine, dup_mine, ddown_mine, db_mine = mlp(
        act_two, g_low, up_mine, down_mine, bias_mine
    )
    output = (mid + (y_mine + y_other + vec[7])).astype(BF16).transpose(2, 0, 1)

    up_swapped, down_swapped = swap_cores(dup_other, ctx), swap_cores(ddown_other, ctx)
    up_total = add_low(dup_mine, up_swapped)
    up_part = scatter_fsdp(up_total)
    ga_mine = after(ga_mine, up_total)

    grad_mid, gain_two, shift_two = norm_back(ga_mine + ga_other, unit_two, inverse_two, vec[5])
    grad_mid = g + grad_mid
    grad_attn = grad_mid.astype(BF16)
    grad_att = jnp.einsum("de,set->sdt", out_w, grad_attn, preferred_element_type=F32).astype(BF16)
    down_part = scatter_fsdp(add_low(after(ddown_mine, grad_att), down_swapped))
    grad_attn_later = after(grad_attn, grad_att)
    grad_att = grad_att.reshape(slots, HEADS, dim, tok)
    last = jnp.repeat(grad_att[:, -1], ctx // slots, axis=0)[:, None]
    first_pairs = lax.all_to_all(to_send(grad_att[0, :-1]), "ctx", 0, 0)
    other_pairs = lax.all_to_all(
        after(jnp.concatenate([to_send(grad_att[1, :-1]), last], axis=1), first_pairs), "ctx", 0, 0
    )

    quarter = width // 4
    spread = jnp.pad(
        grad_attn_later.reshape(slots, 4, quarter, tok),
        ((0, 0), (0, 0), (0, -quarter % 128), (0, 0)),
    )
    out_grad = jnp.einsum("sdt,sket->kde", att, spread, preferred_element_type=F32).astype(BF16)
    out_grad = out_grad.reshape(2, 2, fsdp, share, spread.shape[2])

    def out_half(which):
        return pick(out_grad, which, 0).reshape(2, width, spread.shape[2])

    out_mine, out_swapped = out_half(core), swap_cores(out_half(1 - core), ctx)
    out_total = add_low(out_mine, out_swapped)
    first_heads = attend_back(*results[0][:3], results[0][4], first_pairs)
    last_heads = attend_back(
        *results[2][:3], results[2][4], after(other_pairs[:, -1:], first_heads)
    )
    other_heads = attend_back(
        *results[1][:3], results[1][4], after(other_pairs[:, :-1], last_heads, up_part)
    )
    grad_heads = [first_heads, other_heads, last_heads]

    feat = 3 * dim
    own_sum = own_grad(
        late,
        acts[0],
        acts[1],
        grad_heads[0].reshape(ctx, regular * feat, tok),
        grad_heads[1].reshape(ctx, regular * feat, tok),
        grad_heads[2].reshape(ctx, feat, tok),
    )
    own_sum = own_sum.astype(BF16)
    own_sum = jnp.concatenate(
        [
            jnp.pad(part, ((0, 0), (0, -part.shape[1] % 128)))
            for part in (own_sum[:, : regular * feat], own_sum[:, regular * feat :])
        ]
        + [out_total[0], out_total[1]],
        axis=1,
    )
    head_columns = regular * feat + -regular * feat % 128
    blocks = (fsdp, share)
    sum_mine, sum_other, own_all, last = sum_grads(
        ctx,
        fsdp,
        [up_part, down_part],
        own_sum.reshape(*blocks, own_sum.shape[1]),
        head_columns,
        feat + -feat % 128,
    )
    first_rows, other_rows = to_rows(first_heads), to_rows(other_heads, sum_mine)
    last_rows = last_to_rows(last_heads, sum_mine)
    grad_qkv = []
    for s, rows in enumerate((first_rows, other_rows)):
        rows = jnp.concatenate([rows, last_rows[s]])
        rows = rows.reshape(HEADS, 3, dim, tok).transpose(1, 0, 2, 3)
        grad_qkv.append(rows.reshape(3 * width, tok))
    grad_qkv = jnp.stack(grad_qkv)
    grad_one = jnp.einsum(
        "de,set->sdt", head_w[:, : 3 * width], grad_qkv, preferred_element_type=F32
    )

    unit_one, inverse_one = norm_parts(x, 1)
    grad_in, gain_one, shift_one = norm_back(grad_one, unit_one, inverse_one, vec[0])
    grad_tokens = (grad_mid + grad_in).astype(BF16)

    bias_qkv = jnp.sum(grad_qkv.astype(F32), axis=(0, 2))
    vec_grad = jnp.stack(
        [
            gain_one,
            shift_one,
            bias_qkv[:width],
            bias_qkv[2 * width :],
            jnp.sum(grad_attn.astype(F32), axis=(0, 2)),
            gain_two,
            shift_two,
            jnp.sum(g, axis=(0, 2)),
        ]
    )
    bias_up = ordered(core, db_mine, db_other, 1).reshape(4, width)
    vec_grad = jnp.concatenate([vec_grad, bias_up], axis=0).reshape(12, fsdp, share)
    f = lax.axis_index("fsdp")
    vec_sum = pick(vec_grad, f, 1)
    for value in range(1, fsdp):
        vec_sum = vec_sum + lax.ppermute(pick(vec_grad, f ^ value, 1), "fsdp", flip(fsdp, value))
    for level in range(bits_of(ctx)):
        vec_sum = vec_sum + lax.ppermute(vec_sum, "ctx", flip(ctx, 2**level))

    rows_state = (w_rows, rows_first, rows_second)
    down_state = (w_down.T, down_first.T, down_second.T)
    updated = update(
        rows_state, down_state, own_all, last, sum_mine, sum_other, half, regular
    )
    rows_out, down_out = updated[:3], tuple(part.T for part in updated[3:])
    vec_out = adamw(vectors, vec_first, vec_second, vec_sum, 0.3, 0.0)
    return (output, grad_tokens.transpose(2, 0, 1), *rows_out, *down_out, *vec_out)


def solution(mesh):
    placed = (
        P("ctx", "fsdp", None),
        P("ctx", "fsdp", None),
        P("fsdp"),
        P("fsdp", None),
        P("fsdp", None),
        P("fsdp", None),
        P(None, "fsdp"),
        P(None, "fsdp"),
        P(None, "fsdp"),
        P(None, "fsdp"),
        P(None, "fsdp"),
        P(None, "fsdp"),
    )
    return jax.shard_map(
        functools.partial(body, mesh.shape["ctx"], mesh.shape["fsdp"]),
        mesh=mesh,
        in_specs=placed,
        out_specs=placed[:2] + placed[3:6] + placed[6:9] + placed[9:12],
        check_vma=False,
    )
```

```python
import functools
import math

import jax
import jax.numpy as jnp
from jax import lax
from jax.experimental import pallas as pl
from jax.experimental.pallas import tpu as pltpu
from jax.sharding import PartitionSpec as P

HEADS = 17
HEAD_DIM = 64
FF = 4352
STEP = 10

MASKED = -1e30
NORM_EPS = 1e-05
BETA_ONE = 0.9
BETA_TWO = 0.95
ADAM_EPS = 1e-08
BF16 = jnp.bfloat16
F32 = jnp.float32


def dot(left, right, dims=((1,), (0,))):
    return lax.dot_general(left, right, (dims, ((), ())), preferred_element_type=F32)


def padded(top, rows, width):
    row = lax.broadcasted_iota(jnp.int32, (rows, width), 0)
    out = jnp.zeros((rows, width), F32)
    for index, value in enumerate(top):
        out = jnp.where(row == index, value, out)
    return out.astype(BF16)


def key_rows(lens_ref, key, length):
    pos = lax.broadcasted_iota(jnp.int32, (1, length), 1)
    bias = jnp.where(pos < lens_ref[0], 0.0, MASKED)
    one = jnp.ones((1, length), F32)
    extra = padded([bias, one, one, one], HEAD_DIM, length)
    return jnp.concatenate([key, extra], axis=0).T


def causal(block):
    key = lax.broadcasted_iota(jnp.int32, (block, block), 0)
    query = lax.broadcasted_iota(jnp.int32, (block, block), 1)
    return key <= query


def attend_kernel(block, lens_ref, q_ref, k_ref, v_ref, o_ref, low_ref, lse_ref, keys):
    heads, _, length = k_ref.shape[2:]
    tok = low_ref.shape[-1]
    step = pl.program_id(0)

    @pl.when(step == 0)
    def _():
        for h in range(heads):
            keys[h] = key_rows(lens_ref, k_ref[0, 0, h], length)

    one_row = padded([jnp.ones((1, block), F32)], HEAD_DIM, block)
    queries = []
    for h in range(heads):
        query = (q_ref[0, 0, h].astype(F32) * (1.0 / math.sqrt(HEAD_DIM))).astype(BF16)
        queries.append(jnp.concatenate([query, one_row], axis=0))

    def one(index, states, mask):
        start = pl.multiple_of(index * block, block)
        all_scores = [dot(keys[h, pl.ds(start, block), :], queries[h]) for h in range(heads)]
        results = []
        for h, (top, total, accum) in enumerate(states):
            scores = all_scores[h]
            if mask is not None:
                scores = jnp.where(mask, scores, MASKED)
            new_top = jnp.maximum(top, jnp.max(scores, axis=0, keepdims=True))
            weights = jnp.exp(scores - new_top)
            factor = jnp.exp(top - new_top)
            total = total * factor + jnp.sum(weights, axis=0, keepdims=True)
            value = v_ref[0, 0, h, :, pl.ds(start, block)]
            accum = accum * factor + dot(value, weights.astype(BF16))
            results.append((new_top, total, accum))
        return tuple(results)

    state = (
        jnp.full((1, block), MASKED, F32),
        jnp.zeros((1, block), F32),
        jnp.zeros((HEAD_DIM, block), F32),
    )
    states = lax.fori_loop(0, step, lambda i, s: one(i, s, None), (state,) * heads)
    states = one(step, states, causal(block))
    for h, (top, total, accum) in enumerate(states):
        result = accum / total
        o_ref[h] = result
        for i in range(block // tok):
            low_ref[i, h] = result[:, i * tok : (i + 1) * tok].astype(BF16)
        lse_ref[h] = top + jnp.log(total)


def head_specs(slot, heads, dim, length, block):
    def whole(part):
        return pl.BlockSpec((1, 1, heads, dim, length), lambda i, lens: (slot, part, 0, 0, 0))

    def piece(part):
        return pl.BlockSpec((1, 1, heads, dim, block), lambda i, lens: (slot, part, 0, 0, i))

    return whole, piece


def attend(lens, qkv, slot, tok):
    dim, length = qkv.shape[3:]
    pairs = lens.shape[0]
    block = math.gcd(length, 512)
    whole, piece = head_specs(slot, pairs, dim, length, block)
    return pl.pallas_call(
        functools.partial(attend_kernel, block),
        grid_spec=pltpu.PrefetchScalarGridSpec(
            num_scalar_prefetch=1,
            grid=(length // block,),
            in_specs=[piece(0), whole(1), whole(2)],
            out_specs=[
                pl.BlockSpec((pairs, dim, block), lambda i, lens: (0, 0, i)),
                pl.BlockSpec((block // tok, pairs, dim, tok), lambda i, lens: (i, 0, 0, 0)),
                pl.BlockSpec((pairs, 1, block), lambda i, lens: (0, 0, i)),
            ],
            scratch_shapes=[pltpu.VMEM((pairs, length, 2 * dim), BF16)],
        ),
        out_shape=[
            jax.ShapeDtypeStruct((pairs, dim, length), F32),
            jax.ShapeDtypeStruct((length // tok, pairs, dim, tok), BF16),
            jax.ShapeDtypeStruct((pairs, 1, length), F32),
        ],
        compiler_params=pltpu.CompilerParams(
            vmem_limit_bytes=48 * 2**20
        ),
        cost_estimate=pl.CostEstimate(flops=1000, bytes_accessed=1000, transcendentals=0),
    )(lens, qkv, qkv, qkv)


def split_three(value):
    first = value.astype(BF16).astype(F32)
    second = (value - first).astype(BF16).astype(F32)
    third = (value - first - second).astype(BF16).astype(F32)
    return [-first, -second, -third]


def attend_back_kernel(
    block,
    lens_ref,
    q_ref,
    k_ref,
    v_ref,
    o_ref,
    lse_ref,
    grad_ref,
    out_ref,
    keys,
    values,
    queries,
    grads,
    total,
):
    heads, dim, length = k_ref.shape[2:]
    tok = grad_ref.shape[-1]
    count = length // block
    step = pl.program_id(0)
    scale = 1.0 / math.sqrt(HEAD_DIM)

    @pl.when(step == 0)
    def _():
        one = jnp.ones((1, length), F32)
        for h in range(heads):
            keys[h] = key_rows(lens_ref, k_ref[0, 0, h], length)
            extra = padded([one, one, one], dim, length)
            values[h] = jnp.concatenate([v_ref[0, 0, h], extra], axis=0).T
            queries[h, 0:dim, :] = (q_ref[0, 0, h].astype(F32) * scale).astype(BF16)
            queries[h, dim:, :] = padded([one] + split_three(lse_ref[h]), dim, length)
            for i in range(length // tok):
                grads[h, 0:dim, i * tok : (i + 1) * tok] = grad_ref[i, h]
            delta = jnp.sum(grads[h, 0:dim, :].astype(F32) * o_ref[h], axis=0, keepdims=True)
            grads[h, dim:, :] = padded(split_three(delta), dim, length)
        total[...] = jnp.zeros_like(total)

    mine = pl.ds(pl.multiple_of(step * block, block), block)

    def one(index, states, mask):
        cols = pl.ds(pl.multiple_of(index * block, block), block)
        all_scores = [dot(keys[h, mine, :], queries[h, :, cols]) for h in range(heads)]
        results = []
        for h, (dk, dv) in enumerate(states):
            scores = all_scores[h]
            if mask is not None:
                scores = jnp.where(mask, scores, MASKED)
            probs = jnp.exp(scores)
            grad_scores = (probs * dot(values[h, mine, :], grads[h, :, cols])).astype(BF16)
            probs = probs.astype(BF16)
            dv = dv + dot(grads[h, 0:dim, cols], probs, ((1,), (1,)))
            dk = dk + dot(queries[h, 0:dim, cols], grad_scores, ((1,), (1,)))
            total[h, :, cols] += dot(k_ref[0, 0, h, :, mine], grad_scores)
            results.append((dk, dv))
        return tuple(results)

    zero = jnp.zeros((dim, block), F32)
    states = one(step, ((zero, zero),) * heads, causal(block))
    states = lax.fori_loop(step + 1, count, lambda i, s: one(i, s, None), states)
    for h, (dk, dv) in enumerate(states):
        dq = total[h, :, mine] * scale
        for i in range(block // tok):
            cols = slice(i * tok, (i + 1) * tok)
            out_ref[i, h, 0:dim] = dq[:, cols].astype(BF16)
            out_ref[i, h, dim : 2 * dim] = dk[:, cols].astype(BF16)
            out_ref[i, h, 2 * dim :] = dv[:, cols].astype(BF16)


def attend_back(lens, qkv, slot, out, lse, grad):
    dim, length = qkv.shape[3:]
    pairs, tok = lens.shape[0], grad.shape[-1]
    ctx = length // tok
    block = math.gcd(length, 512)
    whole, _ = head_specs(slot, pairs, dim, length, block)
    return pl.pallas_call(
        functools.partial(attend_back_kernel, block),
        grid_spec=pltpu.PrefetchScalarGridSpec(
            num_scalar_prefetch=1,
            grid=(length // block,),
            in_specs=[
                whole(0),
                whole(1),
                whole(2),
                pl.BlockSpec((pairs, dim, length), lambda i, lens: (0, 0, 0)),
                pl.BlockSpec((pairs, 1, length), lambda i, lens: (0, 0, 0)),
                pl.BlockSpec((ctx, pairs, dim, tok), lambda i, lens: (0, 0, 0, 0)),
            ],
            out_specs=pl.BlockSpec(
                (block // tok, pairs, 3 * dim, tok), lambda i, lens: (i, 0, 0, 0)
            ),
            scratch_shapes=[
                pltpu.VMEM((pairs, length, 2 * dim), BF16),
                pltpu.VMEM((pairs, length, 2 * dim), BF16),
                pltpu.VMEM((pairs, 2 * dim, length), BF16),
                pltpu.VMEM((pairs, 2 * dim, length), BF16),
                pltpu.VMEM((pairs, dim, length), F32),
            ],
        ),
        out_shape=jax.ShapeDtypeStruct((ctx, pairs, 3 * dim, tok), BF16),
        compiler_params=pltpu.CompilerParams(
            vmem_limit_bytes=48 * 2**20
        ),
        cost_estimate=pl.CostEstimate(flops=1000, bytes_accessed=1000, transcendentals=0),
    )(lens, qkv, qkv, qkv, out, lse, grad)


def own_grad_kernel(late_ref, first_ref, second_ref, first_grad_ref, second_grad_ref, last_grad_ref, out_ref, total):
    step = pl.program_id(0)
    nt = ((1,), (1,))
    first, second = first_ref[0, 0], second_ref[0, 0]
    head = dot(first, first_grad_ref[0], nt) + dot(second, second_grad_ref[0], nt)
    last = dot(jnp.where(late_ref[0] == 0, first, second), last_grad_ref[0], nt)
    part = jnp.concatenate([head, last], axis=1)

    @pl.when(step == 0)
    def _():
        total[...] = part

    @pl.when(step > 0)
    def _():
        total[...] += part

    @pl.when(step == pl.num_programs(0) - 1)
    def _():
        out_ref[...] = total[...]


def own_grad(late, act, first_grad, second_grad, last_grad):
    _, ctx, width, tok = act.shape
    feat, last = first_grad.shape[1], last_grad.shape[1]

    def block(rows):
        return pl.BlockSpec((1, rows, tok), lambda i, late: (i, 0, 0))

    def of(slot):
        return pl.BlockSpec((1, 1, width, tok), lambda i, late: (slot, i, 0, 0))

    return pl.pallas_call(
        own_grad_kernel,
        grid_spec=pltpu.PrefetchScalarGridSpec(
            num_scalar_prefetch=1,
            grid=(ctx,),
            in_specs=[of(0), of(1), block(feat), block(feat), block(last)],
            out_specs=pl.BlockSpec((width, feat + last), lambda i, late: (0, 0)),
            scratch_shapes=[pltpu.VMEM((width, feat + last), F32)],
        ),
        out_shape=jax.ShapeDtypeStruct((width, feat + last), F32),
        compiler_params=pltpu.CompilerParams(vmem_limit_bytes=48 * 2**20),
        cost_estimate=pl.CostEstimate(flops=1000, bytes_accessed=1000, transcendentals=0),
    )(late[None], act, act, first_grad, second_grad, last_grad)


def mlp_kernel(
    width,
    a_ref,
    g_ref,
    up_ref,
    down_ref,
    bias_ref,
    y_ref,
    ga_ref,
    dup_ref,
    ddown_ref,
    db_ref,
    a_rows,
    g_rows,
):
    step = pl.program_id(0)
    slots, _, tok = a_ref.shape
    block = up_ref.shape[1]

    @pl.when(step == 0)
    def _():
        for s in range(slots):
            a_rows[s * tok : (s + 1) * tok, :] = a_ref[s].T
            g_rows[s * tok : (s + 1) * tok, :] = g_ref[s].T
        y_ref[...] = jnp.zeros_like(y_ref)
        ga_ref[...] = jnp.zeros_like(ga_ref)

    def run(size):
        up = up_ref[:, :size]
        down = down_ref[:, :size]
        pre = dot(a_rows[...], up) + bias_ref[:, :size]
        cdf = 0.5 * (1.0 + lax.erf(pre * math.sqrt(0.5)))
        hidden = (pre * cdf).astype(BF16)
        slope = cdf + pre * jnp.exp(-0.5 * pre * pre) * (1.0 / math.sqrt(2.0 * math.pi))
        grad = (dot(g_rows[...], down) * slope).astype(BF16)
        db_ref[:, :size] = jnp.sum(grad.astype(F32), axis=0, keepdims=True)
        nt = ((1,), (1,))
        for s in range(slots):
            rows = slice(s * tok, (s + 1) * tok)
            y_ref[s] += dot(down, hidden[rows], nt)
            ga_ref[s] += dot(up, grad[rows], nt)
        dup = sum(dot(a_ref[s], grad[s * tok : (s + 1) * tok]) for s in range(slots))
        dup_ref[:, :size] = dup.astype(dup_ref.dtype)
        ddown = sum(dot(g_ref[s], hidden[s * tok : (s + 1) * tok]) for s in range(slots))
        ddown_ref[:, :size] = ddown.astype(ddown_ref.dtype)

    full = width // block

    @pl.when(step < full)
    def _():
        run(block)

    if width % block:

        @pl.when(step == full)
        def _():
            run(width % block)


def mlp(act, grad, up, down, bias):
    slots, width, tok = act.shape
    units = up.shape[1]
    block = 256

    def fixed(shape):
        return pl.BlockSpec(shape, lambda i: (0,) * len(shape))

    cols = pl.BlockSpec((width, block), lambda i: (0, i))
    line = pl.BlockSpec((1, block), lambda i: (0, i))
    total = jax.ShapeDtypeStruct((slots, width, tok), F32)
    grads = jax.ShapeDtypeStruct((width, units), BF16)
    return pl.pallas_call(
        functools.partial(mlp_kernel, units),
        grid=(pl.cdiv(units, block),),
        in_specs=[fixed(act.shape), fixed(act.shape), cols, cols, line],
        out_specs=[fixed(act.shape), fixed(act.shape), cols, cols, line],
        out_shape=[total, total, grads, grads, jax.ShapeDtypeStruct((1, units), F32)],
        scratch_shapes=[pltpu.VMEM((slots * tok, width), BF16)] * 2,
        compiler_params=pltpu.CompilerParams(vmem_limit_bytes=56 * 2**20),
        cost_estimate=pl.CostEstimate(flops=1000, bytes_accessed=1000, transcendentals=0),
    )(act, grad, up, down, bias)


def other_index(index, bit):
    return index + bit * (1 - 2 * lax.rem(index // bit, 2))


def split_columns(start, size, count):
    tiles = size // 128
    cuts = [start + 128 * (-(-tiles * i // count)) for i in range(count)] + [start + size]
    return [(cuts[i], cuts[i + 1] - cuts[i]) for i in range(count)]


def gather_kernel(
    ctx,
    fsdp,
    regular,
    x_ref,
    w_ref,
    v_ref,
    act_ref,
    qkv_ref,
    wo_ref,
    um_ref,
    uo_ref,
    vo_ref,
    xo_ref,
    wide,
    w_low,
    windows,
    own_w,
    own_t,
    v_all,
    v_rows,
    bias,
    acts,
    qkvs,
    x_send,
    x_recv,
    xc_send,
    xc_recv,
    w_send,
    w_recv,
    wc_send,
    wc_recv,
    v_send,
    v_recv,
    act_sem,
    local,
):
    c, f = lax.axis_index("ctx"), lax.axis_index("fsdp")
    chips = ctx // 2
    z, core = c // 2, lax.rem(c, 2)
    partner = 2 * z + 1 - core
    slots, width, tok = x_ref.shape
    rows = w_ref.shape[0]
    dim = HEAD_DIM
    owned = regular + 1
    levels = bits_of(fsdp)
    half = um_ref.shape[2]

    def combine(number):
        place = f
        for bit in range(levels):
            if number & (1 << bit):
                place = other_index(place, 1 << bit)
        return place

    barrier = pltpu.get_barrier_semaphore()

    def greet(where):
        pl.semaphore_signal(barrier, inc=1, device_id=where, device_id_type=pl.DeviceIdType.MESH)

    greet((partner, f))
    for number in range(1, fsdp):
        greet((c, combine(number)))

    @pl.when(z > 0)
    def _():
        greet((c - 2, f))

    @pl.when(z < chips - 1)
    def _():
        greet((c + 2, f))

    beside = (z > 0).astype(jnp.int32) + (z < chips - 1).astype(jnp.int32)
    pl.semaphore_wait(barrier, fsdp + beside)

    def remote(source, target, send, recv, where):
        return pltpu.make_async_remote_copy(
            src_ref=source,
            dst_ref=target,
            send_sem=send,
            recv_sem=recv,
            device_id=where,
            device_id_type=pl.DeviceIdType.MESH,
        )

    def x_copy(side, s, h):
        sign = 1 - 2 * side
        block = c - 2 * sign * s
        source = x_ref.at[h] if s == 0 else xo_ref.at[block, h]
        return remote(
            source, xo_ref.at[block, h], x_send.at[side, s, h], x_recv.at[side, s, h], (c + 2 * sign, f)
        )

    def x_sends(side, s):
        return (z - s >= 0) & (z < chips - 1) if side == 0 else (z + s < chips) & (z > 0)

    def x_gets(side, s):
        return z - 1 - s >= 0 if side == 0 else z + 1 + s < chips

    def x_arrival(side, s, h):
        sign = 1 - 2 * side
        block = c - 2 * sign * (s + 1)
        return remote(
            xo_ref.at[block, h],
            xo_ref.at[block, h],
            x_send.at[side, s, h],
            x_recv.at[side, s, h],
            (c + 2 * sign, f),
        )

    def x_share(side, s, h):
        sign = 1 - 2 * side
        block = c - 2 * sign * (s + 1)
        return remote(
            xo_ref.at[block, h],
            xo_ref.at[block, h],
            xc_send.at[side, s, h],
            xc_recv.at[side, s, h],
            (partner, f),
        )

    def x_share_arrival(side, s, h):
        sign = 1 - 2 * side
        block = partner - 2 * sign * (s + 1)
        return remote(
            xo_ref.at[block, h],
            xo_ref.at[block, h],
            xc_send.at[side, s, h],
            xc_recv.at[side, s, h],
            (partner, f),
        )

    def x_own(h):
        return remote(
            x_ref.at[h],
            xo_ref.at[c, h],
            xc_send.at[0, chips - 1, h],
            xc_recv.at[0, chips - 1, h],
            (partner, f),
        )

    def x_own_arrival(h):
        return remote(
            x_ref.at[h],
            xo_ref.at[partner, h],
            xc_send.at[0, chips - 1, h],
            xc_recv.at[0, chips - 1, h],
            (partner, f),
        )

    runs = split_columns(0, half, levels)

    def source(unit, stream):
        start, size = runs[stream]
        return w_low.at[:, pl.ds(pl.multiple_of((2 * unit + core) * half + start, 128), size)]

    def kept(unit, stream, place, which):
        start, size = runs[stream]
        if unit == 0:
            return wo_ref.at[place, :, pl.ds(pl.multiple_of(which * half + start, 128), size)]
        return um_ref.at[place, :, pl.ds(start, size)]

    def shared(unit, stream, place, which):
        start, size = runs[stream]
        if unit == 0:
            return kept(unit, stream, place, which)
        return uo_ref.at[place, :, pl.ds(start, size)]

    def w_copy(unit, stream, step, number):
        bit = 1 << ((stream + step) % levels)
        place = combine(number)
        there = kept(unit, stream, place, core)
        return remote(
            source(unit, stream) if number == 0 else there,
            there,
            w_send.at[unit, stream, number | bit],
            w_recv.at[unit, stream, number | bit],
            (c, other_index(f, bit)),
        )

    def w_arrival(unit, stream, number):
        block = kept(unit, stream, combine(number), core)
        sems = w_send.at[unit, stream, number], w_recv.at[unit, stream, number]
        return remote(block, block, *sems, (partner, f))

    def w_share(unit, stream, number):
        place = combine(number)
        sems = wc_send.at[unit, stream, number], wc_recv.at[unit, stream, number]
        block = kept(unit, stream, place, core)
        return remote(block, shared(unit, stream, place, core), *sems, (partner, f))

    def w_share_arrival(unit, stream, number):
        block = shared(unit, stream, combine(number), 1 - core)
        sems = wc_send.at[unit, stream, number], wc_recv.at[unit, stream, number]
        return remote(block, block, *sems, (partner, f))

    def held(stream, step):
        numbers = [0]
        for i in range(step):
            bit = 1 << ((stream + i) % levels)
            numbers += [n | bit for n in numbers]
        return numbers

    def v_copy(number):
        return remote(
            v_ref, v_all.at[f], v_send.at[number], v_recv.at[number], (c, combine(number))
        )

    def v_arrival(number):
        return remote(
            v_ref,
            v_all.at[combine(number)],
            v_send.at[number],
            v_recv.at[number],
            (c, combine(number)),
        )

    def x_begin(h):
        for side in range(2):

            @pl.when(x_sends(side, 0))
            def _(side=side):
                x_copy(side, 0, h).start()

        x_own(h).start()

    def x_step(h, s):
        for side in range(2):

            @pl.when(x_gets(side, s))
            def _(side=side):
                x_arrival(side, s, h).wait_recv()
                x_share(side, s, h).start()

            if s + 1 < chips - 1:

                @pl.when(x_sends(side, s + 1))
                def _(side=side):
                    x_copy(side, s + 1, h).start()

    def w_step(unit, step):
        for stream in range(levels):
            bit = 1 << ((stream + step) % levels)
            arrived = [number | bit for number in held(stream, step)]
            for number in arrived:
                w_arrival(unit, stream, number).wait_recv()
            if step + 1 < levels:
                for number in held(stream, step + 1):
                    w_copy(unit, stream, step + 1, number).start()
            for number in arrived:
                w_share(unit, stream, number).start()

    def fetch(unit):
        cols = pl.ds(2 * unit * half, 2 * half)
        return pltpu.make_async_copy(w_ref.at[:, cols], wide.at[:, cols], local.at[3 + unit])

    def w_begin(unit):
        fetch(unit).wait()
        cols = slice(2 * unit * half, 2 * (unit + 1) * half)

        strip = 16 if rows % 16 == 0 else rows

        def body(i, carry):
            at = pl.ds(pl.multiple_of(i * strip, strip), strip)
            w_low[at, cols] = wide[at, cols].astype(BF16)
            return carry

        lax.fori_loop(0, rows // strip, body, 0)
        for stream in range(levels):
            w_copy(unit, stream, 0, 0).start()

    own_up = w_low.at[:, pl.ds(pl.multiple_of((2 + core) * half, 128), half)]
    other_up = w_low.at[:, pl.ds(pl.multiple_of((3 - core) * half, 128), half)]
    kept_here = [
        pltpu.make_async_copy(w_low.at[:, pl.ds(0, 2 * half)], wo_ref.at[f], local.at[0]),
        pltpu.make_async_copy(own_up, um_ref.at[f], local.at[1]),
        pltpu.make_async_copy(other_up, uo_ref.at[f], local.at[2]),
    ]
    v_own = pltpu.make_async_copy(v_ref, v_all.at[f], local.at[5])
    v_out = pltpu.make_async_copy(v_all, vo_ref, local.at[6])
    x_here = pltpu.make_async_copy(x_ref, xo_ref.at[c], local.at[7])

    head_of = [i * ctx + c for i in range(regular)] + [HEADS - 1]
    places = [part * HEADS + head for part in range(3) for head in head_of]

    def window(i):
        start = pl.multiple_of(places[i] // 2 * 128, 128)
        return pltpu.make_async_copy(
            wo_ref.at[:, :, pl.ds(start, 128)], windows.at[i], local.at[8 + i]
        )

    def ready():
        kept_here[0].wait()
        for number in range(1, fsdp):
            v_arrival(number).wait_recv()
            for stream in range(levels):
                w_share_arrival(0, stream, number).wait_recv()
        v_own.wait()
        v_out.start()
        for i in range(len(places)):
            window(i).start()
        for i in range(fsdp):
            v_rows[i * rows : (i + 1) * rows, :] = v_all[i].astype(F32)
        own_w[...] = jnp.zeros_like(own_w)
        for i, place in enumerate(places):
            window(i).wait()
            odd = lax.rem(place, 2)
            for k in range(fsdp):
                both = windows[i, k]
                mine = jnp.where(odd == 0, both[:, :dim], both[:, dim:])
                own_w[k * rows : (k + 1) * rows, i * dim : (i + 1) * dim] = mine
        own_t[...] = own_w[...].T
        for part, column in ((0, 2), (2, 3)):
            for i, head in enumerate(head_of):
                start = (part * owned + i) * dim
                at = pl.ds(pl.multiple_of(head * dim, dim), dim)
                bias[start : start + dim, :] = v_rows[at, column : column + 1]
        start = owned * dim
        bias[start : 2 * start, :] = jnp.zeros((start, 1), F32)

    def project(h, b):
        unit, _ = norm_parts(xo_ref[b, h].astype(F32), 0)
        act = (unit * v_rows[:, 0:1] + v_rows[:, 1:2]).astype(BF16)
        acts[h, b] = act
        pltpu.make_async_copy(acts.at[h, b], act_ref.at[h, b], act_sem.at[h, b]).start()
        value = dot(own_t[...], act)[: 3 * owned * dim] + bias[...]
        qkvs[h, :, pl.ds(pl.multiple_of(b * tok, tok), tok)] = value.astype(BF16)

    def project_own(h):
        x_own_arrival(h).wait_recv()

        def body(i, carry):
            project(h, 2 * z + i)
            return carry

        lax.fori_loop(0, 2, body, 0)

    def project_step(h, s):
        for side in range(2):

            @pl.when(x_gets(side, s))
            def _(side=side):
                x_share_arrival(side, s, h).wait_recv()

        def body(i, carry):
            side = i // 2
            chip = z - (1 - 2 * side) * (s + 1)

            @pl.when((chip >= 0) & (chip < chips))
            def _():
                project(h, 2 * chip + lax.rem(i, 2))

            return carry

        lax.fori_loop(0, 4, body, 0)

    def out_copy(h):
        return pltpu.make_async_copy(qkvs.at[h], qkv_ref.at[h], local.at[8 + len(places) + h])

    plan = []
    block_time = 0.95

    def at(time, work, *values):
        plan.append((time, functools.partial(work, *values)))

    for h in range(slots):
        for s in range(chips - 1):
            at(block_time * (h * (chips - 1) + s + 1), x_step, h, s)
        if h > 0:
            at(block_time * (h * (chips - 1) - 1) + 0.01, x_begin, h)
    time = 0.0
    for unit in range(2):
        for step in range(levels):
            if unit == 0 and step == levels - 1:
                at(time + 0.9, w_begin, 1)
            time += 2.0 ** (step + 1) / levels
            at(time, w_step, unit, step)
        if unit == 0:
            done = max(time, block_time * (chips - 1))
    at(done + 0.3, ready)
    for h in range(slots):
        for s in range(-1, chips - 1):
            arrived = block_time * (h * (chips - 1) + s + 1) + 0.1
            late = max(arrived, done + 0.31 + 0.2 * (s + 1) + 0.01 * h)
            if s < 0:
                at(late, project_own, h)
            else:
                at(late, project_step, h, s)
        at(max(arrived, done + 0.31 + 0.2 * chips) + 0.02, lambda h: out_copy(h).start(), h)

    fetch(0).start()
    fetch(1).start()
    x_here.start()
    x_begin(0)
    for number in range(1, fsdp):
        v_copy(number).start()
    v_own.start()
    w_begin(0)
    kept_here[0].start()
    x_here.wait()
    for _, work in sorted(plan, key=lambda entry: entry[0]):
        work()

    kept_here[1].start()
    kept_here[2].start()
    kept_here[1].wait()
    kept_here[2].wait()
    v_out.wait()
    for number in range(1, fsdp):
        v_copy(number).wait_send()
        for unit in range(2):
            for stream in range(levels):
                w_arrival(unit, stream, number).wait_send()
                w_share(unit, stream, number).wait_send()
                if unit > 0:
                    w_share_arrival(unit, stream, number).wait_recv()
    for h in range(slots):
        x_own(h).wait_send()
        out_copy(h).wait()
        for b in range(ctx):
            pltpu.make_async_copy(acts.at[h, b], act_ref.at[h, b], act_sem.at[h, b]).wait()
        for s in range(chips - 1):
            for side in range(2):

                @pl.when(x_sends(side, s))
                def _(side=side, h=h, s=s):
                    x_copy(side, s, h).wait_send()

                @pl.when(x_gets(side, s))
                def _(side=side, h=h, s=s):
                    x_share(side, s, h).wait_send()


def gather_first(ctx, fsdp, regular, x, w, v):
    slots, width, tok = x.shape
    rows, columns = w.shape
    levels, chips = bits_of(fsdp), ctx // 2
    owned = regular + 1
    feat = 3 * owned * HEAD_DIM
    room = feat + -feat % 128
    anywhere = pl.BlockSpec(memory_space=pl.ANY)
    dma = pltpu.SemaphoreType.DMA
    return pl.pallas_call(
        functools.partial(gather_kernel, ctx, fsdp, regular),
        in_specs=[anywhere, anywhere, pl.BlockSpec(memory_space=pltpu.VMEM)],
        out_specs=[anywhere] * 6,
        out_shape=[
            jax.ShapeDtypeStruct((slots, ctx, width, tok), BF16),
            jax.ShapeDtypeStruct((slots, feat, ctx * tok), BF16),
            jax.ShapeDtypeStruct((fsdp, rows, columns // 2), BF16),
            jax.ShapeDtypeStruct((fsdp, rows, columns // 4), BF16),
            jax.ShapeDtypeStruct((fsdp, rows, columns // 4), BF16),
            jax.ShapeDtypeStruct((fsdp, rows, 128), BF16),
        ],
        scratch_shapes=[
            pltpu.VMEM((ctx, slots, width, tok), BF16),
            pltpu.VMEM((rows, columns), F32),
            pltpu.VMEM((rows, columns), BF16),
            pltpu.VMEM((3 * owned, fsdp, rows, 128), BF16),
            pltpu.VMEM((width, room), BF16),
            pltpu.VMEM((room, width), BF16),
            pltpu.VMEM((fsdp, rows, 128), BF16),
            pltpu.VMEM((width, 128), F32),
            pltpu.VMEM((feat, 1), F32),
            pltpu.VMEM((slots, ctx, width, tok), BF16),
            pltpu.VMEM((slots, feat, ctx * tok), BF16),
            dma((2, chips - 1, slots)),
            dma((2, chips - 1, slots)),
            dma((2, chips, slots)),
            dma((2, chips, slots)),
            dma((2, levels, fsdp)),
            dma((2, levels, fsdp)),
            dma((2, levels, fsdp)),
            dma((2, levels, fsdp)),
            dma((fsdp,)),
            dma((fsdp,)),
            dma((slots, ctx)),
            dma((8 + 3 * owned + slots,)),
        ],
        compiler_params=pltpu.CompilerParams(
            collective_id=0, has_side_effects=True, vmem_limit_bytes=60 * 2**20
        ),
        cost_estimate=pl.CostEstimate(flops=1000, bytes_accessed=1000, transcendentals=0),
    )(x, w, v)


def bits_of(count):
    return max(count.bit_length() - 1, 0)


def flip(count, value):
    return [(i, i ^ value) for i in range(count)]


def pick(array, index, axis):
    return lax.dynamic_index_in_dim(array, index, axis, keepdims=False)


def ordered(bit, mine, other, axis):
    first = jnp.where(bit == 0, mine, other)
    second = jnp.where(bit == 0, other, mine)
    return jnp.concatenate([first, second], axis=axis)


def after(value, *others):
    return lax.optimization_barrier((value, others))[0]


def add_low(mine, swapped):
    return (mine.astype(F32) + swapped.astype(F32)).astype(BF16)


def scatter_fsdp(total):
    return lax.psum_scatter(total, "fsdp", scatter_dimension=0, tiled=True)


def bar_signal(where):
    pl.semaphore_signal(
        pltpu.get_barrier_semaphore(), inc=1, device_id=where, device_id_type=pl.DeviceIdType.MESH
    )


def remote_copy(source, target, send, recv, where):
    return pltpu.make_async_remote_copy(
        src_ref=source,
        dst_ref=target,
        send_sem=send,
        recv_sem=recv,
        device_id=where,
        device_id_type=pl.DeviceIdType.MESH,
    )


def line_gather(chips, c, f, mine, slot, share, sems, core_sems):
    z, core = c // 2, lax.rem(c, 2)
    partner = 2 * z + 1 - core
    send, recv = sems
    core_send, core_recv = core_sems

    def passing(side, s):
        sign = 1 - 2 * side
        chip = z - sign * s
        source = mine if s == 0 else slot(chip)
        return remote_copy(
            source, slot(chip), send.at[side, s], recv.at[side, s], (c + 2 * sign, f)
        )

    def arrival(side, s):
        block = slot(z - (1 - 2 * side) * (s + 1))
        return remote_copy(block, block, send.at[side, s], recv.at[side, s], (partner, f))

    def sends(side, s):
        return (z - s >= 0) & (z < chips - 1) if side == 0 else (z + s < chips) & (z > 0)

    def gets(side, s):
        return z - 1 - s >= 0 if side == 0 else z + 1 + s < chips

    def shared(side, s):
        chip = z - (1 - 2 * side) * (s + 1)
        return remote_copy(
            slot(chip), share(chip), core_send.at[side, s], core_recv.at[side, s], (partner, f)
        )

    def share_arrival(side, s):
        block = share(z - (1 - 2 * side) * (s + 1))
        sems = core_send.at[side, s], core_recv.at[side, s]
        return remote_copy(block, block, *sems, (partner, f))

    own_sems = core_send.at[0, chips - 1], core_recv.at[0, chips - 1]
    own_share = remote_copy(mine, share(z), *own_sems, (partner, f))

    def start():
        for side in range(2):

            @pl.when(sends(side, 0))
            def _(side=side):
                passing(side, 0).start()

        own_share.start()

    def step(s):
        for side in range(2):

            @pl.when(gets(side, s))
            def _(side=side):
                arrival(side, s).wait_recv()
                shared(side, s).start()

            if s + 1 < chips - 1:

                @pl.when(sends(side, s + 1))
                def _(side=side):
                    passing(side, s + 1).start()

    def end():
        own_share.wait_send()
        remote_copy(share(z), share(z), *own_sems, (partner, f)).wait_recv()
        for s in range(chips - 1):
            for side in range(2):

                @pl.when(sends(side, s))
                def _(side=side, s=s):
                    passing(side, s).wait_send()

                @pl.when(gets(side, s))
                def _(side=side, s=s):
                    shared(side, s).wait_send()
                    share_arrival(side, s).wait_recv()

    return start, [functools.partial(step, s) for s in range(chips - 1)], end


def sum_kernel(ctx, fsdp, batches, *refs):
    levels, chips = bits_of(fsdp), ctx // 2
    pieces = refs[0:2]
    own_ref, mine_out, other_out, own_out, last_out = refs[2:7]
    rest = list(refs[7:])
    own_kept, own_low, beside = rest.pop(0), rest.pop(0), rest.pop(0)
    own_sent = [rest.pop(0) for _ in range(levels)]
    own_got = [rest.pop(0) for _ in range(levels)]
    z_sent, z_got = rest.pop(0), rest.pop(0)
    op_send, op_recv, zs_send, zs_recv, zg_send, zg_recv = (rest.pop(0) for _ in range(6))
    zc_send, zc_recv, og_send, og_recv, oc_send, oc_recv, far_send, far_recv, local = (
        rest.pop(0) for _ in range(9)
    )
    c, f = lax.axis_index("ctx"), lax.axis_index("fsdp")
    z, core = c // 2, lax.rem(c, 2)
    partner = 2 * z + 1 - core
    far = lax.rem(c + ctx // 2, ctx)
    rows = own_low.shape[0]
    chunk = z_sent.shape[-1]
    width = chunk * chips // 2
    parts = chips // 2
    strip = 16 if rows % 16 == 0 else 8

    def own_bit(bit):
        return lax.rem(f // (1 << bit), 2)

    def strips(work):
        def body(i, carry):
            work(pl.ds(pl.multiple_of(i * strip, strip), strip))
            return carry

        lax.fori_loop(0, rows // strip, body, 0)

    bar_signal((partner, f))
    bar_signal((far, f))
    for bit in range(levels):
        bar_signal((c, other_index(f, 1 << bit)))

    @pl.when(z > 0)
    def _():
        bar_signal((c - 2, f))

    @pl.when(z < chips - 1)
    def _():
        bar_signal((c + 2, f))

    neighbours = (z > 0).astype(jnp.int32) + (z < chips - 1).astype(jnp.int32)
    pl.semaphore_wait(pltpu.get_barrier_semaphore(), levels + 2 + neighbours)

    def order(q):
        return [(q + i) % levels for i in range(levels)]

    def place_of(q, flipped, free):
        bits = order(q)
        first = own_bit(bits[0])
        total = (1 - first if flipped else first) * (1 << bits[0])
        for i, bit in enumerate(bits[1:]):
            total += ((free >> i) & 1) * (1 << bit)
        return total

    def kept_index(q, step, flipped, free):
        bits = order(q)
        total = 0
        for i, bit in enumerate(bits[1:]):
            mine = own_bit(bit)
            if i + 1 < step:
                value = mine
            elif i + 1 == step:
                value = 1 - mine if flipped else mine
            else:
                value = (free >> (i - step)) & 1
            total += value * (1 << i)
        return total

    def across(step, q):
        return (c, other_index(f, 1 << order(q)[step]))

    def own_copy(step):
        return remote_copy(
            own_sent[step], own_got[step], op_send.at[step], op_recv.at[step], across(step, 0)
        )

    def own_begin():
        for free in range(fsdp // 2):
            there, here = place_of(0, True, free), place_of(0, False, free)

            def work(at, free=free, there=there, here=here):
                own_sent[0][free, at, :] = own_ref[there, at, :]
                own_kept[free, at, :] = own_ref[here, at, :].astype(F32)

            strips(work)
        own_copy(0).start()

    def later(step, kept_ref, got_ref, sent_ref, q):
        for free in range(fsdp >> (step + 2)):
            there, here = (kept_index(q, step + 1, flipped, free) for flipped in (True, False))
            mine = own_bit(order(q)[step + 1])
            there_got, here_got = free * 2 + 1 - mine, free * 2 + mine

            def work(at, free=free):
                value = kept_ref[there, at, :] + got_ref[there_got, at, :].astype(F32)
                sent_ref[free, at, :] = value.astype(BF16)
                kept_ref[here, at, :] += got_ref[here_got, at, :].astype(F32)

            strips(work)

    def last(kept_ref, got_ref, q, place):
        def work(at):
            place(at, kept_ref[kept_index(q, levels, False, 0), at, :] + got_ref[0, at, :].astype(F32))

        strips(work)

    def own_step(step):
        own_copy(step).wait_recv()
        if step + 1 < levels:
            later(step, own_kept, own_got[step], own_sent[step + 1], 0)
            own_copy(step + 1).start()
            return

        def place(at, value):
            own_low[at, :] = value[:, : head + tail].astype(BF16)
            beside[at, :] = value[:, head + tail :]

        last(own_kept, own_got[step], 0, place)
        for copy in far_copies:
            copy.start()
        own_start()

    head = own_out.shape[2]
    tail = last_out.shape[2]
    far_copies = [
        remote_copy(
            own_low.at[:, pl.ds(head, tail)], last_out.at[1], far_send.at[0], far_recv.at[0], (far, f)
        ),
        pltpu.make_async_copy(own_low.at[:, pl.ds(head, tail)], last_out.at[0], local.at[0]),
        pltpu.make_async_copy(own_low.at[:, pl.ds(0, head)], own_out.at[c], local.at[1]),
    ]
    own_start, own_steps, own_end = line_gather(
        chips,
        c,
        f,
        own_low.at[:, pl.ds(0, head)],
        lambda chip: own_out.at[2 * chip + core],
        lambda chip: own_out.at[2 * chip + core],
        (og_send, og_recv),
        (oc_send, oc_recv),
    )

    def total_of(j, b, at):
        q = j // parts
        start = b * width + (j % parts) * chunk
        stop = start + chunk
        units, room = pieces[q].shape[1], beside.shape[1] // 2
        found = []
        if start < units:
            found.append(pieces[q][at, start : min(stop, units)].astype(F32))
        if stop > units:
            first = max(start, units) - units + q * room
            found.append(beside[at, first : stop - units + q * room])
        return found[0] if len(found) == 1 else jnp.concatenate(found, axis=1)

    def z_copy(side, i, b):
        return remote_copy(
            z_sent.at[side, b, i],
            z_got.at[side, b, i],
            zs_send.at[side, b, i],
            zs_recv.at[side, b, i],
            (c + 2 * (1 - 2 * side), f),
        )

    def z_last(side, chip):
        return chips - 1 - chip if side == 0 else chip

    def z_step(turn, b):
        for chip in range(chips):

            @pl.when(z == chip)
            def _(chip=chip):
                for side in range(2):
                    j_of = (lambda i: chips - 1 - i) if side == 0 else (lambda i: i)
                    begun = chip if side == 0 else chips - 1 - chip
                    i = turn - begun
                    sends = z_last(side, chip)
                    if begun > 0 and 0 <= i <= sends and i < chips - 1:
                        z_copy(side, i, b).wait_recv()
                    if 0 <= i < sends:
                        if i > 0:
                            z_copy(side, i - 1, b).wait_send()

                        def work(at, side=side, i=i, j=j_of(i), begun=begun):
                            value = total_of(j, b, at)
                            if begun > 0:
                                value += z_got[side, b, i, at, :].astype(F32)
                            z_sent[side, b, i, at, :] = value.astype(BF16)

                        strips(work)
                        z_copy(side, i, b).start()

    def chunk_of(ref, chip, b):
        start = pl.multiple_of(b * width + lax.rem(chip, parts) * chunk, 128)
        return ref.at[chip // parts, :, pl.ds(start, chunk)]

    gathers = []
    for b in range(batches):
        gathers.append(
            line_gather(
                chips,
                c,
                f,
                chunk_of(mine_out, z, b),
                lambda chip, b=b: chunk_of(mine_out, chip, b),
                lambda chip, b=b: chunk_of(other_out, chip, b),
                (zg_send.at[:, b], zg_recv.at[:, b]),
                (zc_send.at[:, b], zc_recv.at[:, b]),
            )
        )

    def finish(b):
        for j in range(chips):

            @pl.when(z == j)
            def _(j=j):
                def work(at):
                    value = total_of(j, b, at)
                    if j > 0:
                        value += z_got[0, b, chips - 1 - j, at, :].astype(F32)
                    if j < chips - 1:
                        value += z_got[1, b, j, at, :].astype(F32)
                    start = b * width + (j % parts) * chunk
                    mine_out[j // parts, at, pl.ds(start, chunk)] = value.astype(BF16)

                strips(work)

        gathers[b][0]()

    own_begin()
    waiting = []

    def one_more():
        if waiting:
            waiting.pop(0)()

    def batch(b):
        for i in range(chips):
            z_step(i, b)
            one_more()
        finish(b)
        waiting.extend(gathers[b][1])

    for b in range(batches - 1):
        batch(b)
    for step in range(levels):
        own_step(step)
        one_more()
    waiting.extend(own_steps)
    batch(batches - 1)
    while waiting:
        one_more()

    far_copies[0].wait()
    far_copies[1].wait()
    far_copies[2].wait()
    own_end()
    for step in range(levels):
        own_copy(step).wait_send()
    for b in range(batches):
        gathers[b][2]()
        for chip in range(chips):

            @pl.when(z == chip)
            def _(chip=chip, b=b):
                for side in range(2):
                    if z_last(side, chip):
                        z_copy(side, z_last(side, chip) - 1, b).wait_send()


def sum_grads(ctx, fsdp, pieces, own, head, tail):
    levels, chips = bits_of(fsdp), ctx // 2
    rows, units = pieces[0].shape
    rest = own.shape[-1] - head - tail
    whole = units + rest // 2
    batches = max(n for n in range(1, 3) if whole % n == 0 and 2 * whole // n % (chips * 128) == 0)
    width = whole // batches
    chunk = 2 * width // chips
    own_width = own.shape[-1]
    vmem = pl.BlockSpec(memory_space=pltpu.VMEM)
    dma = pltpu.SemaphoreType.DMA
    steps = [fsdp >> (i + 1) for i in range(levels)]
    result = jax.ShapeDtypeStruct((2, rows, whole), BF16)
    mine, other, own_all, last = pl.pallas_call(
        functools.partial(sum_kernel, ctx, fsdp, batches),
        in_specs=[vmem] * 3,
        out_specs=[vmem] * 4,
        out_shape=[
            result,
            result,
            jax.ShapeDtypeStruct((ctx, rows, head), BF16),
            jax.ShapeDtypeStruct((2, rows, tail), BF16),
        ],
        scratch_shapes=[
            pltpu.VMEM((fsdp // 2, rows, own_width), F32),
            pltpu.VMEM((rows, head + tail), BF16),
            pltpu.VMEM((rows, rest), F32),
        ]
        + [pltpu.VMEM((n, rows, own_width), BF16) for n in steps * 2]
        + [pltpu.VMEM((2, batches, chips - 1, rows, chunk), BF16)] * 2
        + [dma((levels,))] * 2
        + [dma((2, batches, chips - 1))] * 4
        + [dma((2, batches, chips))] * 2
        + [dma((2, chips - 1))] * 2
        + [dma((2, chips))] * 2
        + [dma((1,))] * 2
        + [dma((6,))],
        compiler_params=pltpu.CompilerParams(
            collective_id=1, has_side_effects=True, vmem_limit_bytes=60 * 2**20
        ),
        cost_estimate=pl.CostEstimate(flops=1000, bytes_accessed=1000, transcendentals=0),
    )(*pieces, own)

    return mine, other, own_all, last


def swap_cores(mine, ctx):
    return lax.ppermute(mine, "ctx", flip(ctx, 1))


def norm_parts(rows, axis):
    middle = jnp.mean(rows, axis=axis, keepdims=True)
    centred = rows - middle
    spread = jnp.mean(centred * centred, axis=axis, keepdims=True)
    inverse = lax.rsqrt(spread + NORM_EPS)
    return centred * inverse, inverse


def norm_back(grad, unit, inverse, gain):
    inner = grad * gain
    mean_inner = jnp.mean(inner, axis=1, keepdims=True)
    mean_cross = jnp.mean(inner * unit, axis=1, keepdims=True)
    rows = inverse * (inner - mean_inner - unit * mean_cross)
    return rows, jnp.sum(grad * unit, axis=(0, 2)), jnp.sum(grad, axis=(0, 2))


def adamw(weight, first, second, grad, rate, decay):
    moment = BETA_ONE * first.astype(F32) + (1.0 - BETA_ONE) * grad
    square = BETA_TWO * second + (1.0 - BETA_TWO) * grad * grad
    corrected = moment / (1.0 - BETA_ONE**STEP)
    scaled = square / (1.0 - BETA_TWO**STEP)
    new_weight = weight - rate * (corrected / (jnp.sqrt(scaled) + ADAM_EPS) + decay * weight)
    return (moment, square, new_weight)


def update_kernel(units, regular, *refs):
    (w, first, second, dw, dfirst, dsecond, own, last, mine, other) = refs[:10]
    outs = refs[10:]
    core = lax.rem(lax.axis_index("ctx"), 2)
    width = (w.shape[1] - 2 * units) // 4
    quarter = width // 4
    ctx = own.shape[0]
    dim = HEAD_DIM

    def halves(q, start, size):
        here = mine[q, :, start : start + size].astype(F32)
        there = other[q, :, start : start + size].astype(F32)
        return jnp.where(core == 0, here, there), jnp.where(core == 0, there, here)

    def both(q, start, size):
        return jnp.concatenate(halves(q, start, size), axis=1)

    heads = []
    for part in range(3):
        for i in range(regular):
            for c in range(ctx):
                column = (i * 3 + part) * dim
                heads.append(own[c, :, column : column + dim].astype(F32))
        column = part * dim
        heads.append(
            last[0, :, column : column + dim].astype(F32)
            + last[1, :, column : column + dim].astype(F32)
        )
    out = [halves(q, units, quarter) for q in range(2)]
    heads += [out[0][0], out[1][0], out[0][1], out[1][1]]
    grad = jnp.concatenate(heads, axis=1)

    def put(targets, cols, values):
        for target, value in zip(targets, values):
            target[:, cols] = value

    cols = slice(0, 4 * width)
    put(outs[:3], cols, adamw(w[:, cols], first[:, cols], second[:, cols], grad, 0.03, 0.1))
    cols = slice(4 * width, w.shape[1])
    grad = both(0, 0, units)
    put(outs[:3], cols, adamw(w[:, cols], first[:, cols], second[:, cols], grad, 0.03, 0.1))
    grad = both(1, 0, units)
    put(outs[3:], slice(None), adamw(dw[...], dfirst[...], dsecond[...], grad, 0.02, 0.1))


def update(rows_state, down_state, own, last, mine, other, units, regular):
    rows = rows_state[0].shape[0]
    strip = 16 if rows % 16 == 0 else 8

    def flat(array):
        return pl.BlockSpec((strip, array.shape[1]), lambda i: (i, 0))

    def deep(array):
        return pl.BlockSpec((array.shape[0], strip, array.shape[2]), lambda i: (0, i, 0))

    states, sums = [*rows_state, *down_state], [own, last, mine, other]
    results = [rows_state[0]] * 3 + [down_state[0]] * 3
    return pl.pallas_call(
        functools.partial(update_kernel, units, regular),
        grid=(rows // strip,),
        in_specs=[flat(a) for a in states] + [deep(a) for a in sums],
        out_specs=[flat(a) for a in results],
        out_shape=[jax.ShapeDtypeStruct(a.shape, F32) for a in results],
        compiler_params=pltpu.CompilerParams(vmem_limit_bytes=56 * 2**20),
        cost_estimate=pl.CostEstimate(flops=1000, bytes_accessed=1000, transcendentals=0),
    )(*states, *sums)


def body(
    ctx,
    fsdp,
    tokens,
    cotangent,
    lengths,
    w_rows,
    rows_first,
    rows_second,
    w_down,
    down_first,
    down_second,
    vectors,
    vec_first,
    vec_second,
):
    tok, slots, width = tokens.shape
    dim = HEAD_DIM
    regular = HEADS // ctx
    owned = regular + 1
    share = width // fsdp
    c = lax.axis_index("ctx")
    core = c % 2
    late = (c >= ctx // 2).astype(jnp.int32)
    half = FF // 2

    def my_half(array):
        return lax.dynamic_slice_in_dim(array, core * half, half, 1)

    x_low = tokens.transpose(1, 2, 0)
    vec_part = jnp.pad(vectors.astype(BF16).T, ((0, 0), (0, 128 - vectors.shape[0])))
    act_all, qkv_all, head_w, up_mine, up_other, vec_low = gather_first(
        ctx, fsdp, regular, x_low, w_rows, vec_part
    )
    head_w = head_w.reshape(width, 4 * width)
    up_mine, up_other = up_mine.reshape(width, half), up_other.reshape(width, half)
    vec_low = vec_low.reshape(width, 128)
    down_mine, vec_low = lax.optimization_barrier((my_half(w_down.T).astype(BF16), vec_low))
    down_mine = lax.all_gather(down_mine, "fsdp", axis=0, tiled=True)
    vec = [vec_low[:, i : i + 1].astype(F32) for i in range(12)]
    up_bias = vec_low[:, 8:12].T.astype(F32).reshape(1, FF)

    qkv_all = qkv_all.reshape(slots, 3, owned, dim, ctx * tok)
    far = (c + ctx // 2) % ctx

    def to_rows(array, *gate):
        feat = array.shape[2]
        got = lax.all_to_all(array, "ctx", 0, 0)
        got = after(got, *gate) if gate else got
        return got.transpose(1, 0, 2, 3).reshape(regular * ctx, feat, tok)

    def last_to_rows(array, *gate):
        mine = pick(array, c, 0)
        got = lax.ppermute(pick(array, far, 0), "ctx", flip(ctx, ctx // 2))
        got = after(got, *gate) if gate else got
        return jnp.where(late == 0, mine, got), jnp.where(late == 0, got, mine)

    def to_send(array):
        return array.reshape(regular, ctx, dim, tok).transpose(1, 0, 2, 3)

    def attend_slot(s, *gate):
        lens = after(jnp.repeat(lengths[s : s + 1], regular), *gate)
        return (lens, qkv_all, s, *attend(lens, qkv_all, s, tok))

    results = [attend_slot(0)]
    results.append(attend_slot(1, results[0][3]))
    rows = [to_rows(results[0][4])]
    last_qkv = jnp.where(late == 0, qkv_all[:1, :, regular:], qkv_all[1:, :, regular:])
    last_len = after(lax.dynamic_slice_in_dim(lengths, late, 1, 0), results[1][3], rows[0])
    results.append((last_len, last_qkv, 0, *attend(last_len, last_qkv, 0, tok)))
    rows.append(to_rows(results[1][4]))
    down_mine = after(down_mine, results[2][3], *rows)
    down_other = swap_cores(down_mine, ctx)
    last_rows = last_to_rows(results[2][4])
    att = [jnp.concatenate([rows[s], last_rows[s]]).reshape(width, tok) for s in range(slots)]
    att = jnp.stack(att)

    x = x_low.astype(F32)
    out_w = head_w[:, 3 * width :]
    mid = x + jnp.einsum("de,sdt->set", out_w, att, preferred_element_type=F32) + vec[4]
    unit_two, inverse_two = norm_parts(mid, 1)
    act_two = (unit_two * vec[5] + vec[6]).astype(BF16)

    pos = c * tok + jnp.arange(tok, dtype=jnp.int32)
    valid = pos[None, None, :] < lengths[:, None, None]
    g_low = jnp.where(valid, cotangent.transpose(1, 2, 0), jnp.zeros((), BF16))
    g = g_low.astype(F32)

    bias_mine = lax.dynamic_slice_in_dim(up_bias, core * half, half, 1)
    bias_other = lax.dynamic_slice_in_dim(up_bias, (1 - core) * half, half, 1)
    y_other, ga_other, dup_other, ddown_other, db_other = mlp(
        act_two, g_low, up_other, down_other, bias_other
    )
    y_mine, ga_mine, dup_mine, ddown_mine, db_mine = mlp(
        act_two, g_low, up_mine, down_mine, bias_mine
    )
    output = (mid + (y_mine + y_other + vec[7])).astype(BF16).transpose(2, 0, 1)

    up_swapped, down_swapped = swap_cores(dup_other, ctx), swap_cores(ddown_other, ctx)
    up_total = add_low(dup_mine, up_swapped)
    up_part = scatter_fsdp(up_total)
    ga_mine = after(ga_mine, up_total)

    grad_mid, gain_two, shift_two = norm_back(ga_mine + ga_other, unit_two, inverse_two, vec[5])
    grad_mid = g + grad_mid
    grad_attn = grad_mid.astype(BF16)
    grad_att = jnp.einsum("de,set->sdt", out_w, grad_attn, preferred_element_type=F32).astype(BF16)
    down_part = scatter_fsdp(add_low(after(ddown_mine, grad_att), down_swapped))
    grad_attn_later = after(grad_attn, grad_att)
    grad_att = grad_att.reshape(slots, HEADS, dim, tok)
    last = jnp.repeat(grad_att[:, -1], ctx // slots, axis=0)[:, None]
    first_pairs = lax.all_to_all(to_send(grad_att[0, :-1]), "ctx", 0, 0)
    other_pairs = lax.all_to_all(
        after(jnp.concatenate([to_send(grad_att[1, :-1]), last], axis=1), first_pairs), "ctx", 0, 0
    )

    quarter = width // 4
    spread = jnp.pad(
        grad_attn_later.reshape(slots, 4, quarter, tok),
        ((0, 0), (0, 0), (0, -quarter % 128), (0, 0)),
    )
    out_grad = jnp.einsum("sdt,sket->kde", att, spread, preferred_element_type=F32).astype(BF16)
    out_grad = out_grad.reshape(2, 2, fsdp, share, spread.shape[2])

    def out_half(which):
        return pick(out_grad, which, 0).reshape(2, width, spread.shape[2])

    out_mine, out_swapped = out_half(core), swap_cores(out_half(1 - core), ctx)
    out_total = add_low(out_mine, out_swapped)
    first_heads = attend_back(*results[0][:4], results[0][5], first_pairs)
    last_heads = attend_back(
        *results[2][:4], results[2][5], after(other_pairs[:, -1:], first_heads)
    )
    other_heads = attend_back(
        *results[1][:4], results[1][5], after(other_pairs[:, :-1], last_heads, up_part)
    )
    grad_heads = [first_heads, other_heads, last_heads]

    feat = 3 * dim
    own_sum = own_grad(
        late,
        act_all,
        grad_heads[0].reshape(ctx, regular * feat, tok),
        grad_heads[1].reshape(ctx, regular * feat, tok),
        grad_heads[2].reshape(ctx, feat, tok),
    )
    own_sum = own_sum.astype(BF16)
    own_sum = jnp.concatenate(
        [
            jnp.pad(part, ((0, 0), (0, -part.shape[1] % 128)))
            for part in (own_sum[:, : regular * feat], own_sum[:, regular * feat :])
        ]
        + [out_total[0], out_total[1]],
        axis=1,
    )
    head_columns = regular * feat + -regular * feat % 128
    blocks = (fsdp, share)
    sum_mine, sum_other, own_all, last = sum_grads(
        ctx,
        fsdp,
        [up_part, down_part],
        own_sum.reshape(*blocks, own_sum.shape[1]),
        head_columns,
        feat + -feat % 128,
    )
    first_rows, other_rows = to_rows(first_heads), to_rows(other_heads, sum_mine)
    last_rows = last_to_rows(last_heads, sum_mine)
    grad_qkv = []
    for s, rows in enumerate((first_rows, other_rows)):
        rows = jnp.concatenate([rows, last_rows[s]])
        rows = rows.reshape(HEADS, 3, dim, tok).transpose(1, 0, 2, 3)
        grad_qkv.append(rows.reshape(3 * width, tok))
    grad_qkv = jnp.stack(grad_qkv)
    grad_one = jnp.einsum(
        "de,set->sdt", head_w[:, : 3 * width], grad_qkv, preferred_element_type=F32
    )

    unit_one, inverse_one = norm_parts(x, 1)
    grad_in, gain_one, shift_one = norm_back(grad_one, unit_one, inverse_one, vec[0])
    grad_tokens = (grad_mid + grad_in).astype(BF16)

    bias_qkv = jnp.sum(grad_qkv.astype(F32), axis=(0, 2))
    vec_grad = jnp.stack(
        [
            gain_one,
            shift_one,
            bias_qkv[:width],
            bias_qkv[2 * width :],
            jnp.sum(grad_attn.astype(F32), axis=(0, 2)),
            gain_two,
            shift_two,
            jnp.sum(g, axis=(0, 2)),
        ]
    )
    bias_up = ordered(core, db_mine, db_other, 1).reshape(4, width)
    vec_grad = jnp.concatenate([vec_grad, bias_up], axis=0).reshape(12, fsdp, share)
    f = lax.axis_index("fsdp")
    vec_sum = pick(vec_grad, f, 1)
    for value in range(1, fsdp):
        vec_sum = vec_sum + lax.ppermute(pick(vec_grad, f ^ value, 1), "fsdp", flip(fsdp, value))
    for level in range(bits_of(ctx)):
        vec_sum = vec_sum + lax.ppermute(vec_sum, "ctx", flip(ctx, 2**level))

    rows_state = (w_rows, rows_first, rows_second)
    down_state = (w_down.T, down_first.T, down_second.T)
    updated = update(
        rows_state, down_state, own_all, last, sum_mine, sum_other, half, regular
    )
    rows_out, down_out = updated[:3], tuple(part.T for part in updated[3:])
    vec_out = adamw(vectors, vec_first, vec_second, vec_sum, 0.3, 0.0)
    return (output, grad_tokens.transpose(2, 0, 1), *rows_out, *down_out, *vec_out)


def solution(mesh):
    placed = (
        P("ctx", "fsdp", None),
        P("ctx", "fsdp", None),
        P("fsdp"),
        P("fsdp", None),
        P("fsdp", None),
        P("fsdp", None),
        P(None, "fsdp"),
        P(None, "fsdp"),
        P(None, "fsdp"),
        P(None, "fsdp"),
        P(None, "fsdp"),
        P(None, "fsdp"),
    )
    return jax.shard_map(
        functools.partial(body, mesh.shape["ctx"], mesh.shape["fsdp"]),
        mesh=mesh,
        in_specs=placed,
        out_specs=placed[:2] + placed[3:6] + placed[6:9] + placed[9:12],
        check_vma=False,
    )
```

```python
import functools
import math

import jax
import jax.numpy as jnp
from jax import lax
from jax.experimental import pallas as pl
from jax.experimental.pallas import tpu as pltpu
from jax.sharding import PartitionSpec as P

HEADS = 17
HEAD_DIM = 64
FF = 4352
STEP = 10

MASKED = -1e30
NORM_EPS = 1e-05
BETA_ONE = 0.9
BETA_TWO = 0.95
ADAM_EPS = 1e-08
BF16 = jnp.bfloat16
F32 = jnp.float32


def dot(left, right, dims=((1,), (0,))):
    return lax.dot_general(left, right, (dims, ((), ())), preferred_element_type=F32)


def padded(top, rows, width):
    row = lax.broadcasted_iota(jnp.int32, (rows, width), 0)
    out = jnp.zeros((rows, width), F32)
    for index, value in enumerate(top):
        out = jnp.where(row == index, value, out)
    return out.astype(BF16)


def key_rows(lens_ref, key, length):
    pos = lax.broadcasted_iota(jnp.int32, (1, length), 1)
    bias = jnp.where(pos < lens_ref[0], 0.0, MASKED)
    one = jnp.ones((1, length), F32)
    extra = padded([bias, one, one, one], HEAD_DIM, length)
    return jnp.concatenate([key, extra], axis=0).T


def causal(block):
    key = lax.broadcasted_iota(jnp.int32, (block, block), 0)
    query = lax.broadcasted_iota(jnp.int32, (block, block), 1)
    return key <= query


def attend_kernel(block, lens_ref, q_ref, k_ref, v_ref, o_ref, low_ref, lse_ref, keys):
    heads, _, length = k_ref.shape[2:]
    tok = low_ref.shape[-1]
    step = pl.program_id(0)

    @pl.when(step == 0)
    def _():
        for h in range(heads):
            keys[h] = key_rows(lens_ref, k_ref[0, 0, h], length)

    one_row = padded([jnp.ones((1, block), F32)], HEAD_DIM, block)
    queries = []
    for h in range(heads):
        query = (q_ref[0, 0, h].astype(F32) * (1.0 / math.sqrt(HEAD_DIM))).astype(BF16)
        queries.append(jnp.concatenate([query, one_row], axis=0))

    def one(index, states, mask):
        start = pl.multiple_of(index * block, block)
        all_scores = [dot(keys[h, pl.ds(start, block), :], queries[h]) for h in range(heads)]
        results = []
        for h, (top, total, accum) in enumerate(states):
            scores = all_scores[h]
            if mask is not None:
                scores = jnp.where(mask, scores, MASKED)
            new_top = jnp.maximum(top, jnp.max(scores, axis=0, keepdims=True))
            weights = jnp.exp(scores - new_top)
            factor = jnp.exp(top - new_top)
            total = total * factor + jnp.sum(weights, axis=0, keepdims=True)
            value = v_ref[0, 0, h, :, pl.ds(start, block)]
            accum = accum * factor + dot(value, weights.astype(BF16))
            results.append((new_top, total, accum))
        return tuple(results)

    state = (
        jnp.full((1, block), MASKED, F32),
        jnp.zeros((1, block), F32),
        jnp.zeros((HEAD_DIM, block), F32),
    )
    states = lax.fori_loop(0, step, lambda i, s: one(i, s, None), (state,) * heads)
    states = one(step, states, causal(block))
    for h, (top, total, accum) in enumerate(states):
        result = accum / total
        o_ref[h] = result
        for i in range(block // tok):
            low_ref[i, h] = result[:, i * tok : (i + 1) * tok].astype(BF16)
        lse_ref[h] = top + jnp.log(total)


def head_specs(slot, heads, dim, length, block):
    def whole(part):
        return pl.BlockSpec((1, 1, heads, dim, length), lambda i, lens: (slot, part, 0, 0, 0))

    def piece(part):
        return pl.BlockSpec((1, 1, heads, dim, block), lambda i, lens: (slot, part, 0, 0, i))

    return whole, piece


def attend(lens, qkv, slot, tok):
    dim, length = qkv.shape[3:]
    pairs = lens.shape[0]
    block = math.gcd(length, 512)
    whole, piece = head_specs(slot, pairs, dim, length, block)
    return pl.pallas_call(
        functools.partial(attend_kernel, block),
        grid_spec=pltpu.PrefetchScalarGridSpec(
            num_scalar_prefetch=1,
            grid=(length // block,),
            in_specs=[piece(0), whole(1), whole(2)],
            out_specs=[
                pl.BlockSpec((pairs, dim, block), lambda i, lens: (0, 0, i)),
                pl.BlockSpec((block // tok, pairs, dim, tok), lambda i, lens: (i, 0, 0, 0)),
                pl.BlockSpec((pairs, 1, block), lambda i, lens: (0, 0, i)),
            ],
            scratch_shapes=[pltpu.VMEM((pairs, length, 2 * dim), BF16)],
        ),
        out_shape=[
            jax.ShapeDtypeStruct((pairs, dim, length), F32),
            jax.ShapeDtypeStruct((length // tok, pairs, dim, tok), BF16),
            jax.ShapeDtypeStruct((pairs, 1, length), F32),
        ],
        compiler_params=pltpu.CompilerParams(
            vmem_limit_bytes=48 * 2**20
        ),
        cost_estimate=pl.CostEstimate(flops=1000, bytes_accessed=1000, transcendentals=0),
    )(lens, qkv, qkv, qkv)


def split_three(value):
    first = value.astype(BF16).astype(F32)
    second = (value - first).astype(BF16).astype(F32)
    third = (value - first - second).astype(BF16).astype(F32)
    return [-first, -second, -third]


def attend_back_kernel(
    block,
    lens_ref,
    q_ref,
    k_ref,
    v_ref,
    o_ref,
    lse_ref,
    grad_ref,
    out_ref,
    keys,
    values,
    queries,
    grads,
    total,
):
    heads, dim, length = k_ref.shape[2:]
    tok = grad_ref.shape[-1]
    count = length // block
    step = pl.program_id(0)
    scale = 1.0 / math.sqrt(HEAD_DIM)

    @pl.when(step == 0)
    def _():
        one = jnp.ones((1, length), F32)
        for h in range(heads):
            keys[h] = key_rows(lens_ref, k_ref[0, 0, h], length)
            extra = padded([one, one, one], dim, length)
            values[h] = jnp.concatenate([v_ref[0, 0, h], extra], axis=0).T
            queries[h, 0:dim, :] = (q_ref[0, 0, h].astype(F32) * scale).astype(BF16)
            queries[h, dim:, :] = padded([one] + split_three(lse_ref[h]), dim, length)
            for i in range(length // tok):
                grads[h, 0:dim, i * tok : (i + 1) * tok] = grad_ref[i, h]
            delta = jnp.sum(grads[h, 0:dim, :].astype(F32) * o_ref[h], axis=0, keepdims=True)
            grads[h, dim:, :] = padded(split_three(delta), dim, length)
        total[...] = jnp.zeros_like(total)

    mine = pl.ds(pl.multiple_of(step * block, block), block)

    def one(index, states, mask):
        cols = pl.ds(pl.multiple_of(index * block, block), block)
        all_scores = [dot(keys[h, mine, :], queries[h, :, cols]) for h in range(heads)]
        results = []
        for h, (dk, dv) in enumerate(states):
            scores = all_scores[h]
            if mask is not None:
                scores = jnp.where(mask, scores, MASKED)
            probs = jnp.exp(scores)
            grad_scores = (probs * dot(values[h, mine, :], grads[h, :, cols])).astype(BF16)
            probs = probs.astype(BF16)
            dv = dv + dot(grads[h, 0:dim, cols], probs, ((1,), (1,)))
            dk = dk + dot(queries[h, 0:dim, cols], grad_scores, ((1,), (1,)))
            total[h, :, cols] += dot(k_ref[0, 0, h, :, mine], grad_scores)
            results.append((dk, dv))
        return tuple(results)

    zero = jnp.zeros((dim, block), F32)
    states = one(step, ((zero, zero),) * heads, causal(block))
    states = lax.fori_loop(step + 1, count, lambda i, s: one(i, s, None), states)
    for h, (dk, dv) in enumerate(states):
        dq = total[h, :, mine] * scale
        for i in range(block // tok):
            cols = slice(i * tok, (i + 1) * tok)
            out_ref[i, h, 0:dim] = dq[:, cols].astype(BF16)
            out_ref[i, h, dim : 2 * dim] = dk[:, cols].astype(BF16)
            out_ref[i, h, 2 * dim :] = dv[:, cols].astype(BF16)


def attend_back(lens, qkv, slot, out, lse, grad):
    dim, length = qkv.shape[3:]
    pairs, tok = lens.shape[0], grad.shape[-1]
    ctx = length // tok
    block = math.gcd(length, 512)
    whole, _ = head_specs(slot, pairs, dim, length, block)
    return pl.pallas_call(
        functools.partial(attend_back_kernel, block),
        grid_spec=pltpu.PrefetchScalarGridSpec(
            num_scalar_prefetch=1,
            grid=(length // block,),
            in_specs=[
                whole(0),
                whole(1),
                whole(2),
                pl.BlockSpec((pairs, dim, length), lambda i, lens: (0, 0, 0)),
                pl.BlockSpec((pairs, 1, length), lambda i, lens: (0, 0, 0)),
                pl.BlockSpec((ctx, pairs, dim, tok), lambda i, lens: (0, 0, 0, 0)),
            ],
            out_specs=pl.BlockSpec(
                (block // tok, pairs, 3 * dim, tok), lambda i, lens: (i, 0, 0, 0)
            ),
            scratch_shapes=[
                pltpu.VMEM((pairs, length, 2 * dim), BF16),
                pltpu.VMEM((pairs, length, 2 * dim), BF16),
                pltpu.VMEM((pairs, 2 * dim, length), BF16),
                pltpu.VMEM((pairs, 2 * dim, length), BF16),
                pltpu.VMEM((pairs, dim, length), F32),
            ],
        ),
        out_shape=jax.ShapeDtypeStruct((ctx, pairs, 3 * dim, tok), BF16),
        compiler_params=pltpu.CompilerParams(
            vmem_limit_bytes=48 * 2**20
        ),
        cost_estimate=pl.CostEstimate(flops=1000, bytes_accessed=1000, transcendentals=0),
    )(lens, qkv, qkv, qkv, out, lse, grad)


def own_grad_kernel(late_ref, first_ref, second_ref, first_grad_ref, second_grad_ref, last_grad_ref, out_ref, total):
    step = pl.program_id(0)
    nt = ((1,), (1,))
    first, second = first_ref[0, 0], second_ref[0, 0]
    head = dot(first, first_grad_ref[0], nt) + dot(second, second_grad_ref[0], nt)
    last = dot(jnp.where(late_ref[0] == 0, first, second), last_grad_ref[0], nt)
    part = jnp.concatenate([head, last], axis=1)

    @pl.when(step == 0)
    def _():
        total[...] = part

    @pl.when(step > 0)
    def _():
        total[...] += part

    @pl.when(step == pl.num_programs(0) - 1)
    def _():
        out_ref[...] = total[...]


def own_grad(late, act, first_grad, second_grad, last_grad):
    _, ctx, width, tok = act.shape
    feat, last = first_grad.shape[1], last_grad.shape[1]

    def block(rows):
        return pl.BlockSpec((1, rows, tok), lambda i, late: (i, 0, 0))

    def of(slot):
        return pl.BlockSpec((1, 1, width, tok), lambda i, late: (slot, i, 0, 0))

    return pl.pallas_call(
        own_grad_kernel,
        grid_spec=pltpu.PrefetchScalarGridSpec(
            num_scalar_prefetch=1,
            grid=(ctx,),
            in_specs=[of(0), of(1), block(feat), block(feat), block(last)],
            out_specs=pl.BlockSpec((width, feat + last), lambda i, late: (0, 0)),
            scratch_shapes=[pltpu.VMEM((width, feat + last), F32)],
        ),
        out_shape=jax.ShapeDtypeStruct((width, feat + last), F32),
        compiler_params=pltpu.CompilerParams(vmem_limit_bytes=48 * 2**20),
        cost_estimate=pl.CostEstimate(flops=1000, bytes_accessed=1000, transcendentals=0),
    )(late[None], act, act, first_grad, second_grad, last_grad)


def mlp_kernel(
    width,
    a_ref,
    g_ref,
    up_ref,
    down_ref,
    bias_ref,
    y_ref,
    ga_ref,
    dup_ref,
    ddown_ref,
    db_ref,
    a_rows,
    g_rows,
):
    step = pl.program_id(0)
    slots, _, tok = a_ref.shape
    block = up_ref.shape[1]

    @pl.when(step == 0)
    def _():
        for s in range(slots):
            a_rows[s * tok : (s + 1) * tok, :] = a_ref[s].T
            g_rows[s * tok : (s + 1) * tok, :] = g_ref[s].T
        y_ref[...] = jnp.zeros_like(y_ref)
        ga_ref[...] = jnp.zeros_like(ga_ref)

    def run(size):
        up = up_ref[:, :size]
        down = down_ref[:, :size]
        pre = dot(a_rows[...], up) + bias_ref[:, :size]
        cdf = 0.5 * (1.0 + lax.erf(pre * math.sqrt(0.5)))
        hidden = (pre * cdf).astype(BF16)
        slope = cdf + pre * jnp.exp(-0.5 * pre * pre) * (1.0 / math.sqrt(2.0 * math.pi))
        grad = (dot(g_rows[...], down) * slope).astype(BF16)
        db_ref[:, :size] = jnp.sum(grad.astype(F32), axis=0, keepdims=True)
        nt = ((1,), (1,))
        for s in range(slots):
            rows = slice(s * tok, (s + 1) * tok)
            y_ref[s] += dot(down, hidden[rows], nt)
            ga_ref[s] += dot(up, grad[rows], nt)
        dup = sum(dot(a_ref[s], grad[s * tok : (s + 1) * tok]) for s in range(slots))
        dup_ref[:, :size] = dup.astype(dup_ref.dtype)
        ddown = sum(dot(g_ref[s], hidden[s * tok : (s + 1) * tok]) for s in range(slots))
        ddown_ref[:, :size] = ddown.astype(ddown_ref.dtype)

    full = width // block

    @pl.when(step < full)
    def _():
        run(block)

    if width % block:

        @pl.when(step == full)
        def _():
            run(width % block)


def mlp(act, grad, up, down, bias):
    slots, width, tok = act.shape
    units = up.shape[1]
    block = 256

    def fixed(shape):
        return pl.BlockSpec(shape, lambda i: (0,) * len(shape))

    cols = pl.BlockSpec((width, block), lambda i: (0, i))
    line = pl.BlockSpec((1, block), lambda i: (0, i))
    total = jax.ShapeDtypeStruct((slots, width, tok), F32)
    grads = jax.ShapeDtypeStruct((width, units), BF16)
    return pl.pallas_call(
        functools.partial(mlp_kernel, units),
        grid=(pl.cdiv(units, block),),
        in_specs=[fixed(act.shape), fixed(act.shape), cols, cols, line],
        out_specs=[fixed(act.shape), fixed(act.shape), cols, cols, line],
        out_shape=[total, total, grads, grads, jax.ShapeDtypeStruct((1, units), F32)],
        scratch_shapes=[pltpu.VMEM((slots * tok, width), BF16)] * 2,
        compiler_params=pltpu.CompilerParams(vmem_limit_bytes=56 * 2**20),
        cost_estimate=pl.CostEstimate(flops=1000, bytes_accessed=1000, transcendentals=0),
    )(act, grad, up, down, bias)


def other_index(index, bit):
    return index + bit * (1 - 2 * lax.rem(index // bit, 2))


def split_columns(start, size, count):
    tiles = size // 128
    cuts = [start + 128 * (-(-tiles * i // count)) for i in range(count)] + [start + size]
    return [(cuts[i], cuts[i + 1] - cuts[i]) for i in range(count)]


def gather_kernel(
    ctx,
    fsdp,
    regular,
    x_ref,
    w_ref,
    v_ref,
    act_ref,
    qkv_ref,
    wo_ref,
    um_ref,
    uo_ref,
    vo_ref,
    xo_ref,
    wide,
    w_low,
    windows,
    own_w,
    own_t,
    v_all,
    v_rows,
    bias,
    acts,
    qkvs,
    x_send,
    x_recv,
    xc_send,
    xc_recv,
    w_send,
    w_recv,
    wc_send,
    wc_recv,
    v_send,
    v_recv,
    act_sem,
    local,
):
    c, f = lax.axis_index("ctx"), lax.axis_index("fsdp")
    chips = ctx // 2
    z, core = c // 2, lax.rem(c, 2)
    partner = 2 * z + 1 - core
    slots, width, tok = x_ref.shape
    rows = w_ref.shape[0]
    dim = HEAD_DIM
    owned = regular + 1
    levels = bits_of(fsdp)
    half = um_ref.shape[2]

    def combine(number):
        place = f
        for bit in range(levels):
            if number & (1 << bit):
                place = other_index(place, 1 << bit)
        return place

    barrier = pltpu.get_barrier_semaphore()

    def greet(where):
        pl.semaphore_signal(barrier, inc=1, device_id=where, device_id_type=pl.DeviceIdType.MESH)

    greet((partner, f))
    for number in range(1, fsdp):
        greet((c, combine(number)))

    @pl.when(z > 0)
    def _():
        greet((c - 2, f))

    @pl.when(z < chips - 1)
    def _():
        greet((c + 2, f))

    beside = (z > 0).astype(jnp.int32) + (z < chips - 1).astype(jnp.int32)
    pl.semaphore_wait(barrier, fsdp + beside)

    def remote(source, target, send, recv, where):
        return pltpu.make_async_remote_copy(
            src_ref=source,
            dst_ref=target,
            send_sem=send,
            recv_sem=recv,
            device_id=where,
            device_id_type=pl.DeviceIdType.MESH,
        )

    def x_copy(side, s, h):
        sign = 1 - 2 * side
        block = c - 2 * sign * s
        source = x_ref.at[h] if s == 0 else xo_ref.at[block, h]
        return remote(
            source, xo_ref.at[block, h], x_send.at[side, s, h], x_recv.at[side, s, h], (c + 2 * sign, f)
        )

    def x_sends(side, s):
        return (z - s >= 0) & (z < chips - 1) if side == 0 else (z + s < chips) & (z > 0)

    def x_gets(side, s):
        return z - 1 - s >= 0 if side == 0 else z + 1 + s < chips

    def x_arrival(side, s, h):
        sign = 1 - 2 * side
        block = c - 2 * sign * (s + 1)
        return remote(
            xo_ref.at[block, h],
            xo_ref.at[block, h],
            x_send.at[side, s, h],
            x_recv.at[side, s, h],
            (c + 2 * sign, f),
        )

    def x_share(side, s, h):
        sign = 1 - 2 * side
        block = c - 2 * sign * (s + 1)
        return remote(
            xo_ref.at[block, h],
            xo_ref.at[block, h],
            xc_send.at[side, s, h],
            xc_recv.at[side, s, h],
            (partner, f),
        )

    def x_share_arrival(side, s, h):
        sign = 1 - 2 * side
        block = partner - 2 * sign * (s + 1)
        return remote(
            xo_ref.at[block, h],
            xo_ref.at[block, h],
            xc_send.at[side, s, h],
            xc_recv.at[side, s, h],
            (partner, f),
        )

    def x_own(h):
        return remote(
            x_ref.at[h],
            xo_ref.at[c, h],
            xc_send.at[0, chips - 1, h],
            xc_recv.at[0, chips - 1, h],
            (partner, f),
        )

    def x_own_arrival(h):
        return remote(
            x_ref.at[h],
            xo_ref.at[partner, h],
            xc_send.at[0, chips - 1, h],
            xc_recv.at[0, chips - 1, h],
            (partner, f),
        )

    runs = split_columns(0, half, levels)

    def source(unit, stream):
        start, size = runs[stream]
        return w_low.at[:, pl.ds(pl.multiple_of((2 * unit + core) * half + start, 128), size)]

    def kept(unit, stream, place, which):
        start, size = runs[stream]
        if unit == 0:
            return wo_ref.at[place, :, pl.ds(pl.multiple_of(which * half + start, 128), size)]
        return um_ref.at[place, :, pl.ds(start, size)]

    def shared(unit, stream, place, which):
        start, size = runs[stream]
        if unit == 0:
            return kept(unit, stream, place, which)
        return uo_ref.at[place, :, pl.ds(start, size)]

    def w_copy(unit, stream, step, number):
        bit = 1 << ((stream + step) % levels)
        place = combine(number)
        there = kept(unit, stream, place, core)
        return remote(
            source(unit, stream) if number == 0 else there,
            there,
            w_send.at[unit, stream, number | bit],
            w_recv.at[unit, stream, number | bit],
            (c, other_index(f, bit)),
        )

    def w_arrival(unit, stream, number):
        block = kept(unit, stream, combine(number), core)
        sems = w_send.at[unit, stream, number], w_recv.at[unit, stream, number]
        return remote(block, block, *sems, (partner, f))

    def w_share(unit, stream, number):
        place = combine(number)
        sems = wc_send.at[unit, stream, number], wc_recv.at[unit, stream, number]
        block = kept(unit, stream, place, core)
        return remote(block, shared(unit, stream, place, core), *sems, (partner, f))

    def w_share_arrival(unit, stream, number):
        block = shared(unit, stream, combine(number), 1 - core)
        sems = wc_send.at[unit, stream, number], wc_recv.at[unit, stream, number]
        return remote(block, block, *sems, (partner, f))

    def held(stream, step):
        numbers = [0]
        for i in range(step):
            bit = 1 << ((stream + i) % levels)
            numbers += [n | bit for n in numbers]
        return numbers

    def v_copy(number):
        return remote(
            v_ref, v_all.at[f], v_send.at[number], v_recv.at[number], (c, combine(number))
        )

    def v_arrival(number):
        return remote(
            v_ref,
            v_all.at[combine(number)],
            v_send.at[number],
            v_recv.at[number],
            (c, combine(number)),
        )

    def x_begin(h):
        for side in range(2):

            @pl.when(x_sends(side, 0))
            def _(side=side):
                x_copy(side, 0, h).start()

        x_own(h).start()

    def x_step(h, s):
        for side in range(2):

            @pl.when(x_gets(side, s))
            def _(side=side):
                x_arrival(side, s, h).wait_recv()
                x_share(side, s, h).start()

            if s + 1 < chips - 1:

                @pl.when(x_sends(side, s + 1))
                def _(side=side):
                    x_copy(side, s + 1, h).start()

    def w_step(unit, step):
        for stream in range(levels):
            bit = 1 << ((stream + step) % levels)
            arrived = [number | bit for number in held(stream, step)]
            for number in arrived:
                w_arrival(unit, stream, number).wait_recv()
            if step + 1 < levels:
                for number in held(stream, step + 1):
                    w_copy(unit, stream, step + 1, number).start()
            for number in arrived:
                w_share(unit, stream, number).start()

    def fetch(unit):
        cols = pl.ds(2 * unit * half, 2 * half)
        return pltpu.make_async_copy(w_ref.at[:, cols], wide.at[:, cols], local.at[3 + unit])

    def w_begin(unit):
        fetch(unit).wait()
        cols = slice(2 * unit * half, 2 * (unit + 1) * half)

        strip = 16 if rows % 16 == 0 else rows

        def body(i, carry):
            at = pl.ds(pl.multiple_of(i * strip, strip), strip)
            w_low[at, cols] = wide[at, cols].astype(BF16)
            return carry

        lax.fori_loop(0, rows // strip, body, 0)
        for stream in range(levels):
            w_copy(unit, stream, 0, 0).start()

    own_up = w_low.at[:, pl.ds(pl.multiple_of((2 + core) * half, 128), half)]
    other_up = w_low.at[:, pl.ds(pl.multiple_of((3 - core) * half, 128), half)]
    kept_here = [
        pltpu.make_async_copy(w_low.at[:, pl.ds(0, 2 * half)], wo_ref.at[f], local.at[0]),
        pltpu.make_async_copy(own_up, um_ref.at[f], local.at[1]),
        pltpu.make_async_copy(other_up, uo_ref.at[f], local.at[2]),
    ]
    v_own = pltpu.make_async_copy(v_ref, v_all.at[f], local.at[5])
    v_out = pltpu.make_async_copy(v_all, vo_ref, local.at[6])
    x_here = pltpu.make_async_copy(x_ref, xo_ref.at[c], local.at[7])

    head_of = [i * ctx + c for i in range(regular)] + [HEADS - 1]
    places = [part * HEADS + head for part in range(3) for head in head_of]

    def window(i):
        start = pl.multiple_of(places[i] // 2 * 128, 128)
        return pltpu.make_async_copy(
            wo_ref.at[:, :, pl.ds(start, 128)], windows.at[i], local.at[8 + i]
        )

    def ready():
        kept_here[0].wait()
        for number in range(1, fsdp):
            v_arrival(number).wait_recv()
            for stream in range(levels):
                w_share_arrival(0, stream, number).wait_recv()
        v_own.wait()
        v_out.start()
        for i in range(len(places)):
            window(i).start()
        for i in range(fsdp):
            v_rows[i * rows : (i + 1) * rows, :] = v_all[i].astype(F32)
        own_w[...] = jnp.zeros_like(own_w)
        for i, place in enumerate(places):
            window(i).wait()
            odd = lax.rem(place, 2)
            for k in range(fsdp):
                both = windows[i, k]
                mine = jnp.where(odd == 0, both[:, :dim], both[:, dim:])
                own_w[k * rows : (k + 1) * rows, i * dim : (i + 1) * dim] = mine
        own_t[...] = own_w[...].T
        for part, column in ((0, 2), (2, 3)):
            for i, head in enumerate(head_of):
                start = (part * owned + i) * dim
                at = pl.ds(pl.multiple_of(head * dim, dim), dim)
                bias[start : start + dim, :] = v_rows[at, column : column + 1]
        start = owned * dim
        bias[start : 2 * start, :] = jnp.zeros((start, 1), F32)

    def project(h, b):
        unit, _ = norm_parts(xo_ref[b, h].astype(F32), 0)
        act = (unit * v_rows[:, 0:1] + v_rows[:, 1:2]).astype(BF16)
        acts[h, b] = act
        pltpu.make_async_copy(acts.at[h, b], act_ref.at[h, b], act_sem.at[h, b]).start()
        value = dot(own_t[...], act)[: 3 * owned * dim] + bias[...]
        qkvs[h, :, pl.ds(pl.multiple_of(b * tok, tok), tok)] = value.astype(BF16)

    def project_own(h):
        x_own_arrival(h).wait_recv()

        def body(i, carry):
            project(h, 2 * z + i)
            return carry

        lax.fori_loop(0, 2, body, 0)

    def project_step(h, s):
        for side in range(2):

            @pl.when(x_gets(side, s))
            def _(side=side):
                x_share_arrival(side, s, h).wait_recv()

        def body(i, carry):
            side = i // 2
            chip = z - (1 - 2 * side) * (s + 1)

            @pl.when((chip >= 0) & (chip < chips))
            def _():
                project(h, 2 * chip + lax.rem(i, 2))

            return carry

        lax.fori_loop(0, 4, body, 0)

    def out_copy(h):
        return pltpu.make_async_copy(qkvs.at[h], qkv_ref.at[h], local.at[8 + len(places) + h])

    plan = []
    block_time = 0.95

    def at(time, work, *values):
        plan.append((time, functools.partial(work, *values)))

    for h in range(slots):
        for s in range(chips - 1):
            at(block_time * (h * (chips - 1) + s + 1), x_step, h, s)
        if h > 0:
            at(block_time * (h * (chips - 1) - 1) + 0.01, x_begin, h)
    time = 0.0
    for unit in range(2):
        for step in range(levels):
            if unit == 0 and step == levels - 1:
                at(time + 0.9, w_begin, 1)
            time += 2.0 ** (step + 1) / levels
            at(time, w_step, unit, step)
        if unit == 0:
            done = max(time, block_time * (chips - 1))
    at(done + 0.3, ready)
    time = done + 0.9
    for h in range(slots):
        for s in range(-1, chips - 1):
            arrived = block_time * (h * (chips - 1) + s + 1)
            time = max(time, arrived + 0.1)
            if s < 0:
                at(time, project_own, h)
            else:
                at(time, project_step, h, s)
            time += 0.2 if s < 0 else 0.4
        at(time, lambda h: out_copy(h).start(), h)

    fetch(0).start()
    fetch(1).start()
    x_here.start()
    x_begin(0)
    for number in range(1, fsdp):
        v_copy(number).start()
    v_own.start()
    w_begin(0)
    kept_here[0].start()
    x_here.wait()
    for _, work in sorted(plan, key=lambda entry: entry[0]):
        work()

    kept_here[1].start()
    kept_here[2].start()
    kept_here[1].wait()
    kept_here[2].wait()
    v_out.wait()
    for number in range(1, fsdp):
        v_copy(number).wait_send()
        for unit in range(2):
            for stream in range(levels):
                w_arrival(unit, stream, number).wait_send()
                w_share(unit, stream, number).wait_send()
                if unit > 0:
                    w_share_arrival(unit, stream, number).wait_recv()
    for h in range(slots):
        x_own(h).wait_send()
        out_copy(h).wait()
        for b in range(ctx):
            pltpu.make_async_copy(acts.at[h, b], act_ref.at[h, b], act_sem.at[h, b]).wait()
        for s in range(chips - 1):
            for side in range(2):

                @pl.when(x_sends(side, s))
                def _(side=side, h=h, s=s):
                    x_copy(side, s, h).wait_send()

                @pl.when(x_gets(side, s))
                def _(side=side, h=h, s=s):
                    x_share(side, s, h).wait_send()


def gather_first(ctx, fsdp, regular, x, w, v):
    slots, width, tok = x.shape
    rows, columns = w.shape
    levels, chips = bits_of(fsdp), ctx // 2
    owned = regular + 1
    feat = 3 * owned * HEAD_DIM
    room = feat + -feat % 128
    anywhere = pl.BlockSpec(memory_space=pl.ANY)
    dma = pltpu.SemaphoreType.DMA
    return pl.pallas_call(
        functools.partial(gather_kernel, ctx, fsdp, regular),
        in_specs=[anywhere, anywhere, pl.BlockSpec(memory_space=pltpu.VMEM)],
        out_specs=[anywhere] * 6,
        out_shape=[
            jax.ShapeDtypeStruct((slots, ctx, width, tok), BF16),
            jax.ShapeDtypeStruct((slots, feat, ctx * tok), BF16),
            jax.ShapeDtypeStruct((fsdp, rows, columns // 2), BF16),
            jax.ShapeDtypeStruct((fsdp, rows, columns // 4), BF16),
            jax.ShapeDtypeStruct((fsdp, rows, columns // 4), BF16),
            jax.ShapeDtypeStruct((fsdp, rows, 128), BF16),
        ],
        scratch_shapes=[
            pltpu.VMEM((ctx, slots, width, tok), BF16),
            pltpu.VMEM((rows, columns), F32),
            pltpu.VMEM((rows, columns), BF16),
            pltpu.VMEM((3 * owned, fsdp, rows, 128), BF16),
            pltpu.VMEM((width, room), BF16),
            pltpu.VMEM((room, width), BF16),
            pltpu.VMEM((fsdp, rows, 128), BF16),
            pltpu.VMEM((width, 128), F32),
            pltpu.VMEM((feat, 1), F32),
            pltpu.VMEM((slots, ctx, width, tok), BF16),
            pltpu.VMEM((slots, feat, ctx * tok), BF16),
            dma((2, chips - 1, slots)),
            dma((2, chips - 1, slots)),
            dma((2, chips, slots)),
            dma((2, chips, slots)),
            dma((2, levels, fsdp)),
            dma((2, levels, fsdp)),
            dma((2, levels, fsdp)),
            dma((2, levels, fsdp)),
            dma((fsdp,)),
            dma((fsdp,)),
            dma((slots, ctx)),
            dma((8 + 3 * owned + slots,)),
        ],
        compiler_params=pltpu.CompilerParams(
            collective_id=0, has_side_effects=True, vmem_limit_bytes=60 * 2**20
        ),
        cost_estimate=pl.CostEstimate(flops=1000, bytes_accessed=1000, transcendentals=0),
    )(x, w, v)


def bits_of(count):
    return max(count.bit_length() - 1, 0)


def flip(count, value):
    return [(i, i ^ value) for i in range(count)]


def pick(array, index, axis):
    return lax.dynamic_index_in_dim(array, index, axis, keepdims=False)


def ordered(bit, mine, other, axis):
    first = jnp.where(bit == 0, mine, other)
    second = jnp.where(bit == 0, other, mine)
    return jnp.concatenate([first, second], axis=axis)


def after(value, *others):
    return lax.optimization_barrier((value, others))[0]


def add_low(mine, swapped):
    return (mine.astype(F32) + swapped.astype(F32)).astype(BF16)


def scatter_fsdp(total):
    return lax.psum_scatter(total, "fsdp", scatter_dimension=0, tiled=True)


def bar_signal(where):
    pl.semaphore_signal(
        pltpu.get_barrier_semaphore(), inc=1, device_id=where, device_id_type=pl.DeviceIdType.MESH
    )


def remote_copy(source, target, send, recv, where):
    return pltpu.make_async_remote_copy(
        src_ref=source,
        dst_ref=target,
        send_sem=send,
        recv_sem=recv,
        device_id=where,
        device_id_type=pl.DeviceIdType.MESH,
    )


def line_gather(chips, c, f, mine, slot, share, sems, core_sems):
    z, core = c // 2, lax.rem(c, 2)
    partner = 2 * z + 1 - core
    send, recv = sems
    core_send, core_recv = core_sems

    def passing(side, s):
        sign = 1 - 2 * side
        chip = z - sign * s
        source = mine if s == 0 else slot(chip)
        return remote_copy(
            source, slot(chip), send.at[side, s], recv.at[side, s], (c + 2 * sign, f)
        )

    def arrival(side, s):
        block = slot(z - (1 - 2 * side) * (s + 1))
        return remote_copy(block, block, send.at[side, s], recv.at[side, s], (partner, f))

    def sends(side, s):
        return (z - s >= 0) & (z < chips - 1) if side == 0 else (z + s < chips) & (z > 0)

    def gets(side, s):
        return z - 1 - s >= 0 if side == 0 else z + 1 + s < chips

    def shared(side, s):
        chip = z - (1 - 2 * side) * (s + 1)
        return remote_copy(
            slot(chip), share(chip), core_send.at[side, s], core_recv.at[side, s], (partner, f)
        )

    def share_arrival(side, s):
        block = share(z - (1 - 2 * side) * (s + 1))
        sems = core_send.at[side, s], core_recv.at[side, s]
        return remote_copy(block, block, *sems, (partner, f))

    own_sems = core_send.at[0, chips - 1], core_recv.at[0, chips - 1]
    own_share = remote_copy(mine, share(z), *own_sems, (partner, f))

    def start():
        for side in range(2):

            @pl.when(sends(side, 0))
            def _(side=side):
                passing(side, 0).start()

        own_share.start()

    def step(s):
        for side in range(2):

            @pl.when(gets(side, s))
            def _(side=side):
                arrival(side, s).wait_recv()
                shared(side, s).start()

            if s + 1 < chips - 1:

                @pl.when(sends(side, s + 1))
                def _(side=side):
                    passing(side, s + 1).start()

    def end():
        own_share.wait_send()
        remote_copy(share(z), share(z), *own_sems, (partner, f)).wait_recv()
        for s in range(chips - 1):
            for side in range(2):

                @pl.when(sends(side, s))
                def _(side=side, s=s):
                    passing(side, s).wait_send()

                @pl.when(gets(side, s))
                def _(side=side, s=s):
                    shared(side, s).wait_send()
                    share_arrival(side, s).wait_recv()

    return start, [functools.partial(step, s) for s in range(chips - 1)], end


def sum_kernel(ctx, fsdp, batches, *refs):
    levels, chips = bits_of(fsdp), ctx // 2
    pieces = refs[0:2]
    own_ref, mine_out, other_out, own_out, last_out = refs[2:7]
    rest = list(refs[7:])
    own_kept, own_low, beside = rest.pop(0), rest.pop(0), rest.pop(0)
    own_sent = [rest.pop(0) for _ in range(levels)]
    own_got = [rest.pop(0) for _ in range(levels)]
    z_sent, z_got = rest.pop(0), rest.pop(0)
    op_send, op_recv, zs_send, zs_recv, zg_send, zg_recv = (rest.pop(0) for _ in range(6))
    zc_send, zc_recv, og_send, og_recv, oc_send, oc_recv, far_send, far_recv, local = (
        rest.pop(0) for _ in range(9)
    )
    c, f = lax.axis_index("ctx"), lax.axis_index("fsdp")
    z, core = c // 2, lax.rem(c, 2)
    partner = 2 * z + 1 - core
    far = lax.rem(c + ctx // 2, ctx)
    rows = own_low.shape[0]
    chunk = z_sent.shape[-1]
    width = chunk * chips // 2
    parts = chips // 2
    strip = 16 if rows % 16 == 0 else 8

    def own_bit(bit):
        return lax.rem(f // (1 << bit), 2)

    def strips(work):
        def body(i, carry):
            work(pl.ds(pl.multiple_of(i * strip, strip), strip))
            return carry

        lax.fori_loop(0, rows // strip, body, 0)

    bar_signal((partner, f))
    bar_signal((far, f))
    for bit in range(levels):
        bar_signal((c, other_index(f, 1 << bit)))

    @pl.when(z > 0)
    def _():
        bar_signal((c - 2, f))

    @pl.when(z < chips - 1)
    def _():
        bar_signal((c + 2, f))

    neighbours = (z > 0).astype(jnp.int32) + (z < chips - 1).astype(jnp.int32)
    pl.semaphore_wait(pltpu.get_barrier_semaphore(), levels + 2 + neighbours)

    def order(q):
        return [(q + i) % levels for i in range(levels)]

    def place_of(q, flipped, free):
        bits = order(q)
        first = own_bit(bits[0])
        total = (1 - first if flipped else first) * (1 << bits[0])
        for i, bit in enumerate(bits[1:]):
            total += ((free >> i) & 1) * (1 << bit)
        return total

    def kept_index(q, step, flipped, free):
        bits = order(q)
        total = 0
        for i, bit in enumerate(bits[1:]):
            mine = own_bit(bit)
            if i + 1 < step:
                value = mine
            elif i + 1 == step:
                value = 1 - mine if flipped else mine
            else:
                value = (free >> (i - step)) & 1
            total += value * (1 << i)
        return total

    def across(step, q):
        return (c, other_index(f, 1 << order(q)[step]))

    def own_copy(step):
        return remote_copy(
            own_sent[step], own_got[step], op_send.at[step], op_recv.at[step], across(step, 0)
        )

    def own_begin():
        for free in range(fsdp // 2):
            there, here = place_of(0, True, free), place_of(0, False, free)

            def work(at, free=free, there=there, here=here):
                own_sent[0][free, at, :] = own_ref[there, at, :]
                own_kept[free, at, :] = own_ref[here, at, :].astype(F32)

            strips(work)
        own_copy(0).start()

    def later(step, kept_ref, got_ref, sent_ref, q):
        for free in range(fsdp >> (step + 2)):
            there, here = (kept_index(q, step + 1, flipped, free) for flipped in (True, False))
            mine = own_bit(order(q)[step + 1])
            there_got, here_got = free * 2 + 1 - mine, free * 2 + mine

            def work(at, free=free):
                value = kept_ref[there, at, :] + got_ref[there_got, at, :].astype(F32)
                sent_ref[free, at, :] = value.astype(BF16)
                kept_ref[here, at, :] += got_ref[here_got, at, :].astype(F32)

            strips(work)

    def last(kept_ref, got_ref, q, place):
        def work(at):
            place(at, kept_ref[kept_index(q, levels, False, 0), at, :] + got_ref[0, at, :].astype(F32))

        strips(work)

    def own_step(step):
        own_copy(step).wait_recv()
        if step + 1 < levels:
            later(step, own_kept, own_got[step], own_sent[step + 1], 0)
            own_copy(step + 1).start()
            return

        def place(at, value):
            own_low[at, :] = value[:, : head + tail].astype(BF16)
            beside[at, :] = value[:, head + tail :]

        last(own_kept, own_got[step], 0, place)
        for copy in far_copies:
            copy.start()
        own_start()

    head = own_out.shape[2]
    tail = last_out.shape[2]
    far_copies = [
        remote_copy(
            own_low.at[:, pl.ds(head, tail)], last_out.at[1], far_send.at[0], far_recv.at[0], (far, f)
        ),
        pltpu.make_async_copy(own_low.at[:, pl.ds(head, tail)], last_out.at[0], local.at[0]),
        pltpu.make_async_copy(own_low.at[:, pl.ds(0, head)], own_out.at[c], local.at[1]),
    ]
    own_start, own_steps, own_end = line_gather(
        chips,
        c,
        f,
        own_low.at[:, pl.ds(0, head)],
        lambda chip: own_out.at[2 * chip + core],
        lambda chip: own_out.at[2 * chip + core],
        (og_send, og_recv),
        (oc_send, oc_recv),
    )

    def total_of(j, b, at):
        q = j // parts
        start = b * width + (j % parts) * chunk
        stop = start + chunk
        units, room = pieces[q].shape[1], beside.shape[1] // 2
        found = []
        if start < units:
            found.append(pieces[q][at, start : min(stop, units)].astype(F32))
        if stop > units:
            first = max(start, units) - units + q * room
            found.append(beside[at, first : stop - units + q * room])
        return found[0] if len(found) == 1 else jnp.concatenate(found, axis=1)

    def z_copy(side, i, b):
        return remote_copy(
            z_sent.at[side, b, i],
            z_got.at[side, b, i],
            zs_send.at[side, b, i],
            zs_recv.at[side, b, i],
            (c + 2 * (1 - 2 * side), f),
        )

    def z_last(side, chip):
        return chips - 1 - chip if side == 0 else chip

    def z_step(turn, b):
        for chip in range(chips):

            @pl.when(z == chip)
            def _(chip=chip):
                for side in range(2):
                    j_of = (lambda i: chips - 1 - i) if side == 0 else (lambda i: i)
                    begun = chip if side == 0 else chips - 1 - chip
                    i = turn - begun
                    sends = z_last(side, chip)
                    if begun > 0 and 0 <= i <= sends and i < chips - 1:
                        z_copy(side, i, b).wait_recv()
                    if 0 <= i < sends:
                        if i > 0:
                            z_copy(side, i - 1, b).wait_send()

                        def work(at, side=side, i=i, j=j_of(i), begun=begun):
                            value = total_of(j, b, at)
                            if begun > 0:
                                value += z_got[side, b, i, at, :].astype(F32)
                            z_sent[side, b, i, at, :] = value.astype(BF16)

                        strips(work)
                        z_copy(side, i, b).start()

    def chunk_of(ref, chip, b):
        start = pl.multiple_of(b * width + lax.rem(chip, parts) * chunk, 128)
        return ref.at[chip // parts, :, pl.ds(start, chunk)]

    gathers = []
    for b in range(batches):
        gathers.append(
            line_gather(
                chips,
                c,
                f,
                chunk_of(mine_out, z, b),
                lambda chip, b=b: chunk_of(mine_out, chip, b),
                lambda chip, b=b: chunk_of(other_out, chip, b),
                (zg_send.at[:, b], zg_recv.at[:, b]),
                (zc_send.at[:, b], zc_recv.at[:, b]),
            )
        )

    def finish(b):
        for j in range(chips):

            @pl.when(z == j)
            def _(j=j):
                def work(at):
                    value = total_of(j, b, at)
                    if j > 0:
                        value += z_got[0, b, chips - 1 - j, at, :].astype(F32)
                    if j < chips - 1:
                        value += z_got[1, b, j, at, :].astype(F32)
                    start = b * width + (j % parts) * chunk
                    mine_out[j // parts, at, pl.ds(start, chunk)] = value.astype(BF16)

                strips(work)

        gathers[b][0]()

    own_begin()
    waiting = []

    def one_more():
        if waiting:
            waiting.pop(0)()

    def batch(b):
        for i in range(chips):
            z_step(i, b)
            one_more()
        finish(b)
        waiting.extend(gathers[b][1])

    for b in range(batches - 1):
        batch(b)
    for step in range(levels):
        own_step(step)
        one_more()
    waiting.extend(own_steps)
    batch(batches - 1)
    while waiting:
        one_more()

    far_copies[0].wait()
    far_copies[1].wait()
    far_copies[2].wait()
    own_end()
    for step in range(levels):
        own_copy(step).wait_send()
    for b in range(batches):
        gathers[b][2]()
        for chip in range(chips):

            @pl.when(z == chip)
            def _(chip=chip, b=b):
                for side in range(2):
                    if z_last(side, chip):
                        z_copy(side, z_last(side, chip) - 1, b).wait_send()


def sum_grads(ctx, fsdp, pieces, own, head, tail):
    levels, chips = bits_of(fsdp), ctx // 2
    rows, units = pieces[0].shape
    rest = own.shape[-1] - head - tail
    whole = units + rest // 2
    batches = max(n for n in range(1, 3) if whole % n == 0 and 2 * whole // n % (chips * 128) == 0)
    width = whole // batches
    chunk = 2 * width // chips
    own_width = own.shape[-1]
    vmem = pl.BlockSpec(memory_space=pltpu.VMEM)
    dma = pltpu.SemaphoreType.DMA
    steps = [fsdp >> (i + 1) for i in range(levels)]
    result = jax.ShapeDtypeStruct((2, rows, whole), BF16)
    mine, other, own_all, last = pl.pallas_call(
        functools.partial(sum_kernel, ctx, fsdp, batches),
        in_specs=[vmem] * 3,
        out_specs=[vmem] * 4,
        out_shape=[
            result,
            result,
            jax.ShapeDtypeStruct((ctx, rows, head), BF16),
            jax.ShapeDtypeStruct((2, rows, tail), BF16),
        ],
        scratch_shapes=[
            pltpu.VMEM((fsdp // 2, rows, own_width), F32),
            pltpu.VMEM((rows, head + tail), BF16),
            pltpu.VMEM((rows, rest), F32),
        ]
        + [pltpu.VMEM((n, rows, own_width), BF16) for n in steps * 2]
        + [pltpu.VMEM((2, batches, chips - 1, rows, chunk), BF16)] * 2
        + [dma((levels,))] * 2
        + [dma((2, batches, chips - 1))] * 4
        + [dma((2, batches, chips))] * 2
        + [dma((2, chips - 1))] * 2
        + [dma((2, chips))] * 2
        + [dma((1,))] * 2
        + [dma((6,))],
        compiler_params=pltpu.CompilerParams(
            collective_id=1, has_side_effects=True, vmem_limit_bytes=60 * 2**20
        ),
        cost_estimate=pl.CostEstimate(flops=1000, bytes_accessed=1000, transcendentals=0),
    )(*pieces, own)

    return mine, other, own_all, last


def swap_cores(mine, ctx):
    return lax.ppermute(mine, "ctx", flip(ctx, 1))


def norm_parts(rows, axis):
    middle = jnp.mean(rows, axis=axis, keepdims=True)
    centred = rows - middle
    spread = jnp.mean(centred * centred, axis=axis, keepdims=True)
    inverse = lax.rsqrt(spread + NORM_EPS)
    return centred * inverse, inverse


def norm_back(grad, unit, inverse, gain):
    inner = grad * gain
    mean_inner = jnp.mean(inner, axis=1, keepdims=True)
    mean_cross = jnp.mean(inner * unit, axis=1, keepdims=True)
    rows = inverse * (inner - mean_inner - unit * mean_cross)
    return rows, jnp.sum(grad * unit, axis=(0, 2)), jnp.sum(grad, axis=(0, 2))


def adamw(weight, first, second, grad, rate, decay):
    moment = BETA_ONE * first.astype(F32) + (1.0 - BETA_ONE) * grad
    square = BETA_TWO * second + (1.0 - BETA_TWO) * grad * grad
    corrected = moment / (1.0 - BETA_ONE**STEP)
    scaled = square / (1.0 - BETA_TWO**STEP)
    new_weight = weight - rate * (corrected / (jnp.sqrt(scaled) + ADAM_EPS) + decay * weight)
    return (moment, square, new_weight)


def update_kernel(units, regular, *refs):
    (w, first, second, dw, dfirst, dsecond, own, last, mine, other) = refs[:10]
    outs = refs[10:]
    core = lax.rem(lax.axis_index("ctx"), 2)
    width = (w.shape[1] - 2 * units) // 4
    quarter = width // 4
    ctx = own.shape[0]
    dim = HEAD_DIM

    def halves(q, start, size):
        here = mine[q, :, start : start + size].astype(F32)
        there = other[q, :, start : start + size].astype(F32)
        return jnp.where(core == 0, here, there), jnp.where(core == 0, there, here)

    def both(q, start, size):
        return jnp.concatenate(halves(q, start, size), axis=1)

    heads = []
    for part in range(3):
        for i in range(regular):
            for c in range(ctx):
                column = (i * 3 + part) * dim
                heads.append(own[c, :, column : column + dim].astype(F32))
        column = part * dim
        heads.append(
            last[0, :, column : column + dim].astype(F32)
            + last[1, :, column : column + dim].astype(F32)
        )
    out = [halves(q, units, quarter) for q in range(2)]
    heads += [out[0][0], out[1][0], out[0][1], out[1][1]]
    grad = jnp.concatenate(heads, axis=1)

    def put(targets, cols, values):
        for target, value in zip(targets, values):
            target[:, cols] = value

    cols = slice(0, 4 * width)
    put(outs[:3], cols, adamw(w[:, cols], first[:, cols], second[:, cols], grad, 0.03, 0.1))
    cols = slice(4 * width, w.shape[1])
    grad = both(0, 0, units)
    put(outs[:3], cols, adamw(w[:, cols], first[:, cols], second[:, cols], grad, 0.03, 0.1))
    grad = both(1, 0, units)
    put(outs[3:], slice(None), adamw(dw[...], dfirst[...], dsecond[...], grad, 0.02, 0.1))


def update(rows_state, down_state, own, last, mine, other, units, regular):
    rows = rows_state[0].shape[0]
    strip = 16 if rows % 16 == 0 else 8

    def flat(array):
        return pl.BlockSpec((strip, array.shape[1]), lambda i: (i, 0))

    def deep(array):
        return pl.BlockSpec((array.shape[0], strip, array.shape[2]), lambda i: (0, i, 0))

    states, sums = [*rows_state, *down_state], [own, last, mine, other]
    results = [rows_state[0]] * 3 + [down_state[0]] * 3
    return pl.pallas_call(
        functools.partial(update_kernel, units, regular),
        grid=(rows // strip,),
        in_specs=[flat(a) for a in states] + [deep(a) for a in sums],
        out_specs=[flat(a) for a in results],
        out_shape=[jax.ShapeDtypeStruct(a.shape, F32) for a in results],
        compiler_params=pltpu.CompilerParams(vmem_limit_bytes=56 * 2**20),
        cost_estimate=pl.CostEstimate(flops=1000, bytes_accessed=1000, transcendentals=0),
    )(*states, *sums)


def body(
    ctx,
    fsdp,
    tokens,
    cotangent,
    lengths,
    w_rows,
    rows_first,
    rows_second,
    w_down,
    down_first,
    down_second,
    vectors,
    vec_first,
    vec_second,
):
    tok, slots, width = tokens.shape
    dim = HEAD_DIM
    regular = HEADS // ctx
    owned = regular + 1
    share = width // fsdp
    c = lax.axis_index("ctx")
    core = c % 2
    late = (c >= ctx // 2).astype(jnp.int32)
    half = FF // 2

    def my_half(array):
        return lax.dynamic_slice_in_dim(array, core * half, half, 1)

    x_low = tokens.transpose(1, 2, 0)
    vec_part = jnp.pad(vectors.astype(BF16).T, ((0, 0), (0, 128 - vectors.shape[0])))
    act_all, qkv_all, head_w, up_mine, up_other, vec_low = gather_first(
        ctx, fsdp, regular, x_low, w_rows, vec_part
    )
    head_w = head_w.reshape(width, 4 * width)
    up_mine, up_other = up_mine.reshape(width, half), up_other.reshape(width, half)
    vec_low = vec_low.reshape(width, 128)
    down_mine, vec_low = lax.optimization_barrier((my_half(w_down.T).astype(BF16), vec_low))
    down_mine = lax.all_gather(down_mine, "fsdp", axis=0, tiled=True)
    vec = [vec_low[:, i : i + 1].astype(F32) for i in range(12)]
    up_bias = vec_low[:, 8:12].T.astype(F32).reshape(1, FF)

    qkv_all = qkv_all.reshape(slots, 3, owned, dim, ctx * tok)
    far = (c + ctx // 2) % ctx

    def to_rows(array, *gate):
        feat = array.shape[2]
        got = lax.all_to_all(array, "ctx", 0, 0)
        got = after(got, *gate) if gate else got
        return got.transpose(1, 0, 2, 3).reshape(regular * ctx, feat, tok)

    def last_to_rows(array, *gate):
        mine = pick(array, c, 0)
        got = lax.ppermute(pick(array, far, 0), "ctx", flip(ctx, ctx // 2))
        got = after(got, *gate) if gate else got
        return jnp.where(late == 0, mine, got), jnp.where(late == 0, got, mine)

    def to_send(array):
        return array.reshape(regular, ctx, dim, tok).transpose(1, 0, 2, 3)

    def attend_slot(s, *gate):
        lens = after(jnp.repeat(lengths[s : s + 1], regular), *gate)
        return (lens, qkv_all, s, *attend(lens, qkv_all, s, tok))

    results = [attend_slot(0)]
    results.append(attend_slot(1, results[0][3]))
    rows = [to_rows(results[0][4])]
    last_qkv = jnp.where(late == 0, qkv_all[:1, :, regular:], qkv_all[1:, :, regular:])
    last_len = after(lax.dynamic_slice_in_dim(lengths, late, 1, 0), results[1][3], rows[0])
    results.append((last_len, last_qkv, 0, *attend(last_len, last_qkv, 0, tok)))
    rows.append(to_rows(results[1][4]))
    down_mine = after(down_mine, results[2][3], *rows)
    down_other = swap_cores(down_mine, ctx)
    last_rows = last_to_rows(results[2][4])
    att = [jnp.concatenate([rows[s], last_rows[s]]).reshape(width, tok) for s in range(slots)]
    att = jnp.stack(att)

    x = x_low.astype(F32)
    out_w = head_w[:, 3 * width :]
    mid = x + jnp.einsum("de,sdt->set", out_w, att, preferred_element_type=F32) + vec[4]
    unit_two, inverse_two = norm_parts(mid, 1)
    act_two = (unit_two * vec[5] + vec[6]).astype(BF16)

    pos = c * tok + jnp.arange(tok, dtype=jnp.int32)
    valid = pos[None, None, :] < lengths[:, None, None]
    g_low = jnp.where(valid, cotangent.transpose(1, 2, 0), jnp.zeros((), BF16))
    g = g_low.astype(F32)

    bias_mine = lax.dynamic_slice_in_dim(up_bias, core * half, half, 1)
    bias_other = lax.dynamic_slice_in_dim(up_bias, (1 - core) * half, half, 1)
    y_other, ga_other, dup_other, ddown_other, db_other = mlp(
        act_two, g_low, up_other, down_other, bias_other
    )
    y_mine, ga_mine, dup_mine, ddown_mine, db_mine = mlp(
        act_two, g_low, up_mine, down_mine, bias_mine
    )
    output = (mid + (y_mine + y_other + vec[7])).astype(BF16).transpose(2, 0, 1)

    up_swapped, down_swapped = swap_cores(dup_other, ctx), swap_cores(ddown_other, ctx)

    up_total = add_low(dup_mine, up_swapped)
    up_part = scatter_fsdp(up_total)
    ga_mine = after(ga_mine, up_total)
    grad_mid, gain_two, shift_two = norm_back(ga_mine + ga_other, unit_two, inverse_two, vec[5])
    grad_mid = g + grad_mid
    grad_attn = grad_mid.astype(BF16)
    grad_att = jnp.einsum("de,set->sdt", out_w, grad_attn, preferred_element_type=F32).astype(BF16)
    grad_att = grad_att.reshape(slots, HEADS, dim, tok)
    first_send = to_send(grad_att[0, :-1])
    grad_attn_later = after(grad_attn, first_send)
    last = jnp.repeat(grad_att[:, -1], ctx // slots, axis=0)[:, None]
    first_pairs = lax.all_to_all(first_send, "ctx", 0, 0)
    down_part = scatter_fsdp(add_low(after(ddown_mine, first_pairs), down_swapped))
    other_pairs = lax.all_to_all(
        after(jnp.concatenate([to_send(grad_att[1, :-1]), last], axis=1), first_pairs), "ctx", 0, 0
    )

    quarter = width // 4
    spread = jnp.pad(
        grad_attn_later.reshape(slots, 4, quarter, tok),
        ((0, 0), (0, 0), (0, -quarter % 128), (0, 0)),
    )
    out_grad = jnp.einsum("sdt,sket->kde", att, spread, preferred_element_type=F32).astype(BF16)
    out_grad = out_grad.reshape(2, 2, fsdp, share, spread.shape[2])

    def out_half(which):
        return pick(out_grad, which, 0).reshape(2, width, spread.shape[2])

    out_mine, out_swapped = out_half(core), swap_cores(out_half(1 - core), ctx)
    out_total = add_low(out_mine, out_swapped)
    first_heads = attend_back(*results[0][:4], results[0][5], first_pairs)
    last_heads = attend_back(
        *results[2][:4], results[2][5], after(other_pairs[:, -1:], first_heads)
    )
    other_heads = attend_back(
        *results[1][:4], results[1][5], after(other_pairs[:, :-1], last_heads, up_part)
    )
    grad_heads = [first_heads, other_heads, last_heads]

    feat = 3 * dim
    own_sum = own_grad(
        late,
        act_all,
        grad_heads[0].reshape(ctx, regular * feat, tok),
        grad_heads[1].reshape(ctx, regular * feat, tok),
        grad_heads[2].reshape(ctx, feat, tok),
    )
    own_sum = own_sum.astype(BF16)
    own_sum = jnp.concatenate(
        [
            jnp.pad(part, ((0, 0), (0, -part.shape[1] % 128)))
            for part in (own_sum[:, : regular * feat], own_sum[:, regular * feat :])
        ]
        + [out_total[0], out_total[1]],
        axis=1,
    )
    head_columns = regular * feat + -regular * feat % 128
    blocks = (fsdp, share)
    sum_mine, sum_other, own_all, last = sum_grads(
        ctx,
        fsdp,
        [up_part, down_part],
        own_sum.reshape(*blocks, own_sum.shape[1]),
        head_columns,
        feat + -feat % 128,
    )
    first_rows, other_rows = to_rows(first_heads), to_rows(other_heads, sum_mine)
    last_rows = last_to_rows(last_heads, sum_mine)
    grad_qkv = []
    for s, rows in enumerate((first_rows, other_rows)):
        rows = jnp.concatenate([rows, last_rows[s]])
        rows = rows.reshape(HEADS, 3, dim, tok).transpose(1, 0, 2, 3)
        grad_qkv.append(rows.reshape(3 * width, tok))
    grad_qkv = jnp.stack(grad_qkv)
    grad_one = jnp.einsum(
        "de,set->sdt", head_w[:, : 3 * width], grad_qkv, preferred_element_type=F32
    )

    unit_one, inverse_one = norm_parts(x, 1)
    grad_in, gain_one, shift_one = norm_back(grad_one, unit_one, inverse_one, vec[0])
    grad_tokens = (grad_mid + grad_in).astype(BF16)

    bias_qkv = jnp.sum(grad_qkv.astype(F32), axis=(0, 2))
    vec_grad = jnp.stack(
        [
            gain_one,
            shift_one,
            bias_qkv[:width],
            bias_qkv[2 * width :],
            jnp.sum(grad_attn.astype(F32), axis=(0, 2)),
            gain_two,
            shift_two,
            jnp.sum(g, axis=(0, 2)),
        ]
    )
    bias_up = ordered(core, db_mine, db_other, 1).reshape(4, width)
    vec_grad = jnp.concatenate([vec_grad, bias_up], axis=0).reshape(12, fsdp, share)
    f = lax.axis_index("fsdp")
    vec_sum = pick(vec_grad, f, 1)
    for value in range(1, fsdp):
        vec_sum = vec_sum + lax.ppermute(pick(vec_grad, f ^ value, 1), "fsdp", flip(fsdp, value))
    for level in range(bits_of(ctx)):
        vec_sum = vec_sum + lax.ppermute(vec_sum, "ctx", flip(ctx, 2**level))

    rows_state = (w_rows, rows_first, rows_second)
    down_state = (w_down.T, down_first.T, down_second.T)
    updated = update(
        rows_state, down_state, own_all, last, sum_mine, sum_other, half, regular
    )
    rows_out, down_out = updated[:3], tuple(part.T for part in updated[3:])
    vec_out = adamw(vectors, vec_first, vec_second, vec_sum, 0.3, 0.0)
    return (output, grad_tokens.transpose(2, 0, 1), *rows_out, *down_out, *vec_out)


def solution(mesh):
    placed = (
        P("ctx", "fsdp", None),
        P("ctx", "fsdp", None),
        P("fsdp"),
        P("fsdp", None),
        P("fsdp", None),
        P("fsdp", None),
        P(None, "fsdp"),
        P(None, "fsdp"),
        P(None, "fsdp"),
        P(None, "fsdp"),
        P(None, "fsdp"),
        P(None, "fsdp"),
    )
    return jax.shard_map(
        functools.partial(body, mesh.shape["ctx"], mesh.shape["fsdp"]),
        mesh=mesh,
        in_specs=placed,
        out_specs=placed[:2] + placed[3:6] + placed[6:9] + placed[9:12],
        check_vma=False,
    )
```

```python
import functools
import math

import jax
import jax.numpy as jnp
from jax import lax
from jax.experimental import pallas as pl
from jax.experimental.pallas import tpu as pltpu
from jax.sharding import PartitionSpec as P

HEADS = 17
HEAD_DIM = 64
FF = 4352
STEP = 10

MASKED = -1e30
NORM_EPS = 1e-05
BETA_ONE = 0.9
BETA_TWO = 0.95
ADAM_EPS = 1e-08
BF16 = jnp.bfloat16
F32 = jnp.float32


def dot(left, right, dims=((1,), (0,))):
    return lax.dot_general(left, right, (dims, ((), ())), preferred_element_type=F32)


def padded(top, rows, width):
    row = lax.broadcasted_iota(jnp.int32, (rows, width), 0)
    out = jnp.zeros((rows, width), F32)
    for index, value in enumerate(top):
        out = jnp.where(row == index, value, out)
    return out.astype(BF16)


def key_rows(lens_ref, key, length):
    pos = lax.broadcasted_iota(jnp.int32, (1, length), 1)
    bias = jnp.where(pos < lens_ref[0], 0.0, MASKED)
    one = jnp.ones((1, length), F32)
    extra = padded([bias, one, one, one], HEAD_DIM, length)
    return jnp.concatenate([key, extra], axis=0).T


def causal(block):
    key = lax.broadcasted_iota(jnp.int32, (block, block), 0)
    query = lax.broadcasted_iota(jnp.int32, (block, block), 1)
    return key <= query


def attend_kernel(block, lens_ref, q_ref, k_ref, v_ref, o_ref, low_ref, lse_ref, keys):
    heads, _, length = k_ref.shape[2:]
    tok = low_ref.shape[-1]
    step = pl.program_id(0)

    @pl.when(step == 0)
    def _():
        for h in range(heads):
            keys[h] = key_rows(lens_ref, k_ref[0, 0, h], length)

    one_row = padded([jnp.ones((1, block), F32)], HEAD_DIM, block)
    queries = []
    for h in range(heads):
        query = (q_ref[0, 0, h].astype(F32) * (1.0 / math.sqrt(HEAD_DIM))).astype(BF16)
        queries.append(jnp.concatenate([query, one_row], axis=0))

    def one(index, states, mask):
        start = pl.multiple_of(index * block, block)
        all_scores = [dot(keys[h, pl.ds(start, block), :], queries[h]) for h in range(heads)]
        results = []
        for h, (top, total, accum) in enumerate(states):
            scores = all_scores[h]
            if mask is not None:
                scores = jnp.where(mask, scores, MASKED)
            new_top = jnp.maximum(top, jnp.max(scores, axis=0, keepdims=True))
            weights = jnp.exp(scores - new_top)
            factor = jnp.exp(top - new_top)
            total = total * factor + jnp.sum(weights, axis=0, keepdims=True)
            value = v_ref[0, 0, h, :, pl.ds(start, block)]
            accum = accum * factor + dot(value, weights.astype(BF16))
            results.append((new_top, total, accum))
        return tuple(results)

    state = (
        jnp.full((1, block), MASKED, F32),
        jnp.zeros((1, block), F32),
        jnp.zeros((HEAD_DIM, block), F32),
    )
    states = lax.fori_loop(0, step, lambda i, s: one(i, s, None), (state,) * heads)
    states = one(step, states, causal(block))
    for h, (top, total, accum) in enumerate(states):
        result = accum / total
        o_ref[h] = result
        for i in range(block // tok):
            low_ref[i, h] = result[:, i * tok : (i + 1) * tok].astype(BF16)
        lse_ref[h] = top + jnp.log(total)


def head_specs(slot, heads, dim, length, block):
    def whole(part):
        return pl.BlockSpec((1, 1, heads, dim, length), lambda i, lens: (slot, part, 0, 0, 0))

    def piece(part):
        return pl.BlockSpec((1, 1, heads, dim, block), lambda i, lens: (slot, part, 0, 0, i))

    return whole, piece


def attend(lens, qkv, slot, tok):
    dim, length = qkv.shape[3:]
    pairs = lens.shape[0]
    block = math.gcd(length, 512)
    whole, piece = head_specs(slot, pairs, dim, length, block)
    return pl.pallas_call(
        functools.partial(attend_kernel, block),
        grid_spec=pltpu.PrefetchScalarGridSpec(
            num_scalar_prefetch=1,
            grid=(length // block,),
            in_specs=[piece(0), whole(1), whole(2)],
            out_specs=[
                pl.BlockSpec((pairs, dim, block), lambda i, lens: (0, 0, i)),
                pl.BlockSpec((block // tok, pairs, dim, tok), lambda i, lens: (i, 0, 0, 0)),
                pl.BlockSpec((pairs, 1, block), lambda i, lens: (0, 0, i)),
            ],
            scratch_shapes=[pltpu.VMEM((pairs, length, 2 * dim), BF16)],
        ),
        out_shape=[
            jax.ShapeDtypeStruct((pairs, dim, length), F32),
            jax.ShapeDtypeStruct((length // tok, pairs, dim, tok), BF16),
            jax.ShapeDtypeStruct((pairs, 1, length), F32),
        ],
        compiler_params=pltpu.CompilerParams(
            vmem_limit_bytes=48 * 2**20
        ),
        cost_estimate=pl.CostEstimate(flops=1000, bytes_accessed=1000, transcendentals=0),
    )(lens, qkv, qkv, qkv)


def split_three(value):
    first = value.astype(BF16).astype(F32)
    second = (value - first).astype(BF16).astype(F32)
    third = (value - first - second).astype(BF16).astype(F32)
    return [-first, -second, -third]


def attend_back_kernel(
    block,
    lens_ref,
    q_ref,
    k_ref,
    v_ref,
    o_ref,
    lse_ref,
    grad_ref,
    out_ref,
    keys,
    values,
    queries,
    grads,
    total,
):
    heads, dim, length = k_ref.shape[2:]
    tok = grad_ref.shape[-1]
    count = length // block
    step = pl.program_id(0)
    scale = 1.0 / math.sqrt(HEAD_DIM)

    @pl.when(step == 0)
    def _():
        one = jnp.ones((1, length), F32)
        for h in range(heads):
            keys[h] = key_rows(lens_ref, k_ref[0, 0, h], length)
            extra = padded([one, one, one], dim, length)
            values[h] = jnp.concatenate([v_ref[0, 0, h], extra], axis=0).T
            queries[h, 0:dim, :] = (q_ref[0, 0, h].astype(F32) * scale).astype(BF16)
            queries[h, dim:, :] = padded([one] + split_three(lse_ref[h]), dim, length)
            for i in range(length // tok):
                grads[h, 0:dim, i * tok : (i + 1) * tok] = grad_ref[i, h]
            delta = jnp.sum(grads[h, 0:dim, :].astype(F32) * o_ref[h], axis=0, keepdims=True)
            grads[h, dim:, :] = padded(split_three(delta), dim, length)
        total[...] = jnp.zeros_like(total)

    mine = pl.ds(pl.multiple_of(step * block, block), block)

    def one(index, states, mask):
        cols = pl.ds(pl.multiple_of(index * block, block), block)
        all_scores = [dot(keys[h, mine, :], queries[h, :, cols]) for h in range(heads)]
        results = []
        for h, (dk, dv) in enumerate(states):
            scores = all_scores[h]
            if mask is not None:
                scores = jnp.where(mask, scores, MASKED)
            probs = jnp.exp(scores)
            grad_scores = (probs * dot(values[h, mine, :], grads[h, :, cols])).astype(BF16)
            probs = probs.astype(BF16)
            dv = dv + dot(grads[h, 0:dim, cols], probs, ((1,), (1,)))
            dk = dk + dot(queries[h, 0:dim, cols], grad_scores, ((1,), (1,)))
            total[h, :, cols] += dot(k_ref[0, 0, h, :, mine], grad_scores)
            results.append((dk, dv))
        return tuple(results)

    zero = jnp.zeros((dim, block), F32)
    states = one(step, ((zero, zero),) * heads, causal(block))
    states = lax.fori_loop(step + 1, count, lambda i, s: one(i, s, None), states)
    for h, (dk, dv) in enumerate(states):
        dq = total[h, :, mine] * scale
        for i in range(block // tok):
            cols = slice(i * tok, (i + 1) * tok)
            out_ref[i, h, 0:dim] = dq[:, cols].astype(BF16)
            out_ref[i, h, dim : 2 * dim] = dk[:, cols].astype(BF16)
            out_ref[i, h, 2 * dim :] = dv[:, cols].astype(BF16)


def attend_back(lens, qkv, slot, out, lse, grad):
    dim, length = qkv.shape[3:]
    pairs, tok = lens.shape[0], grad.shape[-1]
    ctx = length // tok
    block = math.gcd(length, 512)
    whole, _ = head_specs(slot, pairs, dim, length, block)
    return pl.pallas_call(
        functools.partial(attend_back_kernel, block),
        grid_spec=pltpu.PrefetchScalarGridSpec(
            num_scalar_prefetch=1,
            grid=(length // block,),
            in_specs=[
                whole(0),
                whole(1),
                whole(2),
                pl.BlockSpec((pairs, dim, length), lambda i, lens: (0, 0, 0)),
                pl.BlockSpec((pairs, 1, length), lambda i, lens: (0, 0, 0)),
                pl.BlockSpec((ctx, pairs, dim, tok), lambda i, lens: (0, 0, 0, 0)),
            ],
            out_specs=pl.BlockSpec(
                (block // tok, pairs, 3 * dim, tok), lambda i, lens: (i, 0, 0, 0)
            ),
            scratch_shapes=[
                pltpu.VMEM((pairs, length, 2 * dim), BF16),
                pltpu.VMEM((pairs, length, 2 * dim), BF16),
                pltpu.VMEM((pairs, 2 * dim, length), BF16),
                pltpu.VMEM((pairs, 2 * dim, length), BF16),
                pltpu.VMEM((pairs, dim, length), F32),
            ],
        ),
        out_shape=jax.ShapeDtypeStruct((ctx, pairs, 3 * dim, tok), BF16),
        compiler_params=pltpu.CompilerParams(
            vmem_limit_bytes=48 * 2**20
        ),
        cost_estimate=pl.CostEstimate(flops=1000, bytes_accessed=1000, transcendentals=0),
    )(lens, qkv, qkv, qkv, out, lse, grad)


def own_grad_kernel(late_ref, first_ref, second_ref, first_grad_ref, second_grad_ref, last_grad_ref, out_ref, total):
    step = pl.program_id(0)
    nt = ((1,), (1,))
    first, second = first_ref[0, 0], second_ref[0, 0]
    head = dot(first, first_grad_ref[0], nt) + dot(second, second_grad_ref[0], nt)
    last = dot(jnp.where(late_ref[0] == 0, first, second), last_grad_ref[0], nt)
    part = jnp.concatenate([head, last], axis=1)

    @pl.when(step == 0)
    def _():
        total[...] = part

    @pl.when(step > 0)
    def _():
        total[...] += part

    @pl.when(step == pl.num_programs(0) - 1)
    def _():
        out_ref[...] = total[...]


def own_grad(late, act, first_grad, second_grad, last_grad):
    _, ctx, width, tok = act.shape
    feat, last = first_grad.shape[1], last_grad.shape[1]

    def block(rows):
        return pl.BlockSpec((1, rows, tok), lambda i, late: (i, 0, 0))

    def of(slot):
        return pl.BlockSpec((1, 1, width, tok), lambda i, late: (slot, i, 0, 0))

    return pl.pallas_call(
        own_grad_kernel,
        grid_spec=pltpu.PrefetchScalarGridSpec(
            num_scalar_prefetch=1,
            grid=(ctx,),
            in_specs=[of(0), of(1), block(feat), block(feat), block(last)],
            out_specs=pl.BlockSpec((width, feat + last), lambda i, late: (0, 0)),
            scratch_shapes=[pltpu.VMEM((width, feat + last), F32)],
        ),
        out_shape=jax.ShapeDtypeStruct((width, feat + last), F32),
        compiler_params=pltpu.CompilerParams(vmem_limit_bytes=48 * 2**20),
        cost_estimate=pl.CostEstimate(flops=1000, bytes_accessed=1000, transcendentals=0),
    )(late[None], act, act, first_grad, second_grad, last_grad)


def mlp_kernel(
    width,
    a_ref,
    g_ref,
    up_ref,
    down_ref,
    bias_ref,
    y_ref,
    ga_ref,
    dup_ref,
    ddown_ref,
    db_ref,
    a_rows,
    g_rows,
):
    step = pl.program_id(0)
    slots, _, tok = a_ref.shape
    block = up_ref.shape[1]

    @pl.when(step == 0)
    def _():
        for s in range(slots):
            a_rows[s * tok : (s + 1) * tok, :] = a_ref[s].T
            g_rows[s * tok : (s + 1) * tok, :] = g_ref[s].T
        y_ref[...] = jnp.zeros_like(y_ref)
        ga_ref[...] = jnp.zeros_like(ga_ref)

    def run(size):
        up = up_ref[:, :size]
        down = down_ref[:, :size]
        pre = dot(a_rows[...], up) + bias_ref[:, :size]
        cdf = 0.5 * (1.0 + lax.erf(pre * math.sqrt(0.5)))
        hidden = (pre * cdf).astype(BF16)
        slope = cdf + pre * jnp.exp(-0.5 * pre * pre) * (1.0 / math.sqrt(2.0 * math.pi))
        grad = (dot(g_rows[...], down) * slope).astype(BF16)
        db_ref[:, :size] = jnp.sum(grad.astype(F32), axis=0, keepdims=True)
        nt = ((1,), (1,))
        for s in range(slots):
            rows = slice(s * tok, (s + 1) * tok)
            y_ref[s] += dot(down, hidden[rows], nt)
            ga_ref[s] += dot(up, grad[rows], nt)
        dup = sum(dot(a_ref[s], grad[s * tok : (s + 1) * tok]) for s in range(slots))
        dup_ref[:, :size] = dup.astype(dup_ref.dtype)
        ddown = sum(dot(g_ref[s], hidden[s * tok : (s + 1) * tok]) for s in range(slots))
        ddown_ref[:, :size] = ddown.astype(ddown_ref.dtype)

    full = width // block

    @pl.when(step < full)
    def _():
        run(block)

    if width % block:

        @pl.when(step == full)
        def _():
            run(width % block)


def mlp(act, grad, up, down, bias):
    slots, width, tok = act.shape
    units = up.shape[1]
    block = 256

    def fixed(shape):
        return pl.BlockSpec(shape, lambda i: (0,) * len(shape))

    cols = pl.BlockSpec((width, block), lambda i: (0, i))
    line = pl.BlockSpec((1, block), lambda i: (0, i))
    total = jax.ShapeDtypeStruct((slots, width, tok), F32)
    grads = jax.ShapeDtypeStruct((width, units), BF16)
    return pl.pallas_call(
        functools.partial(mlp_kernel, units),
        grid=(pl.cdiv(units, block),),
        in_specs=[fixed(act.shape), fixed(act.shape), cols, cols, line],
        out_specs=[fixed(act.shape), fixed(act.shape), cols, cols, line],
        out_shape=[total, total, grads, grads, jax.ShapeDtypeStruct((1, units), F32)],
        scratch_shapes=[pltpu.VMEM((slots * tok, width), BF16)] * 2,
        compiler_params=pltpu.CompilerParams(vmem_limit_bytes=56 * 2**20),
        cost_estimate=pl.CostEstimate(flops=1000, bytes_accessed=1000, transcendentals=0),
    )(act, grad, up, down, bias)


def other_index(index, bit):
    return index + bit * (1 - 2 * lax.rem(index // bit, 2))


def split_columns(start, size, count):
    tiles = size // 128
    cuts = [start + 128 * (-(-tiles * i // count)) for i in range(count)] + [start + size]
    return [(cuts[i], cuts[i + 1] - cuts[i]) for i in range(count)]


def gather_kernel(
    ctx,
    fsdp,
    regular,
    x_ref,
    w_ref,
    v_ref,
    act_ref,
    qkv_ref,
    wo_ref,
    um_ref,
    uo_ref,
    vo_ref,
    xo_ref,
    wide,
    w_low,
    windows,
    own_w,
    own_t,
    v_all,
    v_rows,
    bias,
    acts,
    qkvs,
    x_send,
    x_recv,
    xc_send,
    xc_recv,
    w_send,
    w_recv,
    wc_send,
    wc_recv,
    v_send,
    v_recv,
    act_sem,
    local,
):
    c, f = lax.axis_index("ctx"), lax.axis_index("fsdp")
    chips = ctx // 2
    z, core = c // 2, lax.rem(c, 2)
    partner = 2 * z + 1 - core
    slots, width, tok = x_ref.shape
    rows = w_ref.shape[0]
    dim = HEAD_DIM
    owned = regular + 1
    levels = bits_of(fsdp)
    half = um_ref.shape[2]

    def combine(number):
        place = f
        for bit in range(levels):
            if number & (1 << bit):
                place = other_index(place, 1 << bit)
        return place

    barrier = pltpu.get_barrier_semaphore()

    def greet(where):
        pl.semaphore_signal(barrier, inc=1, device_id=where, device_id_type=pl.DeviceIdType.MESH)

    greet((partner, f))
    for number in range(1, fsdp):
        greet((c, combine(number)))

    @pl.when(z > 0)
    def _():
        greet((c - 2, f))

    @pl.when(z < chips - 1)
    def _():
        greet((c + 2, f))

    beside = (z > 0).astype(jnp.int32) + (z < chips - 1).astype(jnp.int32)
    pl.semaphore_wait(barrier, fsdp + beside)

    def remote(source, target, send, recv, where):
        return pltpu.make_async_remote_copy(
            src_ref=source,
            dst_ref=target,
            send_sem=send,
            recv_sem=recv,
            device_id=where,
            device_id_type=pl.DeviceIdType.MESH,
        )

    def x_copy(side, s, h):
        sign = 1 - 2 * side
        block = c - 2 * sign * s
        source = x_ref.at[h] if s == 0 else xo_ref.at[block, h]
        return remote(
            source, xo_ref.at[block, h], x_send.at[side, s, h], x_recv.at[side, s, h], (c + 2 * sign, f)
        )

    def x_sends(side, s):
        return (z - s >= 0) & (z < chips - 1) if side == 0 else (z + s < chips) & (z > 0)

    def x_gets(side, s):
        return z - 1 - s >= 0 if side == 0 else z + 1 + s < chips

    def x_arrival(side, s, h):
        sign = 1 - 2 * side
        block = c - 2 * sign * (s + 1)
        return remote(
            xo_ref.at[block, h],
            xo_ref.at[block, h],
            x_send.at[side, s, h],
            x_recv.at[side, s, h],
            (c + 2 * sign, f),
        )

    def x_share(side, s, h):
        sign = 1 - 2 * side
        block = c - 2 * sign * (s + 1)
        return remote(
            xo_ref.at[block, h],
            xo_ref.at[block, h],
            xc_send.at[side, s, h],
            xc_recv.at[side, s, h],
            (partner, f),
        )

    def x_share_arrival(side, s, h):
        sign = 1 - 2 * side
        block = partner - 2 * sign * (s + 1)
        return remote(
            xo_ref.at[block, h],
            xo_ref.at[block, h],
            xc_send.at[side, s, h],
            xc_recv.at[side, s, h],
            (partner, f),
        )

    def x_own(h):
        return remote(
            x_ref.at[h],
            xo_ref.at[c, h],
            xc_send.at[0, chips - 1, h],
            xc_recv.at[0, chips - 1, h],
            (partner, f),
        )

    def x_own_arrival(h):
        return remote(
            x_ref.at[h],
            xo_ref.at[partner, h],
            xc_send.at[0, chips - 1, h],
            xc_recv.at[0, chips - 1, h],
            (partner, f),
        )

    runs = split_columns(0, half, levels)

    def source(unit, stream):
        start, size = runs[stream]
        return w_low.at[:, pl.ds(pl.multiple_of((2 * unit + core) * half + start, 128), size)]

    def kept(unit, stream, place, which):
        start, size = runs[stream]
        if unit == 0:
            return wo_ref.at[place, :, pl.ds(pl.multiple_of(which * half + start, 128), size)]
        return um_ref.at[place, :, pl.ds(start, size)]

    def shared(unit, stream, place, which):
        start, size = runs[stream]
        if unit == 0:
            return kept(unit, stream, place, which)
        return uo_ref.at[place, :, pl.ds(start, size)]

    def w_copy(unit, stream, step, number):
        bit = 1 << ((stream + step) % levels)
        place = combine(number)
        there = kept(unit, stream, place, core)
        return remote(
            source(unit, stream) if number == 0 else there,
            there,
            w_send.at[unit, stream, number | bit],
            w_recv.at[unit, stream, number | bit],
            (c, other_index(f, bit)),
        )

    def w_arrival(unit, stream, number):
        block = kept(unit, stream, combine(number), core)
        sems = w_send.at[unit, stream, number], w_recv.at[unit, stream, number]
        return remote(block, block, *sems, (partner, f))

    def w_share(unit, stream, number):
        place = combine(number)
        sems = wc_send.at[unit, stream, number], wc_recv.at[unit, stream, number]
        block = kept(unit, stream, place, core)
        return remote(block, shared(unit, stream, place, core), *sems, (partner, f))

    def w_share_arrival(unit, stream, number):
        block = shared(unit, stream, combine(number), 1 - core)
        sems = wc_send.at[unit, stream, number], wc_recv.at[unit, stream, number]
        return remote(block, block, *sems, (partner, f))

    def held(stream, step):
        numbers = [0]
        for i in range(step):
            bit = 1 << ((stream + i) % levels)
            numbers += [n | bit for n in numbers]
        return numbers

    def v_copy(number):
        return remote(
            v_ref, v_all.at[f], v_send.at[number], v_recv.at[number], (c, combine(number))
        )

    def v_arrival(number):
        return remote(
            v_ref,
            v_all.at[combine(number)],
            v_send.at[number],
            v_recv.at[number],
            (c, combine(number)),
        )

    def x_begin(h):
        for side in range(2):

            @pl.when(x_sends(side, 0))
            def _(side=side):
                x_copy(side, 0, h).start()

        x_own(h).start()

    def x_step(h, s):
        for side in range(2):

            @pl.when(x_gets(side, s))
            def _(side=side):
                x_arrival(side, s, h).wait_recv()
                x_share(side, s, h).start()

            if s + 1 < chips - 1:

                @pl.when(x_sends(side, s + 1))
                def _(side=side):
                    x_copy(side, s + 1, h).start()

    def w_step(unit, step):
        for stream in range(levels):
            bit = 1 << ((stream + step) % levels)
            arrived = [number | bit for number in held(stream, step)]
            for number in arrived:
                w_arrival(unit, stream, number).wait_recv()
            if step + 1 < levels:
                for number in held(stream, step + 1):
                    w_copy(unit, stream, step + 1, number).start()
            for number in arrived:
                w_share(unit, stream, number).start()

    def fetch(unit):
        cols = pl.ds(2 * unit * half, 2 * half)
        return pltpu.make_async_copy(w_ref.at[:, cols], wide.at[:, cols], local.at[3 + unit])

    def w_begin(unit):
        fetch(unit).wait()
        cols = slice(2 * unit * half, 2 * (unit + 1) * half)

        strip = 16 if rows % 16 == 0 else rows

        def body(i, carry):
            at = pl.ds(pl.multiple_of(i * strip, strip), strip)
            w_low[at, cols] = wide[at, cols].astype(BF16)
            return carry

        lax.fori_loop(0, rows // strip, body, 0)
        for stream in range(levels):
            w_copy(unit, stream, 0, 0).start()

    own_up = w_low.at[:, pl.ds(pl.multiple_of((2 + core) * half, 128), half)]
    other_up = w_low.at[:, pl.ds(pl.multiple_of((3 - core) * half, 128), half)]
    kept_here = [
        pltpu.make_async_copy(w_low.at[:, pl.ds(0, 2 * half)], wo_ref.at[f], local.at[0]),
        pltpu.make_async_copy(own_up, um_ref.at[f], local.at[1]),
        pltpu.make_async_copy(other_up, uo_ref.at[f], local.at[2]),
    ]
    v_own = pltpu.make_async_copy(v_ref, v_all.at[f], local.at[5])
    v_out = pltpu.make_async_copy(v_all, vo_ref, local.at[6])
    x_here = pltpu.make_async_copy(x_ref, xo_ref.at[c], local.at[7])

    head_of = [i * ctx + c for i in range(regular)] + [HEADS - 1]
    places = [part * HEADS + head for part in range(3) for head in head_of]

    def window(i):
        start = pl.multiple_of(places[i] // 2 * 128, 128)
        return pltpu.make_async_copy(
            wo_ref.at[:, :, pl.ds(start, 128)], windows.at[i], local.at[8 + i]
        )

    def ready():
        kept_here[0].wait()
        for number in range(1, fsdp):
            v_arrival(number).wait_recv()
            for stream in range(levels):
                w_share_arrival(0, stream, number).wait_recv()
        v_own.wait()
        v_out.start()
        for i in range(len(places)):
            window(i).start()
        for i in range(fsdp):
            v_rows[i * rows : (i + 1) * rows, :] = v_all[i].astype(F32)
        own_w[...] = jnp.zeros_like(own_w)
        for i, place in enumerate(places):
            window(i).wait()
            odd = lax.rem(place, 2)
            for k in range(fsdp):
                both = windows[i, k]
                mine = jnp.where(odd == 0, both[:, :dim], both[:, dim:])
                own_w[k * rows : (k + 1) * rows, i * dim : (i + 1) * dim] = mine
        own_t[...] = own_w[...].T
        for part, column in ((0, 2), (2, 3)):
            for i, head in enumerate(head_of):
                start = (part * owned + i) * dim
                at = pl.ds(pl.multiple_of(head * dim, dim), dim)
                bias[start : start + dim, :] = v_rows[at, column : column + 1]
        start = owned * dim
        bias[start : 2 * start, :] = jnp.zeros((start, 1), F32)

    def project(h, b):
        unit, _ = norm_parts(xo_ref[b, h].astype(F32), 0)
        act = (unit * v_rows[:, 0:1] + v_rows[:, 1:2]).astype(BF16)
        acts[h, b] = act
        pltpu.make_async_copy(acts.at[h, b], act_ref.at[h, b], act_sem.at[h, b]).start()
        value = dot(own_t[...], act)[: 3 * owned * dim] + bias[...]
        qkvs[h, :, pl.ds(pl.multiple_of(b * tok, tok), tok)] = value.astype(BF16)

    def project_own(h):
        x_own_arrival(h).wait_recv()

        def body(i, carry):
            project(h, 2 * z + i)
            return carry

        lax.fori_loop(0, 2, body, 0)

    def project_step(h, s):
        for side in range(2):

            @pl.when(x_gets(side, s))
            def _(side=side):
                x_share_arrival(side, s, h).wait_recv()

        def body(i, carry):
            side = i // 2
            chip = z - (1 - 2 * side) * (s + 1)

            @pl.when((chip >= 0) & (chip < chips))
            def _():
                project(h, 2 * chip + lax.rem(i, 2))

            return carry

        lax.fori_loop(0, 4, body, 0)

    def out_copy(h):
        return pltpu.make_async_copy(qkvs.at[h], qkv_ref.at[h], local.at[8 + len(places) + h])

    plan = []
    block_time = 0.95

    def at(time, work, *values):
        plan.append((time, functools.partial(work, *values)))

    for h in range(slots):
        for s in range(chips - 1):
            at(block_time * (h * (chips - 1) + s + 1), x_step, h, s)
        if h > 0:
            at(block_time * (h * (chips - 1) - 1) + 0.01, x_begin, h)
    time = 0.0
    for unit in range(2):
        for step in range(levels):
            if unit == 0 and step == levels - 1:
                at(time + 0.9, w_begin, 1)
            time += 2.0 ** (step + 1) / levels
            at(time, w_step, unit, step)
        if unit == 0:
            done = max(time, block_time * (chips - 1))
    at(done + 0.3, ready)
    time = done + 0.9
    for h in range(slots):
        for s in range(-1, chips - 1):
            arrived = block_time * (h * (chips - 1) + s + 1)
            time = max(time, arrived + 0.1)
            if s < 0:
                at(time, project_own, h)
            else:
                at(time, project_step, h, s)
            time += 0.2 if s < 0 else 0.4
        at(time, lambda h: out_copy(h).start(), h)

    fetch(0).start()
    fetch(1).start()
    x_here.start()
    x_begin(0)
    for number in range(1, fsdp):
        v_copy(number).start()
    v_own.start()
    w_begin(0)
    kept_here[0].start()
    x_here.wait()
    for _, work in sorted(plan, key=lambda entry: entry[0]):
        work()

    kept_here[1].start()
    kept_here[2].start()
    kept_here[1].wait()
    kept_here[2].wait()
    v_out.wait()
    for number in range(1, fsdp):
        v_copy(number).wait_send()
        for unit in range(2):
            for stream in range(levels):
                w_arrival(unit, stream, number).wait_send()
                w_share(unit, stream, number).wait_send()
                if unit > 0:
                    w_share_arrival(unit, stream, number).wait_recv()
    for h in range(slots):
        x_own(h).wait_send()
        out_copy(h).wait()
        for b in range(ctx):
            pltpu.make_async_copy(acts.at[h, b], act_ref.at[h, b], act_sem.at[h, b]).wait()
        for s in range(chips - 1):
            for side in range(2):

                @pl.when(x_sends(side, s))
                def _(side=side, h=h, s=s):
                    x_copy(side, s, h).wait_send()

                @pl.when(x_gets(side, s))
                def _(side=side, h=h, s=s):
                    x_share(side, s, h).wait_send()


def gather_first(ctx, fsdp, regular, x, w, v):
    slots, width, tok = x.shape
    rows, columns = w.shape
    levels, chips = bits_of(fsdp), ctx // 2
    owned = regular + 1
    feat = 3 * owned * HEAD_DIM
    room = feat + -feat % 128
    anywhere = pl.BlockSpec(memory_space=pl.ANY)
    dma = pltpu.SemaphoreType.DMA
    return pl.pallas_call(
        functools.partial(gather_kernel, ctx, fsdp, regular),
        in_specs=[anywhere, anywhere, pl.BlockSpec(memory_space=pltpu.VMEM)],
        out_specs=[anywhere] * 6,
        out_shape=[
            jax.ShapeDtypeStruct((slots, ctx, width, tok), BF16),
            jax.ShapeDtypeStruct((slots, feat, ctx * tok), BF16),
            jax.ShapeDtypeStruct((fsdp, rows, columns // 2), BF16),
            jax.ShapeDtypeStruct((fsdp, rows, columns // 4), BF16),
            jax.ShapeDtypeStruct((fsdp, rows, columns // 4), BF16),
            jax.ShapeDtypeStruct((fsdp, rows, 128), BF16),
        ],
        scratch_shapes=[
            pltpu.VMEM((ctx, slots, width, tok), BF16),
            pltpu.VMEM((rows, columns), F32),
            pltpu.VMEM((rows, columns), BF16),
            pltpu.VMEM((3 * owned, fsdp, rows, 128), BF16),
            pltpu.VMEM((width, room), BF16),
            pltpu.VMEM((room, width), BF16),
            pltpu.VMEM((fsdp, rows, 128), BF16),
            pltpu.VMEM((width, 128), F32),
            pltpu.VMEM((feat, 1), F32),
            pltpu.VMEM((slots, ctx, width, tok), BF16),
            pltpu.VMEM((slots, feat, ctx * tok), BF16),
            dma((2, chips - 1, slots)),
            dma((2, chips - 1, slots)),
            dma((2, chips, slots)),
            dma((2, chips, slots)),
            dma((2, levels, fsdp)),
            dma((2, levels, fsdp)),
            dma((2, levels, fsdp)),
            dma((2, levels, fsdp)),
            dma((fsdp,)),
            dma((fsdp,)),
            dma((slots, ctx)),
            dma((8 + 3 * owned + slots,)),
        ],
        compiler_params=pltpu.CompilerParams(
            collective_id=0, has_side_effects=True, vmem_limit_bytes=60 * 2**20
        ),
        cost_estimate=pl.CostEstimate(flops=1000, bytes_accessed=1000, transcendentals=0),
    )(x, w, v)


def bits_of(count):
    return max(count.bit_length() - 1, 0)


def flip(count, value):
    return [(i, i ^ value) for i in range(count)]


def pick(array, index, axis):
    return lax.dynamic_index_in_dim(array, index, axis, keepdims=False)


def ordered(bit, mine, other, axis):
    first = jnp.where(bit == 0, mine, other)
    second = jnp.where(bit == 0, other, mine)
    return jnp.concatenate([first, second], axis=axis)


def after(value, *others):
    return lax.optimization_barrier((value, others))[0]


def add_low(mine, swapped):
    return (mine.astype(F32) + swapped.astype(F32)).astype(BF16)


def scatter_fsdp(total):
    return lax.psum_scatter(total, "fsdp", scatter_dimension=0, tiled=True)


def bar_signal(where):
    pl.semaphore_signal(
        pltpu.get_barrier_semaphore(), inc=1, device_id=where, device_id_type=pl.DeviceIdType.MESH
    )


def remote_copy(source, target, send, recv, where):
    return pltpu.make_async_remote_copy(
        src_ref=source,
        dst_ref=target,
        send_sem=send,
        recv_sem=recv,
        device_id=where,
        device_id_type=pl.DeviceIdType.MESH,
    )


def line_gather(chips, c, f, mine, slot, share, sems, core_sems):
    z, core = c // 2, lax.rem(c, 2)
    partner = 2 * z + 1 - core
    send, recv = sems
    core_send, core_recv = core_sems

    def passing(side, s):
        sign = 1 - 2 * side
        chip = z - sign * s
        source = mine if s == 0 else slot(chip)
        return remote_copy(
            source, slot(chip), send.at[side, s], recv.at[side, s], (c + 2 * sign, f)
        )

    def arrival(side, s):
        block = slot(z - (1 - 2 * side) * (s + 1))
        return remote_copy(block, block, send.at[side, s], recv.at[side, s], (partner, f))

    def sends(side, s):
        return (z - s >= 0) & (z < chips - 1) if side == 0 else (z + s < chips) & (z > 0)

    def gets(side, s):
        return z - 1 - s >= 0 if side == 0 else z + 1 + s < chips

    def shared(side, s):
        chip = z - (1 - 2 * side) * (s + 1)
        return remote_copy(
            slot(chip), share(chip), core_send.at[side, s], core_recv.at[side, s], (partner, f)
        )

    def share_arrival(side, s):
        block = share(z - (1 - 2 * side) * (s + 1))
        sems = core_send.at[side, s], core_recv.at[side, s]
        return remote_copy(block, block, *sems, (partner, f))

    own_sems = core_send.at[0, chips - 1], core_recv.at[0, chips - 1]
    own_share = remote_copy(mine, share(z), *own_sems, (partner, f))

    def start():
        for side in range(2):

            @pl.when(sends(side, 0))
            def _(side=side):
                passing(side, 0).start()

        own_share.start()

    def step(s):
        for side in range(2):

            @pl.when(gets(side, s))
            def _(side=side):
                arrival(side, s).wait_recv()
                shared(side, s).start()

            if s + 1 < chips - 1:

                @pl.when(sends(side, s + 1))
                def _(side=side):
                    passing(side, s + 1).start()

    def end():
        own_share.wait_send()
        remote_copy(share(z), share(z), *own_sems, (partner, f)).wait_recv()
        for s in range(chips - 1):
            for side in range(2):

                @pl.when(sends(side, s))
                def _(side=side, s=s):
                    passing(side, s).wait_send()

                @pl.when(gets(side, s))
                def _(side=side, s=s):
                    shared(side, s).wait_send()
                    share_arrival(side, s).wait_recv()

    return start, [functools.partial(step, s) for s in range(chips - 1)], end


def sum_kernel(ctx, fsdp, batches, *refs):
    levels, chips = bits_of(fsdp), ctx // 2
    pieces = refs[0:2]
    group_refs = refs[2:4]
    mine_out, other_out, own_out, last_out = refs[4:8]
    rest = list(refs[8:])
    own_kept = [rest.pop(0) for _ in range(2)]
    own_low, beside = rest.pop(0), rest.pop(0)
    own_sent = [[rest.pop(0) for _ in range(levels)] for _ in range(2)]
    own_got = [[rest.pop(0) for _ in range(levels)] for _ in range(2)]
    z_sent, z_got = rest.pop(0), rest.pop(0)
    op_send, op_recv, zs_send, zs_recv, zg_send, zg_recv = (rest.pop(0) for _ in range(6))
    zc_send, zc_recv, og_send, og_recv, oc_send, oc_recv, far_send, far_recv, local = (
        rest.pop(0) for _ in range(9)
    )
    c, f = lax.axis_index("ctx"), lax.axis_index("fsdp")
    z, core = c // 2, lax.rem(c, 2)
    partner = 2 * z + 1 - core
    far = lax.rem(c + ctx // 2, ctx)
    rows = own_low.shape[0]
    chunk = z_sent.shape[-1]
    width = chunk * chips // 2
    parts = chips // 2
    strip = 16 if rows % 16 == 0 else 8

    def own_bit(bit):
        return lax.rem(f // (1 << bit), 2)

    def strips(work):
        def body(i, carry):
            work(pl.ds(pl.multiple_of(i * strip, strip), strip))
            return carry

        lax.fori_loop(0, rows // strip, body, 0)

    bar_signal((partner, f))
    bar_signal((far, f))
    for bit in range(levels):
        bar_signal((c, other_index(f, 1 << bit)))

    @pl.when(z > 0)
    def _():
        bar_signal((c - 2, f))

    @pl.when(z < chips - 1)
    def _():
        bar_signal((c + 2, f))

    neighbours = (z > 0).astype(jnp.int32) + (z < chips - 1).astype(jnp.int32)
    pl.semaphore_wait(pltpu.get_barrier_semaphore(), levels + 2 + neighbours)

    def order(q):
        return [(q + i) % levels for i in range(levels)]

    def place_of(q, flipped, free):
        bits = order(q)
        first = own_bit(bits[0])
        total = (1 - first if flipped else first) * (1 << bits[0])
        for i, bit in enumerate(bits[1:]):
            total += ((free >> i) & 1) * (1 << bit)
        return total

    def kept_index(q, step, flipped, free):
        bits = order(q)
        total = 0
        for i, bit in enumerate(bits[1:]):
            mine = own_bit(bit)
            if i + 1 < step:
                value = mine
            elif i + 1 == step:
                value = 1 - mine if flipped else mine
            else:
                value = (free >> (i - step)) & 1
            total += value * (1 << i)
        return total

    def across(step, q):
        return (c, other_index(f, 1 << order(q)[step]))

    def own_copy(g, step):
        return remote_copy(
            own_sent[g][step],
            own_got[g][step],
            op_send.at[g, step],
            op_recv.at[g, step],
            across(step, g),
        )

    def own_begin(g):
        for free in range(fsdp // 2):
            there, here = place_of(g, True, free), place_of(g, False, free)

            def work(at, free=free, there=there, here=here):
                own_sent[g][0][free, at, :] = group_refs[g][there, at, :]
                own_kept[g][free, at, :] = group_refs[g][here, at, :].astype(F32)

            strips(work)
        own_copy(g, 0).start()

    def later(step, kept_ref, got_ref, sent_ref, q):
        for free in range(fsdp >> (step + 2)):
            there, here = (kept_index(q, step + 1, flipped, free) for flipped in (True, False))
            mine = own_bit(order(q)[step + 1])
            there_got, here_got = free * 2 + 1 - mine, free * 2 + mine

            def work(at, free=free):
                value = kept_ref[there, at, :] + got_ref[there_got, at, :].astype(F32)
                sent_ref[free, at, :] = value.astype(BF16)
                kept_ref[here, at, :] += got_ref[here_got, at, :].astype(F32)

            strips(work)

    def last(kept_ref, got_ref, q, place):
        def work(at):
            place(at, kept_ref[kept_index(q, levels, False, 0), at, :] + got_ref[0, at, :].astype(F32))

        strips(work)

    def own_step(g, step):
        own_copy(g, step).wait_recv()
        if step + 1 < levels:
            later(step, own_kept[g], own_got[g][step], own_sent[g][step + 1], g)
            own_copy(g, step + 1).start()
            return

        def place(at, value):
            if g == 0:
                beside[at, :] = value
            else:
                own_low[at, :] = value.astype(BF16)

        last(own_kept[g], own_got[g][step], g, place)
        if g == 1:
            for copy in far_copies:
                copy.start()
            own_start()

    head = own_out.shape[2]
    tail = last_out.shape[2]
    far_copies = [
        remote_copy(
            own_low.at[:, pl.ds(head, tail)], last_out.at[1], far_send.at[0], far_recv.at[0], (far, f)
        ),
        pltpu.make_async_copy(own_low.at[:, pl.ds(head, tail)], last_out.at[0], local.at[0]),
        pltpu.make_async_copy(own_low.at[:, pl.ds(0, head)], own_out.at[c], local.at[1]),
    ]
    own_start, own_steps, own_end = line_gather(
        chips,
        c,
        f,
        own_low.at[:, pl.ds(0, head)],
        lambda chip: own_out.at[2 * chip + core],
        lambda chip: own_out.at[2 * chip + core],
        (og_send, og_recv),
        (oc_send, oc_recv),
    )

    def total_of(j, b, at):
        q = j // parts
        start = b * width + (j % parts) * chunk
        stop = start + chunk
        units, room = pieces[q].shape[1], beside.shape[1] // 2
        found = []
        if start < units:
            found.append(pieces[q][at, start : min(stop, units)].astype(F32))
        if stop > units:
            first = max(start, units) - units + q * room
            found.append(beside[at, first : stop - units + q * room])
        return found[0] if len(found) == 1 else jnp.concatenate(found, axis=1)

    def z_copy(side, i, b):
        return remote_copy(
            z_sent.at[side, b, i],
            z_got.at[side, b, i],
            zs_send.at[side, b, i],
            zs_recv.at[side, b, i],
            (c + 2 * (1 - 2 * side), f),
        )

    def z_last(side, chip):
        return chips - 1 - chip if side == 0 else chip

    def z_step(turn, b):
        for chip in range(chips):

            @pl.when(z == chip)
            def _(chip=chip):
                for side in range(2):
                    j_of = (lambda i: chips - 1 - i) if side == 0 else (lambda i: i)
                    begun = chip if side == 0 else chips - 1 - chip
                    i = turn - begun
                    sends = z_last(side, chip)
                    if begun > 0 and 0 <= i <= sends and i < chips - 1:
                        z_copy(side, i, b).wait_recv()
                    if 0 <= i < sends:
                        if i > 0:
                            z_copy(side, i - 1, b).wait_send()

                        def work(at, side=side, i=i, j=j_of(i), begun=begun):
                            value = total_of(j, b, at)
                            if begun > 0:
                                value += z_got[side, b, i, at, :].astype(F32)
                            z_sent[side, b, i, at, :] = value.astype(BF16)

                        strips(work)
                        z_copy(side, i, b).start()

    def chunk_of(ref, chip, b):
        start = pl.multiple_of(b * width + lax.rem(chip, parts) * chunk, 128)
        return ref.at[chip // parts, :, pl.ds(start, chunk)]

    gathers = []
    for b in range(batches):
        gathers.append(
            line_gather(
                chips,
                c,
                f,
                chunk_of(mine_out, z, b),
                lambda chip, b=b: chunk_of(mine_out, chip, b),
                lambda chip, b=b: chunk_of(other_out, chip, b),
                (zg_send.at[:, b], zg_recv.at[:, b]),
                (zc_send.at[:, b], zc_recv.at[:, b]),
            )
        )

    def finish(b):
        for j in range(chips):

            @pl.when(z == j)
            def _(j=j):
                def work(at):
                    value = total_of(j, b, at)
                    if j > 0:
                        value += z_got[0, b, chips - 1 - j, at, :].astype(F32)
                    if j < chips - 1:
                        value += z_got[1, b, j, at, :].astype(F32)
                    start = b * width + (j % parts) * chunk
                    mine_out[j // parts, at, pl.ds(start, chunk)] = value.astype(BF16)

                strips(work)

        gathers[b][0]()

    own_begin(0)
    own_begin(1)
    waiting = []

    def one_more():
        if waiting:
            waiting.pop(0)()

    def batch(b):
        for i in range(chips):
            z_step(i, b)
            one_more()
        finish(b)
        waiting.extend(gathers[b][1])

    for b in range(batches - 1):
        batch(b)
    for step in range(levels):
        own_step(0, step)
        own_step(1, step)
        one_more()
    waiting.extend(own_steps)
    batch(batches - 1)
    while waiting:
        one_more()

    far_copies[0].wait()
    far_copies[1].wait()
    far_copies[2].wait()
    own_end()
    for step in range(levels):
        own_copy(0, step).wait_send()
        own_copy(1, step).wait_send()
    for b in range(batches):
        gathers[b][2]()
        for chip in range(chips):

            @pl.when(z == chip)
            def _(chip=chip, b=b):
                for side in range(2):
                    if z_last(side, chip):
                        z_copy(side, z_last(side, chip) - 1, b).wait_send()


def sum_grads(ctx, fsdp, pieces, out, own, head):
    levels, chips = bits_of(fsdp), ctx // 2
    rows, units = pieces[0].shape
    beside, own_width = out.shape[-1], own.shape[-1]
    whole = units + beside // 2
    batches = max(n for n in range(1, 3) if whole % n == 0 and 2 * whole // n % (chips * 128) == 0)
    width = whole // batches
    chunk = 2 * width // chips
    vmem = pl.BlockSpec(memory_space=pltpu.VMEM)
    dma = pltpu.SemaphoreType.DMA
    steps = [fsdp >> (i + 1) for i in range(levels)]
    result = jax.ShapeDtypeStruct((2, rows, whole), BF16)
    mine, other, own_all, last = pl.pallas_call(
        functools.partial(sum_kernel, ctx, fsdp, batches),
        in_specs=[vmem] * 4,
        out_specs=[vmem] * 4,
        out_shape=[
            result,
            result,
            jax.ShapeDtypeStruct((ctx, rows, head), BF16),
            jax.ShapeDtypeStruct((2, rows, own_width - head), BF16),
        ],
        scratch_shapes=[
            pltpu.VMEM((fsdp // 2, rows, beside), F32),
            pltpu.VMEM((fsdp // 2, rows, own_width), F32),
            pltpu.VMEM((rows, own_width), BF16),
            pltpu.VMEM((rows, beside), F32),
        ]
        + [pltpu.VMEM((n, rows, size), BF16) for size in (beside, own_width) * 2 for n in steps]
        + [pltpu.VMEM((2, batches, chips - 1, rows, chunk), BF16)] * 2
        + [dma((2, levels))] * 2
        + [dma((2, batches, chips - 1))] * 4
        + [dma((2, batches, chips))] * 2
        + [dma((2, chips - 1))] * 2
        + [dma((2, chips))] * 2
        + [dma((1,))] * 2
        + [dma((6,))],
        compiler_params=pltpu.CompilerParams(
            collective_id=1, has_side_effects=True, vmem_limit_bytes=60 * 2**20
        ),
        cost_estimate=pl.CostEstimate(flops=1000, bytes_accessed=1000, transcendentals=0),
    )(*pieces, out, own)

    return mine, other, own_all, last


def swap_cores(mine, ctx):
    return lax.ppermute(mine, "ctx", flip(ctx, 1))


def norm_parts(rows, axis):
    middle = jnp.mean(rows, axis=axis, keepdims=True)
    centred = rows - middle
    spread = jnp.mean(centred * centred, axis=axis, keepdims=True)
    inverse = lax.rsqrt(spread + NORM_EPS)
    return centred * inverse, inverse


def norm_back(grad, unit, inverse, gain):
    inner = grad * gain
    mean_inner = jnp.mean(inner, axis=1, keepdims=True)
    mean_cross = jnp.mean(inner * unit, axis=1, keepdims=True)
    rows = inverse * (inner - mean_inner - unit * mean_cross)
    return rows, jnp.sum(grad * unit, axis=(0, 2)), jnp.sum(grad, axis=(0, 2))


def adamw(weight, first, second, grad, rate, decay):
    moment = BETA_ONE * first.astype(F32) + (1.0 - BETA_ONE) * grad
    square = BETA_TWO * second + (1.0 - BETA_TWO) * grad * grad
    corrected = moment / (1.0 - BETA_ONE**STEP)
    scaled = square / (1.0 - BETA_TWO**STEP)
    new_weight = weight - rate * (corrected / (jnp.sqrt(scaled) + ADAM_EPS) + decay * weight)
    return (moment, square, new_weight)


def update_kernel(units, regular, *refs):
    (w, first, second, dw, dfirst, dsecond, own, last, mine, other) = refs[:10]
    outs = refs[10:]
    core = lax.rem(lax.axis_index("ctx"), 2)
    width = (w.shape[1] - 2 * units) // 4
    quarter = width // 4
    ctx = own.shape[0]
    dim = HEAD_DIM

    def halves(q, start, size):
        here = mine[q, :, start : start + size].astype(F32)
        there = other[q, :, start : start + size].astype(F32)
        return jnp.where(core == 0, here, there), jnp.where(core == 0, there, here)

    def both(q, start, size):
        return jnp.concatenate(halves(q, start, size), axis=1)

    heads = []
    for part in range(3):
        for i in range(regular):
            for c in range(ctx):
                column = (i * 3 + part) * dim
                heads.append(own[c, :, column : column + dim].astype(F32))
        column = part * dim
        heads.append(
            last[0, :, column : column + dim].astype(F32)
            + last[1, :, column : column + dim].astype(F32)
        )
    out = [halves(q, units, quarter) for q in range(2)]
    heads += [out[0][0], out[1][0], out[0][1], out[1][1]]
    grad = jnp.concatenate(heads, axis=1)

    def put(targets, cols, values):
        for target, value in zip(targets, values):
            target[:, cols] = value

    cols = slice(0, 4 * width)
    put(outs[:3], cols, adamw(w[:, cols], first[:, cols], second[:, cols], grad, 0.03, 0.1))
    cols = slice(4 * width, w.shape[1])
    grad = both(0, 0, units)
    put(outs[:3], cols, adamw(w[:, cols], first[:, cols], second[:, cols], grad, 0.03, 0.1))
    grad = both(1, 0, units)
    put(outs[3:], slice(None), adamw(dw[...], dfirst[...], dsecond[...], grad, 0.02, 0.1))


def update(rows_state, down_state, own, last, mine, other, units, regular):
    rows = rows_state[0].shape[0]
    strip = 16 if rows % 16 == 0 else 8

    def flat(array):
        return pl.BlockSpec((strip, array.shape[1]), lambda i: (i, 0))

    def deep(array):
        return pl.BlockSpec((array.shape[0], strip, array.shape[2]), lambda i: (0, i, 0))

    states, sums = [*rows_state, *down_state], [own, last, mine, other]
    results = [rows_state[0]] * 3 + [down_state[0]] * 3
    return pl.pallas_call(
        functools.partial(update_kernel, units, regular),
        grid=(rows // strip,),
        in_specs=[flat(a) for a in states] + [deep(a) for a in sums],
        out_specs=[flat(a) for a in results],
        out_shape=[jax.ShapeDtypeStruct(a.shape, F32) for a in results],
        compiler_params=pltpu.CompilerParams(vmem_limit_bytes=56 * 2**20),
        cost_estimate=pl.CostEstimate(flops=1000, bytes_accessed=1000, transcendentals=0),
    )(*states, *sums)


def body(
    ctx,
    fsdp,
    tokens,
    cotangent,
    lengths,
    w_rows,
    rows_first,
    rows_second,
    w_down,
    down_first,
    down_second,
    vectors,
    vec_first,
    vec_second,
):
    tok, slots, width = tokens.shape
    dim = HEAD_DIM
    regular = HEADS // ctx
    owned = regular + 1
    share = width // fsdp
    c = lax.axis_index("ctx")
    core = c % 2
    late = (c >= ctx // 2).astype(jnp.int32)
    half = FF // 2

    def my_half(array):
        return lax.dynamic_slice_in_dim(array, core * half, half, 1)

    x_low = tokens.transpose(1, 2, 0)
    vec_part = jnp.pad(vectors.astype(BF16).T, ((0, 0), (0, 128 - vectors.shape[0])))
    act_all, qkv_all, head_w, up_mine, up_other, vec_low = gather_first(
        ctx, fsdp, regular, x_low, w_rows, vec_part
    )
    head_w = head_w.reshape(width, 4 * width)
    up_mine, up_other = up_mine.reshape(width, half), up_other.reshape(width, half)
    vec_low = vec_low.reshape(width, 128)
    down_mine, vec_low = lax.optimization_barrier((my_half(w_down.T).astype(BF16), vec_low))
    down_mine = lax.all_gather(down_mine, "fsdp", axis=0, tiled=True)
    vec = [vec_low[:, i : i + 1].astype(F32) for i in range(12)]
    up_bias = vec_low[:, 8:12].T.astype(F32).reshape(1, FF)

    qkv_all = qkv_all.reshape(slots, 3, owned, dim, ctx * tok)
    far = (c + ctx // 2) % ctx

    def to_rows(array, *gate):
        feat = array.shape[2]
        got = lax.all_to_all(array, "ctx", 0, 0)
        got = after(got, *gate) if gate else got
        return got.transpose(1, 0, 2, 3).reshape(regular * ctx, feat, tok)

    def last_to_rows(array, *gate):
        mine = pick(array, c, 0)
        got = lax.ppermute(pick(array, far, 0), "ctx", flip(ctx, ctx // 2))
        got = after(got, *gate) if gate else got
        return jnp.where(late == 0, mine, got), jnp.where(late == 0, got, mine)

    def to_send(array):
        return array.reshape(regular, ctx, dim, tok).transpose(1, 0, 2, 3)

    def attend_slot(s, *gate):
        lens = after(jnp.repeat(lengths[s : s + 1], regular), *gate)
        return (lens, qkv_all, s, *attend(lens, qkv_all, s, tok))

    results = [attend_slot(0)]
    results.append(attend_slot(1, results[0][3]))
    rows = [to_rows(results[0][4])]
    last_qkv = jnp.where(late == 0, qkv_all[:1, :, regular:], qkv_all[1:, :, regular:])
    last_len = after(lax.dynamic_slice_in_dim(lengths, late, 1, 0), results[1][3], rows[0])
    results.append((last_len, last_qkv, 0, *attend(last_len, last_qkv, 0, tok)))
    rows.append(to_rows(results[1][4]))
    down_mine = after(down_mine, results[2][3], *rows)
    down_other = swap_cores(down_mine, ctx)
    last_rows = last_to_rows(results[2][4])
    att = [jnp.concatenate([rows[s], last_rows[s]]).reshape(width, tok) for s in range(slots)]
    att = jnp.stack(att)

    x = x_low.astype(F32)
    out_w = head_w[:, 3 * width :]
    mid = x + jnp.einsum("de,sdt->set", out_w, att, preferred_element_type=F32) + vec[4]
    unit_two, inverse_two = norm_parts(mid, 1)
    act_two = (unit_two * vec[5] + vec[6]).astype(BF16)

    pos = c * tok + jnp.arange(tok, dtype=jnp.int32)
    valid = pos[None, None, :] < lengths[:, None, None]
    g_low = jnp.where(valid, cotangent.transpose(1, 2, 0), jnp.zeros((), BF16))
    g = g_low.astype(F32)

    bias_mine = lax.dynamic_slice_in_dim(up_bias, core * half, half, 1)
    bias_other = lax.dynamic_slice_in_dim(up_bias, (1 - core) * half, half, 1)
    y_other, ga_other, dup_other, ddown_other, db_other = mlp(
        act_two, g_low, up_other, down_other, bias_other
    )
    y_mine, ga_mine, dup_mine, ddown_mine, db_mine = mlp(
        act_two, g_low, up_mine, down_mine, bias_mine
    )
    output = (mid + (y_mine + y_other + vec[7])).astype(BF16).transpose(2, 0, 1)

    up_swapped, down_swapped = swap_cores(dup_other, ctx), swap_cores(ddown_other, ctx)

    up_total = add_low(dup_mine, up_swapped)
    up_part = scatter_fsdp(up_total)
    ga_mine = after(ga_mine, up_total)
    grad_mid, gain_two, shift_two = norm_back(ga_mine + ga_other, unit_two, inverse_two, vec[5])
    grad_mid = g + grad_mid
    grad_attn = grad_mid.astype(BF16)
    grad_att = jnp.einsum("de,set->sdt", out_w, grad_attn, preferred_element_type=F32).astype(BF16)
    grad_att = grad_att.reshape(slots, HEADS, dim, tok)
    first_send = to_send(grad_att[0, :-1])
    grad_attn_later = after(grad_attn, first_send)
    last = jnp.repeat(grad_att[:, -1], ctx // slots, axis=0)[:, None]
    first_pairs = lax.all_to_all(first_send, "ctx", 0, 0)
    down_part = scatter_fsdp(add_low(after(ddown_mine, first_pairs), down_swapped))
    other_pairs = lax.all_to_all(
        after(jnp.concatenate([to_send(grad_att[1, :-1]), last], axis=1), first_pairs), "ctx", 0, 0
    )

    quarter = width // 4
    spread = jnp.pad(
        grad_attn_later.reshape(slots, 4, quarter, tok),
        ((0, 0), (0, 0), (0, -quarter % 128), (0, 0)),
    )
    out_grad = jnp.einsum("sdt,sket->kde", att, spread, preferred_element_type=F32).astype(BF16)
    out_grad = out_grad.reshape(2, 2, fsdp, share, spread.shape[2])

    def out_half(which):
        return pick(out_grad, which, 0).reshape(2, width, spread.shape[2])

    out_mine, out_swapped = out_half(core), swap_cores(out_half(1 - core), ctx)
    out_total = add_low(out_mine, out_swapped)
    first_heads = attend_back(*results[0][:4], results[0][5], first_pairs)
    last_heads = attend_back(
        *results[2][:4], results[2][5], after(other_pairs[:, -1:], first_heads)
    )
    other_heads = attend_back(
        *results[1][:4], results[1][5], after(other_pairs[:, :-1], last_heads, up_part)
    )
    grad_heads = [first_heads, other_heads, last_heads]

    feat = 3 * dim
    own_sum = own_grad(
        late,
        act_all,
        grad_heads[0].reshape(ctx, regular * feat, tok),
        grad_heads[1].reshape(ctx, regular * feat, tok),
        grad_heads[2].reshape(ctx, feat, tok),
    )
    own_sum = own_sum.astype(BF16)
    own_sum = jnp.concatenate(
        [
            jnp.pad(part, ((0, 0), (0, -part.shape[1] % 128)))
            for part in (own_sum[:, : regular * feat], own_sum[:, regular * feat :])
        ],
        axis=1,
    )
    head_columns = regular * feat + -regular * feat % 128
    blocks = (fsdp, share)
    sum_mine, sum_other, own_all, last = sum_grads(
        ctx,
        fsdp,
        [up_part, down_part],
        jnp.concatenate([out_total[0], out_total[1]], axis=1).reshape(*blocks, -1),
        own_sum.reshape(*blocks, own_sum.shape[1]),
        head_columns,
    )
    first_rows, other_rows = to_rows(first_heads), to_rows(other_heads, sum_mine)
    last_rows = last_to_rows(last_heads, sum_mine)
    grad_qkv = []
    for s, rows in enumerate((first_rows, other_rows)):
        rows = jnp.concatenate([rows, last_rows[s]])
        rows = rows.reshape(HEADS, 3, dim, tok).transpose(1, 0, 2, 3)
        grad_qkv.append(rows.reshape(3 * width, tok))
    grad_qkv = jnp.stack(grad_qkv)
    grad_one = jnp.einsum(
        "de,set->sdt", head_w[:, : 3 * width], grad_qkv, preferred_element_type=F32
    )

    unit_one, inverse_one = norm_parts(x, 1)
    grad_in, gain_one, shift_one = norm_back(grad_one, unit_one, inverse_one, vec[0])
    grad_tokens = (grad_mid + grad_in).astype(BF16)

    bias_qkv = jnp.sum(grad_qkv.astype(F32), axis=(0, 2))
    vec_grad = jnp.stack(
        [
            gain_one,
            shift_one,
            bias_qkv[:width],
            bias_qkv[2 * width :],
            jnp.sum(grad_attn.astype(F32), axis=(0, 2)),
            gain_two,
            shift_two,
            jnp.sum(g, axis=(0, 2)),
        ]
    )
    bias_up = ordered(core, db_mine, db_other, 1).reshape(4, width)
    vec_grad = jnp.concatenate([vec_grad, bias_up], axis=0).reshape(12, fsdp, share)
    f = lax.axis_index("fsdp")
    vec_sum = pick(vec_grad, f, 1)
    for value in range(1, fsdp):
        vec_sum = vec_sum + lax.ppermute(pick(vec_grad, f ^ value, 1), "fsdp", flip(fsdp, value))
    for level in range(bits_of(ctx)):
        vec_sum = vec_sum + lax.ppermute(vec_sum, "ctx", flip(ctx, 2**level))

    rows_state = (w_rows, rows_first, rows_second)
    down_state = (w_down.T, down_first.T, down_second.T)
    updated = update(
        rows_state, down_state, own_all, last, sum_mine, sum_other, half, regular
    )
    rows_out, down_out = updated[:3], tuple(part.T for part in updated[3:])
    vec_out = adamw(vectors, vec_first, vec_second, vec_sum, 0.3, 0.0)
    return (output, grad_tokens.transpose(2, 0, 1), *rows_out, *down_out, *vec_out)


def solution(mesh):
    placed = (
        P("ctx", "fsdp", None),
        P("ctx", "fsdp", None),
        P("fsdp"),
        P("fsdp", None),
        P("fsdp", None),
        P("fsdp", None),
        P(None, "fsdp"),
        P(None, "fsdp"),
        P(None, "fsdp"),
        P(None, "fsdp"),
        P(None, "fsdp"),
        P(None, "fsdp"),
    )
    return jax.shard_map(
        functools.partial(body, mesh.shape["ctx"], mesh.shape["fsdp"]),
        mesh=mesh,
        in_specs=placed,
        out_specs=placed[:2] + placed[3:6] + placed[6:9] + placed[9:12],
        check_vma=False,
    )
```

```python
import functools
import math

import jax
import jax.numpy as jnp
from jax import lax
from jax.experimental import pallas as pl
from jax.experimental.pallas import tpu as pltpu
from jax.sharding import PartitionSpec as P

HEADS = 17
HEAD_DIM = 64
FF = 4352
STEP = 10

MASKED = -1e30
NORM_EPS = 1e-05
BETA_ONE = 0.9
BETA_TWO = 0.95
ADAM_EPS = 1e-08
BF16 = jnp.bfloat16
F32 = jnp.float32


def dot(left, right, dims=((1,), (0,))):
    return lax.dot_general(left, right, (dims, ((), ())), preferred_element_type=F32)


def padded(top, rows, width):
    row = lax.broadcasted_iota(jnp.int32, (rows, width), 0)
    out = jnp.zeros((rows, width), F32)
    for index, value in enumerate(top):
        out = jnp.where(row == index, value, out)
    return out.astype(BF16)


def key_rows(lens_ref, key, length):
    pos = lax.broadcasted_iota(jnp.int32, (1, length), 1)
    bias = jnp.where(pos < lens_ref[0], 0.0, MASKED)
    one = jnp.ones((1, length), F32)
    extra = padded([bias, one, one, one], HEAD_DIM, length)
    return jnp.concatenate([key, extra], axis=0).T


def causal(block):
    key = lax.broadcasted_iota(jnp.int32, (block, block), 0)
    query = lax.broadcasted_iota(jnp.int32, (block, block), 1)
    return key <= query


def attend_kernel(block, lens_ref, q_ref, k_ref, v_ref, o_ref, low_ref, lse_ref, keys):
    heads, _, length = k_ref.shape[2:]
    tok = low_ref.shape[-1]
    step = pl.program_id(0)

    @pl.when(step == 0)
    def _():
        for h in range(heads):
            keys[h] = key_rows(lens_ref, k_ref[0, 0, h], length)

    one_row = padded([jnp.ones((1, block), F32)], HEAD_DIM, block)
    queries = []
    for h in range(heads):
        query = (q_ref[0, 0, h].astype(F32) * (1.0 / math.sqrt(HEAD_DIM))).astype(BF16)
        queries.append(jnp.concatenate([query, one_row], axis=0))

    def one(index, states, mask):
        start = pl.multiple_of(index * block, block)
        all_scores = [dot(keys[h, pl.ds(start, block), :], queries[h]) for h in range(heads)]
        results = []
        for h, (top, total, accum) in enumerate(states):
            scores = all_scores[h]
            if mask is not None:
                scores = jnp.where(mask, scores, MASKED)
            new_top = jnp.maximum(top, jnp.max(scores, axis=0, keepdims=True))
            weights = jnp.exp(scores - new_top)
            factor = jnp.exp(top - new_top)
            total = total * factor + jnp.sum(weights, axis=0, keepdims=True)
            value = v_ref[0, 0, h, :, pl.ds(start, block)]
            accum = accum * factor + dot(value, weights.astype(BF16))
            results.append((new_top, total, accum))
        return tuple(results)

    state = (
        jnp.full((1, block), MASKED, F32),
        jnp.zeros((1, block), F32),
        jnp.zeros((HEAD_DIM, block), F32),
    )
    states = lax.fori_loop(0, step, lambda i, s: one(i, s, None), (state,) * heads)
    states = one(step, states, causal(block))
    for h, (top, total, accum) in enumerate(states):
        result = accum / total
        o_ref[h] = result
        for i in range(block // tok):
            low_ref[i, h] = result[:, i * tok : (i + 1) * tok].astype(BF16)
        lse_ref[h] = top + jnp.log(total)


def head_specs(slot, heads, dim, length, block):
    def whole(part):
        return pl.BlockSpec((1, 1, heads, dim, length), lambda i, lens: (slot, part, 0, 0, 0))

    def piece(part):
        return pl.BlockSpec((1, 1, heads, dim, block), lambda i, lens: (slot, part, 0, 0, i))

    return whole, piece


def attend(lens, qkv, slot, tok):
    dim, length = qkv.shape[3:]
    pairs = lens.shape[0]
    block = math.gcd(length, 512)
    whole, piece = head_specs(slot, pairs, dim, length, block)
    return pl.pallas_call(
        functools.partial(attend_kernel, block),
        grid_spec=pltpu.PrefetchScalarGridSpec(
            num_scalar_prefetch=1,
            grid=(length // block,),
            in_specs=[piece(0), whole(1), whole(2)],
            out_specs=[
                pl.BlockSpec((pairs, dim, block), lambda i, lens: (0, 0, i)),
                pl.BlockSpec((block // tok, pairs, dim, tok), lambda i, lens: (i, 0, 0, 0)),
                pl.BlockSpec((pairs, 1, block), lambda i, lens: (0, 0, i)),
            ],
            scratch_shapes=[pltpu.VMEM((pairs, length, 2 * dim), BF16)],
        ),
        out_shape=[
            jax.ShapeDtypeStruct((pairs, dim, length), F32),
            jax.ShapeDtypeStruct((length // tok, pairs, dim, tok), BF16),
            jax.ShapeDtypeStruct((pairs, 1, length), F32),
        ],
        compiler_params=pltpu.CompilerParams(
            vmem_limit_bytes=48 * 2**20
        ),
        cost_estimate=pl.CostEstimate(flops=1000, bytes_accessed=1000, transcendentals=0),
    )(lens, qkv, qkv, qkv)


def split_three(value):
    first = value.astype(BF16).astype(F32)
    second = (value - first).astype(BF16).astype(F32)
    third = (value - first - second).astype(BF16).astype(F32)
    return [-first, -second, -third]


def attend_back_kernel(
    block,
    lens_ref,
    q_ref,
    k_ref,
    v_ref,
    o_ref,
    lse_ref,
    grad_ref,
    out_ref,
    keys,
    values,
    queries,
    grads,
    total,
):
    heads, dim, length = k_ref.shape[2:]
    tok = grad_ref.shape[-1]
    count = length // block
    step = pl.program_id(0)
    scale = 1.0 / math.sqrt(HEAD_DIM)

    @pl.when(step == 0)
    def _():
        one = jnp.ones((1, length), F32)
        for h in range(heads):
            keys[h] = key_rows(lens_ref, k_ref[0, 0, h], length)
            extra = padded([one, one, one], dim, length)
            values[h] = jnp.concatenate([v_ref[0, 0, h], extra], axis=0).T
            queries[h, 0:dim, :] = (q_ref[0, 0, h].astype(F32) * scale).astype(BF16)
            queries[h, dim:, :] = padded([one] + split_three(lse_ref[h]), dim, length)
            for i in range(length // tok):
                grads[h, 0:dim, i * tok : (i + 1) * tok] = grad_ref[i, h]
            delta = jnp.sum(grads[h, 0:dim, :].astype(F32) * o_ref[h], axis=0, keepdims=True)
            grads[h, dim:, :] = padded(split_three(delta), dim, length)
        total[...] = jnp.zeros_like(total)

    mine = pl.ds(pl.multiple_of(step * block, block), block)

    def one(index, states, mask):
        cols = pl.ds(pl.multiple_of(index * block, block), block)
        all_scores = [dot(keys[h, mine, :], queries[h, :, cols]) for h in range(heads)]
        results = []
        for h, (dk, dv) in enumerate(states):
            scores = all_scores[h]
            if mask is not None:
                scores = jnp.where(mask, scores, MASKED)
            probs = jnp.exp(scores)
            grad_scores = (probs * dot(values[h, mine, :], grads[h, :, cols])).astype(BF16)
            probs = probs.astype(BF16)
            dv = dv + dot(grads[h, 0:dim, cols], probs, ((1,), (1,)))
            dk = dk + dot(queries[h, 0:dim, cols], grad_scores, ((1,), (1,)))
            total[h, :, cols] += dot(k_ref[0, 0, h, :, mine], grad_scores)
            results.append((dk, dv))
        return tuple(results)

    zero = jnp.zeros((dim, block), F32)
    states = one(step, ((zero, zero),) * heads, causal(block))
    states = lax.fori_loop(step + 1, count, lambda i, s: one(i, s, None), states)
    for h, (dk, dv) in enumerate(states):
        dq = total[h, :, mine] * scale
        for i in range(block // tok):
            cols = slice(i * tok, (i + 1) * tok)
            out_ref[i, h, 0:dim] = dq[:, cols].astype(BF16)
            out_ref[i, h, dim : 2 * dim] = dk[:, cols].astype(BF16)
            out_ref[i, h, 2 * dim :] = dv[:, cols].astype(BF16)


def attend_back(lens, qkv, slot, out, lse, grad):
    dim, length = qkv.shape[3:]
    pairs, tok = lens.shape[0], grad.shape[-1]
    ctx = length // tok
    block = math.gcd(length, 512)
    whole, _ = head_specs(slot, pairs, dim, length, block)
    return pl.pallas_call(
        functools.partial(attend_back_kernel, block),
        grid_spec=pltpu.PrefetchScalarGridSpec(
            num_scalar_prefetch=1,
            grid=(length // block,),
            in_specs=[
                whole(0),
                whole(1),
                whole(2),
                pl.BlockSpec((pairs, dim, length), lambda i, lens: (0, 0, 0)),
                pl.BlockSpec((pairs, 1, length), lambda i, lens: (0, 0, 0)),
                pl.BlockSpec((ctx, pairs, dim, tok), lambda i, lens: (0, 0, 0, 0)),
            ],
            out_specs=pl.BlockSpec(
                (block // tok, pairs, 3 * dim, tok), lambda i, lens: (i, 0, 0, 0)
            ),
            scratch_shapes=[
                pltpu.VMEM((pairs, length, 2 * dim), BF16),
                pltpu.VMEM((pairs, length, 2 * dim), BF16),
                pltpu.VMEM((pairs, 2 * dim, length), BF16),
                pltpu.VMEM((pairs, 2 * dim, length), BF16),
                pltpu.VMEM((pairs, dim, length), F32),
            ],
        ),
        out_shape=jax.ShapeDtypeStruct((ctx, pairs, 3 * dim, tok), BF16),
        compiler_params=pltpu.CompilerParams(
            vmem_limit_bytes=48 * 2**20
        ),
        cost_estimate=pl.CostEstimate(flops=1000, bytes_accessed=1000, transcendentals=0),
    )(lens, qkv, qkv, qkv, out, lse, grad)


def own_grad_kernel(late_ref, first_ref, second_ref, first_grad_ref, second_grad_ref, last_grad_ref, out_ref, total):
    step = pl.program_id(0)
    nt = ((1,), (1,))
    first, second = first_ref[0, 0], second_ref[0, 0]
    head = dot(first, first_grad_ref[0], nt) + dot(second, second_grad_ref[0], nt)
    last = dot(jnp.where(late_ref[0] == 0, first, second), last_grad_ref[0], nt)
    part = jnp.concatenate([head, last], axis=1)

    @pl.when(step == 0)
    def _():
        total[...] = part

    @pl.when(step > 0)
    def _():
        total[...] += part

    @pl.when(step == pl.num_programs(0) - 1)
    def _():
        out_ref[...] = total[...]


def own_grad(late, act, first_grad, second_grad, last_grad):
    _, ctx, width, tok = act.shape
    feat, last = first_grad.shape[1], last_grad.shape[1]

    def block(rows):
        return pl.BlockSpec((1, rows, tok), lambda i, late: (i, 0, 0))

    def of(slot):
        return pl.BlockSpec((1, 1, width, tok), lambda i, late: (slot, i, 0, 0))

    return pl.pallas_call(
        own_grad_kernel,
        grid_spec=pltpu.PrefetchScalarGridSpec(
            num_scalar_prefetch=1,
            grid=(ctx,),
            in_specs=[of(0), of(1), block(feat), block(feat), block(last)],
            out_specs=pl.BlockSpec((width, feat + last), lambda i, late: (0, 0)),
            scratch_shapes=[pltpu.VMEM((width, feat + last), F32)],
        ),
        out_shape=jax.ShapeDtypeStruct((width, feat + last), F32),
        compiler_params=pltpu.CompilerParams(vmem_limit_bytes=48 * 2**20),
        cost_estimate=pl.CostEstimate(flops=1000, bytes_accessed=1000, transcendentals=0),
    )(late[None], act, act, first_grad, second_grad, last_grad)


def mlp_kernel(
    width,
    a_ref,
    g_ref,
    up_ref,
    down_ref,
    bias_ref,
    y_ref,
    ga_ref,
    dup_ref,
    ddown_ref,
    db_ref,
    a_rows,
    g_rows,
):
    step = pl.program_id(0)
    slots, _, tok = a_ref.shape
    block = up_ref.shape[1]

    @pl.when(step == 0)
    def _():
        for s in range(slots):
            a_rows[s * tok : (s + 1) * tok, :] = a_ref[s].T
            g_rows[s * tok : (s + 1) * tok, :] = g_ref[s].T
        y_ref[...] = jnp.zeros_like(y_ref)
        ga_ref[...] = jnp.zeros_like(ga_ref)

    def run(size):
        up = up_ref[:, :size]
        down = down_ref[:, :size]
        pre = dot(a_rows[...], up) + bias_ref[:, :size]
        cdf = 0.5 * (1.0 + lax.erf(pre * math.sqrt(0.5)))
        hidden = (pre * cdf).astype(BF16)
        slope = cdf + pre * jnp.exp(-0.5 * pre * pre) * (1.0 / math.sqrt(2.0 * math.pi))
        grad = (dot(g_rows[...], down) * slope).astype(BF16)
        db_ref[:, :size] = jnp.sum(grad.astype(F32), axis=0, keepdims=True)
        nt = ((1,), (1,))
        for s in range(slots):
            rows = slice(s * tok, (s + 1) * tok)
            y_ref[s] += dot(down, hidden[rows], nt)
            ga_ref[s] += dot(up, grad[rows], nt)
        dup = sum(dot(a_ref[s], grad[s * tok : (s + 1) * tok]) for s in range(slots))
        dup_ref[:, :size] = dup.astype(dup_ref.dtype)
        ddown = sum(dot(g_ref[s], hidden[s * tok : (s + 1) * tok]) for s in range(slots))
        ddown_ref[:, :size] = ddown.astype(ddown_ref.dtype)

    full = width // block

    @pl.when(step < full)
    def _():
        run(block)

    if width % block:

        @pl.when(step == full)
        def _():
            run(width % block)


def mlp(act, grad, up, down, bias):
    slots, width, tok = act.shape
    units = up.shape[1]
    block = 512

    def fixed(shape):
        return pl.BlockSpec(shape, lambda i: (0,) * len(shape))

    cols = pl.BlockSpec((width, block), lambda i: (0, i))
    line = pl.BlockSpec((1, block), lambda i: (0, i))
    total = jax.ShapeDtypeStruct((slots, width, tok), F32)
    grads = jax.ShapeDtypeStruct((width, units), BF16)
    return pl.pallas_call(
        functools.partial(mlp_kernel, units),
        grid=(pl.cdiv(units, block),),
        in_specs=[fixed(act.shape), fixed(act.shape), cols, cols, line],
        out_specs=[fixed(act.shape), fixed(act.shape), cols, cols, line],
        out_shape=[total, total, grads, grads, jax.ShapeDtypeStruct((1, units), F32)],
        scratch_shapes=[pltpu.VMEM((slots * tok, width), BF16)] * 2,
        compiler_params=pltpu.CompilerParams(vmem_limit_bytes=56 * 2**20),
        cost_estimate=pl.CostEstimate(flops=1000, bytes_accessed=1000, transcendentals=0),
    )(act, grad, up, down, bias)


def other_index(index, bit):
    return index + bit * (1 - 2 * lax.rem(index // bit, 2))


def split_columns(start, size, count):
    tiles = size // 128
    cuts = [start + 128 * (-(-tiles * i // count)) for i in range(count)] + [start + size]
    return [(cuts[i], cuts[i + 1] - cuts[i]) for i in range(count)]


def gather_kernel(
    ctx,
    fsdp,
    regular,
    x_ref,
    w_ref,
    v_ref,
    act_ref,
    qkv_ref,
    wo_ref,
    um_ref,
    uo_ref,
    vo_ref,
    xo_ref,
    wide,
    w_low,
    windows,
    own_w,
    own_t,
    v_all,
    v_rows,
    bias,
    acts,
    qkvs,
    x_send,
    x_recv,
    xc_send,
    xc_recv,
    w_send,
    w_recv,
    wc_send,
    wc_recv,
    v_send,
    v_recv,
    act_sem,
    local,
):
    c, f = lax.axis_index("ctx"), lax.axis_index("fsdp")
    chips = ctx // 2
    z, core = c // 2, lax.rem(c, 2)
    partner = 2 * z + 1 - core
    slots, width, tok = x_ref.shape
    rows = w_ref.shape[0]
    dim = HEAD_DIM
    owned = regular + 1
    levels = bits_of(fsdp)
    half = um_ref.shape[2]

    def combine(number):
        place = f
        for bit in range(levels):
            if number & (1 << bit):
                place = other_index(place, 1 << bit)
        return place

    barrier = pltpu.get_barrier_semaphore()

    def greet(where):
        pl.semaphore_signal(barrier, inc=1, device_id=where, device_id_type=pl.DeviceIdType.MESH)

    greet((partner, f))
    for number in range(1, fsdp):
        greet((c, combine(number)))

    @pl.when(z > 0)
    def _():
        greet((c - 2, f))

    @pl.when(z < chips - 1)
    def _():
        greet((c + 2, f))

    beside = (z > 0).astype(jnp.int32) + (z < chips - 1).astype(jnp.int32)
    pl.semaphore_wait(barrier, fsdp + beside)

    def remote(source, target, send, recv, where):
        return pltpu.make_async_remote_copy(
            src_ref=source,
            dst_ref=target,
            send_sem=send,
            recv_sem=recv,
            device_id=where,
            device_id_type=pl.DeviceIdType.MESH,
        )

    def x_copy(side, s, h):
        sign = 1 - 2 * side
        block = c - 2 * sign * s
        source = x_ref.at[h] if s == 0 else xo_ref.at[block, h]
        return remote(
            source, xo_ref.at[block, h], x_send.at[side, s, h], x_recv.at[side, s, h], (c + 2 * sign, f)
        )

    def x_sends(side, s):
        return (z - s >= 0) & (z < chips - 1) if side == 0 else (z + s < chips) & (z > 0)

    def x_gets(side, s):
        return z - 1 - s >= 0 if side == 0 else z + 1 + s < chips

    def x_arrival(side, s, h):
        sign = 1 - 2 * side
        block = c - 2 * sign * (s + 1)
        return remote(
            xo_ref.at[block, h],
            xo_ref.at[block, h],
            x_send.at[side, s, h],
            x_recv.at[side, s, h],
            (c + 2 * sign, f),
        )

    def x_share(side, s, h):
        sign = 1 - 2 * side
        block = c - 2 * sign * (s + 1)
        return remote(
            xo_ref.at[block, h],
            xo_ref.at[block, h],
            xc_send.at[side, s, h],
            xc_recv.at[side, s, h],
            (partner, f),
        )

    def x_share_arrival(side, s, h):
        sign = 1 - 2 * side
        block = partner - 2 * sign * (s + 1)
        return remote(
            xo_ref.at[block, h],
            xo_ref.at[block, h],
            xc_send.at[side, s, h],
            xc_recv.at[side, s, h],
            (partner, f),
        )

    def x_own(h):
        return remote(
            x_ref.at[h],
            xo_ref.at[c, h],
            xc_send.at[0, chips - 1, h],
            xc_recv.at[0, chips - 1, h],
            (partner, f),
        )

    def x_own_arrival(h):
        return remote(
            x_ref.at[h],
            xo_ref.at[partner, h],
            xc_send.at[0, chips - 1, h],
            xc_recv.at[0, chips - 1, h],
            (partner, f),
        )

    runs = split_columns(0, half, levels)

    def source(unit, stream):
        start, size = runs[stream]
        return w_low.at[:, pl.ds(pl.multiple_of((2 * unit + core) * half + start, 128), size)]

    def kept(unit, stream, place, which):
        start, size = runs[stream]
        if unit == 0:
            return wo_ref.at[place, :, pl.ds(pl.multiple_of(which * half + start, 128), size)]
        return um_ref.at[place, :, pl.ds(start, size)]

    def shared(unit, stream, place, which):
        start, size = runs[stream]
        if unit == 0:
            return kept(unit, stream, place, which)
        return uo_ref.at[place, :, pl.ds(start, size)]

    def w_copy(unit, stream, step, number):
        bit = 1 << ((stream + step) % levels)
        place = combine(number)
        there = kept(unit, stream, place, core)
        return remote(
            source(unit, stream) if number == 0 else there,
            there,
            w_send.at[unit, stream, number | bit],
            w_recv.at[unit, stream, number | bit],
            (c, other_index(f, bit)),
        )

    def w_arrival(unit, stream, number):
        block = kept(unit, stream, combine(number), core)
        sems = w_send.at[unit, stream, number], w_recv.at[unit, stream, number]
        return remote(block, block, *sems, (partner, f))

    def w_share(unit, stream, number):
        place = combine(number)
        sems = wc_send.at[unit, stream, number], wc_recv.at[unit, stream, number]
        block = kept(unit, stream, place, core)
        return remote(block, shared(unit, stream, place, core), *sems, (partner, f))

    def w_share_arrival(unit, stream, number):
        block = shared(unit, stream, combine(number), 1 - core)
        sems = wc_send.at[unit, stream, number], wc_recv.at[unit, stream, number]
        return remote(block, block, *sems, (partner, f))

    def held(stream, step):
        numbers = [0]
        for i in range(step):
            bit = 1 << ((stream + i) % levels)
            numbers += [n | bit for n in numbers]
        return numbers

    def v_copy(number):
        return remote(
            v_ref, v_all.at[f], v_send.at[number], v_recv.at[number], (c, combine(number))
        )

    def v_arrival(number):
        return remote(
            v_ref,
            v_all.at[combine(number)],
            v_send.at[number],
            v_recv.at[number],
            (c, combine(number)),
        )

    def x_begin(h):
        for side in range(2):

            @pl.when(x_sends(side, 0))
            def _(side=side):
                x_copy(side, 0, h).start()

        x_own(h).start()

    def x_step(h, s):
        for side in range(2):

            @pl.when(x_gets(side, s))
            def _(side=side):
                x_arrival(side, s, h).wait_recv()
                x_share(side, s, h).start()

            if s + 1 < chips - 1:

                @pl.when(x_sends(side, s + 1))
                def _(side=side):
                    x_copy(side, s + 1, h).start()

    def w_step(unit, step):
        for stream in range(levels):
            bit = 1 << ((stream + step) % levels)
            arrived = [number | bit for number in held(stream, step)]
            for number in arrived:
                w_arrival(unit, stream, number).wait_recv()
            if step + 1 < levels:
                for number in held(stream, step + 1):
                    w_copy(unit, stream, step + 1, number).start()
            for number in arrived:
                w_share(unit, stream, number).start()

    def fetch(unit):
        cols = pl.ds(2 * unit * half, 2 * half)
        return pltpu.make_async_copy(w_ref.at[:, cols], wide.at[:, cols], local.at[3 + unit])

    def w_begin(unit):
        fetch(unit).wait()
        cols = slice(2 * unit * half, 2 * (unit + 1) * half)

        strip = 16 if rows % 16 == 0 else rows

        def body(i, carry):
            at = pl.ds(pl.multiple_of(i * strip, strip), strip)
            w_low[at, cols] = wide[at, cols].astype(BF16)
            return carry

        lax.fori_loop(0, rows // strip, body, 0)
        for stream in range(levels):
            w_copy(unit, stream, 0, 0).start()

    own_up = w_low.at[:, pl.ds(pl.multiple_of((2 + core) * half, 128), half)]
    other_up = w_low.at[:, pl.ds(pl.multiple_of((3 - core) * half, 128), half)]
    kept_here = [
        pltpu.make_async_copy(w_low.at[:, pl.ds(0, 2 * half)], wo_ref.at[f], local.at[0]),
        pltpu.make_async_copy(own_up, um_ref.at[f], local.at[1]),
        pltpu.make_async_copy(other_up, uo_ref.at[f], local.at[2]),
    ]
    v_own = pltpu.make_async_copy(v_ref, v_all.at[f], local.at[5])
    v_out = pltpu.make_async_copy(v_all, vo_ref, local.at[6])
    x_here = pltpu.make_async_copy(x_ref, xo_ref.at[c], local.at[7])

    head_of = [i * ctx + c for i in range(regular)] + [HEADS - 1]
    places = [part * HEADS + head for part in range(3) for head in head_of]

    def window(i):
        start = pl.multiple_of(places[i] // 2 * 128, 128)
        return pltpu.make_async_copy(
            wo_ref.at[:, :, pl.ds(start, 128)], windows.at[i], local.at[8 + i]
        )

    def ready():
        kept_here[0].wait()
        for number in range(1, fsdp):
            v_arrival(number).wait_recv()
            for stream in range(levels):
                w_share_arrival(0, stream, number).wait_recv()
        v_own.wait()
        v_out.start()
        for i in range(len(places)):
            window(i).start()
        for i in range(fsdp):
            v_rows[i * rows : (i + 1) * rows, :] = v_all[i].astype(F32)
        own_w[...] = jnp.zeros_like(own_w)
        for i, place in enumerate(places):
            window(i).wait()
            odd = lax.rem(place, 2)
            for k in range(fsdp):
                both = windows[i, k]
                mine = jnp.where(odd == 0, both[:, :dim], both[:, dim:])
                own_w[k * rows : (k + 1) * rows, i * dim : (i + 1) * dim] = mine
        own_t[...] = own_w[...].T
        for part, column in ((0, 2), (2, 3)):
            for i, head in enumerate(head_of):
                start = (part * owned + i) * dim
                at = pl.ds(pl.multiple_of(head * dim, dim), dim)
                bias[start : start + dim, :] = v_rows[at, column : column + 1]
        start = owned * dim
        bias[start : 2 * start, :] = jnp.zeros((start, 1), F32)

    def project(h, b):
        unit, _ = norm_parts(xo_ref[b, h].astype(F32), 0)
        act = (unit * v_rows[:, 0:1] + v_rows[:, 1:2]).astype(BF16)
        acts[h, b] = act
        pltpu.make_async_copy(acts.at[h, b], act_ref.at[h, b], act_sem.at[h, b]).start()
        value = dot(own_t[...], act)[: 3 * owned * dim] + bias[...]
        qkvs[h, :, pl.ds(pl.multiple_of(b * tok, tok), tok)] = value.astype(BF16)

    def project_own(h):
        x_own_arrival(h).wait_recv()

        def body(i, carry):
            project(h, 2 * z + i)
            return carry

        lax.fori_loop(0, 2, body, 0)

    def project_step(h, s):
        for side in range(2):

            @pl.when(x_gets(side, s))
            def _(side=side):
                x_share_arrival(side, s, h).wait_recv()

        def body(i, carry):
            side = i // 2
            chip = z - (1 - 2 * side) * (s + 1)

            @pl.when((chip >= 0) & (chip < chips))
            def _():
                project(h, 2 * chip + lax.rem(i, 2))

            return carry

        lax.fori_loop(0, 4, body, 0)

    def out_copy(h):
        return pltpu.make_async_copy(qkvs.at[h], qkv_ref.at[h], local.at[8 + len(places) + h])

    plan = []
    block_time = 0.95

    def at(time, work, *values):
        plan.append((time, functools.partial(work, *values)))

    for h in range(slots):
        for s in range(chips - 1):
            at(block_time * (h * (chips - 1) + s + 1), x_step, h, s)
        if h > 0:
            at(block_time * (h * (chips - 1) - 1) + 0.01, x_begin, h)
    time = 0.0
    for unit in range(2):
        for step in range(levels):
            if unit == 0 and step == levels - 1:
                at(time + 0.9, w_begin, 1)
            time += 2.0 ** (step + 1) / levels
            at(time, w_step, unit, step)
        if unit == 0:
            done = max(time, block_time * (chips - 1))
    at(done + 0.3, ready)
    time = done + 0.9
    for h in range(slots):
        for s in range(-1, chips - 1):
            arrived = block_time * (h * (chips - 1) + s + 1)
            time = max(time, arrived + 0.1)
            if s < 0:
                at(time, project_own, h)
            else:
                at(time, project_step, h, s)
            time += 0.2 if s < 0 else 0.4
        at(time, lambda h: out_copy(h).start(), h)

    fetch(0).start()
    fetch(1).start()
    x_here.start()
    x_begin(0)
    for number in range(1, fsdp):
        v_copy(number).start()
    v_own.start()
    w_begin(0)
    kept_here[0].start()
    x_here.wait()
    for _, work in sorted(plan, key=lambda entry: entry[0]):
        work()

    kept_here[1].start()
    kept_here[2].start()
    kept_here[1].wait()
    kept_here[2].wait()
    v_out.wait()
    for number in range(1, fsdp):
        v_copy(number).wait_send()
        for unit in range(2):
            for stream in range(levels):
                w_arrival(unit, stream, number).wait_send()
                w_share(unit, stream, number).wait_send()
                if unit > 0:
                    w_share_arrival(unit, stream, number).wait_recv()
    for h in range(slots):
        x_own(h).wait_send()
        out_copy(h).wait()
        for b in range(ctx):
            pltpu.make_async_copy(acts.at[h, b], act_ref.at[h, b], act_sem.at[h, b]).wait()
        for s in range(chips - 1):
            for side in range(2):

                @pl.when(x_sends(side, s))
                def _(side=side, h=h, s=s):
                    x_copy(side, s, h).wait_send()

                @pl.when(x_gets(side, s))
                def _(side=side, h=h, s=s):
                    x_share(side, s, h).wait_send()


def gather_first(ctx, fsdp, regular, x, w, v):
    slots, width, tok = x.shape
    rows, columns = w.shape
    levels, chips = bits_of(fsdp), ctx // 2
    owned = regular + 1
    feat = 3 * owned * HEAD_DIM
    room = feat + -feat % 128
    anywhere = pl.BlockSpec(memory_space=pl.ANY)
    dma = pltpu.SemaphoreType.DMA
    return pl.pallas_call(
        functools.partial(gather_kernel, ctx, fsdp, regular),
        in_specs=[anywhere, anywhere, pl.BlockSpec(memory_space=pltpu.VMEM)],
        out_specs=[anywhere] * 6,
        out_shape=[
            jax.ShapeDtypeStruct((slots, ctx, width, tok), BF16),
            jax.ShapeDtypeStruct((slots, feat, ctx * tok), BF16),
            jax.ShapeDtypeStruct((fsdp, rows, columns // 2), BF16),
            jax.ShapeDtypeStruct((fsdp, rows, columns // 4), BF16),
            jax.ShapeDtypeStruct((fsdp, rows, columns // 4), BF16),
            jax.ShapeDtypeStruct((fsdp, rows, 128), BF16),
        ],
        scratch_shapes=[
            pltpu.VMEM((ctx, slots, width, tok), BF16),
            pltpu.VMEM((rows, columns), F32),
            pltpu.VMEM((rows, columns), BF16),
            pltpu.VMEM((3 * owned, fsdp, rows, 128), BF16),
            pltpu.VMEM((width, room), BF16),
            pltpu.VMEM((room, width), BF16),
            pltpu.VMEM((fsdp, rows, 128), BF16),
            pltpu.VMEM((width, 128), F32),
            pltpu.VMEM((feat, 1), F32),
            pltpu.VMEM((slots, ctx, width, tok), BF16),
            pltpu.VMEM((slots, feat, ctx * tok), BF16),
            dma((2, chips - 1, slots)),
            dma((2, chips - 1, slots)),
            dma((2, chips, slots)),
            dma((2, chips, slots)),
            dma((2, levels, fsdp)),
            dma((2, levels, fsdp)),
            dma((2, levels, fsdp)),
            dma((2, levels, fsdp)),
            dma((fsdp,)),
            dma((fsdp,)),
            dma((slots, ctx)),
            dma((8 + 3 * owned + slots,)),
        ],
        compiler_params=pltpu.CompilerParams(
            collective_id=0, has_side_effects=True, vmem_limit_bytes=60 * 2**20
        ),
        cost_estimate=pl.CostEstimate(flops=1000, bytes_accessed=1000, transcendentals=0),
    )(x, w, v)


def bits_of(count):
    return max(count.bit_length() - 1, 0)


def flip(count, value):
    return [(i, i ^ value) for i in range(count)]


def pick(array, index, axis):
    return lax.dynamic_index_in_dim(array, index, axis, keepdims=False)


def ordered(bit, mine, other, axis):
    first = jnp.where(bit == 0, mine, other)
    second = jnp.where(bit == 0, other, mine)
    return jnp.concatenate([first, second], axis=axis)


def after(value, *others):
    return lax.optimization_barrier((value, others))[0]


def add_low(mine, swapped):
    return (mine.astype(F32) + swapped.astype(F32)).astype(BF16)


def scatter_fsdp(total):
    return lax.psum_scatter(total, "fsdp", scatter_dimension=0, tiled=True)


def bar_signal(where):
    pl.semaphore_signal(
        pltpu.get_barrier_semaphore(), inc=1, device_id=where, device_id_type=pl.DeviceIdType.MESH
    )


def remote_copy(source, target, send, recv, where):
    return pltpu.make_async_remote_copy(
        src_ref=source,
        dst_ref=target,
        send_sem=send,
        recv_sem=recv,
        device_id=where,
        device_id_type=pl.DeviceIdType.MESH,
    )


def line_gather(chips, c, f, mine, slot, share, sems, core_sems):
    z, core = c // 2, lax.rem(c, 2)
    partner = 2 * z + 1 - core
    send, recv = sems
    core_send, core_recv = core_sems

    def passing(side, s):
        sign = 1 - 2 * side
        chip = z - sign * s
        source = mine if s == 0 else slot(chip)
        return remote_copy(
            source, slot(chip), send.at[side, s], recv.at[side, s], (c + 2 * sign, f)
        )

    def arrival(side, s):
        block = slot(z - (1 - 2 * side) * (s + 1))
        return remote_copy(block, block, send.at[side, s], recv.at[side, s], (partner, f))

    def sends(side, s):
        return (z - s >= 0) & (z < chips - 1) if side == 0 else (z + s < chips) & (z > 0)

    def gets(side, s):
        return z - 1 - s >= 0 if side == 0 else z + 1 + s < chips

    def shared(side, s):
        chip = z - (1 - 2 * side) * (s + 1)
        return remote_copy(
            slot(chip), share(chip), core_send.at[side, s], core_recv.at[side, s], (partner, f)
        )

    def share_arrival(side, s):
        block = share(z - (1 - 2 * side) * (s + 1))
        sems = core_send.at[side, s], core_recv.at[side, s]
        return remote_copy(block, block, *sems, (partner, f))

    own_sems = core_send.at[0, chips - 1], core_recv.at[0, chips - 1]
    own_share = remote_copy(mine, share(z), *own_sems, (partner, f))

    def start():
        for side in range(2):

            @pl.when(sends(side, 0))
            def _(side=side):
                passing(side, 0).start()

        own_share.start()

    def step(s):
        for side in range(2):

            @pl.when(gets(side, s))
            def _(side=side):
                arrival(side, s).wait_recv()
                shared(side, s).start()

            if s + 1 < chips - 1:

                @pl.when(sends(side, s + 1))
                def _(side=side):
                    passing(side, s + 1).start()

    def end():
        own_share.wait_send()
        remote_copy(share(z), share(z), *own_sems, (partner, f)).wait_recv()
        for s in range(chips - 1):
            for side in range(2):

                @pl.when(sends(side, s))
                def _(side=side, s=s):
                    passing(side, s).wait_send()

                @pl.when(gets(side, s))
                def _(side=side, s=s):
                    shared(side, s).wait_send()
                    share_arrival(side, s).wait_recv()

    return start, [functools.partial(step, s) for s in range(chips - 1)], end


def sum_kernel(ctx, fsdp, batches, *refs):
    levels, chips = bits_of(fsdp), ctx // 2
    pieces = refs[0:2]
    group_refs = refs[2:4]
    mine_out, other_out, own_out, last_out = refs[4:8]
    rest = list(refs[8:])
    own_kept = [rest.pop(0) for _ in range(2)]
    own_low, beside = rest.pop(0), rest.pop(0)
    own_sent = [[rest.pop(0) for _ in range(levels)] for _ in range(2)]
    own_got = [[rest.pop(0) for _ in range(levels)] for _ in range(2)]
    z_sent, z_got = rest.pop(0), rest.pop(0)
    op_send, op_recv, zs_send, zs_recv, zg_send, zg_recv = (rest.pop(0) for _ in range(6))
    zc_send, zc_recv, og_send, og_recv, oc_send, oc_recv, far_send, far_recv, local = (
        rest.pop(0) for _ in range(9)
    )
    c, f = lax.axis_index("ctx"), lax.axis_index("fsdp")
    z, core = c // 2, lax.rem(c, 2)
    partner = 2 * z + 1 - core
    far = lax.rem(c + ctx // 2, ctx)
    rows = own_low.shape[0]
    chunk = z_sent.shape[-1]
    width = chunk * chips // 2
    parts = chips // 2
    strip = 16 if rows % 16 == 0 else 8

    def own_bit(bit):
        return lax.rem(f // (1 << bit), 2)

    def strips(work):
        def body(i, carry):
            work(pl.ds(pl.multiple_of(i * strip, strip), strip))
            return carry

        lax.fori_loop(0, rows // strip, body, 0)

    bar_signal((partner, f))
    bar_signal((far, f))
    for bit in range(levels):
        bar_signal((c, other_index(f, 1 << bit)))

    @pl.when(z > 0)
    def _():
        bar_signal((c - 2, f))

    @pl.when(z < chips - 1)
    def _():
        bar_signal((c + 2, f))

    neighbours = (z > 0).astype(jnp.int32) + (z < chips - 1).astype(jnp.int32)
    pl.semaphore_wait(pltpu.get_barrier_semaphore(), levels + 2 + neighbours)

    def order(q):
        return [(q + i) % levels for i in range(levels)]

    def place_of(q, flipped, free):
        bits = order(q)
        first = own_bit(bits[0])
        total = (1 - first if flipped else first) * (1 << bits[0])
        for i, bit in enumerate(bits[1:]):
            total += ((free >> i) & 1) * (1 << bit)
        return total

    def kept_index(q, step, flipped, free):
        bits = order(q)
        total = 0
        for i, bit in enumerate(bits[1:]):
            mine = own_bit(bit)
            if i + 1 < step:
                value = mine
            elif i + 1 == step:
                value = 1 - mine if flipped else mine
            else:
                value = (free >> (i - step)) & 1
            total += value * (1 << i)
        return total

    def across(step, q):
        return (c, other_index(f, 1 << order(q)[step]))

    def own_copy(g, step):
        return remote_copy(
            own_sent[g][step],
            own_got[g][step],
            op_send.at[g, step],
            op_recv.at[g, step],
            across(step, g),
        )

    def own_begin(g):
        for free in range(fsdp // 2):
            there, here = place_of(g, True, free), place_of(g, False, free)

            def work(at, free=free, there=there, here=here):
                own_sent[g][0][free, at, :] = group_refs[g][there, at, :]
                own_kept[g][free, at, :] = group_refs[g][here, at, :].astype(F32)

            strips(work)
        own_copy(g, 0).start()

    def later(step, kept_ref, got_ref, sent_ref, q):
        for free in range(fsdp >> (step + 2)):
            there, here = (kept_index(q, step + 1, flipped, free) for flipped in (True, False))
            mine = own_bit(order(q)[step + 1])
            there_got, here_got = free * 2 + 1 - mine, free * 2 + mine

            def work(at, free=free):
                value = kept_ref[there, at, :] + got_ref[there_got, at, :].astype(F32)
                sent_ref[free, at, :] = value.astype(BF16)
                kept_ref[here, at, :] += got_ref[here_got, at, :].astype(F32)

            strips(work)

    def last(kept_ref, got_ref, q, place):
        def work(at):
            place(at, kept_ref[kept_index(q, levels, False, 0), at, :] + got_ref[0, at, :].astype(F32))

        strips(work)

    def own_step(g, step):
        own_copy(g, step).wait_recv()
        if step + 1 < levels:
            later(step, own_kept[g], own_got[g][step], own_sent[g][step + 1], g)
            own_copy(g, step + 1).start()
            return

        def place(at, value):
            if g == 0:
                beside[at, :] = value
            else:
                own_low[at, :] = value.astype(BF16)

        last(own_kept[g], own_got[g][step], g, place)
        if g == 1:
            for copy in far_copies:
                copy.start()
            own_start()

    head = own_out.shape[2]
    tail = last_out.shape[2]
    far_copies = [
        remote_copy(
            own_low.at[:, pl.ds(head, tail)], last_out.at[1], far_send.at[0], far_recv.at[0], (far, f)
        ),
        pltpu.make_async_copy(own_low.at[:, pl.ds(head, tail)], last_out.at[0], local.at[0]),
        pltpu.make_async_copy(own_low.at[:, pl.ds(0, head)], own_out.at[c], local.at[1]),
    ]
    own_start, own_steps, own_end = line_gather(
        chips,
        c,
        f,
        own_low.at[:, pl.ds(0, head)],
        lambda chip: own_out.at[2 * chip + core],
        lambda chip: own_out.at[2 * chip + core],
        (og_send, og_recv),
        (oc_send, oc_recv),
    )

    def total_of(j, b, at):
        q = j // parts
        start = b * width + (j % parts) * chunk
        stop = start + chunk
        units, room = pieces[q].shape[1], beside.shape[1] // 2
        found = []
        if start < units:
            found.append(pieces[q][at, start : min(stop, units)].astype(F32))
        if stop > units:
            first = max(start, units) - units + q * room
            found.append(beside[at, first : stop - units + q * room])
        return found[0] if len(found) == 1 else jnp.concatenate(found, axis=1)

    def z_copy(side, i, b):
        return remote_copy(
            z_sent.at[side, b, i],
            z_got.at[side, b, i],
            zs_send.at[side, b, i],
            zs_recv.at[side, b, i],
            (c + 2 * (1 - 2 * side), f),
        )

    def z_last(side, chip):
        return chips - 1 - chip if side == 0 else chip

    def z_step(turn, b):
        for chip in range(chips):

            @pl.when(z == chip)
            def _(chip=chip):
                for side in range(2):
                    j_of = (lambda i: chips - 1 - i) if side == 0 else (lambda i: i)
                    begun = chip if side == 0 else chips - 1 - chip
                    i = turn - begun
                    sends = z_last(side, chip)
                    if begun > 0 and 0 <= i <= sends and i < chips - 1:
                        z_copy(side, i, b).wait_recv()
                    if 0 <= i < sends:
                        if i > 0:
                            z_copy(side, i - 1, b).wait_send()

                        def work(at, side=side, i=i, j=j_of(i), begun=begun):
                            value = total_of(j, b, at)
                            if begun > 0:
                                value += z_got[side, b, i, at, :].astype(F32)
                            z_sent[side, b, i, at, :] = value.astype(BF16)

                        strips(work)
                        z_copy(side, i, b).start()

    def chunk_of(ref, chip, b):
        start = pl.multiple_of(b * width + lax.rem(chip, parts) * chunk, 128)
        return ref.at[chip // parts, :, pl.ds(start, chunk)]

    gathers = []
    for b in range(batches):
        gathers.append(
            line_gather(
                chips,
                c,
                f,
                chunk_of(mine_out, z, b),
                lambda chip, b=b: chunk_of(mine_out, chip, b),
                lambda chip, b=b: chunk_of(other_out, chip, b),
                (zg_send.at[:, b], zg_recv.at[:, b]),
                (zc_send.at[:, b], zc_recv.at[:, b]),
            )
        )

    def finish(b):
        for j in range(chips):

            @pl.when(z == j)
            def _(j=j):
                def work(at):
                    value = total_of(j, b, at)
                    if j > 0:
                        value += z_got[0, b, chips - 1 - j, at, :].astype(F32)
                    if j < chips - 1:
                        value += z_got[1, b, j, at, :].astype(F32)
                    start = b * width + (j % parts) * chunk
                    mine_out[j // parts, at, pl.ds(start, chunk)] = value.astype(BF16)

                strips(work)

        gathers[b][0]()

    own_begin(0)
    own_begin(1)
    waiting = []

    def one_more():
        if waiting:
            waiting.pop(0)()

    def batch(b):
        for i in range(chips):
            z_step(i, b)
            one_more()
        finish(b)
        waiting.extend(gathers[b][1])

    for b in range(batches - 1):
        batch(b)
    for step in range(levels):
        own_step(0, step)
        own_step(1, step)
        one_more()
    waiting.extend(own_steps)
    batch(batches - 1)
    while waiting:
        one_more()

    far_copies[0].wait()
    far_copies[1].wait()
    far_copies[2].wait()
    own_end()
    for step in range(levels):
        own_copy(0, step).wait_send()
        own_copy(1, step).wait_send()
    for b in range(batches):
        gathers[b][2]()
        for chip in range(chips):

            @pl.when(z == chip)
            def _(chip=chip, b=b):
                for side in range(2):
                    if z_last(side, chip):
                        z_copy(side, z_last(side, chip) - 1, b).wait_send()


def sum_grads(ctx, fsdp, pieces, out, own, head):
    levels, chips = bits_of(fsdp), ctx // 2
    rows, units = pieces[0].shape
    beside, own_width = out.shape[-1], own.shape[-1]
    whole = units + beside // 2
    batches = max(n for n in range(1, 3) if whole % n == 0 and 2 * whole // n % (chips * 128) == 0)
    width = whole // batches
    chunk = 2 * width // chips
    vmem = pl.BlockSpec(memory_space=pltpu.VMEM)
    dma = pltpu.SemaphoreType.DMA
    steps = [fsdp >> (i + 1) for i in range(levels)]
    result = jax.ShapeDtypeStruct((2, rows, whole), BF16)
    mine, other, own_all, last = pl.pallas_call(
        functools.partial(sum_kernel, ctx, fsdp, batches),
        in_specs=[vmem] * 4,
        out_specs=[vmem] * 4,
        out_shape=[
            result,
            result,
            jax.ShapeDtypeStruct((ctx, rows, head), BF16),
            jax.ShapeDtypeStruct((2, rows, own_width - head), BF16),
        ],
        scratch_shapes=[
            pltpu.VMEM((fsdp // 2, rows, beside), F32),
            pltpu.VMEM((fsdp // 2, rows, own_width), F32),
            pltpu.VMEM((rows, own_width), BF16),
            pltpu.VMEM((rows, beside), F32),
        ]
        + [pltpu.VMEM((n, rows, size), BF16) for size in (beside, own_width) * 2 for n in steps]
        + [pltpu.VMEM((2, batches, chips - 1, rows, chunk), BF16)] * 2
        + [dma((2, levels))] * 2
        + [dma((2, batches, chips - 1))] * 4
        + [dma((2, batches, chips))] * 2
        + [dma((2, chips - 1))] * 2
        + [dma((2, chips))] * 2
        + [dma((1,))] * 2
        + [dma((6,))],
        compiler_params=pltpu.CompilerParams(
            collective_id=1, has_side_effects=True, vmem_limit_bytes=60 * 2**20
        ),
        cost_estimate=pl.CostEstimate(flops=1000, bytes_accessed=1000, transcendentals=0),
    )(*pieces, out, own)

    return mine, other, own_all, last


def swap_cores(mine, ctx):
    return lax.ppermute(mine, "ctx", flip(ctx, 1))


def norm_parts(rows, axis):
    middle = jnp.mean(rows, axis=axis, keepdims=True)
    centred = rows - middle
    spread = jnp.mean(centred * centred, axis=axis, keepdims=True)
    inverse = lax.rsqrt(spread + NORM_EPS)
    return centred * inverse, inverse


def norm_back(grad, unit, inverse, gain):
    inner = grad * gain
    mean_inner = jnp.mean(inner, axis=1, keepdims=True)
    mean_cross = jnp.mean(inner * unit, axis=1, keepdims=True)
    rows = inverse * (inner - mean_inner - unit * mean_cross)
    return rows, jnp.sum(grad * unit, axis=(0, 2)), jnp.sum(grad, axis=(0, 2))


def adamw(weight, first, second, grad, rate, decay):
    moment = BETA_ONE * first.astype(F32) + (1.0 - BETA_ONE) * grad
    square = BETA_TWO * second + (1.0 - BETA_TWO) * grad * grad
    corrected = moment / (1.0 - BETA_ONE**STEP)
    scaled = square / (1.0 - BETA_TWO**STEP)
    new_weight = weight - rate * (corrected / (jnp.sqrt(scaled) + ADAM_EPS) + decay * weight)
    return (moment, square, new_weight)


def update_kernel(units, regular, *refs):
    (w, first, second, dw, dfirst, dsecond, own, last, mine, other) = refs[:10]
    outs = refs[10:]
    core = lax.rem(lax.axis_index("ctx"), 2)
    width = (w.shape[1] - 2 * units) // 4
    quarter = width // 4
    ctx = own.shape[0]
    dim = HEAD_DIM

    def halves(q, start, size):
        here = mine[q, :, start : start + size].astype(F32)
        there = other[q, :, start : start + size].astype(F32)
        return jnp.where(core == 0, here, there), jnp.where(core == 0, there, here)

    def both(q, start, size):
        return jnp.concatenate(halves(q, start, size), axis=1)

    heads = []
    for part in range(3):
        for i in range(regular):
            for c in range(ctx):
                column = (i * 3 + part) * dim
                heads.append(own[c, :, column : column + dim].astype(F32))
        column = part * dim
        heads.append(
            last[0, :, column : column + dim].astype(F32)
            + last[1, :, column : column + dim].astype(F32)
        )
    out = [halves(q, units, quarter) for q in range(2)]
    heads += [out[0][0], out[1][0], out[0][1], out[1][1]]
    grad = jnp.concatenate(heads, axis=1)

    def put(targets, cols, values):
        for target, value in zip(targets, values):
            target[:, cols] = value

    cols = slice(0, 4 * width)
    put(outs[:3], cols, adamw(w[:, cols], first[:, cols], second[:, cols], grad, 0.03, 0.1))
    cols = slice(4 * width, w.shape[1])
    grad = both(0, 0, units)
    put(outs[:3], cols, adamw(w[:, cols], first[:, cols], second[:, cols], grad, 0.03, 0.1))
    grad = both(1, 0, units)
    put(outs[3:], slice(None), adamw(dw[...], dfirst[...], dsecond[...], grad, 0.02, 0.1))


def update(rows_state, down_state, own, last, mine, other, units, regular):
    rows = rows_state[0].shape[0]
    strip = 16 if rows % 16 == 0 else 8

    def flat(array):
        return pl.BlockSpec((strip, array.shape[1]), lambda i: (i, 0))

    def deep(array):
        return pl.BlockSpec((array.shape[0], strip, array.shape[2]), lambda i: (0, i, 0))

    states, sums = [*rows_state, *down_state], [own, last, mine, other]
    results = [rows_state[0]] * 3 + [down_state[0]] * 3
    return pl.pallas_call(
        functools.partial(update_kernel, units, regular),
        grid=(rows // strip,),
        in_specs=[flat(a) for a in states] + [deep(a) for a in sums],
        out_specs=[flat(a) for a in results],
        out_shape=[jax.ShapeDtypeStruct(a.shape, F32) for a in results],
        compiler_params=pltpu.CompilerParams(vmem_limit_bytes=56 * 2**20),
        cost_estimate=pl.CostEstimate(flops=1000, bytes_accessed=1000, transcendentals=0),
    )(*states, *sums)


def body(
    ctx,
    fsdp,
    tokens,
    cotangent,
    lengths,
    w_rows,
    rows_first,
    rows_second,
    w_down,
    down_first,
    down_second,
    vectors,
    vec_first,
    vec_second,
):
    tok, slots, width = tokens.shape
    dim = HEAD_DIM
    regular = HEADS // ctx
    owned = regular + 1
    share = width // fsdp
    c = lax.axis_index("ctx")
    core = c % 2
    late = (c >= ctx // 2).astype(jnp.int32)
    half = FF // 2

    def my_half(array):
        return lax.dynamic_slice_in_dim(array, core * half, half, 1)

    x_low = tokens.transpose(1, 2, 0)
    vec_part = jnp.pad(vectors.astype(BF16).T, ((0, 0), (0, 128 - vectors.shape[0])))
    act_all, qkv_all, head_w, up_mine, up_other, vec_low = gather_first(
        ctx, fsdp, regular, x_low, w_rows, vec_part
    )
    head_w = head_w.reshape(width, 4 * width)
    up_mine, up_other = up_mine.reshape(width, half), up_other.reshape(width, half)
    vec_low = vec_low.reshape(width, 128)
    down_mine, vec_low = lax.optimization_barrier((my_half(w_down.T).astype(BF16), vec_low))
    down_mine = lax.all_gather(down_mine, "fsdp", axis=0, tiled=True)
    vec = [vec_low[:, i : i + 1].astype(F32) for i in range(12)]
    up_bias = vec_low[:, 8:12].T.astype(F32).reshape(1, FF)

    qkv_all = qkv_all.reshape(slots, 3, owned, dim, ctx * tok)
    far = (c + ctx // 2) % ctx

    def to_rows(array, *gate):
        feat = array.shape[2]
        got = lax.all_to_all(array, "ctx", 0, 0)
        got = after(got, *gate) if gate else got
        return got.transpose(1, 0, 2, 3).reshape(regular * ctx, feat, tok)

    def last_to_rows(array, *gate):
        mine = pick(array, c, 0)
        got = lax.ppermute(pick(array, far, 0), "ctx", flip(ctx, ctx // 2))
        got = after(got, *gate) if gate else got
        return jnp.where(late == 0, mine, got), jnp.where(late == 0, got, mine)

    def to_send(array):
        return array.reshape(regular, ctx, dim, tok).transpose(1, 0, 2, 3)

    def attend_slot(s, *gate):
        lens = after(jnp.repeat(lengths[s : s + 1], regular), *gate)
        return (lens, qkv_all, s, *attend(lens, qkv_all, s, tok))

    results = [attend_slot(0)]
    results.append(attend_slot(1, results[0][3]))
    rows = [to_rows(results[0][4])]
    last_qkv = jnp.where(late == 0, qkv_all[:1, :, regular:], qkv_all[1:, :, regular:])
    last_len = after(lax.dynamic_slice_in_dim(lengths, late, 1, 0), results[1][3], rows[0])
    results.append((last_len, last_qkv, 0, *attend(last_len, last_qkv, 0, tok)))
    rows.append(to_rows(results[1][4]))
    down_mine = after(down_mine, results[2][3], *rows)
    down_other = swap_cores(down_mine, ctx)
    last_rows = last_to_rows(results[2][4])
    att = [jnp.concatenate([rows[s], last_rows[s]]).reshape(width, tok) for s in range(slots)]
    att = jnp.stack(att)

    x = x_low.astype(F32)
    out_w = head_w[:, 3 * width :]
    mid = x + jnp.einsum("de,sdt->set", out_w, att, preferred_element_type=F32) + vec[4]
    unit_two, inverse_two = norm_parts(mid, 1)
    act_two = (unit_two * vec[5] + vec[6]).astype(BF16)

    pos = c * tok + jnp.arange(tok, dtype=jnp.int32)
    valid = pos[None, None, :] < lengths[:, None, None]
    g_low = jnp.where(valid, cotangent.transpose(1, 2, 0), jnp.zeros((), BF16))
    g = g_low.astype(F32)

    bias_mine = lax.dynamic_slice_in_dim(up_bias, core * half, half, 1)
    bias_other = lax.dynamic_slice_in_dim(up_bias, (1 - core) * half, half, 1)
    y_other, ga_other, dup_other, ddown_other, db_other = mlp(
        act_two, g_low, up_other, down_other, bias_other
    )
    y_mine, ga_mine, dup_mine, ddown_mine, db_mine = mlp(
        act_two, g_low, up_mine, down_mine, bias_mine
    )
    output = (mid + (y_mine + y_other + vec[7])).astype(BF16).transpose(2, 0, 1)

    up_swapped, down_swapped = swap_cores(dup_other, ctx), swap_cores(ddown_other, ctx)

    up_total = add_low(dup_mine, up_swapped)
    up_part = scatter_fsdp(up_total)
    ga_mine = after(ga_mine, up_total)
    grad_mid, gain_two, shift_two = norm_back(ga_mine + ga_other, unit_two, inverse_two, vec[5])
    grad_mid = g + grad_mid
    grad_attn = grad_mid.astype(BF16)
    grad_att = jnp.einsum("de,set->sdt", out_w, grad_attn, preferred_element_type=F32).astype(BF16)
    grad_att = grad_att.reshape(slots, HEADS, dim, tok)
    first_send = to_send(grad_att[0, :-1])
    grad_attn_later = after(grad_attn, first_send)
    last = jnp.repeat(grad_att[:, -1], ctx // slots, axis=0)[:, None]
    first_pairs = lax.all_to_all(first_send, "ctx", 0, 0)
    down_part = scatter_fsdp(add_low(after(ddown_mine, first_pairs), down_swapped))
    other_pairs = lax.all_to_all(
        after(jnp.concatenate([to_send(grad_att[1, :-1]), last], axis=1), first_pairs), "ctx", 0, 0
    )

    quarter = width // 4
    spread = jnp.pad(
        grad_attn_later.reshape(slots, 4, quarter, tok),
        ((0, 0), (0, 0), (0, -quarter % 128), (0, 0)),
    )
    out_grad = jnp.einsum("sdt,sket->kde", att, spread, preferred_element_type=F32).astype(BF16)
    out_grad = out_grad.reshape(2, 2, fsdp, share, spread.shape[2])

    def out_half(which):
        return pick(out_grad, which, 0).reshape(2, width, spread.shape[2])

    out_mine, out_swapped = out_half(core), swap_cores(out_half(1 - core), ctx)
    out_total = add_low(out_mine, out_swapped)
    first_heads = attend_back(*results[0][:4], results[0][5], first_pairs)
    last_heads = attend_back(
        *results[2][:4], results[2][5], after(other_pairs[:, -1:], first_heads)
    )
    other_heads = attend_back(
        *results[1][:4], results[1][5], after(other_pairs[:, :-1], last_heads, up_part)
    )
    grad_heads = [first_heads, other_heads, last_heads]

    feat = 3 * dim
    own_sum = own_grad(
        late,
        act_all,
        grad_heads[0].reshape(ctx, regular * feat, tok),
        grad_heads[1].reshape(ctx, regular * feat, tok),
        grad_heads[2].reshape(ctx, feat, tok),
    )
    own_sum = own_sum.astype(BF16)
    own_sum = jnp.concatenate(
        [
            jnp.pad(part, ((0, 0), (0, -part.shape[1] % 128)))
            for part in (own_sum[:, : regular * feat], own_sum[:, regular * feat :])
        ],
        axis=1,
    )
    head_columns = regular * feat + -regular * feat % 128
    blocks = (fsdp, share)
    sum_mine, sum_other, own_all, last = sum_grads(
        ctx,
        fsdp,
        [up_part, down_part],
        jnp.concatenate([out_total[0], out_total[1]], axis=1).reshape(*blocks, -1),
        own_sum.reshape(*blocks, own_sum.shape[1]),
        head_columns,
    )
    first_rows, other_rows = to_rows(first_heads), to_rows(other_heads, sum_mine)
    last_rows = last_to_rows(last_heads, sum_mine)
    grad_qkv = []
    for s, rows in enumerate((first_rows, other_rows)):
        rows = jnp.concatenate([rows, last_rows[s]])
        rows = rows.reshape(HEADS, 3, dim, tok).transpose(1, 0, 2, 3)
        grad_qkv.append(rows.reshape(3 * width, tok))
    grad_qkv = jnp.stack(grad_qkv)
    grad_one = jnp.einsum(
        "de,set->sdt", head_w[:, : 3 * width], grad_qkv, preferred_element_type=F32
    )

    unit_one, inverse_one = norm_parts(x, 1)
    grad_in, gain_one, shift_one = norm_back(grad_one, unit_one, inverse_one, vec[0])
    grad_tokens = (grad_mid + grad_in).astype(BF16)

    bias_qkv = jnp.sum(grad_qkv.astype(F32), axis=(0, 2))
    vec_grad = jnp.stack(
        [
            gain_one,
            shift_one,
            bias_qkv[:width],
            bias_qkv[2 * width :],
            jnp.sum(grad_attn.astype(F32), axis=(0, 2)),
            gain_two,
            shift_two,
            jnp.sum(g, axis=(0, 2)),
        ]
    )
    bias_up = ordered(core, db_mine, db_other, 1).reshape(4, width)
    vec_grad = jnp.concatenate([vec_grad, bias_up], axis=0).reshape(12, fsdp, share)
    f = lax.axis_index("fsdp")
    vec_sum = pick(vec_grad, f, 1)
    for value in range(1, fsdp):
        vec_sum = vec_sum + lax.ppermute(pick(vec_grad, f ^ value, 1), "fsdp", flip(fsdp, value))
    for level in range(bits_of(ctx)):
        vec_sum = vec_sum + lax.ppermute(vec_sum, "ctx", flip(ctx, 2**level))

    rows_state = (w_rows, rows_first, rows_second)
    down_state = (w_down.T, down_first.T, down_second.T)
    updated = update(
        rows_state, down_state, own_all, last, sum_mine, sum_other, half, regular
    )
    rows_out, down_out = updated[:3], tuple(part.T for part in updated[3:])
    vec_out = adamw(vectors, vec_first, vec_second, vec_sum, 0.3, 0.0)
    return (output, grad_tokens.transpose(2, 0, 1), *rows_out, *down_out, *vec_out)


def solution(mesh):
    placed = (
        P("ctx", "fsdp", None),
        P("ctx", "fsdp", None),
        P("fsdp"),
        P("fsdp", None),
        P("fsdp", None),
        P("fsdp", None),
        P(None, "fsdp"),
        P(None, "fsdp"),
        P(None, "fsdp"),
        P(None, "fsdp"),
        P(None, "fsdp"),
        P(None, "fsdp"),
    )
    return jax.shard_map(
        functools.partial(body, mesh.shape["ctx"], mesh.shape["fsdp"]),
        mesh=mesh,
        in_specs=placed,
        out_specs=placed[:2] + placed[3:6] + placed[6:9] + placed[9:12],
        check_vma=False,
    )
```
